32 devices in a mesh: groups: 2 (over y), shard: 8 (over z, x), sub: 2 (over core).
Axes of the slice: x: 2, y: 2, z: 4, core: 2. Of those that a mesh axis runs over, the one named last changes fastest.
Arguments:
- embeddings: bfloat16 [4096, 1024], P(('groups', 'shard', 'sub')), parts along dimension 0, may hold values from -24 to 24
- cluster_id: int32 [4096], P(('groups', 'shard', 'sub')), parts along dimension 0, may hold values from 0 to 255, as said below
- item_order: int32 [4096], P(('groups', 'shard', 'sub')), parts along dimension 0, may hold values from 0 to 2047, each once
- owner_map: int32 [512], P('groups'), parts along dimension 0, may hold values from 0 to 7, as said below
Outputs:
- max_cosine: float32 [4096], P(('groups', 'shard', 'sub')), parts along dimension 0
- centroid_dist: float32 [4096], P(('groups', 'shard', 'sub')), parts along dimension 0
- cluster_cohesion: float32 [512], P(('groups', 'shard')), parts along dimension 0
The draws below stay inside these ranges and needn't reach their ends.
There are 2 independent parts, one for each index of `groups`. The reference program is written for one: setup_inputs(seed, part) draws one part's arguments, and reference() takes and returns one part's arrays. A program takes and returns all parts, laid end to end along the dimension named above; each array names one. Nothing has to cross between parts.
Inputs may be any that keep to these rules, and one draw needn't show every extreme that they name: `cluster_id`: among the rows of one device, at most 32 name clusters of one owner index (owner_map of the cluster); in every draw some owner index gets exactly 32 rows from every device. `owner_map`: every owner index holds exactly 32 clusters.
All inputs are finite; a program needn't handle non-finite values.
Results may differ from the reference program's by a relative error of at most 0.0015.
Values may be sent and summed in bfloat16 or wider, within the bound.
No kernel may reach another device: no remote copies, remote signals or barrier semaphores. Data moves between devices by JAX's collectives and lax.ppermute only.
A program may use at most 64 MiB of HBM per device.

```python
import math
import jax
import jax.numpy as jnp
from jax import lax

D = 1024
CLUS_DEV = 32
ROW_DEV = 128
CAP = 32
CLUSTERS = 256
ROWS = 2048
N_SHARD = 8
N_SUB = 2


def cluster_layout(key):
    owners = CLUSTERS // CLUS_DEV
    blocks = ROWS // ROW_DEV
    slot_summary = owners * CAP
    shuffled = jax.random.permutation(jax.random.fold_in(key, 101), CLUSTERS).astype(jnp.int32)
    owner_map = jnp.zeros((CLUSTERS,), jnp.int32).at[shuffled].set(jnp.arange(CLUSTERS, dtype=jnp.int32) // CLUS_DEV)
    warmth_sqrt = jax.random.randint(jax.random.fold_in(key, 102), (owners,), 0, 64)
    normalized_heat = warmth_sqrt * warmth_sqrt
    mandatory_pick = jax.random.randint(jax.random.fold_in(key, 103), (), 0, owners)
    perturbed_draw = jax.random.randint(jax.random.fold_in(key, 104), (blocks, slot_summary), 0, 4096)
    slot_flag = jnp.arange(slot_summary, dtype=jnp.int32)
    flag_store = slot_flag // CAP
    increment_weight = jnp.where(flag_store == mandatory_pick, 1 << 26, 0)
    slot_merit = (perturbed_draw + normalized_heat[flag_store][None, :]) * slot_summary + slot_flag[None, :] + increment_weight[None, :]
    chosen = lax.top_k(slot_merit, ROW_DEV)[1]
    pick_owner = chosen // CAP
    first = jax.random.randint(jax.random.fold_in(key, 105), (blocks, ROW_DEV), 0, CLUS_DEV)
    second = jax.random.randint(jax.random.fold_in(key, 106), (blocks, ROW_DEV), 0, CLUS_DEV)
    within = jnp.minimum(first, second)
    cluster = shuffled[pick_owner * CLUS_DEV + within]
    order_score = jax.random.randint(jax.random.fold_in(key, 107), (blocks, ROW_DEV), 0, 1 << 16) * ROW_DEV + jnp.arange(ROW_DEV, dtype=jnp.int32)[None, :]
    placing = jnp.argsort(order_score, axis=1)
    cluster = jnp.take_along_axis(cluster, placing, axis=1)
    return (owner_map, cluster.reshape(ROWS).astype(jnp.int32))


def draw_cluster_id(key, part):
    shared = cluster_layout(key)
    return shared[1]


def draw_owner_map(key, part):
    shared = cluster_layout(key)
    return shared[0]


def draw_embeddings(key, part):
    shared = cluster_layout(key)
    cluster = shared[1]
    key = jax.random.fold_in(key, 3)
    centers = jax.random.truncated_normal(jax.random.fold_in(key, 1), -4.0, 4.0, (CLUSTERS, D), jnp.float32)
    spread = jnp.exp(jax.random.uniform(jax.random.fold_in(key, 2), (ROWS, 1), jnp.float32, math.log(0.3), math.log(3.0)))
    perturbed_draw = jax.random.truncated_normal(jax.random.fold_in(key, 4), -4.0, 4.0, (ROWS, D), jnp.float32)
    row_scale = jnp.exp(jax.random.uniform(jax.random.fold_in(key, 5), (ROWS, 1), jnp.float32, math.log(0.5), math.log(5.0)))
    drawn = (centers[cluster] + spread * perturbed_draw) * row_scale
    return jnp.clip(drawn, -24.0, 24.0).astype(jnp.bfloat16)


def setup_inputs(seed: int = 0, part: int = 0) -> dict:
    key_of = jax.random.split(jax.random.key(seed), 5)
    part_splits = jax.random.split(jax.random.fold_in(key_of[4], part), 5)
    return {
        "embeddings": draw_embeddings(jax.random.fold_in(jax.random.fold_in(key_of[4], part), 71), part),
        "cluster_id": draw_cluster_id(jax.random.fold_in(jax.random.fold_in(key_of[4], part), 71), part),
        "item_order": jax.random.permutation(part_splits[2], ROWS).astype(jnp.int32),
        "owner_map": draw_owner_map(jax.random.fold_in(jax.random.fold_in(key_of[4], part), 71), part),
    }


def reference(embeddings, cluster_id, item_order, owner_map):
    values = embeddings.astype(jnp.float32)
    mean_sq = lax.optimization_barrier(jnp.mean(values * values, axis=1, keepdims=True))
    unit_rows = (values * lax.rsqrt(D * (mean_sq + 1e-06))).astype(jnp.bfloat16)
    unit_float = unit_rows.astype(jnp.float32)
    cluster_sums = jax.ops.segment_sum(unit_float, cluster_id, num_segments=CLUSTERS)
    counts = jax.ops.segment_sum(jnp.ones((ROWS,), jnp.float32), cluster_id, num_segments=CLUSTERS)
    centroid = cluster_sums / jnp.maximum(counts, 1.0)[:, None]
    owned = jnp.argsort(owner_map * CLUSTERS + jnp.arange(CLUSTERS, dtype=jnp.int32)).astype(jnp.int32)
    cohesion = lax.optimization_barrier(jnp.sum(centroid * centroid, axis=1))[owned]
    sort_key = cluster_id * ROWS + item_order
    sorted_order = jnp.argsort(sort_key).astype(jnp.int32)
    sorted_units = unit_rows[sorted_order]
    sorted_keys = sort_key[sorted_order]
    window = N_SHARD * N_SUB * CAP
    block_rows = 512
    padded_units = jnp.concatenate([jnp.zeros((window, D), unit_rows.dtype), sorted_units])
    padded_keys = jnp.concatenate([jnp.full((window,), -1, jnp.int32), sorted_keys])

    def one_block(block_index):
        offset = block_index * block_rows
        query = lax.dynamic_slice_in_dim(sorted_units, offset, block_rows)
        query_keys = lax.dynamic_slice_in_dim(sorted_keys, offset, block_rows)
        near_rows = lax.dynamic_slice_in_dim(padded_units, offset, window + block_rows)
        near_keys = lax.dynamic_slice_in_dim(padded_keys, offset, window + block_rows)
        scores = jnp.dot(query, near_rows.T, preferred_element_type=jnp.float32)
        earlier = (near_keys[None, :] // ROWS == query_keys[:, None] // ROWS) & (near_keys[None, :] < query_keys[:, None])
        best_cos = lax.optimization_barrier(jnp.max(jnp.where(earlier, scores, -3.0), axis=1))
        best_cos = jnp.where(best_cos > -2.0, best_cos, 0.0)
        centre_rows = centroid[query_keys // ROWS]
        offset_rows = query.astype(jnp.float32) - centre_rows
        return (best_cos, lax.optimization_barrier(jnp.sum(offset_rows * offset_rows, axis=1)))
    block_best, block_distance = lax.map(one_block, jnp.arange(ROWS // block_rows, dtype=jnp.int32))
    max_cosine = jnp.zeros((ROWS,), block_best.dtype).at[sorted_order].set(block_best.reshape(ROWS))
    centroid_dist = jnp.zeros((ROWS,), block_distance.dtype).at[sorted_order].set(block_distance.reshape(ROWS))
    return (max_cosine, centroid_dist, cohesion)
```

```python
import functools

import jax
import jax.numpy as jnp
from jax import lax
from jax.experimental import pallas as pl
from jax.experimental.pallas import tpu as pltpu
from jax.sharding import PartitionSpec as P

VMEM = pltpu.VMEM
GATHER_BYTES = 8 << 20


def normalize(embeddings):
    values = embeddings.astype(jnp.float32)
    mean_sq = jnp.mean(values * values, axis=1, keepdims=True)
    return (values * lax.rsqrt(embeddings.shape[1] * (mean_sq + 1e-06))).astype(jnp.bfloat16)


def as_column(row):
    return jnp.transpose(jnp.broadcast_to(row, (128, row.shape[1])))[:, :1]


def ranked(hot):
    at = [lax.broadcasted_iota(jnp.int32, (128, 128), d) for d in (0, 1)]
    upto = (at[0] <= at[1]).astype(jnp.bfloat16)
    before, parts = jnp.zeros((1, 1), jnp.float32), []
    for start in range(0, hot.shape[1], 128):
        piece = hot[:, start : start + 128]
        count = jnp.dot(
            jnp.broadcast_to(piece, (16, 128)).astype(jnp.bfloat16),
            upto,
            preferred_element_type=jnp.float32,
        )[:1]
        parts.append(count + before)
        before = before + jnp.sum(piece, axis=1, keepdims=True)
    return jnp.concatenate(parts, axis=1)


def window_kernel(
    rows_all, clus_dev, owner_ref, map_ref, qkey_ref, qlow_ref, key_ref, query_ref, rows_ref,
    best_ref, dist_ref, cohesion_ref,
):
    queries = query_ref.shape[0]
    keys = key_ref[...]
    query = query_ref[...]
    rows = rows_ref[...]
    hot = (map_ref[...] == owner_ref[0]).astype(jnp.float32)
    rank = ranked(hot)
    width = hot.shape[1]
    kth = lax.broadcasted_iota(jnp.int32, (clus_dev, width), 0).astype(jnp.float32) + 1.0
    name = lax.broadcasted_iota(jnp.int32, (clus_dev, width), 1).astype(jnp.float32)
    own = jnp.sum(jnp.where((rank == kth) & (hot > 0.0), name, 0.0), axis=1, keepdims=True)
    low = as_column(qlow_ref[...])
    lows = jnp.concatenate([low, own.astype(jnp.int32) * rows_all], axis=0)
    above = keys >= lows
    member = (above & (keys < lows + rows_all)).astype(jnp.float32)
    counts = jnp.sum(member, axis=1, keepdims=True)
    sums = jnp.dot(member.astype(jnp.bfloat16), rows, preferred_element_type=jnp.float32)
    centroid = sums * (1.0 / jnp.maximum(counts, 1.0))
    scores = lax.dot_general(
        query, rows, (((1,), (1,)), ((), ())), preferred_element_type=jnp.float32
    )
    earlier = above[:queries] & (keys < as_column(qkey_ref[...]))
    best = jnp.max(jnp.where(earlier, scores, -3.0), axis=1, keepdims=True)
    best = jnp.where(best > -2.0, best, 0.0)
    offset = query.astype(jnp.float32) - centroid[:queries]
    distance = jnp.sum(offset * offset, axis=1, keepdims=True)
    centre = centroid[queries:]
    cohesion = jnp.sum(centre * centre, axis=1, keepdims=True)
    best_ref[...] = jnp.transpose(jnp.broadcast_to(best, (queries, 128)))[:1]
    dist_ref[...] = jnp.transpose(jnp.broadcast_to(distance, (queries, 128)))[:1]
    cohesion_ref[...] = jnp.transpose(jnp.broadcast_to(cohesion, (clus_dev, 128)))[:1]


def window(owner_index, owner_map, query_keys, query_lows, keys, query, rows, rows_all, clus_dev):
    queries, count, width = query.shape[0], rows.shape[0], rows.shape[1]
    best, distance, cohesion = pl.pallas_call(
        functools.partial(window_kernel, rows_all, clus_dev),
        out_shape=(
            jax.ShapeDtypeStruct((1, queries), jnp.float32),
            jax.ShapeDtypeStruct((1, queries), jnp.float32),
            jax.ShapeDtypeStruct((1, clus_dev), jnp.float32),
        ),
        in_specs=[pl.BlockSpec(memory_space=pltpu.SMEM)]
        + [pl.BlockSpec(memory_space=VMEM)] * 6,
        out_specs=[pl.BlockSpec(memory_space=VMEM)] * 3,
        compiler_params=pltpu.CompilerParams(vmem_limit_bytes=32 << 20),
        cost_estimate=pl.CostEstimate(
            flops=4 * queries * count * width, bytes_accessed=2 * count * width, transcendentals=0
        ),
        name="window",
    )(
        owner_index.reshape(1).astype(jnp.int32),
        owner_map.reshape(1, -1),
        query_keys.reshape(1, -1),
        query_lows.reshape(1, -1),
        keys.reshape(1, -1),
        query,
        rows,
    )
    return best.reshape(queries), distance.reshape(queries), cohesion.reshape(clus_dev)


def gathered(embeddings, cluster_id, item_order, owner_map, rows_all, clus_dev):
    axes = ("shard", "sub")
    low = cluster_id * rows_all
    sort_key = low + item_order
    unit_rows = normalize(embeddings)
    rows = lax.all_gather(unit_rows, axes, axis=0, tiled=True)
    keys = lax.all_gather(sort_key, axes, axis=0, tiled=True)
    return window(
        lax.axis_index("shard"), owner_map, sort_key, low, keys, unit_rows, rows, rows_all, clus_dev
    )


def routed(embeddings, cluster_id, item_order, owner_map, rows_all, clus_dev):
    owners = lax.axis_size("shard")
    local_rows, width = embeddings.shape
    capacity = 2 * local_rows // owners
    slots = owners * capacity
    unit_rows = normalize(embeddings)
    sort_key = cluster_id * rows_all + item_order
    owner_of = owner_map[cluster_id]
    owner_hot = (owner_of[:, None] == jnp.arange(owners, dtype=jnp.int32)[None, :]).astype(jnp.int32)
    rank_within = jnp.sum(owner_hot * (jnp.cumsum(owner_hot, axis=0) - 1), axis=1)
    slot_index = owner_of * capacity + rank_within
    row_buffer = jnp.zeros((slots, width), jnp.bfloat16).at[slot_index].set(unit_rows)
    key_buffer = jnp.full((slots,), -1, jnp.int32).at[slot_index].set(sort_key)
    query = lax.all_to_all(
        row_buffer.reshape(owners, capacity, width), "shard", 0, 0, tiled=True
    ).reshape(slots, width)
    query_keys = lax.all_to_all(
        key_buffer.reshape(owners, capacity), "shard", 0, 0, tiled=True
    ).reshape(slots)
    rows = lax.all_gather(query, "sub", axis=0, tiled=True)
    keys = lax.all_gather(query_keys, "sub", axis=0, tiled=True)
    query_lows = query_keys // rows_all * rows_all
    best, distance, cohesion = window(
        lax.axis_index("shard"), owner_map, query_keys, query_lows, keys, query, rows, rows_all, clus_dev
    )
    results = jnp.stack([best.reshape(owners, capacity), distance.reshape(owners, capacity)])
    returned = lax.all_to_all(results, "shard", 1, 1, tiled=True).reshape(2, slots)
    return returned[0][slot_index], returned[1][slot_index], cohesion


def local(embeddings, cluster_id, item_order, owner_map):
    owners = lax.axis_size("shard")
    local_rows, width = embeddings.shape
    rows_all = local_rows * owners * lax.axis_size("sub")
    clus_dev = owner_map.shape[0] // owners
    plan = gathered if rows_all * width * embeddings.dtype.itemsize <= GATHER_BYTES else routed
    return plan(embeddings, cluster_id, item_order, owner_map, rows_all, clus_dev)


def solution(mesh):
    in_specs = (
        P(("groups", "shard", "sub"), None),
        P(("groups", "shard", "sub")),
        P(("groups", "shard", "sub")),
        P("groups"),
    )
    out_specs = (
        P(("groups", "shard", "sub")),
        P(("groups", "shard", "sub")),
        P(("groups", "shard")),
    )
    return jax.shard_map(local, mesh=mesh, in_specs=in_specs, out_specs=out_specs, check_vma=False)
```

```python
import functools

import jax
import jax.numpy as jnp
from jax import lax
from jax.experimental import pallas as pl
from jax.experimental.pallas import tpu as pltpu
from jax.sharding import PartitionSpec as P

LANES = 128
DIGITS = 3
MOST_PERMUTES = 16
WHOLE = pl.BlockSpec(memory_space=pltpu.VMEM)
SCALAR = pl.BlockSpec(memory_space=pltpu.SMEM)


def iota(shape, dim):
    return lax.broadcasted_iota(jnp.int32, shape, dim)


def as_column(row):
    return jnp.transpose(jnp.broadcast_to(row, (LANES, row.shape[1])))[:, :1]


def as_row(column):
    return jnp.transpose(jnp.broadcast_to(column, (column.shape[0], LANES)))[:1]


def matmul(a, b):
    return jnp.dot(a, b, preferred_element_type=jnp.float32)


def ranked(hot):
    upto = (iota((LANES, LANES), 0) <= iota((LANES, LANES), 1)).astype(jnp.bfloat16)
    before, parts = jnp.zeros((1, 1), jnp.float32), []
    for start in range(0, hot.shape[1], LANES):
        piece = hot[:, start : start + LANES]
        spread = jnp.broadcast_to(piece, (16, LANES)).astype(jnp.bfloat16)
        parts.append(matmul(spread, upto)[:1] + before)
        before = before + jnp.sum(piece, axis=1, keepdims=True)
    return jnp.concatenate(parts, axis=1)


def pack_kernel(
    rows_all, owners, capacity, me_ref, map_ref, cluster_ref, order_ref, embed_ref, slot_ref, *out_refs
):
    rows, width = embed_ref.shape
    values = embed_ref[...].astype(jnp.float32)
    mean_sq = jnp.sum(values * values, axis=1, keepdims=True) * (1.0 / width)
    unit = (values * lax.rsqrt(width * (mean_sq + 1e-06))).astype(jnp.bfloat16)

    cluster = as_column(cluster_ref[...])
    clusters = map_ref.shape[1]
    named = cluster == iota((rows, clusters), 1)
    owner = jnp.sum(jnp.where(named, map_ref[...], 0).astype(jnp.float32), axis=1, keepdims=True)
    owner = owner.astype(jnp.int32)
    hot = (owner == iota((rows, max(owners, LANES)), 1)).astype(jnp.float32)
    upto = (iota((rows, rows), 1) <= iota((rows, rows), 0)).astype(jnp.bfloat16)
    rank = jnp.sum(hot * matmul(upto, hot.astype(jnp.bfloat16)), axis=1, keepdims=True) - 1.0
    slot = as_row((owner ^ me_ref[0]) * capacity + rank.astype(jnp.int32))
    slot_ref[...] = slot

    lane = iota((rows, LANES), 1)
    digit = jnp.zeros((rows, LANES), jnp.int32)
    for first, number in ((0, cluster + 1), (DIGITS, as_column(order_ref[...]))):
        for place in range(DIGITS):
            digit = jnp.where(lane == first + place, (number >> (8 * place)) & 255, digit)
    digit = digit.astype(jnp.float32).astype(jnp.bfloat16)

    slots = owners * capacity
    move = (iota((slots, rows), 0) == slot).astype(jnp.float32).astype(jnp.bfloat16)
    moved = matmul(move, unit).astype(jnp.bfloat16)
    moved_digit = matmul(move, digit).astype(jnp.bfloat16)
    each = slots // len(out_refs)
    for index, out_ref in enumerate(out_refs):
        part = slice(index * each, (index + 1) * each)
        out_ref[:, :width] = moved[part]
        out_ref[:, width:] = moved_digit[part]


def window_kernel(rows_all, clus_dev, me_ref, map_ref, query_ref, rows_ref, result_ref, cohesion_ref):
    queries = query_ref.shape[0]
    width = query_ref.shape[1] - LANES
    query = query_ref[:, :width]
    rows = rows_ref[:, :width]
    digit = query_ref[:, width:].astype(jnp.float32)
    low, order = (
        sum(digit[:, i + place : i + place + 1] * (256.0**place) for place in range(DIGITS))
        for i in (0, DIGITS)
    )
    low = (low.astype(jnp.int32) - 1) * rows_all
    query_key = low + order.astype(jnp.int32)
    digit = jnp.transpose(rows_ref[:, width:].astype(jnp.float32))
    keys, order = (
        sum(digit[i + place : i + place + 1] * (256.0**place) for place in range(DIGITS))
        for i in (0, DIGITS)
    )
    keys = (keys.astype(jnp.int32) - 1) * rows_all + order.astype(jnp.int32)

    hot = (map_ref[...] == me_ref[0]).astype(jnp.float32)
    rank = ranked(hot)
    shape = (clus_dev, hot.shape[1])
    kth = (rank == iota(shape, 0).astype(jnp.float32) + 1.0) & (hot > 0.0)
    own = jnp.sum(jnp.where(kth, iota(shape, 1).astype(jnp.float32), 0.0), axis=1, keepdims=True)
    lows = jnp.concatenate([low, own.astype(jnp.int32) * rows_all], axis=0)
    above = keys >= lows
    member = (above & (keys < lows + rows_all)).astype(jnp.float32)
    counts = jnp.sum(member, axis=1, keepdims=True)
    centroid = matmul(member.astype(jnp.bfloat16), rows) * (1.0 / jnp.maximum(counts, 1.0))
    scores = lax.dot_general(
        query, rows, (((1,), (1,)), ((), ())), preferred_element_type=jnp.float32
    )
    earlier = above[:queries] & (keys < query_key)
    best = jnp.max(jnp.where(earlier, scores, -3.0), axis=1, keepdims=True)
    best = jnp.where(best > -2.0, best, 0.0)
    offset = query.astype(jnp.float32) - centroid[:queries]
    distance = jnp.sum(offset * offset, axis=1, keepdims=True)
    lane = iota((queries, LANES), 1)
    result_ref[...] = jnp.transpose(jnp.where(lane == 0, best, distance))[: result_ref.shape[0]]
    centre = centroid[queries:]
    cohesion_ref[...] = as_row(jnp.sum(centre * centre, axis=1, keepdims=True))


def pick_kernel(slot_ref, *refs):
    *result_refs, best_ref, distance_ref = refs
    rows = slot_ref.shape[1]
    slots = result_refs[0].shape[1]
    each = slots // len(result_refs)
    part = iota((1, slots), 1) // each
    at = as_column(slot_ref[...]) == iota((rows, slots), 1)
    for line, out_ref in enumerate((best_ref, distance_ref)):
        values = result_refs[0][line : line + 1]
        for index, result_ref in enumerate(result_refs[1:]):
            values = jnp.where(part == index + 1, result_ref[line : line + 1], values)
        out_ref[...] = as_row(jnp.sum(jnp.where(at, values, 0.0), axis=1, keepdims=True))


def local(embeddings, cluster_id, item_order, owner_map):
    owners = lax.axis_size("shard")
    local_rows, width = embeddings.shape
    rows_all = local_rows * owners * lax.axis_size("sub")
    clus_dev = owner_map.shape[0] // owners
    capacity = 2 * local_rows // owners
    slots = owners * capacity
    wide = width + LANES
    params = pltpu.CompilerParams(vmem_limit_bytes=32 << 20)
    direct = owners <= MOST_PERMUTES and owners & (owners - 1) == 0
    me = lax.axis_index("shard").astype(jnp.int32).reshape(1)
    owner_row = owner_map.reshape(1, -1)

    def from_partner(value, k):
        pairs = [(i, i ^ k) for i in range(owners)]
        return lax.ppermute(value, "shard", pairs) if k else value

    parts = owners if direct else 1
    slot, *packed = pl.pallas_call(
        functools.partial(pack_kernel, rows_all, owners, capacity),
        out_shape=[jax.ShapeDtypeStruct((1, local_rows), jnp.int32)]
        + [jax.ShapeDtypeStruct((slots // parts, wide), jnp.bfloat16)] * parts,
        in_specs=[SCALAR] + [WHOLE] * 4,
        out_specs=[WHOLE] * (1 + parts),
        compiler_params=params,
        name="pack",
    )(
        me if direct else jnp.zeros_like(me),
        owner_row,
        cluster_id.reshape(1, -1),
        item_order.reshape(1, -1),
        embeddings,
    )
    if direct:
        query = jnp.concatenate([from_partner(block, k) for k, block in enumerate(packed)])
    else:
        query = lax.all_to_all(
            packed[0].reshape(owners, capacity, wide), "shard", 0, 0, tiled=True
        ).reshape(slots, wide)
    rows = lax.all_gather(query, "sub", axis=0, tiled=True)

    results, cohesion = pl.pallas_call(
        functools.partial(window_kernel, rows_all, clus_dev),
        out_shape=[
            jax.ShapeDtypeStruct((2, slots), jnp.float32),
            jax.ShapeDtypeStruct((1, clus_dev), jnp.float32),
        ],
        in_specs=[SCALAR] + [WHOLE] * 3,
        out_specs=[WHOLE] * 2,
        compiler_params=params,
        name="window",
    )(me, owner_row, query, rows)

    if direct:
        returned = [from_partner(results, k) for k in range(owners)]
    else:
        returned = [
            lax.all_to_all(
                results.reshape(2, owners, capacity), "shard", 1, 1, tiled=True
            ).reshape(2, slots)
        ]
    best, distance = pl.pallas_call(
        pick_kernel,
        out_shape=[jax.ShapeDtypeStruct((1, local_rows), jnp.float32)] * 2,
        in_specs=[WHOLE] * (1 + len(returned)),
        out_specs=[WHOLE] * 2,
        compiler_params=params,
        name="pick",
    )(slot, *returned)
    return best.reshape(local_rows), distance.reshape(local_rows), cohesion.reshape(clus_dev)


def solution(mesh):
    in_specs = (
        P(("groups", "shard", "sub"), None),
        P(("groups", "shard", "sub")),
        P(("groups", "shard", "sub")),
        P("groups"),
    )
    out_specs = (
        P(("groups", "shard", "sub")),
        P(("groups", "shard", "sub")),
        P(("groups", "shard")),
    )
    return jax.shard_map(local, mesh=mesh, in_specs=in_specs, out_specs=out_specs, check_vma=False)
```

```python
import functools

import jax
import jax.numpy as jnp
from jax import lax
from jax.experimental import pallas as pl
from jax.experimental.pallas import tpu as pltpu
from jax.sharding import PartitionSpec as P

LANES = 128
DIGITS = 3
SCALAR = pl.BlockSpec(memory_space=pltpu.SMEM)


def iota(shape, dim):
    return lax.broadcasted_iota(jnp.int32, shape, dim)


def as_column(row):
    return jnp.transpose(jnp.broadcast_to(row, (LANES, row.shape[1])))[:, :1]


def as_row(column):
    return jnp.transpose(jnp.broadcast_to(column, (column.shape[0], LANES)))[:1]


def matmul(a, b):
    return jnp.dot(a, b, preferred_element_type=jnp.float32)


def ranked(hot):
    upto = (iota((LANES, LANES), 0) <= iota((LANES, LANES), 1)).astype(jnp.bfloat16)
    before, parts = jnp.zeros((1, 1), jnp.float32), []
    for start in range(0, hot.shape[1], LANES):
        piece = hot[:, start : start + LANES]
        spread = jnp.broadcast_to(piece, (16, LANES)).astype(jnp.bfloat16)
        parts.append(matmul(spread, upto)[:1] + before)
        before = before + jnp.sum(piece, axis=1, keepdims=True)
    return jnp.concatenate(parts, axis=1)


def call(kernel, out_shape, name, *operands):
    def whole(x):
        return pl.BlockSpec(x.shape, lambda i: (0,) * len(x.shape))

    return pl.pallas_call(
        kernel,
        grid=(1,),
        out_shape=out_shape,
        in_specs=[SCALAR] + [whole(x) for x in operands[1:]],
        out_specs=[whole(x) for x in out_shape],
        compiler_params=pltpu.CompilerParams(vmem_limit_bytes=32 << 20),
        name=name,
    )(*operands)


def pack_kernel(
    rows_all, owners, capacity, me_ref, map_ref, cluster_ref, order_ref, embed_ref, slot_ref, packed_ref
):
    rows, width = embed_ref.shape
    values = embed_ref[...].astype(jnp.float32)
    mean_sq = jnp.sum(values * values, axis=1, keepdims=True) * (1.0 / width)
    unit = (values * lax.rsqrt(width * (mean_sq + 1e-06))).astype(jnp.bfloat16)

    cluster = as_column(cluster_ref[...])
    clusters = map_ref.shape[1]
    named = cluster == iota((rows, clusters), 1)
    owner = jnp.sum(jnp.where(named, map_ref[...], 0).astype(jnp.float32), axis=1, keepdims=True)
    owner = owner.astype(jnp.int32)
    hot = (owner == iota((rows, max(owners, LANES)), 1)).astype(jnp.float32)
    upto = (iota((rows, rows), 1) <= iota((rows, rows), 0)).astype(jnp.bfloat16)
    rank = jnp.sum(hot * matmul(upto, hot.astype(jnp.bfloat16)), axis=1, keepdims=True) - 1.0
    slot = as_row(owner * capacity + rank.astype(jnp.int32))
    slot_ref[...] = slot

    lane = iota((rows, LANES), 1)
    digit = jnp.zeros((rows, LANES), jnp.int32)
    for first, number in ((0, cluster + 1), (DIGITS, as_column(order_ref[...]))):
        for place in range(DIGITS):
            digit = jnp.where(lane == first + place, (number >> (8 * place)) & 255, digit)
    digit = digit.astype(jnp.float32).astype(jnp.bfloat16)

    slots = owners * capacity
    move = (iota((slots, rows), 0) == slot).astype(jnp.float32).astype(jnp.bfloat16)
    packed_ref[:, :width] = matmul(move, unit).astype(jnp.bfloat16)
    packed_ref[:, width:] = matmul(move, digit).astype(jnp.bfloat16)


def window_kernel(rows_all, clus_dev, me_ref, map_ref, query_ref, other_ref, result_ref, cohesion_ref):
    queries = query_ref.shape[0]
    width = query_ref.shape[1] - LANES
    query = query_ref[:, :width]

    def numbers(take):
        return (
            sum(take(i + place) * (256.0**place) for place in range(DIGITS)).astype(jnp.int32)
            for i in (0, DIGITS)
        )

    hot = (map_ref[...] == me_ref[0]).astype(jnp.float32)
    rank = ranked(hot)
    shape = (clus_dev, hot.shape[1])
    kth = (rank == iota(shape, 0).astype(jnp.float32) + 1.0) & (hot > 0.0)
    own = jnp.sum(jnp.where(kth, iota(shape, 1).astype(jnp.float32), 0.0), axis=1, keepdims=True)
    digit = query_ref[:, width:].astype(jnp.float32)
    name, order = numbers(lambda i: digit[:, i : i + 1])
    low = (name - 1) * rows_all
    query_key = low + order
    lows = jnp.concatenate([low, own.astype(jnp.int32) * rows_all], axis=0)

    best, counts, sums = None, None, None
    for rows_ref in (query_ref, other_ref):
        rows = rows_ref[:, :width]
        across = jnp.transpose(rows_ref[:, width:].astype(jnp.float32))
        name, order = numbers(lambda i: across[i : i + 1])
        keys = (name - 1) * rows_all + order
        above = keys >= lows
        member = (above & (keys < lows + rows_all)).astype(jnp.float32)
        count = jnp.sum(member, axis=1, keepdims=True)
        total = matmul(member.astype(jnp.bfloat16), rows)
        scores = lax.dot_general(
            query, rows, (((1,), (1,)), ((), ())), preferred_element_type=jnp.float32
        )
        earlier = above[:queries] & (keys < query_key)
        most = jnp.max(jnp.where(earlier, scores, -3.0), axis=1, keepdims=True)
        best = most if best is None else jnp.maximum(best, most)
        counts = count if counts is None else counts + count
        sums = total if sums is None else sums + total
    centroid = sums * (1.0 / jnp.maximum(counts, 1.0))
    best = jnp.where(best > -2.0, best, 0.0)
    offset = query.astype(jnp.float32) - centroid[:queries]
    distance = jnp.sum(offset * offset, axis=1, keepdims=True)
    lane = iota((queries, LANES), 1)
    result = jnp.transpose(jnp.where(lane == 0, best, distance))[: result_ref.shape[1]]
    for owner in range(result_ref.shape[0]):
        result_ref[owner] = result
    centre = centroid[queries:]
    cohesion_ref[...] = as_row(jnp.sum(centre * centre, axis=1, keepdims=True))


def pick_kernel(capacity, me_ref, slot_ref, result_ref, best_ref, distance_ref):
    rows = slot_ref.shape[1]
    owners, _, slots = result_ref.shape
    slot = as_column(slot_ref[...])
    best = jnp.zeros((rows, slots), jnp.float32)
    distance = jnp.zeros((rows, slots), jnp.float32)
    for owner in range(owners):
        shift = (me_ref[0] - owner) * capacity
        first = owner * capacity
        lane = jnp.where((slot >= first) & (slot < first + capacity), slot + shift, -1)
        at = lane == iota((rows, slots), 1)
        best = jnp.where(at, result_ref[owner, 0:1], best)
        distance = jnp.where(at, result_ref[owner, 1:2], distance)
    best_ref[...] = as_row(jnp.sum(best, axis=1, keepdims=True))
    distance_ref[...] = as_row(jnp.sum(distance, axis=1, keepdims=True))


def local(embeddings, cluster_id, item_order, owner_map):
    owners = lax.axis_size("shard")
    local_rows, width = embeddings.shape
    rows_all = local_rows * owners * lax.axis_size("sub")
    clus_dev = owner_map.shape[0] // owners
    capacity = 2 * local_rows // owners
    slots = owners * capacity
    wide = width + LANES
    me = lax.axis_index("shard").astype(jnp.int32).reshape(1)
    owner_row = owner_map.reshape(1, -1)

    slot, packed = call(
        functools.partial(pack_kernel, rows_all, owners, capacity),
        [
            jax.ShapeDtypeStruct((1, local_rows), jnp.int32),
            jax.ShapeDtypeStruct((slots, wide), jnp.bfloat16),
        ],
        "pack",
        me,
        owner_row,
        cluster_id.reshape(1, -1),
        item_order.reshape(1, -1),
        embeddings,
    )
    query = lax.all_to_all(
        packed.reshape(owners, capacity, wide), "shard", 0, 0, tiled=True
    ).reshape(slots, wide)
    other = lax.ppermute(query, "sub", [(0, 1), (1, 0)])
    results, cohesion = call(
        functools.partial(window_kernel, rows_all, clus_dev),
        [
            jax.ShapeDtypeStruct((owners, 2, slots), jnp.float32),
            jax.ShapeDtypeStruct((1, clus_dev), jnp.float32),
        ],
        "window",
        me,
        owner_row,
        query,
        other,
    )
    returned = lax.all_to_all(results, "shard", 0, 0, tiled=True)
    best, distance = call(
        functools.partial(pick_kernel, capacity),
        [jax.ShapeDtypeStruct((1, local_rows), jnp.float32)] * 2,
        "pick",
        me,
        slot,
        returned,
    )
    return best.reshape(local_rows), distance.reshape(local_rows), cohesion.reshape(clus_dev)


def solution(mesh):
    in_specs = (
        P(("groups", "shard", "sub"), None),
        P(("groups", "shard", "sub")),
        P(("groups", "shard", "sub")),
        P("groups"),
    )
    out_specs = (
        P(("groups", "shard", "sub")),
        P(("groups", "shard", "sub")),
        P(("groups", "shard")),
    )
    return jax.shard_map(local, mesh=mesh, in_specs=in_specs, out_specs=out_specs, check_vma=False)
```

```python
import functools

import jax
import jax.numpy as jnp
from jax import lax
from jax.experimental import pallas as pl
from jax.experimental.pallas import tpu as pltpu
from jax.sharding import PartitionSpec as P

LANES = 128
DIGITS = 3
MOST_PERMUTES = 16
WHOLE = pl.BlockSpec(memory_space=pltpu.VMEM)
SCALAR = pl.BlockSpec(memory_space=pltpu.SMEM)
HBM = pl.BlockSpec(memory_space=pltpu.HBM)


def iota(shape, dim):
    return lax.broadcasted_iota(jnp.int32, shape, dim)


def as_column(row):
    return jnp.transpose(jnp.broadcast_to(row, (LANES, row.shape[1])))[:, :1]


def as_row(column):
    return jnp.transpose(jnp.broadcast_to(column, (column.shape[0], LANES)))[:1]


def matmul(a, b):
    return jnp.dot(a, b, preferred_element_type=jnp.float32)


def ranked(hot):
    upto = (iota((LANES, LANES), 0) <= iota((LANES, LANES), 1)).astype(jnp.bfloat16)
    before, parts = jnp.zeros((1, 1), jnp.float32), []
    for start in range(0, hot.shape[1], LANES):
        piece = hot[:, start : start + LANES]
        spread = jnp.broadcast_to(piece, (16, LANES)).astype(jnp.bfloat16)
        parts.append(matmul(spread, upto)[:1] + before)
        before = before + jnp.sum(piece, axis=1, keepdims=True)
    return jnp.concatenate(parts, axis=1)


def pack_kernel(rows_all, owners, capacity, order, *refs):
    me_ref, *sources = refs[:5]
    slot_ref, *out_refs = refs[5:-5]
    *held, sems = refs[-5:]
    copies = [
        pltpu.make_async_copy(source, target, sems.at[i])
        for i, (source, target) in enumerate(zip(sources, held))
    ]
    for copy in copies:
        copy.start()
    map_ref, cluster_ref, order_ref, embed_ref = held
    rows, width = embed_ref.shape
    for copy in copies[:3]:
        copy.wait()

    cluster = as_column(cluster_ref[...])
    clusters = map_ref.shape[1]
    named = cluster == iota((rows, clusters), 1)
    owner = jnp.sum(jnp.where(named, map_ref[...], 0).astype(jnp.float32), axis=1, keepdims=True)
    owner = owner.astype(jnp.int32)
    hot = (owner == iota((rows, max(owners, LANES)), 1)).astype(jnp.float32)
    upto = (iota((rows, rows), 1) <= iota((rows, rows), 0)).astype(jnp.bfloat16)
    rank = jnp.sum(hot * matmul(upto, hot.astype(jnp.bfloat16)), axis=1, keepdims=True) - 1.0
    partner = owner ^ me_ref[0]
    place = partner
    for index, k in enumerate(order):
        place = jnp.where(partner == k, index, place)
    slot = as_row(place * capacity + rank.astype(jnp.int32))
    slot_ref[...] = slot
    slots = owners * capacity
    move = (iota((slots, rows), 0) == slot).astype(jnp.float32).astype(jnp.bfloat16)

    lane = iota((rows, LANES), 1)
    digit = jnp.zeros((rows, LANES), jnp.int32)
    for first, number in ((0, cluster + 1), (DIGITS, as_column(order_ref[...]))):
        for place in range(DIGITS):
            digit = jnp.where(lane == first + place, (number >> (8 * place)) & 255, digit)
    digit = digit.astype(jnp.float32).astype(jnp.bfloat16)
    moved_digit = matmul(move, digit).astype(jnp.bfloat16)

    copies[3].wait()
    values = embed_ref[...].astype(jnp.float32)
    mean_sq = jnp.sum(values * values, axis=1, keepdims=True) * (1.0 / width)
    unit = (values * lax.rsqrt(width * (mean_sq + 1e-06))).astype(jnp.bfloat16)
    moved = matmul(move, unit).astype(jnp.bfloat16)
    each = slots // len(out_refs)
    for index, out_ref in enumerate(out_refs):
        part = slice(index * each, (index + 1) * each)
        out_ref[:, :width] = moved[part]
        out_ref[:, width:] = moved_digit[part]


def window_kernel(rows_all, clus_dev, me_ref, map_ref, query_ref, other_ref, result_ref, cohesion_ref):
    queries = query_ref.shape[0]
    width = query_ref.shape[1] - LANES
    query = query_ref[:, :width]

    def numbers(take):
        return (
            sum(take(i + place) * (256.0**place) for place in range(DIGITS)).astype(jnp.int32)
            for i in (0, DIGITS)
        )

    hot = (map_ref[...] == me_ref[0]).astype(jnp.float32)
    rank = ranked(hot)
    shape = (clus_dev, hot.shape[1])
    kth = (rank == iota(shape, 0).astype(jnp.float32) + 1.0) & (hot > 0.0)
    own = jnp.sum(jnp.where(kth, iota(shape, 1).astype(jnp.float32), 0.0), axis=1, keepdims=True)
    digit = query_ref[:, width:].astype(jnp.float32)
    name, order = numbers(lambda i: digit[:, i : i + 1])
    low = (name - 1) * rows_all
    query_key = low + order
    lows = jnp.concatenate([low, own.astype(jnp.int32) * rows_all], axis=0)

    best, counts, sums = None, None, None
    for rows_ref in (query_ref, other_ref):
        rows = rows_ref[:, :width]
        across = jnp.transpose(rows_ref[:, width:].astype(jnp.float32))
        name, order = numbers(lambda i: across[i : i + 1])
        keys = (name - 1) * rows_all + order
        above = keys >= lows
        member = (above & (keys < lows + rows_all)).astype(jnp.float32)
        count = jnp.sum(member, axis=1, keepdims=True)
        total = matmul(member.astype(jnp.bfloat16), rows)
        scores = lax.dot_general(
            query, rows, (((1,), (1,)), ((), ())), preferred_element_type=jnp.float32
        )
        earlier = above[:queries] & (keys < query_key)
        most = jnp.max(jnp.where(earlier, scores, -3.0), axis=1, keepdims=True)
        best = most if best is None else jnp.maximum(best, most)
        counts = count if counts is None else counts + count
        sums = total if sums is None else sums + total
    centroid = sums * (1.0 / jnp.maximum(counts, 1.0))
    best = jnp.where(best > -2.0, best, 0.0)
    offset = query.astype(jnp.float32) - centroid[:queries]
    distance = jnp.sum(offset * offset, axis=1, keepdims=True)
    lane = iota((queries, LANES), 1)
    result_ref[0] = jnp.transpose(jnp.where(lane == 0, best, distance))[: result_ref.shape[1]]
    centre = centroid[queries:]
    cohesion_ref[...] = as_row(jnp.sum(centre * centre, axis=1, keepdims=True))


def pick_kernel(order, slot_ref, result_ref, best_ref, distance_ref):
    rows = slot_ref.shape[1]
    owners, _, slots = result_ref.shape
    place = iota((1, slots), 1) // (slots // owners)
    at = as_column(slot_ref[...]) == iota((rows, slots), 1)
    for line, out_ref in enumerate((best_ref, distance_ref)):
        values = result_ref[0, line : line + 1]
        for k in range(1, owners):
            values = jnp.where(place == order.index(k), result_ref[k, line : line + 1], values)
        out_ref[...] = as_row(jnp.sum(jnp.where(at, values, 0.0), axis=1, keepdims=True))


def from_partner(value, k, axis):
    return lax.ppermute(value, axis, [(i, i ^ k) for i in range(lax.axis_size(axis))])


def exchange(blocks, order, me):
    if len(blocks) > 1:
        return jnp.concatenate(
            [from_partner(block, k, "shard") if k else block for k, block in zip(order, blocks)]
        )
    owners = lax.axis_size("shard")
    partner = me ^ jnp.array(order, jnp.int32)
    place = jnp.argsort(partner)
    parted = blocks[0].reshape(owners, -1, blocks[0].shape[1])
    got = lax.all_to_all(parted[place], "shard", 0, 0, tiled=True)
    return got[partner].reshape(blocks[0].shape)


def partner_order(owners):
    half = owners // 2
    near, far = list(range(1, half)), list(range(half, owners))
    return [0] + far[:1] + near[:1] + far[1:] + near[1:]


def local(embeddings, cluster_id, item_order, owner_map):
    owners = lax.axis_size("shard")
    local_rows, width = embeddings.shape
    rows_all = local_rows * owners * lax.axis_size("sub")
    clus_dev = owner_map.shape[0] // owners
    capacity = 2 * local_rows // owners
    slots = owners * capacity
    wide = width + LANES
    params = pltpu.CompilerParams(vmem_limit_bytes=32 << 20)
    me = lax.axis_index("shard").astype(jnp.int32).reshape(1)
    owner_row = owner_map.reshape(1, -1)

    order = partner_order(owners)
    parts = owners if owners <= MOST_PERMUTES else 1
    sources = (owner_row, cluster_id.reshape(1, -1), item_order.reshape(1, -1), embeddings)
    slot, *packed = pl.pallas_call(
        functools.partial(pack_kernel, rows_all, owners, capacity, order),
        out_shape=[jax.ShapeDtypeStruct((1, local_rows), jnp.int32)]
        + [jax.ShapeDtypeStruct((slots // parts, wide), jnp.bfloat16)] * parts,
        in_specs=[SCALAR] + [HBM] * 4,
        out_specs=[WHOLE] * (1 + parts),
        scratch_shapes=[pltpu.VMEM(x.shape, x.dtype) for x in sources]
        + [pltpu.SemaphoreType.DMA((4,))],
        compiler_params=params,
        name="pack",
    )(me, *sources)
    query = exchange(packed, order, me)
    other = from_partner(query, 1, "sub")
    results, cohesion = pl.pallas_call(
        functools.partial(window_kernel, rows_all, clus_dev),
        out_shape=[
            jax.ShapeDtypeStruct((1, 2, slots), jnp.float32),
            jax.ShapeDtypeStruct((1, clus_dev), jnp.float32),
        ],
        in_specs=[SCALAR] + [WHOLE] * 3,
        out_specs=[WHOLE] * 2,
        compiler_params=params,
        name="window",
    )(me, owner_row, query, other)
    k = 1
    while k < owners:
        results = jnp.concatenate([results, from_partner(results, k, "shard")])
        k *= 2
    best, distance = pl.pallas_call(
        functools.partial(pick_kernel, order),
        out_shape=[jax.ShapeDtypeStruct((1, local_rows), jnp.float32)] * 2,
        in_specs=[WHOLE] * 2,
        out_specs=[WHOLE] * 2,
        compiler_params=params,
        name="pick",
    )(slot, results)
    return best.reshape(local_rows), distance.reshape(local_rows), cohesion.reshape(clus_dev)


def solution(mesh):
    in_specs = (
        P(("groups", "shard", "sub"), None),
        P(("groups", "shard", "sub")),
        P(("groups", "shard", "sub")),
        P("groups"),
    )
    out_specs = (
        P(("groups", "shard", "sub")),
        P(("groups", "shard", "sub")),
        P(("groups", "shard")),
    )
    return jax.shard_map(local, mesh=mesh, in_specs=in_specs, out_specs=out_specs, check_vma=False)
```

```python
import functools

import jax
import jax.numpy as jnp
from jax import lax
from jax.experimental import pallas as pl
from jax.experimental.pallas import tpu as pltpu
from jax.sharding import PartitionSpec as P

LANES = 128
DIGITS = 3
MOST_PERMUTES = 16
WHOLE = pl.BlockSpec(memory_space=pltpu.VMEM)
SCALAR = pl.BlockSpec(memory_space=pltpu.SMEM)


def iota(shape, dim):
    return lax.broadcasted_iota(jnp.int32, shape, dim)


def as_column(row):
    return jnp.transpose(jnp.broadcast_to(row, (LANES, row.shape[1])))[:, :1]


def as_row(column):
    return jnp.transpose(jnp.broadcast_to(column, (column.shape[0], LANES)))[:1]


def matmul(a, b):
    return jnp.dot(a, b, preferred_element_type=jnp.float32)


def ranked(hot):
    upto = (iota((LANES, LANES), 0) <= iota((LANES, LANES), 1)).astype(jnp.bfloat16)
    before, parts = jnp.zeros((1, 1), jnp.float32), []
    for start in range(0, hot.shape[1], LANES):
        piece = hot[:, start : start + LANES]
        spread = jnp.broadcast_to(piece, (16, LANES)).astype(jnp.bfloat16)
        parts.append(matmul(spread, upto)[:1] + before)
        before = before + jnp.sum(piece, axis=1, keepdims=True)
    return jnp.concatenate(parts, axis=1)


def slot_kernel(
    owners, capacity, order, me_ref, map_ref, cluster_ref, order_ref, slot_ref, digit_ref
):
    rows = cluster_ref.shape[1]
    cluster = as_column(cluster_ref[...])
    named = cluster == iota((rows, map_ref.shape[1]), 1)
    owner = jnp.sum(jnp.where(named, map_ref[...], 0).astype(jnp.float32), axis=1, keepdims=True)
    owner = owner.astype(jnp.int32)
    hot = (owner == iota((rows, max(owners, LANES)), 1)).astype(jnp.float32)
    upto = (iota((rows, rows), 1) <= iota((rows, rows), 0)).astype(jnp.bfloat16)
    rank = jnp.sum(hot * matmul(upto, hot.astype(jnp.bfloat16)), axis=1, keepdims=True) - 1.0
    partner = owner ^ me_ref[0]
    place = partner
    for index, k in enumerate(order):
        place = jnp.where(partner == k, index, place)
    slot_ref[...] = as_row(place * capacity + rank.astype(jnp.int32))

    lane = iota((rows, LANES), 1)
    digit = jnp.zeros((rows, LANES), jnp.int32)
    for first, number in ((0, cluster + 1), (DIGITS, as_column(order_ref[...]))):
        for at in range(DIGITS):
            digit = jnp.where(lane == first + at, (number >> (8 * at)) & 255, digit)
    digit_ref[...] = digit.astype(jnp.float32).astype(jnp.bfloat16)


def pack_kernel(slot_ref, digit_ref, embed_ref, *out_refs):
    rows, width = embed_ref.shape
    each = out_refs[0].shape[0]
    values = embed_ref[...].astype(jnp.float32)
    mean_sq = jnp.sum(values * values, axis=1, keepdims=True) * (1.0 / width)
    unit = (values * lax.rsqrt(width * (mean_sq + 1e-06))).astype(jnp.bfloat16)
    slots = each * len(out_refs)
    move = (iota((slots, rows), 0) == slot_ref[...]).astype(jnp.float32).astype(jnp.bfloat16)
    moved = matmul(move, unit).astype(jnp.bfloat16)
    moved_digit = matmul(move, digit_ref[...]).astype(jnp.bfloat16)
    for index, out_ref in enumerate(out_refs):
        part = slice(index * each, (index + 1) * each)
        out_ref[:, :width] = moved[part]
        out_ref[:, width:] = moved_digit[part]


def window_kernel(rows_all, clus_dev, me_ref, map_ref, query_ref, other_ref, result_ref, cohesion_ref):
    queries = query_ref.shape[0]
    width = query_ref.shape[1] - LANES
    query = query_ref[:, :width]

    def numbers(take):
        return (
            sum(take(i + place) * (256.0**place) for place in range(DIGITS)).astype(jnp.int32)
            for i in (0, DIGITS)
        )

    hot = (map_ref[...] == me_ref[0]).astype(jnp.float32)
    rank = ranked(hot)
    shape = (clus_dev, hot.shape[1])
    kth = (rank == iota(shape, 0).astype(jnp.float32) + 1.0) & (hot > 0.0)
    own = jnp.sum(jnp.where(kth, iota(shape, 1).astype(jnp.float32), 0.0), axis=1, keepdims=True)
    digit = query_ref[:, width:].astype(jnp.float32)
    name, order = numbers(lambda i: digit[:, i : i + 1])
    low = (name - 1) * rows_all
    query_key = low + order
    lows = jnp.concatenate([low, own.astype(jnp.int32) * rows_all], axis=0)

    best, counts, sums = None, None, None
    for rows_ref in (query_ref, other_ref):
        rows = rows_ref[:, :width]
        across = jnp.transpose(rows_ref[:, width:].astype(jnp.float32))
        name, order = numbers(lambda i: across[i : i + 1])
        keys = (name - 1) * rows_all + order
        above = keys >= lows
        member = (above & (keys < lows + rows_all)).astype(jnp.float32)
        count = jnp.sum(member, axis=1, keepdims=True)
        total = matmul(member.astype(jnp.bfloat16), rows)
        scores = lax.dot_general(
            query, rows, (((1,), (1,)), ((), ())), preferred_element_type=jnp.float32
        )
        earlier = above[:queries] & (keys < query_key)
        most = jnp.max(jnp.where(earlier, scores, -3.0), axis=1, keepdims=True)
        best = most if best is None else jnp.maximum(best, most)
        counts = count if counts is None else counts + count
        sums = total if sums is None else sums + total
    centroid = sums * (1.0 / jnp.maximum(counts, 1.0))
    best = jnp.where(best > -2.0, best, 0.0)
    offset = query.astype(jnp.float32) - centroid[:queries]
    distance = jnp.sum(offset * offset, axis=1, keepdims=True)
    lane = iota((queries, LANES), 1)
    result_ref[0] = jnp.transpose(jnp.where(lane == 0, best, distance))[: result_ref.shape[1]]
    centre = centroid[queries:]
    cohesion_ref[...] = as_row(jnp.sum(centre * centre, axis=1, keepdims=True))


def pick_kernel(order, me_ref, slot_ref, result_ref, best_ref, distance_ref):
    rows = slot_ref.shape[1]
    owners, _, slots = result_ref.shape
    place = iota((1, slots), 1) // (slots // owners)
    at = as_column(slot_ref[...]) == iota((rows, slots), 1)
    for line, out_ref in enumerate((best_ref, distance_ref)):
        values = result_ref[me_ref[0], line : line + 1]
        for index in range(1, owners):
            given = result_ref[me_ref[0] ^ order[index], line : line + 1]
            values = jnp.where(place == index, given, values)
        out_ref[...] = as_row(jnp.sum(jnp.where(at, values, 0.0), axis=1, keepdims=True))


def from_partner(value, k, axis):
    return lax.ppermute(value, axis, [(i, i ^ k) for i in range(lax.axis_size(axis))])


def exchange(blocks, order, me):
    if len(blocks) > 1:
        return jnp.concatenate(
            [from_partner(block, k, "shard") if k else block for k, block in zip(order, blocks)]
        )
    owners = lax.axis_size("shard")
    partner = me ^ jnp.array(order, jnp.int32)
    place = jnp.argsort(partner)
    parted = blocks[0].reshape(owners, -1, blocks[0].shape[1])
    got = lax.all_to_all(parted[place], "shard", 0, 0, tiled=True)
    return got[partner].reshape(blocks[0].shape)


def partner_order(owners):
    half = owners // 2
    near, far = list(range(1, half)), list(range(half, owners))
    return [0] + far[:1] + near[:1] + far[1:] + near[1:]


def local(embeddings, cluster_id, item_order, owner_map):
    owners = lax.axis_size("shard")
    local_rows, width = embeddings.shape
    rows_all = local_rows * owners * lax.axis_size("sub")
    clus_dev = owner_map.shape[0] // owners
    capacity = 2 * local_rows // owners
    slots = owners * capacity
    wide = width + LANES
    params = pltpu.CompilerParams(vmem_limit_bytes=32 << 20)
    me = lax.axis_index("shard").astype(jnp.int32).reshape(1)
    owner_row = owner_map.reshape(1, -1)

    order = partner_order(owners)
    parts = owners if owners <= MOST_PERMUTES else 1
    slot, digit = pl.pallas_call(
        functools.partial(slot_kernel, owners, capacity, order),
        out_shape=[
            jax.ShapeDtypeStruct((1, local_rows), jnp.int32),
            jax.ShapeDtypeStruct((local_rows, LANES), jnp.bfloat16),
        ],
        in_specs=[SCALAR] + [WHOLE] * 3,
        out_specs=[WHOLE] * 2,
        compiler_params=params,
        name="slots",
    )(me, owner_row, cluster_id.reshape(1, -1), item_order.reshape(1, -1))
    packed = pl.pallas_call(
        pack_kernel,
        out_shape=[jax.ShapeDtypeStruct((slots // parts, wide), jnp.bfloat16)] * parts,
        in_specs=[WHOLE] * 3,
        out_specs=[WHOLE] * parts,
        compiler_params=params,
        name="pack",
    )(slot, digit, embeddings)
    query = exchange(packed, order, me)
    other = from_partner(query, 1, "sub")
    results, cohesion = pl.pallas_call(
        functools.partial(window_kernel, rows_all, clus_dev),
        out_shape=[
            jax.ShapeDtypeStruct((1, 2, slots), jnp.float32),
            jax.ShapeDtypeStruct((1, clus_dev), jnp.float32),
        ],
        in_specs=[SCALAR] + [WHOLE] * 3,
        out_specs=[WHOLE] * 2,
        compiler_params=params,
        name="window",
    )(me, owner_row, query, other)
    results = lax.all_gather(results, "shard", axis=0, tiled=True)
    best, distance = pl.pallas_call(
        functools.partial(pick_kernel, order),
        out_shape=[jax.ShapeDtypeStruct((1, local_rows), jnp.float32)] * 2,
        in_specs=[SCALAR] + [WHOLE] * 2,
        out_specs=[WHOLE] * 2,
        compiler_params=params,
        name="pick",
    )(me, slot, results)
    return best.reshape(local_rows), distance.reshape(local_rows), cohesion.reshape(clus_dev)


def solution(mesh):
    in_specs = (
        P(("groups", "shard", "sub"), None),
        P(("groups", "shard", "sub")),
        P(("groups", "shard", "sub")),
        P("groups"),
    )
    out_specs = (
        P(("groups", "shard", "sub")),
        P(("groups", "shard", "sub")),
        P(("groups", "shard")),
    )
    return jax.shard_map(local, mesh=mesh, in_specs=in_specs, out_specs=out_specs, check_vma=False)
```

```python
import functools

import jax
import jax.numpy as jnp
from jax import lax
from jax.experimental import pallas as pl
from jax.experimental.pallas import tpu as pltpu
from jax.sharding import PartitionSpec as P

LANES = 128
DIGITS = 3
MOST_PERMUTES = 16
WHOLE = pl.BlockSpec(memory_space=pltpu.VMEM)
SCALAR = pl.BlockSpec(memory_space=pltpu.SMEM)


def iota(shape, dim):
    return lax.broadcasted_iota(jnp.int32, shape, dim)


def as_column(row):
    return jnp.transpose(jnp.broadcast_to(row, (LANES, row.shape[1])))[:, :1]


def as_row(column):
    return jnp.transpose(jnp.broadcast_to(column, (column.shape[0], LANES)))[:1]


def matmul(a, b):
    return jnp.dot(a, b, preferred_element_type=jnp.float32)


def ranked(hot):
    upto = (iota((LANES, LANES), 0) <= iota((LANES, LANES), 1)).astype(jnp.bfloat16)
    before, parts = jnp.zeros((1, 1), jnp.float32), []
    for start in range(0, hot.shape[1], LANES):
        piece = hot[:, start : start + LANES]
        spread = jnp.broadcast_to(piece, (16, LANES)).astype(jnp.bfloat16)
        parts.append(matmul(spread, upto)[:1] + before)
        before = before + jnp.sum(piece, axis=1, keepdims=True)
    return jnp.concatenate(parts, axis=1)


def slot_kernel(
    owners, capacity, order, rows, me_ref, ints_ref, slot_ref, digit_ref
):
    clusters = ints_ref.shape[1] - 2 * rows
    cluster = as_column(ints_ref[:, clusters : clusters + rows])
    named = cluster == iota((rows, clusters), 1)
    owner = jnp.sum(jnp.where(named, ints_ref[:, :clusters], 0).astype(jnp.float32), axis=1, keepdims=True)
    owner = owner.astype(jnp.int32)
    hot = (owner == iota((rows, max(owners, LANES)), 1)).astype(jnp.float32)
    upto = (iota((rows, rows), 1) <= iota((rows, rows), 0)).astype(jnp.bfloat16)
    rank = jnp.sum(hot * matmul(upto, hot.astype(jnp.bfloat16)), axis=1, keepdims=True) - 1.0
    partner = owner ^ me_ref[0]
    place = partner
    for index, k in enumerate(order):
        place = jnp.where(partner == k, index, place)
    slot_ref[...] = as_row(place * capacity + rank.astype(jnp.int32))

    lane = iota((rows, LANES), 1)
    digit = jnp.zeros((rows, LANES), jnp.int32)
    for first, number in ((0, cluster + 1), (DIGITS, as_column(ints_ref[:, clusters + rows :]))):
        for at in range(DIGITS):
            digit = jnp.where(lane == first + at, (number >> (8 * at)) & 255, digit)
    digit_ref[...] = digit.astype(jnp.float32).astype(jnp.bfloat16)


def pack_kernel(slot_ref, digit_ref, embed_ref, *out_refs):
    rows, width = embed_ref.shape
    each = out_refs[0].shape[0]
    values = embed_ref[...].astype(jnp.float32)
    mean_sq = jnp.sum(values * values, axis=1, keepdims=True) * (1.0 / width)
    unit = (values * lax.rsqrt(width * (mean_sq + 1e-06))).astype(jnp.bfloat16)
    slots = each * len(out_refs)
    move = (iota((slots, rows), 0) == slot_ref[...]).astype(jnp.float32).astype(jnp.bfloat16)
    moved = matmul(move, unit).astype(jnp.bfloat16)
    moved_digit = matmul(move, digit_ref[...]).astype(jnp.bfloat16)
    for index, out_ref in enumerate(out_refs):
        part = slice(index * each, (index + 1) * each)
        out_ref[:, :width] = moved[part]
        out_ref[:, width:] = moved_digit[part]


def key_numbers(take):
    name, order = (
        sum(take(i + at) * (256.0**at) for at in range(DIGITS)).astype(jnp.int32)
        for i in (0, DIGITS)
    )
    return name - 1, order


def compare(rows_all, query, query_key, lows, rows_ref):
    queries, width = query.shape
    rows = rows_ref[:, :width]
    across = jnp.transpose(rows_ref[:, width:].astype(jnp.float32))
    name, order = key_numbers(lambda i: across[i : i + 1])
    keys = name * rows_all + order
    above = keys >= lows
    member = (above & (keys < lows + rows_all)).astype(jnp.float32)
    counts = jnp.sum(member, axis=1, keepdims=True)
    sums = matmul(member.astype(jnp.bfloat16), rows)
    scores = lax.dot_general(
        query, rows, (((1,), (1,)), ((), ())), preferred_element_type=jnp.float32
    )
    earlier = above[:queries] & (keys < query_key)
    best = jnp.max(jnp.where(earlier, scores, -3.0), axis=1, keepdims=True)
    return best, counts, sums


def near_kernel(
    rows_all, clusters, clus_dev, me_ref, ints_ref, query_ref, column_ref, number_ref, sums_ref
):
    queries = query_ref.shape[0]
    width = query_ref.shape[1] - LANES
    hot = (ints_ref[:, :clusters] == me_ref[0]).astype(jnp.float32)
    rank = ranked(hot)
    shape = (clus_dev, hot.shape[1])
    kth = (rank == iota(shape, 0).astype(jnp.float32) + 1.0) & (hot > 0.0)
    own = jnp.sum(jnp.where(kth, iota(shape, 1).astype(jnp.float32), 0.0), axis=1, keepdims=True)
    digit = query_ref[:, width:].astype(jnp.float32)
    name, order = key_numbers(lambda i: digit[:, i : i + 1])
    low = name * rows_all
    lows = jnp.concatenate([low, own.astype(jnp.int32) * rows_all], axis=0)
    best, counts, sums = compare(rows_all, query_ref[:, :width], low + order, lows, query_ref)
    count = counts.shape[0]
    lane = iota((count, LANES), 1)
    best = jnp.concatenate([best, jnp.zeros((clus_dev, 1), jnp.float32)], axis=0)
    order = jnp.concatenate([order, jnp.zeros((clus_dev, 1), jnp.int32)], axis=0)
    column_ref[...] = jnp.where(lane == 0, best, counts)
    number_ref[...] = jnp.where(lane == 0, lows, order)
    sums_ref[...] = sums


def far_kernel(
    rows_all, query_ref, other_ref, column_ref, number_ref, sums_ref, result_ref, cohesion_ref
):
    queries = query_ref.shape[0]
    width = query_ref.shape[1] - LANES
    query = query_ref[:, :width]
    lows = number_ref[:, 0:1]
    query_key = lows[:queries] + number_ref[:queries, 1:2]
    best, counts, sums = compare(rows_all, query, query_key, lows, other_ref)
    best = jnp.maximum(best, column_ref[:queries, 0:1])
    counts = counts + column_ref[:, 1:2]
    centroid = (sums + sums_ref[...]) * (1.0 / jnp.maximum(counts, 1.0))
    best = jnp.where(best > -2.0, best, 0.0)
    offset = query.astype(jnp.float32) - centroid[:queries]
    distance = jnp.sum(offset * offset, axis=1, keepdims=True)
    lane = iota((queries, LANES), 1)
    result = jnp.transpose(jnp.where(lane == 0, best, distance))[: result_ref.shape[1]]
    for owner in range(result_ref.shape[0]):
        result_ref[owner] = result
    centre = centroid[queries:]
    cohesion_ref[...] = as_row(jnp.sum(centre * centre, axis=1, keepdims=True))


def pick_kernel(order, me_ref, slot_ref, result_ref, best_ref, distance_ref):
    rows = slot_ref.shape[1]
    owners, _, slots = result_ref.shape
    place = iota((1, slots), 1) // (slots // owners)
    at = as_column(slot_ref[...]) == iota((rows, slots), 1)
    for line, out_ref in enumerate((best_ref, distance_ref)):
        values = result_ref[me_ref[0], line : line + 1]
        for index in range(1, owners):
            given = result_ref[me_ref[0] ^ order[index], line : line + 1]
            values = jnp.where(place == index, given, values)
        out_ref[...] = as_row(jnp.sum(jnp.where(at, values, 0.0), axis=1, keepdims=True))


def from_partner(value, k, axis):
    return lax.ppermute(value, axis, [(i, i ^ k) for i in range(lax.axis_size(axis))])


def exchange(blocks, order, me):
    if len(blocks) > 1:
        return jnp.concatenate(
            [from_partner(block, k, "shard") if k else block for k, block in zip(order, blocks)]
        )
    owners = lax.axis_size("shard")
    partner = me ^ jnp.array(order, jnp.int32)
    place = jnp.argsort(partner)
    parted = blocks[0].reshape(owners, -1, blocks[0].shape[1])
    got = lax.all_to_all(parted[place], "shard", 0, 0, tiled=True)
    return got[partner].reshape(blocks[0].shape)


def partner_order(owners):
    half = owners // 2
    near, far = list(range(1, half)), list(range(half, owners))
    return [0] + far[:1] + near[:1] + far[1:] + near[1:]


def local(embeddings, cluster_id, item_order, owner_map):
    owners = lax.axis_size("shard")
    local_rows, width = embeddings.shape
    rows_all = local_rows * owners * lax.axis_size("sub")
    clus_dev = owner_map.shape[0] // owners
    capacity = 2 * local_rows // owners
    slots = owners * capacity
    wide = width + LANES
    params = pltpu.CompilerParams(vmem_limit_bytes=32 << 20)
    compare_cost = pl.CostEstimate(
        flops=4 * slots * slots * width, bytes_accessed=4 * slots * wide, transcendentals=0
    )
    me = lax.axis_index("shard").astype(jnp.int32).reshape(1)
    ints = jnp.concatenate([owner_map, cluster_id, item_order]).reshape(1, -1)

    order = partner_order(owners)
    parts = owners if owners <= MOST_PERMUTES else 1
    slot, digit = pl.pallas_call(
        functools.partial(slot_kernel, owners, capacity, order, local_rows),
        out_shape=[
            jax.ShapeDtypeStruct((1, local_rows), jnp.int32),
            jax.ShapeDtypeStruct((local_rows, LANES), jnp.bfloat16),
        ],
        in_specs=[SCALAR, WHOLE],
        out_specs=[WHOLE] * 2,
        compiler_params=params,
        cost_estimate=pl.CostEstimate(flops=1 << 28, bytes_accessed=1 << 16, transcendentals=0),
        name="slots",
    )(me, ints)
    packed = pl.pallas_call(
        pack_kernel,
        out_shape=[jax.ShapeDtypeStruct((slots // parts, wide), jnp.bfloat16)] * parts,
        in_specs=[WHOLE] * 3,
        out_specs=[WHOLE] * parts,
        compiler_params=params,
        name="pack",
    )(slot, digit, embeddings)
    query = exchange(packed, order, me)
    other = from_partner(query, 1, "sub")
    asked = slots + clus_dev
    near = pl.pallas_call(
        functools.partial(near_kernel, rows_all, owner_map.shape[0], clus_dev),
        out_shape=[
            jax.ShapeDtypeStruct((asked, LANES), jnp.float32),
            jax.ShapeDtypeStruct((asked, LANES), jnp.int32),
            jax.ShapeDtypeStruct((asked, width), jnp.float32),
        ],
        in_specs=[SCALAR] + [WHOLE] * 2,
        out_specs=[WHOLE] * 3,
        compiler_params=params,
        cost_estimate=compare_cost,
        name="near",
    )(me, ints, query)
    results, cohesion = pl.pallas_call(
        functools.partial(far_kernel, rows_all),
        out_shape=[
            jax.ShapeDtypeStruct((owners, 2, slots), jnp.float32),
            jax.ShapeDtypeStruct((1, clus_dev), jnp.float32),
        ],
        in_specs=[WHOLE] * 5,
        out_specs=[WHOLE] * 2,
        compiler_params=params,
        cost_estimate=compare_cost,
        name="far",
    )(query, other, *near)
    results = lax.all_to_all(results, "shard", 0, 0, tiled=True)
    best, distance = pl.pallas_call(
        functools.partial(pick_kernel, order),
        out_shape=[jax.ShapeDtypeStruct((1, local_rows), jnp.float32)] * 2,
        in_specs=[SCALAR] + [WHOLE] * 2,
        out_specs=[WHOLE] * 2,
        compiler_params=params,
        name="pick",
    )(me, slot, results)
    return best.reshape(local_rows), distance.reshape(local_rows), cohesion.reshape(clus_dev)


def solution(mesh):
    in_specs = (
        P(("groups", "shard", "sub"), None),
        P(("groups", "shard", "sub")),
        P(("groups", "shard", "sub")),
        P("groups"),
    )
    out_specs = (
        P(("groups", "shard", "sub")),
        P(("groups", "shard", "sub")),
        P(("groups", "shard")),
    )
    return jax.shard_map(local, mesh=mesh, in_specs=in_specs, out_specs=out_specs, check_vma=False)
```

```python
import functools

import jax
import jax.numpy as jnp
from jax import lax
from jax.experimental import pallas as pl
from jax.experimental.pallas import tpu as pltpu
from jax.sharding import PartitionSpec as P

LANES = 128
DIGITS = 3
MOST_PERMUTES = 8
WHOLE = pl.BlockSpec(memory_space=pltpu.VMEM)
SCALAR = pl.BlockSpec(memory_space=pltpu.SMEM)


def iota(shape, dim):
    return lax.broadcasted_iota(jnp.int32, shape, dim)


def as_column(row):
    return jnp.transpose(jnp.broadcast_to(row, (LANES, row.shape[1])))[:, :1]


def as_row(column):
    return jnp.transpose(jnp.broadcast_to(column, (column.shape[0], LANES)))[:1]


def matmul(a, b):
    return jnp.dot(a, b, preferred_element_type=jnp.float32)


def ranked(hot):
    upto = (iota((LANES, LANES), 0) <= iota((LANES, LANES), 1)).astype(jnp.bfloat16)
    before, parts = jnp.zeros((1, 1), jnp.float32), []
    for start in range(0, hot.shape[1], LANES):
        piece = hot[:, start : start + LANES]
        spread = jnp.broadcast_to(piece, (16, LANES)).astype(jnp.bfloat16)
        parts.append(matmul(spread, upto)[:1] + before)
        before = before + jnp.sum(piece, axis=1, keepdims=True)
    return jnp.concatenate(parts, axis=1)


def slot_kernel(
    owners, capacity, order, rows, me_ref, ints_ref, slot_ref, digit_ref
):
    clusters = ints_ref.shape[1] - 2 * rows
    cluster = as_column(ints_ref[:, clusters : clusters + rows])
    named = cluster == iota((rows, clusters), 1)
    owner = jnp.sum(jnp.where(named, ints_ref[:, :clusters], 0).astype(jnp.float32), axis=1, keepdims=True)
    owner = owner.astype(jnp.int32)
    hot = (owner == iota((rows, max(owners, LANES)), 1)).astype(jnp.float32)
    upto = (iota((rows, rows), 1) <= iota((rows, rows), 0)).astype(jnp.bfloat16)
    rank = jnp.sum(hot * matmul(upto, hot.astype(jnp.bfloat16)), axis=1, keepdims=True) - 1.0
    partner = owner ^ me_ref[0]
    place = partner
    for index, k in enumerate(order):
        place = jnp.where(partner == k, index, place)
    slot_ref[...] = as_row(place * capacity + rank.astype(jnp.int32))

    lane = iota((rows, LANES), 1)
    digit = jnp.zeros((rows, LANES), jnp.int32)
    for first, number in ((0, cluster + 1), (DIGITS, as_column(ints_ref[:, clusters + rows :]))):
        for at in range(DIGITS):
            digit = jnp.where(lane == first + at, (number >> (8 * at)) & 255, digit)
    digit_ref[...] = digit.astype(jnp.float32).astype(jnp.bfloat16)


def pack_kernel(slot_ref, digit_ref, embed_ref, *out_refs):
    rows, width = embed_ref.shape
    values = embed_ref[...].astype(jnp.float32)
    mean_sq = jnp.sum(values * values, axis=1, keepdims=True) * (1.0 / width)
    unit = (values * lax.rsqrt(width * (mean_sq + 1e-06))).astype(jnp.bfloat16)
    slots = sum(out_ref.shape[0] for out_ref in out_refs)
    move = (iota((slots, rows), 0) == slot_ref[...]).astype(jnp.float32).astype(jnp.bfloat16)
    moved = matmul(move, unit).astype(jnp.bfloat16)
    moved_digit = matmul(move, digit_ref[...]).astype(jnp.bfloat16)
    first = 0
    for out_ref in out_refs:
        part = slice(first, first + out_ref.shape[0])
        out_ref[:, :width] = moved[part]
        out_ref[:, width:] = moved_digit[part]
        first = part.stop


def key_numbers(take):
    name, order = (
        sum(take(i + at) * (256.0**at) for at in range(DIGITS)).astype(jnp.int32)
        for i in (0, DIGITS)
    )
    return name - 1, order


def compare(rows_all, query, query_key, lows, rows_ref):
    queries, width = query.shape
    rows = rows_ref[:, :width]
    across = jnp.transpose(rows_ref[:, width:].astype(jnp.float32))
    name, order = key_numbers(lambda i: across[i : i + 1])
    keys = name * rows_all + order
    above = keys >= lows
    member = (above & (keys < lows + rows_all)).astype(jnp.float32)
    counts = jnp.sum(member, axis=1, keepdims=True)
    sums = matmul(member.astype(jnp.bfloat16), rows)
    scores = lax.dot_general(
        query, rows, (((1,), (1,)), ((), ())), preferred_element_type=jnp.float32
    )
    earlier = above[:queries] & (keys < query_key)
    best = jnp.max(jnp.where(earlier, scores, -3.0), axis=1, keepdims=True)
    return best, counts, sums


def near_kernel(
    rows_all, clusters, clus_dev, me_ref, ints_ref, query_ref, column_ref, number_ref, sums_ref
):
    queries = query_ref.shape[0]
    width = query_ref.shape[1] - LANES
    hot = (ints_ref[:, :clusters] == me_ref[0]).astype(jnp.float32)
    rank = ranked(hot)
    shape = (clus_dev, hot.shape[1])
    kth = (rank == iota(shape, 0).astype(jnp.float32) + 1.0) & (hot > 0.0)
    own = jnp.sum(jnp.where(kth, iota(shape, 1).astype(jnp.float32), 0.0), axis=1, keepdims=True)
    digit = query_ref[:, width:].astype(jnp.float32)
    name, order = key_numbers(lambda i: digit[:, i : i + 1])
    low = name * rows_all
    lows = jnp.concatenate([low, own.astype(jnp.int32) * rows_all], axis=0)
    best, counts, sums = compare(rows_all, query_ref[:, :width], low + order, lows, query_ref)
    count = counts.shape[0]
    lane = iota((count, LANES), 1)
    best = jnp.concatenate([best, jnp.zeros((clus_dev, 1), jnp.float32)], axis=0)
    order = jnp.concatenate([order, jnp.zeros((clus_dev, 1), jnp.int32)], axis=0)
    column_ref[...] = jnp.where(lane == 0, best, counts)
    number_ref[...] = jnp.where(lane == 0, lows, order)
    sums_ref[...] = sums


def far_kernel(
    rows_all, query_ref, other_ref, column_ref, number_ref, sums_ref, result_ref, cohesion_ref
):
    queries = query_ref.shape[0]
    width = query_ref.shape[1] - LANES
    query = query_ref[:, :width]
    lows = number_ref[:, 0:1]
    query_key = lows[:queries] + number_ref[:queries, 1:2]
    best, counts, sums = compare(rows_all, query, query_key, lows, other_ref)
    best = jnp.maximum(best, column_ref[:queries, 0:1])
    counts = counts + column_ref[:, 1:2]
    centroid = (sums + sums_ref[...]) * (1.0 / jnp.maximum(counts, 1.0))
    best = jnp.where(best > -2.0, best, 0.0)
    offset = query.astype(jnp.float32) - centroid[:queries]
    distance = jnp.sum(offset * offset, axis=1, keepdims=True)
    lane = iota((queries, LANES), 1)
    result = jnp.transpose(jnp.where(lane == 0, best, distance))[: result_ref.shape[1]]
    for owner in range(result_ref.shape[0]):
        result_ref[owner] = result
    centre = centroid[queries:]
    cohesion_ref[...] = as_row(jnp.sum(centre * centre, axis=1, keepdims=True))


def pick_kernel(order, me_ref, slot_ref, result_ref, best_ref, distance_ref):
    rows = slot_ref.shape[1]
    owners, _, slots = result_ref.shape
    place = iota((1, slots), 1) // (slots // owners)
    at = as_column(slot_ref[...]) == iota((rows, slots), 1)
    for line, out_ref in enumerate((best_ref, distance_ref)):
        values = jnp.zeros((1, slots), jnp.float32)
        for index, k in enumerate(order):
            given = result_ref[me_ref[0] ^ k, line : line + 1]
            values = jnp.where(place == index, given, values)
        out_ref[...] = as_row(jnp.sum(jnp.where(at, values, 0.0), axis=1, keepdims=True))


def from_partner(value, k, axis):
    return lax.ppermute(value, axis, [(i, i ^ k) for i in range(lax.axis_size(axis))])


def partner_groups(owners):
    half = owners // 2
    odd = [list(range(1, half, 2))] if half > 1 else []
    return [[k] for k in range(0, half, 2)] + odd + [[k] for k in range(half, owners)]


def exchange(packed, groups):
    owners = lax.axis_size("shard")
    half = owners // 2
    rows = packed[0].shape[0]
    blocks = {}
    for group, block in zip(groups, packed):
        if len(group) > 1:
            near = from_partner(block, 1, "shard")
            for i, k in enumerate(group):
                blocks[k] = near[i * rows : (i + 1) * rows]
        else:
            k = group[0]
            blocks[k] = from_partner(block, k, "shard") if k >= half else block
    step = 2
    while step < half:
        sent = [k for k in range(half) if k & step]
        near = from_partner(jnp.concatenate([blocks[k] for k in sent]), step, "shard")
        for i, k in enumerate(sent):
            blocks[k] = near[i * rows : (i + 1) * rows]
        step *= 2
    return jnp.concatenate([blocks[k] for group in groups for k in group])


def exchange_all(packed, order, me):
    owners = lax.axis_size("shard")
    partner = me ^ jnp.array(order, jnp.int32)
    parted = packed.reshape(owners, -1, packed.shape[1])
    got = lax.all_to_all(parted[jnp.argsort(partner)], "shard", 0, 0, tiled=True)
    return got[partner].reshape(packed.shape)


def local(embeddings, cluster_id, item_order, owner_map):
    owners = lax.axis_size("shard")
    local_rows, width = embeddings.shape
    rows_all = local_rows * owners * lax.axis_size("sub")
    clus_dev = owner_map.shape[0] // owners
    capacity = 2 * local_rows // owners
    slots = owners * capacity
    wide = width + LANES
    params = pltpu.CompilerParams(vmem_limit_bytes=32 << 20)
    compare_cost = pl.CostEstimate(
        flops=4 * slots * slots * width, bytes_accessed=4 * slots * wide, transcendentals=0
    )
    me = lax.axis_index("shard").astype(jnp.int32).reshape(1)
    ints = jnp.concatenate([owner_map, cluster_id, item_order]).reshape(1, -1)

    direct = owners <= MOST_PERMUTES
    groups = partner_groups(owners) if direct else [list(range(owners))]
    order = [k for group in groups for k in group]
    slot, digit = pl.pallas_call(
        functools.partial(slot_kernel, owners, capacity, order, local_rows),
        out_shape=[
            jax.ShapeDtypeStruct((1, local_rows), jnp.int32),
            jax.ShapeDtypeStruct((local_rows, LANES), jnp.bfloat16),
        ],
        in_specs=[SCALAR, WHOLE],
        out_specs=[WHOLE] * 2,
        compiler_params=params,
        cost_estimate=pl.CostEstimate(flops=1 << 28, bytes_accessed=1 << 16, transcendentals=0),
        name="slots",
    )(me, ints)
    packed = pl.pallas_call(
        pack_kernel,
        out_shape=[jax.ShapeDtypeStruct((len(g) * capacity, wide), jnp.bfloat16) for g in groups],
        in_specs=[WHOLE] * 3,
        out_specs=[WHOLE] * len(groups),
        compiler_params=params,
        name="pack",
    )(slot, digit, embeddings)
    query = exchange(packed, groups) if direct else exchange_all(packed[0], order, me)
    other = from_partner(query, 1, "sub")
    asked = slots + clus_dev
    near = pl.pallas_call(
        functools.partial(near_kernel, rows_all, owner_map.shape[0], clus_dev),
        out_shape=[
            jax.ShapeDtypeStruct((asked, LANES), jnp.float32),
            jax.ShapeDtypeStruct((asked, LANES), jnp.int32),
            jax.ShapeDtypeStruct((asked, width), jnp.float32),
        ],
        in_specs=[SCALAR] + [WHOLE] * 2,
        out_specs=[WHOLE] * 3,
        compiler_params=params,
        cost_estimate=compare_cost,
        name="near",
    )(me, ints, query)
    results, cohesion = pl.pallas_call(
        functools.partial(far_kernel, rows_all),
        out_shape=[
            jax.ShapeDtypeStruct((owners, 2, slots), jnp.float32),
            jax.ShapeDtypeStruct((1, clus_dev), jnp.float32),
        ],
        in_specs=[WHOLE] * 5,
        out_specs=[WHOLE] * 2,
        compiler_params=params,
        cost_estimate=compare_cost,
        name="far",
    )(query, other, *near)
    results = lax.all_to_all(results, "shard", 0, 0, tiled=True)
    best, distance = pl.pallas_call(
        functools.partial(pick_kernel, order),
        out_shape=[jax.ShapeDtypeStruct((1, local_rows), jnp.float32)] * 2,
        in_specs=[SCALAR] + [WHOLE] * 2,
        out_specs=[WHOLE] * 2,
        compiler_params=params,
        name="pick",
    )(me, slot, results)
    return best.reshape(local_rows), distance.reshape(local_rows), cohesion.reshape(clus_dev)


def solution(mesh):
    in_specs = (
        P(("groups", "shard", "sub"), None),
        P(("groups", "shard", "sub")),
        P(("groups", "shard", "sub")),
        P("groups"),
    )
    out_specs = (
        P(("groups", "shard", "sub")),
        P(("groups", "shard", "sub")),
        P(("groups", "shard")),
    )
    return jax.shard_map(local, mesh=mesh, in_specs=in_specs, out_specs=out_specs, check_vma=False)
```

```python
import functools

import jax
import jax.numpy as jnp
from jax import lax
from jax.experimental import pallas as pl
from jax.experimental.pallas import tpu as pltpu
from jax.sharding import PartitionSpec as P

LANES = 128
DIGITS = 3
MOST_PERMUTES = 8
WHOLE = pl.BlockSpec(memory_space=pltpu.VMEM)
SCALAR = pl.BlockSpec(memory_space=pltpu.SMEM)


def iota(shape, dim):
    return lax.broadcasted_iota(jnp.int32, shape, dim)


def as_column(row):
    return jnp.transpose(jnp.broadcast_to(row, (LANES, row.shape[1])))[:, :1]


def as_row(column):
    return jnp.transpose(jnp.broadcast_to(column, (column.shape[0], LANES)))[:1]


def matmul(a, b):
    return jnp.dot(a, b, preferred_element_type=jnp.float32)


def ranked(hot):
    upto = (iota((LANES, LANES), 0) <= iota((LANES, LANES), 1)).astype(jnp.bfloat16)
    before, parts = jnp.zeros((1, 1), jnp.float32), []
    for start in range(0, hot.shape[1], LANES):
        piece = hot[:, start : start + LANES]
        spread = jnp.broadcast_to(piece, (16, LANES)).astype(jnp.bfloat16)
        parts.append(matmul(spread, upto)[:1] + before)
        before = before + jnp.sum(piece, axis=1, keepdims=True)
    return jnp.concatenate(parts, axis=1)


def slot_kernel(
    owners, capacity, order, rows, me_ref, ints_ref, slot_ref, digit_ref
):
    clusters = ints_ref.shape[1] - 2 * rows
    cluster = as_column(ints_ref[:, clusters : clusters + rows])
    named = cluster == iota((rows, clusters), 1)
    owner = jnp.sum(jnp.where(named, ints_ref[:, :clusters], 0).astype(jnp.float32), axis=1, keepdims=True)
    owner = owner.astype(jnp.int32)
    hot = (owner == iota((rows, max(owners, LANES)), 1)).astype(jnp.float32)
    upto = (iota((rows, rows), 1) <= iota((rows, rows), 0)).astype(jnp.bfloat16)
    rank = jnp.sum(hot * matmul(upto, hot.astype(jnp.bfloat16)), axis=1, keepdims=True) - 1.0
    partner = owner ^ me_ref[0]
    place = partner
    for index, k in enumerate(order):
        place = jnp.where(partner == k, index, place)
    slot_ref[...] = as_row(place * capacity + rank.astype(jnp.int32))

    lane = iota((rows, LANES), 1)
    digit = jnp.zeros((rows, LANES), jnp.int32)
    for first, number in ((0, cluster + 1), (DIGITS, as_column(ints_ref[:, clusters + rows :]))):
        for at in range(DIGITS):
            digit = jnp.where(lane == first + at, (number >> (8 * at)) & 255, digit)
    digit_ref[...] = digit.astype(jnp.float32).astype(jnp.bfloat16)


def pack_kernel(slot_ref, digit_ref, embed_ref, *out_refs):
    rows, width = embed_ref.shape
    values = embed_ref[...].astype(jnp.float32)
    mean_sq = jnp.sum(values * values, axis=1, keepdims=True) * (1.0 / width)
    unit = (values * lax.rsqrt(width * (mean_sq + 1e-06))).astype(jnp.bfloat16)
    slots = sum(out_ref.shape[0] for out_ref in out_refs)
    move = (iota((slots, rows), 0) == slot_ref[...]).astype(jnp.float32).astype(jnp.bfloat16)
    moved = matmul(move, unit).astype(jnp.bfloat16)
    moved_digit = matmul(move, digit_ref[...]).astype(jnp.bfloat16)
    first = 0
    for out_ref in out_refs:
        part = slice(first, first + out_ref.shape[0])
        out_ref[:, :width] = moved[part]
        out_ref[:, width:] = moved_digit[part]
        first = part.stop


def key_numbers(take):
    name, order = (
        sum(take(i + at) * (256.0**at) for at in range(DIGITS)).astype(jnp.int32)
        for i in (0, DIGITS)
    )
    return name - 1, order


def compare(rows_all, query, query_key, lows, rows_ref):
    queries, width = query.shape
    rows = rows_ref[:, :width]
    across = jnp.transpose(rows_ref[:, width:].astype(jnp.float32))
    name, order = key_numbers(lambda i: across[i : i + 1])
    keys = name * rows_all + order
    above = keys >= lows
    member = (above & (keys < lows + rows_all)).astype(jnp.float32)
    counts = jnp.sum(member, axis=1, keepdims=True)
    sums = matmul(member.astype(jnp.bfloat16), rows)
    scores = lax.dot_general(
        query, rows, (((1,), (1,)), ((), ())), preferred_element_type=jnp.float32
    )
    earlier = above[:queries] & (keys < query_key)
    best = jnp.max(jnp.where(earlier, scores, -3.0), axis=1, keepdims=True)
    return best, counts, sums


def near_kernel(
    rows_all, clusters, clus_dev, me_ref, ints_ref, query_ref, column_ref, number_ref, sums_ref
):
    queries = query_ref.shape[0]
    width = query_ref.shape[1] - LANES
    hot = (ints_ref[:, :clusters] == me_ref[0]).astype(jnp.float32)
    rank = ranked(hot)
    shape = (clus_dev, hot.shape[1])
    kth = (rank == iota(shape, 0).astype(jnp.float32) + 1.0) & (hot > 0.0)
    own = jnp.sum(jnp.where(kth, iota(shape, 1).astype(jnp.float32), 0.0), axis=1, keepdims=True)
    digit = query_ref[:, width:].astype(jnp.float32)
    name, order = key_numbers(lambda i: digit[:, i : i + 1])
    low = name * rows_all
    lows = jnp.concatenate([low, own.astype(jnp.int32) * rows_all], axis=0)
    best, counts, sums = compare(rows_all, query_ref[:, :width], low + order, lows, query_ref)
    count = counts.shape[0]
    lane = iota((count, LANES), 1)
    best = jnp.concatenate([best, jnp.zeros((clus_dev, 1), jnp.float32)], axis=0)
    order = jnp.concatenate([order, jnp.zeros((clus_dev, 1), jnp.int32)], axis=0)
    column_ref[...] = jnp.where(lane == 0, best, counts)
    number_ref[...] = jnp.where(lane == 0, lows, order)
    sums_ref[...] = sums


def far_kernel(
    rows_all, query_ref, other_ref, column_ref, number_ref, sums_ref, result_ref, cohesion_ref
):
    queries = query_ref.shape[0]
    width = query_ref.shape[1] - LANES
    query = query_ref[:, :width]
    lows = number_ref[:, 0:1]
    query_key = lows[:queries] + number_ref[:queries, 1:2]
    best, counts, sums = compare(rows_all, query, query_key, lows, other_ref)
    best = jnp.maximum(best, column_ref[:queries, 0:1])
    counts = counts + column_ref[:, 1:2]
    centroid = (sums + sums_ref[...]) * (1.0 / jnp.maximum(counts, 1.0))
    best = jnp.where(best > -2.0, best, 0.0)
    offset = query.astype(jnp.float32) - centroid[:queries]
    distance = jnp.sum(offset * offset, axis=1, keepdims=True)
    lane = iota((queries, LANES), 1)
    result = jnp.transpose(jnp.where(lane == 0, best, distance))[: result_ref.shape[1]]
    for owner in range(result_ref.shape[0]):
        result_ref[owner] = result
    centre = centroid[queries:]
    cohesion_ref[...] = as_row(jnp.sum(centre * centre, axis=1, keepdims=True))


def pick_kernel(order, me_ref, slot_ref, result_ref, best_ref, distance_ref):
    rows = slot_ref.shape[1]
    owners, _, slots = result_ref.shape
    place = iota((1, slots), 1) // (slots // owners)
    at = as_column(slot_ref[...]) == iota((rows, slots), 1)
    for line, out_ref in enumerate((best_ref, distance_ref)):
        values = jnp.zeros((1, slots), jnp.float32)
        for index, k in enumerate(order):
            given = result_ref[me_ref[0] ^ k, line : line + 1]
            values = jnp.where(place == index, given, values)
        out_ref[...] = as_row(jnp.sum(jnp.where(at, values, 0.0), axis=1, keepdims=True))


def from_partner(value, k, axis):
    return lax.ppermute(value, axis, [(i, i ^ k) for i in range(lax.axis_size(axis))])


def partner_order(owners):
    half = owners // 2
    far, near = list(range(half, owners)), list(range(2, half))
    return far[:1] + near + far[1:] + list(range(1, min(half, 2))) + [0]


def exchange(packed, order):
    return jnp.concatenate(
        [from_partner(block, k, "shard") if k else block for k, block in zip(order, packed)]
    )


def exchange_all(packed, order, me):
    owners = lax.axis_size("shard")
    partner = me ^ jnp.array(order, jnp.int32)
    parted = packed.reshape(owners, -1, packed.shape[1])
    got = lax.all_to_all(parted[jnp.argsort(partner)], "shard", 0, 0, tiled=True)
    return got[partner].reshape(packed.shape)


def local(embeddings, cluster_id, item_order, owner_map):
    owners = lax.axis_size("shard")
    local_rows, width = embeddings.shape
    rows_all = local_rows * owners * lax.axis_size("sub")
    clus_dev = owner_map.shape[0] // owners
    capacity = 2 * local_rows // owners
    slots = owners * capacity
    wide = width + LANES
    params = pltpu.CompilerParams(vmem_limit_bytes=32 << 20)
    compare_cost = pl.CostEstimate(
        flops=4 * slots * slots * width, bytes_accessed=4 * slots * wide, transcendentals=0
    )
    me = lax.axis_index("shard").astype(jnp.int32).reshape(1)
    ints = jnp.concatenate([owner_map, cluster_id, item_order]).reshape(1, -1)

    direct = owners <= MOST_PERMUTES
    order = partner_order(owners)
    parts = owners if direct else 1
    slot, digit = pl.pallas_call(
        functools.partial(slot_kernel, owners, capacity, order, local_rows),
        out_shape=[
            jax.ShapeDtypeStruct((1, local_rows), jnp.int32),
            jax.ShapeDtypeStruct((local_rows, LANES), jnp.bfloat16),
        ],
        in_specs=[SCALAR, WHOLE],
        out_specs=[WHOLE] * 2,
        compiler_params=params,
        cost_estimate=pl.CostEstimate(flops=1 << 28, bytes_accessed=1 << 16, transcendentals=0),
        name="slots",
    )(me, ints)
    packed = pl.pallas_call(
        pack_kernel,
        out_shape=[jax.ShapeDtypeStruct((slots // parts, wide), jnp.bfloat16)] * parts,
        in_specs=[WHOLE] * 3,
        out_specs=[WHOLE] * parts,
        compiler_params=params,
        name="pack",
    )(slot, digit, embeddings)
    query = exchange(packed, order) if direct else exchange_all(packed[0], order, me)
    other = from_partner(query, 1, "sub")
    asked = slots + clus_dev
    near = pl.pallas_call(
        functools.partial(near_kernel, rows_all, owner_map.shape[0], clus_dev),
        out_shape=[
            jax.ShapeDtypeStruct((asked, LANES), jnp.float32),
            jax.ShapeDtypeStruct((asked, LANES), jnp.int32),
            jax.ShapeDtypeStruct((asked, width), jnp.float32),
        ],
        in_specs=[SCALAR] + [WHOLE] * 2,
        out_specs=[WHOLE] * 3,
        compiler_params=params,
        cost_estimate=compare_cost,
        name="near",
    )(me, ints, query)
    results, cohesion = pl.pallas_call(
        functools.partial(far_kernel, rows_all),
        out_shape=[
            jax.ShapeDtypeStruct((owners, 2, slots), jnp.float32),
            jax.ShapeDtypeStruct((1, clus_dev), jnp.float32),
        ],
        in_specs=[WHOLE] * 5,
        out_specs=[WHOLE] * 2,
        compiler_params=params,
        cost_estimate=compare_cost,
        name="far",
    )(query, other, *near)
    results = lax.all_to_all(results, "shard", 0, 0, tiled=True)
    best, distance = pl.pallas_call(
        functools.partial(pick_kernel, order),
        out_shape=[jax.ShapeDtypeStruct((1, local_rows), jnp.float32)] * 2,
        in_specs=[SCALAR] + [WHOLE] * 2,
        out_specs=[WHOLE] * 2,
        compiler_params=params,
        name="pick",
    )(me, slot, results)
    return best.reshape(local_rows), distance.reshape(local_rows), cohesion.reshape(clus_dev)


def solution(mesh):
    in_specs = (
        P(("groups", "shard", "sub"), None),
        P(("groups", "shard", "sub")),
        P(("groups", "shard", "sub")),
        P("groups"),
    )
    out_specs = (
        P(("groups", "shard", "sub")),
        P(("groups", "shard", "sub")),
        P(("groups", "shard")),
    )
    return jax.shard_map(local, mesh=mesh, in_specs=in_specs, out_specs=out_specs, check_vma=False)
```

```python
import functools

import jax
import jax.numpy as jnp
from jax import lax
from jax.experimental import pallas as pl
from jax.experimental.pallas import tpu as pltpu
from jax.sharding import PartitionSpec as P

LANES = 128
DIGITS = 3
MOST_PERMUTES = 8
WHOLE = pl.BlockSpec(memory_space=pltpu.VMEM)
SCALAR = pl.BlockSpec(memory_space=pltpu.SMEM)


def iota(shape, dim):
    return lax.broadcasted_iota(jnp.int32, shape, dim)


def as_column(row):
    return jnp.transpose(jnp.broadcast_to(row, (LANES, row.shape[1])))[:, :1]


def as_row(column):
    return jnp.transpose(jnp.broadcast_to(column, (column.shape[0], LANES)))[:1]


def matmul(a, b):
    return jnp.dot(a, b, preferred_element_type=jnp.float32)


def ranked(hot):
    upto = (iota((LANES, LANES), 0) <= iota((LANES, LANES), 1)).astype(jnp.bfloat16)
    before, parts = jnp.zeros((1, 1), jnp.float32), []
    for start in range(0, hot.shape[1], LANES):
        piece = hot[:, start : start + LANES]
        spread = jnp.broadcast_to(piece, (16, LANES)).astype(jnp.bfloat16)
        parts.append(matmul(spread, upto)[:1] + before)
        before = before + jnp.sum(piece, axis=1, keepdims=True)
    return jnp.concatenate(parts, axis=1)


def slot_kernel(
    owners, capacity, order, rows, me_ref, ints_ref, slot_ref, digit_ref
):
    clusters = ints_ref.shape[1] - 2 * rows
    cluster = as_column(ints_ref[:, clusters : clusters + rows])
    named = cluster == iota((rows, clusters), 1)
    owner = jnp.sum(jnp.where(named, ints_ref[:, :clusters], 0).astype(jnp.float32), axis=1, keepdims=True)
    owner = owner.astype(jnp.int32)
    hot = (owner == iota((rows, max(owners, LANES)), 1)).astype(jnp.float32)
    upto = (iota((rows, rows), 1) <= iota((rows, rows), 0)).astype(jnp.bfloat16)
    rank = jnp.sum(hot * matmul(upto, hot.astype(jnp.bfloat16)), axis=1, keepdims=True) - 1.0
    partner = owner ^ me_ref[0]
    place = partner
    for index, k in enumerate(order):
        place = jnp.where(partner == k, index, place)
    slot_ref[...] = as_row(place * capacity + rank.astype(jnp.int32))

    lane = iota((rows, LANES), 1)
    digit = jnp.zeros((rows, LANES), jnp.int32)
    for first, number in ((0, cluster + 1), (DIGITS, as_column(ints_ref[:, clusters + rows :]))):
        for at in range(DIGITS):
            digit = jnp.where(lane == first + at, (number >> (8 * at)) & 255, digit)
    digit_ref[...] = digit.astype(jnp.float32).astype(jnp.bfloat16)


def pack_kernel(slot_ref, digit_ref, embed_ref, *out_refs):
    rows, width = embed_ref.shape
    values = embed_ref[...].astype(jnp.float32)
    mean_sq = jnp.sum(values * values, axis=1, keepdims=True) * (1.0 / width)
    unit = (values * lax.rsqrt(width * (mean_sq + 1e-06))).astype(jnp.bfloat16)
    slots = sum(out_ref.shape[0] for out_ref in out_refs)
    move = (iota((slots, rows), 0) == slot_ref[...]).astype(jnp.float32).astype(jnp.bfloat16)
    moved = matmul(move, unit).astype(jnp.bfloat16)
    moved_digit = matmul(move, digit_ref[...]).astype(jnp.bfloat16)
    first = 0
    for out_ref in out_refs:
        part = slice(first, first + out_ref.shape[0])
        out_ref[:, :width] = moved[part]
        out_ref[:, width:] = moved_digit[part]
        first = part.stop


def key_numbers(take):
    name, order = (
        sum(take(i + at) * (256.0**at) for at in range(DIGITS)).astype(jnp.int32)
        for i in (0, DIGITS)
    )
    return name - 1, order


def compare(rows_all, query, query_key, lows, rows_ref):
    queries, width = query.shape
    rows = rows_ref[:, :width]
    across = jnp.transpose(rows_ref[:, width:].astype(jnp.float32))
    name, order = key_numbers(lambda i: across[i : i + 1])
    keys = name * rows_all + order
    above = keys >= lows
    member = (above & (keys < lows + rows_all)).astype(jnp.float32)
    counts = jnp.sum(member, axis=1, keepdims=True)
    sums = matmul(member.astype(jnp.bfloat16), rows)
    scores = lax.dot_general(
        query, rows, (((1,), (1,)), ((), ())), preferred_element_type=jnp.float32
    )
    earlier = above[:queries] & (keys < query_key)
    best = jnp.max(jnp.where(earlier, scores, -3.0), axis=1, keepdims=True)
    return best, counts, sums


def near_kernel(
    rows_all, clusters, clus_dev, me_ref, ints_ref, query_ref, column_ref, number_ref, sums_ref
):
    queries = query_ref.shape[0]
    width = query_ref.shape[1] - LANES
    hot = (ints_ref[:, :clusters] == me_ref[0]).astype(jnp.float32)
    rank = ranked(hot)
    shape = (clus_dev, hot.shape[1])
    kth = (rank == iota(shape, 0).astype(jnp.float32) + 1.0) & (hot > 0.0)
    own = jnp.sum(jnp.where(kth, iota(shape, 1).astype(jnp.float32), 0.0), axis=1, keepdims=True)
    digit = query_ref[:, width:].astype(jnp.float32)
    name, order = key_numbers(lambda i: digit[:, i : i + 1])
    low = name * rows_all
    lows = jnp.concatenate([low, own.astype(jnp.int32) * rows_all], axis=0)
    best, counts, sums = compare(rows_all, query_ref[:, :width], low + order, lows, query_ref)
    count = counts.shape[0]
    lane = iota((count, LANES), 1)
    best = jnp.concatenate([best, jnp.zeros((clus_dev, 1), jnp.float32)], axis=0)
    order = jnp.concatenate([order, jnp.zeros((clus_dev, 1), jnp.int32)], axis=0)
    column_ref[...] = jnp.where(lane == 0, best, counts)
    number_ref[...] = jnp.where(lane == 0, lows, order)
    sums_ref[...] = sums


def far_kernel(
    rows_all, query_ref, other_ref, column_ref, number_ref, sums_ref, result_ref, cohesion_ref
):
    queries = query_ref.shape[0]
    width = query_ref.shape[1] - LANES
    query = query_ref[:, :width]
    lows = number_ref[:, 0:1]
    query_key = lows[:queries] + number_ref[:queries, 1:2]
    best, counts, sums = compare(rows_all, query, query_key, lows, other_ref)
    best = jnp.maximum(best, column_ref[:queries, 0:1])
    counts = counts + column_ref[:, 1:2]
    centroid = (sums + sums_ref[...]) * (1.0 / jnp.maximum(counts, 1.0))
    best = jnp.where(best > -2.0, best, 0.0)
    offset = query.astype(jnp.float32) - centroid[:queries]
    distance = jnp.sum(offset * offset, axis=1, keepdims=True)
    lane = iota((queries, LANES), 1)
    result = jnp.transpose(jnp.where(lane == 0, best, distance))[: result_ref.shape[1]]
    for owner in range(result_ref.shape[0]):
        result_ref[owner] = result
    centre = centroid[queries:]
    cohesion_ref[...] = as_row(jnp.sum(centre * centre, axis=1, keepdims=True))


def pick_kernel(order, me_ref, slot_ref, result_ref, best_ref, distance_ref):
    rows = slot_ref.shape[1]
    owners, _, slots = result_ref.shape
    place = iota((1, slots), 1) // (slots // owners)
    at = as_column(slot_ref[...]) == iota((rows, slots), 1)
    for line, out_ref in enumerate((best_ref, distance_ref)):
        values = jnp.zeros((1, slots), jnp.float32)
        for index, k in enumerate(order):
            given = result_ref[me_ref[0] ^ k, line : line + 1]
            values = jnp.where(place == index, given, values)
        out_ref[...] = as_row(jnp.sum(jnp.where(at, values, 0.0), axis=1, keepdims=True))


def from_partner(value, k, axis):
    return lax.ppermute(value, axis, [(i, i ^ k) for i in range(lax.axis_size(axis))])


def partner_order(owners):
    half = owners // 2
    far, near = list(range(half, owners)), list(range(2, half))
    return far[:2] + near + far[2:] + list(range(1, min(half, 2))) + [0]


def exchange(packed, order):
    return jnp.concatenate(
        [from_partner(block, k, "shard") if k else block for k, block in zip(order, packed)]
    )


def exchange_all(packed, order, me):
    owners = lax.axis_size("shard")
    partner = me ^ jnp.array(order, jnp.int32)
    parted = packed.reshape(owners, -1, packed.shape[1])
    got = lax.all_to_all(parted[jnp.argsort(partner)], "shard", 0, 0, tiled=True)
    return got[partner].reshape(packed.shape)


def local(embeddings, cluster_id, item_order, owner_map):
    owners = lax.axis_size("shard")
    local_rows, width = embeddings.shape
    rows_all = local_rows * owners * lax.axis_size("sub")
    clus_dev = owner_map.shape[0] // owners
    capacity = 2 * local_rows // owners
    slots = owners * capacity
    wide = width + LANES
    params = pltpu.CompilerParams(vmem_limit_bytes=32 << 20)
    compare_cost = pl.CostEstimate(
        flops=4 * slots * slots * width, bytes_accessed=4 * slots * wide, transcendentals=0
    )
    me = lax.axis_index("shard").astype(jnp.int32).reshape(1)
    ints = jnp.concatenate([owner_map, cluster_id, item_order]).reshape(1, -1)

    direct = owners <= MOST_PERMUTES
    order = partner_order(owners)
    parts = owners if direct else 1
    slot, digit = pl.pallas_call(
        functools.partial(slot_kernel, owners, capacity, order, local_rows),
        out_shape=[
            jax.ShapeDtypeStruct((1, local_rows), jnp.int32),
            jax.ShapeDtypeStruct((local_rows, LANES), jnp.bfloat16),
        ],
        in_specs=[SCALAR, WHOLE],
        out_specs=[WHOLE] * 2,
        compiler_params=params,
        cost_estimate=pl.CostEstimate(flops=1 << 28, bytes_accessed=1 << 16, transcendentals=0),
        name="slots",
    )(me, ints)
    packed = pl.pallas_call(
        pack_kernel,
        out_shape=[jax.ShapeDtypeStruct((slots // parts, wide), jnp.bfloat16)] * parts,
        in_specs=[WHOLE] * 3,
        out_specs=[WHOLE] * parts,
        compiler_params=params,
        name="pack",
    )(slot, digit, embeddings)
    query = exchange(packed, order) if direct else exchange_all(packed[0], order, me)
    other = from_partner(query, 1, "sub")
    asked = slots + clus_dev
    near = pl.pallas_call(
        functools.partial(near_kernel, rows_all, owner_map.shape[0], clus_dev),
        out_shape=[
            jax.ShapeDtypeStruct((asked, LANES), jnp.float32),
            jax.ShapeDtypeStruct((asked, LANES), jnp.int32),
            jax.ShapeDtypeStruct((asked, width), jnp.float32),
        ],
        in_specs=[SCALAR] + [WHOLE] * 2,
        out_specs=[WHOLE] * 3,
        compiler_params=params,
        cost_estimate=compare_cost,
        name="near",
    )(me, ints, query)
    results, cohesion = pl.pallas_call(
        functools.partial(far_kernel, rows_all),
        out_shape=[
            jax.ShapeDtypeStruct((owners, 2, slots), jnp.float32),
            jax.ShapeDtypeStruct((1, clus_dev), jnp.float32),
        ],
        in_specs=[WHOLE] * 5,
        out_specs=[WHOLE] * 2,
        compiler_params=params,
        cost_estimate=compare_cost,
        name="far",
    )(query, other, *near)
    results = lax.all_to_all(results, "shard", 0, 0, tiled=True)
    best, distance = pl.pallas_call(
        functools.partial(pick_kernel, order),
        out_shape=[jax.ShapeDtypeStruct((1, local_rows), jnp.float32)] * 2,
        in_specs=[SCALAR] + [WHOLE] * 2,
        out_specs=[WHOLE] * 2,
        compiler_params=params,
        name="pick",
    )(me, slot, results)
    return best.reshape(local_rows), distance.reshape(local_rows), cohesion.reshape(clus_dev)


def solution(mesh):
    in_specs = (
        P(("groups", "shard", "sub"), None),
        P(("groups", "shard", "sub")),
        P(("groups", "shard", "sub")),
        P("groups"),
    )
    out_specs = (
        P(("groups", "shard", "sub")),
        P(("groups", "shard", "sub")),
        P(("groups", "shard")),
    )
    return jax.shard_map(local, mesh=mesh, in_specs=in_specs, out_specs=out_specs, check_vma=False)
```

```python
import functools

import jax
import jax.numpy as jnp
from jax import lax
from jax.experimental import pallas as pl
from jax.experimental.pallas import tpu as pltpu
from jax.sharding import PartitionSpec as P

LANES = 128
DIGITS = 3
ONE = 2 * DIGITS
MOST_PERMUTES = 8
WHOLE = pl.BlockSpec(memory_space=pltpu.VMEM)
SCALAR = pl.BlockSpec(memory_space=pltpu.SMEM)


def iota(shape, dim):
    return lax.broadcasted_iota(jnp.int32, shape, dim)


def matmul(a, b):
    return jnp.dot(a, b, preferred_element_type=jnp.float32)


def matmul_t(a, b, precision=None):
    return lax.dot_general(
        a, b, (((1,), (1,)), ((), ())), precision=precision, preferred_element_type=jnp.float32
    )


def bf16(x):
    return x.astype(jnp.float32).astype(jnp.bfloat16)


def ranked(hot):
    upto = (iota((LANES, LANES), 0) <= iota((LANES, LANES), 1)).astype(jnp.bfloat16)
    before, parts = jnp.zeros((1, 1), jnp.float32), []
    for start in range(0, hot.shape[1], LANES):
        piece = hot[:, start : start + LANES]
        spread = jnp.broadcast_to(piece, (16, LANES)).astype(jnp.bfloat16)
        parts.append(matmul(spread, upto)[:1] + before)
        before = before + jnp.sum(piece, axis=1, keepdims=True)
    return jnp.concatenate(parts, axis=1)


def slot_kernel(
    owners, capacity, order, rows, me_ref, ints_ref, slot_ref, digit_ref
):
    clusters = ints_ref.shape[1] - 2 * rows
    cluster = ints_ref[:, clusters : clusters + rows]
    named = bf16(iota((clusters, rows), 0) == cluster)
    owner_map = bf16(jnp.broadcast_to(ints_ref[:, :clusters], (16, clusters)))
    owner = matmul(owner_map, named)[:1].astype(jnp.int32)
    hot = (iota((max(owners, 16), rows), 0) == owner).astype(jnp.float32)
    upto = bf16(iota((rows, rows), 0) <= iota((rows, rows), 1))
    rank = jnp.sum(hot * matmul(bf16(hot), upto), axis=0, keepdims=True) - 1.0
    partner = owner ^ me_ref[0]
    place = partner
    for index, k in enumerate(order):
        place = jnp.where(partner == k, index, place)
    slot_ref[...] = place * capacity + rank.astype(jnp.int32)

    line = iota((8, rows), 0)
    digit = (line == ONE).astype(jnp.int32)
    for first, number in ((0, cluster + 1), (DIGITS, ints_ref[:, clusters + rows :])):
        for at in range(DIGITS):
            digit = jnp.where(line == first + at, (number >> (8 * at)) & 255, digit)
    digit = jnp.concatenate([digit, jnp.zeros((LANES - 8, rows), jnp.int32)], axis=0)
    digit_ref[...] = bf16(digit)


def pack_kernel(slot_ref, digit_ref, embed_ref, *out_refs):
    rows, width = embed_ref.shape
    each = out_refs[0].shape[0]
    values = embed_ref[...].astype(jnp.float32)
    mean_sq = jnp.sum(values * values, axis=1, keepdims=True) * (1.0 / width)
    unit = (values * lax.rsqrt(width * (mean_sq + 1e-06))).astype(jnp.bfloat16)
    slots = each * len(out_refs)
    move = bf16(iota((slots, rows), 0) == slot_ref[...])
    moved = matmul(move, unit).astype(jnp.bfloat16)
    moved_digit = matmul_t(move, digit_ref[...]).astype(jnp.bfloat16)
    for index, out_ref in enumerate(out_refs):
        part = slice(index * each, (index + 1) * each)
        out_ref[:, :width] = moved[part]
        out_ref[:, width:] = moved_digit[part]


def weights(number, at):
    value = jnp.zeros(at.shape, jnp.float32)
    for place in range(DIGITS):
        for which in (0, 1):
            here = (at == which * DIGITS + place) & (number == which)
            value = jnp.where(here, 256.0**place, value)
    return value.astype(jnp.bfloat16)


def key_rows(rows_all, digit):
    numbers = matmul_t(weights(iota((16, LANES), 0), iota((16, LANES), 1)), digit)
    low = (numbers[0:1].astype(jnp.int32) - 1) * rows_all
    return low, low + numbers[1:2].astype(jnp.int32)


def key_columns(rows_all, digit):
    shape = (LANES, 2 * LANES)
    numbers = matmul(digit, weights(iota(shape, 1) // LANES, iota(shape, 0)))
    low = (numbers[:, :LANES].astype(jnp.int32) - 1) * rows_all
    return low, low + numbers[:, LANES:].astype(jnp.int32)


def across(column, count):
    return jnp.concatenate([column] * (count // LANES), axis=1)


def compare(rows_all, query, query_low, query_key, lows, rows_ref):
    count, width = query.shape
    digit = rows_ref[:, width:]
    _, key = key_rows(rows_all, digit)
    bound = across(lows, key.shape[1])
    member = bf16((key >= bound) & (key < bound + rows_all))
    sums = matmul(member, rows_ref[...])
    scores = matmul_t(rows_ref[:, :width], query)
    _, key = key_columns(rows_all, digit)
    key = across(key, count)
    earlier = (key >= query_low) & (key < query_key)
    best = jnp.max(jnp.where(earlier, scores, -3.0), axis=0, keepdims=True)
    return best, sums


def near_kernel(
    rows_all, clusters, clus_dev, me_ref, ints_ref, query_ref, lows_ref, key_ref, best_ref, sums_ref
):
    width = query_ref.shape[1] - LANES
    hot = (ints_ref[:, :clusters] == me_ref[0]).astype(jnp.float32)
    rank = ranked(hot)
    shape = (clus_dev, clusters)
    kth = (rank == iota(shape, 0).astype(jnp.float32) + 1.0) & (hot > 0.0)
    own = jnp.sum(jnp.where(kth, iota(shape, 1).astype(jnp.float32), 0.0), axis=1, keepdims=True)
    own = jnp.broadcast_to(own.astype(jnp.int32) * rows_all, (clus_dev, LANES))
    digit = query_ref[:, width:]
    low, _ = key_columns(rows_all, digit)
    lows = jnp.concatenate([low, own], axis=0)
    query_low, query_key = key_rows(rows_all, digit)
    best, sums = compare(rows_all, query_ref[:, :width], query_low, query_key, lows, query_ref)
    lows_ref[...] = lows
    key_ref[...] = jnp.concatenate([query_low, query_key], axis=0)
    best_ref[...] = best
    sums_ref[...] = sums


def far_kernel(
    rows_all, query_ref, other_ref, lows_ref, key_ref, best_ref, sums_ref, result_ref, cohesion_ref
):
    queries = query_ref.shape[0]
    width = query_ref.shape[1] - LANES
    query = query_ref[:, :width]
    best, sums = compare(
        rows_all, query, key_ref[0:1], key_ref[1:2], lows_ref[...], other_ref
    )
    best = jnp.maximum(best, best_ref[...])
    best = jnp.where(best > -2.0, best, 0.0)
    sums = sums + sums_ref[...]
    counts = sums[:, width + ONE : width + ONE + 1]
    centroid = sums[:, :width] * (1.0 / jnp.maximum(counts, 1.0))
    offset = jnp.concatenate(
        [query.astype(jnp.float32) - centroid[:queries], centroid[queries:]], axis=0
    )
    offset = offset * offset
    squares = offset[:, :LANES]
    for start in range(LANES, width, LANES):
        squares = squares + offset[:, start : start + LANES]
    ones = jnp.ones((8, LANES), jnp.float32)
    total = matmul_t(ones, squares, lax.Precision.HIGHEST)[:1]
    result = jnp.concatenate([best, total[:, :queries]], axis=0)
    for owner in range(result_ref.shape[0]):
        result_ref[owner] = result
    cohesion_ref[...] = total[:, queries:]


def pick_kernel(order, me_ref, slot_ref, result_ref, best_ref, distance_ref):
    rows = slot_ref.shape[1]
    owners, lines, slots = result_ref.shape
    place = iota((lines, slots), 1) // (slots // owners)
    values = jnp.zeros((lines, slots), jnp.float32)
    for index, k in enumerate(order):
        values = jnp.where(place == index, result_ref[me_ref[0] ^ k], values)
    values = jnp.concatenate([values, jnp.zeros((8 - lines, slots), jnp.float32)], axis=0)
    at = (iota((slots, rows), 0) == slot_ref[...]).astype(jnp.float32)
    picked = jnp.dot(
        values, at, precision=lax.Precision.HIGHEST, preferred_element_type=jnp.float32
    )
    best_ref[...] = picked[0:1]
    distance_ref[...] = picked[1:2]


def from_partner(value, k, axis):
    return lax.ppermute(value, axis, [(i, i ^ k) for i in range(lax.axis_size(axis))])


def partner_order(owners):
    half = owners // 2
    far, near = list(range(half, owners)), list(range(2, half))
    return far[:1] + near + far[1:] + list(range(1, min(half, 2))) + [0]


def exchange(packed, order):
    return jnp.concatenate(
        [from_partner(block, k, "shard") if k else block for k, block in zip(order, packed)]
    )


def exchange_all(packed, order, me):
    owners = lax.axis_size("shard")
    partner = me ^ jnp.array(order, jnp.int32)
    parted = packed.reshape(owners, -1, packed.shape[1])
    got = lax.all_to_all(parted[jnp.argsort(partner)], "shard", 0, 0, tiled=True)
    return got[partner].reshape(packed.shape)


def local(embeddings, cluster_id, item_order, owner_map):
    owners = lax.axis_size("shard")
    local_rows, width = embeddings.shape
    rows_all = local_rows * owners * lax.axis_size("sub")
    clus_dev = owner_map.shape[0] // owners
    capacity = 2 * local_rows // owners
    slots = owners * capacity
    wide = width + LANES
    params = pltpu.CompilerParams(vmem_limit_bytes=32 << 20)
    compare_cost = pl.CostEstimate(
        flops=4 * slots * slots * width, bytes_accessed=4 * slots * wide, transcendentals=0
    )
    me = lax.axis_index("shard").astype(jnp.int32).reshape(1)
    ints = jnp.concatenate([owner_map, cluster_id, item_order]).reshape(1, -1)

    direct = owners <= MOST_PERMUTES
    order = partner_order(owners)
    parts = owners if direct else 1
    slot, digit = pl.pallas_call(
        functools.partial(slot_kernel, owners, capacity, order, local_rows),
        out_shape=[
            jax.ShapeDtypeStruct((1, local_rows), jnp.int32),
            jax.ShapeDtypeStruct((LANES, local_rows), jnp.bfloat16),
        ],
        in_specs=[SCALAR, WHOLE],
        out_specs=[WHOLE] * 2,
        compiler_params=params,
        cost_estimate=pl.CostEstimate(flops=1 << 28, bytes_accessed=1 << 16, transcendentals=0),
        name="slots",
    )(me, ints)
    packed = pl.pallas_call(
        pack_kernel,
        out_shape=[jax.ShapeDtypeStruct((slots // parts, wide), jnp.bfloat16)] * parts,
        in_specs=[WHOLE] * 3,
        out_specs=[WHOLE] * parts,
        compiler_params=params,
        name="pack",
    )(slot, digit, embeddings)
    query = exchange(packed, order) if direct else exchange_all(packed[0], order, me)
    other = from_partner(query, 1, "sub")
    asked = slots + clus_dev
    near = pl.pallas_call(
        functools.partial(near_kernel, rows_all, owner_map.shape[0], clus_dev),
        out_shape=[
            jax.ShapeDtypeStruct((asked, LANES), jnp.int32),
            jax.ShapeDtypeStruct((2, slots), jnp.int32),
            jax.ShapeDtypeStruct((1, slots), jnp.float32),
            jax.ShapeDtypeStruct((asked, wide), jnp.float32),
        ],
        in_specs=[SCALAR] + [WHOLE] * 2,
        out_specs=[WHOLE] * 4,
        compiler_params=params,
        cost_estimate=compare_cost,
        name="near",
    )(me, ints, query)
    results, cohesion = pl.pallas_call(
        functools.partial(far_kernel, rows_all),
        out_shape=[
            jax.ShapeDtypeStruct((owners, 2, slots), jnp.float32),
            jax.ShapeDtypeStruct((1, clus_dev), jnp.float32),
        ],
        in_specs=[WHOLE] * 6,
        out_specs=[WHOLE] * 2,
        compiler_params=params,
        cost_estimate=compare_cost,
        name="far",
    )(query, other, *near)
    results = lax.all_to_all(results, "shard", 0, 0, tiled=True)
    best, distance = pl.pallas_call(
        functools.partial(pick_kernel, order),
        out_shape=[jax.ShapeDtypeStruct((1, local_rows), jnp.float32)] * 2,
        in_specs=[SCALAR] + [WHOLE] * 2,
        out_specs=[WHOLE] * 2,
        compiler_params=params,
        name="pick",
    )(me, slot, results)
    return best.reshape(local_rows), distance.reshape(local_rows), cohesion.reshape(clus_dev)


def solution(mesh):
    in_specs = (
        P(("groups", "shard", "sub"), None),
        P(("groups", "shard", "sub")),
        P(("groups", "shard", "sub")),
        P("groups"),
    )
    out_specs = (
        P(("groups", "shard", "sub")),
        P(("groups", "shard", "sub")),
        P(("groups", "shard")),
    )
    return jax.shard_map(local, mesh=mesh, in_specs=in_specs, out_specs=out_specs, check_vma=False)
```

```python
import functools

import jax
import jax.numpy as jnp
from jax import lax
from jax.experimental import pallas as pl
from jax.experimental.pallas import tpu as pltpu
from jax.sharding import PartitionSpec as P

LANES = 128
DIGITS = 3
ONE = 2 * DIGITS
MOST_PERMUTES = 8
WHOLE = pl.BlockSpec(memory_space=pltpu.VMEM)
SCALAR = pl.BlockSpec(memory_space=pltpu.SMEM)


def iota(shape, dim):
    return lax.broadcasted_iota(jnp.int32, shape, dim)


def matmul(a, b):
    return jnp.dot(a, b, preferred_element_type=jnp.float32)


def matmul_t(a, b, precision=None):
    return lax.dot_general(
        a, b, (((1,), (1,)), ((), ())), precision=precision, preferred_element_type=jnp.float32
    )


def bf16(x):
    return x.astype(jnp.float32).astype(jnp.bfloat16)


def ranked(hot):
    upto = (iota((LANES, LANES), 0) <= iota((LANES, LANES), 1)).astype(jnp.bfloat16)
    before, parts = jnp.zeros((1, 1), jnp.float32), []
    for start in range(0, hot.shape[1], LANES):
        piece = hot[:, start : start + LANES]
        spread = jnp.broadcast_to(piece, (16, LANES)).astype(jnp.bfloat16)
        parts.append(matmul(spread, upto)[:1] + before)
        before = before + jnp.sum(piece, axis=1, keepdims=True)
    return jnp.concatenate(parts, axis=1)


def slot_kernel(
    owners, capacity, order, rows, me_ref, ints_ref, slot_ref, digit_ref
):
    clusters = ints_ref.shape[1] - 2 * rows
    cluster = ints_ref[:, clusters : clusters + rows]
    named = bf16(iota((clusters, rows), 0) == cluster)
    owner_map = bf16(jnp.broadcast_to(ints_ref[:, :clusters], (16, clusters)))
    owner = matmul(owner_map, named)[:1].astype(jnp.int32)
    hot = (iota((max(owners, 16), rows), 0) == owner).astype(jnp.float32)
    upto = bf16(iota((rows, rows), 0) <= iota((rows, rows), 1))
    rank = jnp.sum(hot * matmul(bf16(hot), upto), axis=0, keepdims=True) - 1.0
    partner = owner ^ me_ref[0]
    place = partner
    for index, k in enumerate(order):
        place = jnp.where(partner == k, index, place)
    slot_ref[...] = place * capacity + rank.astype(jnp.int32)

    line = iota((8, rows), 0)
    digit = (line == ONE).astype(jnp.int32)
    for first, number in ((0, cluster + 1), (DIGITS, ints_ref[:, clusters + rows :])):
        for at in range(DIGITS):
            digit = jnp.where(line == first + at, (number >> (8 * at)) & 255, digit)
    digit = jnp.concatenate([digit, jnp.zeros((LANES - 8, rows), jnp.int32)], axis=0)
    digit_ref[...] = bf16(digit)


def pack_kernel(slot_ref, digit_ref, embed_ref, *out_refs):
    rows, width = embed_ref.shape
    each = out_refs[0].shape[0]
    values = embed_ref[...].astype(jnp.float32)
    mean_sq = jnp.sum(values * values, axis=1, keepdims=True) * (1.0 / width)
    unit = (values * lax.rsqrt(width * (mean_sq + 1e-06))).astype(jnp.bfloat16)
    slots = each * len(out_refs)
    move = bf16(iota((slots, rows), 0) == slot_ref[...])
    moved = matmul(move, unit).astype(jnp.bfloat16)
    moved_digit = matmul_t(move, digit_ref[...]).astype(jnp.bfloat16)
    for index, out_ref in enumerate(out_refs):
        part = slice(index * each, (index + 1) * each)
        out_ref[:, :width] = moved[part]
        out_ref[:, width:] = moved_digit[part]


def weights(number, at):
    value = jnp.zeros(at.shape, jnp.float32)
    for place in range(DIGITS):
        for which in (0, 1):
            here = (at == which * DIGITS + place) & (number == which)
            value = jnp.where(here, 256.0**place, value)
    return value.astype(jnp.bfloat16)


def key_rows(rows_all, digit):
    numbers = matmul_t(weights(iota((16, LANES), 0), iota((16, LANES), 1)), digit)
    low = (numbers[0:1].astype(jnp.int32) - 1) * rows_all
    return low, low + numbers[1:2].astype(jnp.int32)


def key_columns(rows_all, digit):
    shape = (LANES, 2 * LANES)
    numbers = matmul(digit, weights(iota(shape, 1) // LANES, iota(shape, 0)))
    low = (numbers[:, :LANES].astype(jnp.int32) - 1) * rows_all
    return low, low + numbers[:, LANES:].astype(jnp.int32)


def across(column, count):
    return jnp.concatenate([column] * (count // LANES), axis=1)


def compare(rows_all, query, query_low, query_key, lows, rows_ref):
    count, width = query.shape
    digit = rows_ref[:, width:]
    _, key = key_rows(rows_all, digit)
    bound = across(lows, key.shape[1])
    member = bf16((key >= bound) & (key < bound + rows_all))
    sums = matmul(member, rows_ref[...])
    scores = matmul_t(rows_ref[:, :width], query)
    _, key = key_columns(rows_all, digit)
    key = across(key, count)
    earlier = (key >= query_low) & (key < query_key)
    best = jnp.max(jnp.where(earlier, scores, -3.0), axis=0, keepdims=True)
    return best, sums


def near_kernel(
    rows_all, clusters, clus_dev, me_ref, ints_ref, query_ref, lows_ref, key_ref, best_ref, sums_ref
):
    width = query_ref.shape[1] - LANES
    hot = (ints_ref[:, :clusters] == me_ref[0]).astype(jnp.float32)
    rank = ranked(hot)
    shape = (clus_dev, clusters)
    kth = (rank == iota(shape, 0).astype(jnp.float32) + 1.0) & (hot > 0.0)
    own = jnp.sum(jnp.where(kth, iota(shape, 1).astype(jnp.float32), 0.0), axis=1, keepdims=True)
    own = jnp.broadcast_to(own.astype(jnp.int32) * rows_all, (clus_dev, LANES))
    digit = query_ref[:, width:]
    low, _ = key_columns(rows_all, digit)
    lows = jnp.concatenate([low, own], axis=0)
    query_low, query_key = key_rows(rows_all, digit)
    best, sums = compare(rows_all, query_ref[:, :width], query_low, query_key, lows, query_ref)
    lows_ref[...] = lows
    key_ref[...] = jnp.concatenate([query_low, query_key], axis=0)
    best_ref[...] = best
    sums_ref[...] = sums


def far_kernel(
    rows_all, query_ref, other_ref, lows_ref, key_ref, best_ref, sums_ref, result_ref, norm_ref
):
    queries = query_ref.shape[0]
    width = query_ref.shape[1] - LANES
    query = query_ref[:, :width]
    best, sums = compare(
        rows_all, query, key_ref[0:1], key_ref[1:2], lows_ref[...], other_ref
    )
    best = jnp.maximum(best, best_ref[...])
    best = jnp.where(best > -2.0, best, 0.0)
    sums = sums + sums_ref[...]
    counts = sums[:, width + ONE : width + ONE + 1]
    centroid = sums[:, :width] * (1.0 / jnp.maximum(counts, 1.0))
    offset = jnp.concatenate(
        [query.astype(jnp.float32) - centroid[:queries], centroid[queries:]], axis=0
    )
    offset = offset * offset
    squares = offset[:, :LANES]
    for start in range(LANES, width, LANES):
        squares = squares + offset[:, start : start + LANES]
    ones = jnp.ones((8, LANES), jnp.float32)
    total = matmul_t(ones, squares, lax.Precision.HIGHEST)[:1]
    result = jnp.concatenate([best, total[:, :queries]], axis=0)
    for owner in range(result_ref.shape[0]):
        result_ref[owner] = result
    norm_ref[...] = total[:, queries:]


def pick_kernel(
    order, me_ref, slot_ref, result_ref, norm_ref, best_ref, distance_ref, cohesion_ref
):
    cohesion_ref[...] = norm_ref[...]
    rows = slot_ref.shape[1]
    owners, lines, slots = result_ref.shape
    place = iota((lines, slots), 1) // (slots // owners)
    values = jnp.zeros((lines, slots), jnp.float32)
    for index, k in enumerate(order):
        values = jnp.where(place == index, result_ref[me_ref[0] ^ k], values)
    values = jnp.concatenate([values, jnp.zeros((8 - lines, slots), jnp.float32)], axis=0)
    at = (iota((slots, rows), 0) == slot_ref[...]).astype(jnp.float32)
    picked = jnp.dot(
        values, at, precision=lax.Precision.HIGHEST, preferred_element_type=jnp.float32
    )
    best_ref[...] = picked[0:1]
    distance_ref[...] = picked[1:2]


def from_partner(value, k, axis):
    return lax.ppermute(value, axis, [(i, i ^ k) for i in range(lax.axis_size(axis))])


def partner_order(owners):
    half = owners // 2
    far, near = list(range(half, owners)), list(range(2, half))
    return far[:1] + near + far[1:] + list(range(1, min(half, 2))) + [0]


def exchange(packed, order):
    return jnp.concatenate(
        [from_partner(block, k, "shard") if k else block for k, block in zip(order, packed)]
    )


def exchange_all(packed, order, me):
    owners = lax.axis_size("shard")
    partner = me ^ jnp.array(order, jnp.int32)
    parted = packed.reshape(owners, -1, packed.shape[1])
    got = lax.all_to_all(parted[jnp.argsort(partner)], "shard", 0, 0, tiled=True)
    return got[partner].reshape(packed.shape)


def local(embeddings, cluster_id, item_order, owner_map):
    owners = lax.axis_size("shard")
    local_rows, width = embeddings.shape
    rows_all = local_rows * owners * lax.axis_size("sub")
    clus_dev = owner_map.shape[0] // owners
    capacity = 2 * local_rows // owners
    slots = owners * capacity
    wide = width + LANES
    params = pltpu.CompilerParams(vmem_limit_bytes=32 << 20)
    compare_cost = pl.CostEstimate(
        flops=4 * slots * slots * width, bytes_accessed=4 * slots * wide, transcendentals=0
    )
    me = lax.axis_index("shard").astype(jnp.int32).reshape(1)
    ints = jnp.concatenate([owner_map, cluster_id, item_order]).reshape(1, -1)

    direct = owners <= MOST_PERMUTES
    order = partner_order(owners)
    parts = owners if direct else 1
    slot, digit = pl.pallas_call(
        functools.partial(slot_kernel, owners, capacity, order, local_rows),
        out_shape=[
            jax.ShapeDtypeStruct((1, local_rows), jnp.int32),
            jax.ShapeDtypeStruct((LANES, local_rows), jnp.bfloat16),
        ],
        in_specs=[SCALAR, WHOLE],
        out_specs=[WHOLE] * 2,
        compiler_params=params,
        cost_estimate=pl.CostEstimate(flops=1 << 29, bytes_accessed=1 << 16, transcendentals=0),
        name="slots",
    )(me, ints)
    packed = pl.pallas_call(
        pack_kernel,
        out_shape=[jax.ShapeDtypeStruct((slots // parts, wide), jnp.bfloat16)] * parts,
        in_specs=[WHOLE] * 3,
        out_specs=[WHOLE] * parts,
        compiler_params=params,
        name="pack",
    )(slot, digit, embeddings)
    query = exchange(packed, order) if direct else exchange_all(packed[0], order, me)
    other = from_partner(query, 1, "sub")
    asked = slots + clus_dev
    near = pl.pallas_call(
        functools.partial(near_kernel, rows_all, owner_map.shape[0], clus_dev),
        out_shape=[
            jax.ShapeDtypeStruct((asked, LANES), jnp.int32),
            jax.ShapeDtypeStruct((2, slots), jnp.int32),
            jax.ShapeDtypeStruct((1, slots), jnp.float32),
            jax.ShapeDtypeStruct((asked, wide), jnp.float32),
        ],
        in_specs=[SCALAR] + [WHOLE] * 2,
        out_specs=[WHOLE] * 4,
        compiler_params=params,
        cost_estimate=compare_cost,
        name="near",
    )(me, ints, query)
    results, norms = pl.pallas_call(
        functools.partial(far_kernel, rows_all),
        out_shape=[
            jax.ShapeDtypeStruct((owners, 2, slots), jnp.float32),
            jax.ShapeDtypeStruct((1, clus_dev), jnp.float32),
        ],
        in_specs=[WHOLE] * 6,
        out_specs=[WHOLE] * 2,
        compiler_params=params,
        cost_estimate=compare_cost,
        name="far",
    )(query, other, *near)
    results = lax.all_to_all(results, "shard", 0, 0, tiled=True)
    best, distance, cohesion = pl.pallas_call(
        functools.partial(pick_kernel, order),
        out_shape=[jax.ShapeDtypeStruct((1, local_rows), jnp.float32)] * 2
        + [jax.ShapeDtypeStruct((1, clus_dev), jnp.float32)],
        in_specs=[SCALAR] + [WHOLE] * 3,
        out_specs=[WHOLE] * 3,
        compiler_params=params,
        name="pick",
    )(me, slot, results, norms)
    return best.reshape(local_rows), distance.reshape(local_rows), cohesion.reshape(clus_dev)


def solution(mesh):
    in_specs = (
        P(("groups", "shard", "sub"), None),
        P(("groups", "shard", "sub")),
        P(("groups", "shard", "sub")),
        P("groups"),
    )
    out_specs = (
        P(("groups", "shard", "sub")),
        P(("groups", "shard", "sub")),
        P(("groups", "shard")),
    )
    return jax.shard_map(local, mesh=mesh, in_specs=in_specs, out_specs=out_specs, check_vma=False)
```

```python
import functools

import jax
import jax.numpy as jnp
from jax import lax
from jax.experimental import pallas as pl
from jax.experimental.pallas import tpu as pltpu
from jax.sharding import PartitionSpec as P

LANES = 128
DIGITS = 3
ONE = 2 * DIGITS
MOST_PERMUTES = 8
WHOLE = pl.BlockSpec(memory_space=pltpu.VMEM)
SCALAR = pl.BlockSpec(memory_space=pltpu.SMEM)


def iota(shape, dim):
    return lax.broadcasted_iota(jnp.int32, shape, dim)


def matmul(a, b):
    return jnp.dot(a, b, preferred_element_type=jnp.float32)


def matmul_t(a, b, precision=None):
    return lax.dot_general(
        a, b, (((1,), (1,)), ((), ())), precision=precision, preferred_element_type=jnp.float32
    )


def bf16(x):
    return x.astype(jnp.float32).astype(jnp.bfloat16)


def ranked(hot):
    upto = (iota((LANES, LANES), 0) <= iota((LANES, LANES), 1)).astype(jnp.bfloat16)
    before, parts = jnp.zeros((1, 1), jnp.float32), []
    for start in range(0, hot.shape[1], LANES):
        piece = hot[:, start : start + LANES]
        spread = jnp.broadcast_to(piece, (16, LANES)).astype(jnp.bfloat16)
        parts.append(matmul(spread, upto)[:1] + before)
        before = before + jnp.sum(piece, axis=1, keepdims=True)
    return jnp.concatenate(parts, axis=1)


def of_core(me_ref, values):
    value = values[0]
    for core, other in enumerate(values[1:], 1):
        value = jnp.where(me_ref[0] % len(values) == core, other, value)
    return value


def slot_kernel(
    owners, capacity, orders, rows, me_ref, ints_ref, slot_ref, digit_ref
):
    clusters = ints_ref.shape[1] - 2 * rows
    cluster = ints_ref[:, clusters : clusters + rows]
    named = bf16(iota((clusters, rows), 0) == cluster)
    owner_map = bf16(jnp.broadcast_to(ints_ref[:, :clusters], (16, clusters)))
    owner = matmul(owner_map, named)[:1].astype(jnp.int32)
    hot = (iota((max(owners, 16), rows), 0) == owner).astype(jnp.float32)
    upto = bf16(iota((rows, rows), 0) <= iota((rows, rows), 1))
    rank = jnp.sum(hot * matmul(bf16(hot), upto), axis=0, keepdims=True) - 1.0
    partner = owner ^ (me_ref[0] // len(orders))
    place = partner
    for index, ks in enumerate(zip(*orders)):
        place = jnp.where(partner == of_core(me_ref, ks), index, place)
    slot_ref[...] = place * capacity + rank.astype(jnp.int32)

    line = iota((8, rows), 0)
    digit = (line == ONE).astype(jnp.int32)
    for first, number in ((0, cluster + 1), (DIGITS, ints_ref[:, clusters + rows :])):
        for at in range(DIGITS):
            digit = jnp.where(line == first + at, (number >> (8 * at)) & 255, digit)
    digit = jnp.concatenate([digit, jnp.zeros((LANES - 8, rows), jnp.int32)], axis=0)
    digit_ref[...] = bf16(digit)


def pack_kernel(slot_ref, digit_ref, embed_ref, *out_refs):
    rows, width = embed_ref.shape
    each = out_refs[0].shape[0]
    values = embed_ref[...].astype(jnp.float32)
    mean_sq = jnp.sum(values * values, axis=1, keepdims=True) * (1.0 / width)
    unit = (values * lax.rsqrt(width * (mean_sq + 1e-06))).astype(jnp.bfloat16)
    slots = each * len(out_refs)
    move = bf16(iota((slots, rows), 0) == slot_ref[...])
    moved = matmul(move, unit).astype(jnp.bfloat16)
    moved_digit = matmul_t(move, digit_ref[...]).astype(jnp.bfloat16)
    for index, out_ref in enumerate(out_refs):
        part = slice(index * each, (index + 1) * each)
        out_ref[:, :width] = moved[part]
        out_ref[:, width:] = moved_digit[part]


def weights(number, at):
    value = jnp.zeros(at.shape, jnp.float32)
    for place in range(DIGITS):
        for which in (0, 1):
            here = (at == which * DIGITS + place) & (number == which)
            value = jnp.where(here, 256.0**place, value)
    return value.astype(jnp.bfloat16)


def key_rows(rows_all, digit):
    numbers = matmul_t(weights(iota((16, LANES), 0), iota((16, LANES), 1)), digit)
    low = (numbers[0:1].astype(jnp.int32) - 1) * rows_all
    return low, low + numbers[1:2].astype(jnp.int32)


def key_columns(rows_all, digit):
    shape = (LANES, 2 * LANES)
    numbers = matmul(digit, weights(iota(shape, 1) // LANES, iota(shape, 0)))
    low = (numbers[:, :LANES].astype(jnp.int32) - 1) * rows_all
    return low, low + numbers[:, LANES:].astype(jnp.int32)


def across(column, count):
    return jnp.concatenate([column] * (count // LANES), axis=1)


def compare(rows_all, query, query_low, query_key, lows, rows_ref):
    count, width = query.shape
    digit = rows_ref[:, width:]
    _, key = key_rows(rows_all, digit)
    bound = across(lows, key.shape[1])
    member = bf16((key >= bound) & (key < bound + rows_all))
    sums = matmul(member, rows_ref[...])
    scores = matmul_t(rows_ref[:, :width], query)
    _, key = key_columns(rows_all, digit)
    key = across(key, count)
    earlier = (key >= query_low) & (key < query_key)
    best = jnp.max(jnp.where(earlier, scores, -3.0), axis=0, keepdims=True)
    return best, sums


def near_kernel(
    rows_all, clusters, clus_dev, cores, me_ref, ints_ref, query_ref, lows_ref, key_ref, best_ref, sums_ref
):
    width = query_ref.shape[1] - LANES
    hot = (ints_ref[:, :clusters] == me_ref[0] // cores).astype(jnp.float32)
    rank = ranked(hot)
    shape = (clus_dev, clusters)
    kth = (rank == iota(shape, 0).astype(jnp.float32) + 1.0) & (hot > 0.0)
    own = jnp.sum(jnp.where(kth, iota(shape, 1).astype(jnp.float32), 0.0), axis=1, keepdims=True)
    own = jnp.broadcast_to(own.astype(jnp.int32) * rows_all, (clus_dev, LANES))
    digit = query_ref[:, width:]
    low, _ = key_columns(rows_all, digit)
    lows = jnp.concatenate([low, own], axis=0)
    query_low, query_key = key_rows(rows_all, digit)
    best, sums = compare(rows_all, query_ref[:, :width], query_low, query_key, lows, query_ref)
    lows_ref[...] = lows
    key_ref[...] = jnp.concatenate([query_low, query_key], axis=0)
    best_ref[...] = best
    sums_ref[...] = sums


def far_kernel(
    rows_all, query_ref, other_ref, lows_ref, key_ref, best_ref, sums_ref, result_ref, norm_ref
):
    queries = query_ref.shape[0]
    width = query_ref.shape[1] - LANES
    query = query_ref[:, :width]
    best, sums = compare(
        rows_all, query, key_ref[0:1], key_ref[1:2], lows_ref[...], other_ref
    )
    best = jnp.maximum(best, best_ref[...])
    best = jnp.where(best > -2.0, best, 0.0)
    sums = sums + sums_ref[...]
    counts = sums[:, width + ONE : width + ONE + 1]
    centroid = sums[:, :width] * (1.0 / jnp.maximum(counts, 1.0))
    offset = jnp.concatenate(
        [query.astype(jnp.float32) - centroid[:queries], centroid[queries:]], axis=0
    )
    offset = offset * offset
    squares = offset[:, :LANES]
    for start in range(LANES, width, LANES):
        squares = squares + offset[:, start : start + LANES]
    ones = jnp.ones((8, LANES), jnp.float32)
    total = matmul_t(ones, squares, lax.Precision.HIGHEST)[:1]
    result = jnp.concatenate([best, total[:, :queries]], axis=0)
    for owner in range(result_ref.shape[0]):
        result_ref[owner] = result
    norm_ref[...] = total[:, queries:]


def pick_kernel(
    orders, me_ref, slot_ref, result_ref, norm_ref, best_ref, distance_ref, cohesion_ref
):
    cohesion_ref[...] = norm_ref[...]
    rows = slot_ref.shape[1]
    owners, lines, slots = result_ref.shape
    place = iota((lines, slots), 1) // (slots // owners)
    values = jnp.zeros((lines, slots), jnp.float32)
    for index, ks in enumerate(zip(*orders)):
        partner = (me_ref[0] // len(orders)) ^ of_core(me_ref, ks)
        values = jnp.where(place == index, result_ref[partner], values)
    values = jnp.concatenate([values, jnp.zeros((8 - lines, slots), jnp.float32)], axis=0)
    at = (iota((slots, rows), 0) == slot_ref[...]).astype(jnp.float32)
    picked = jnp.dot(
        values, at, precision=lax.Precision.HIGHEST, preferred_element_type=jnp.float32
    )
    best_ref[...] = picked[0:1]
    distance_ref[...] = picked[1:2]


def partner_orders(owners, cores):
    half = owners // 2
    far, near = list(range(half, owners)), list(range(2, half))
    orders = []
    for core in range(cores):
        order, f, n = [], list(far), list(near)
        take = [f, n] if core % 2 == 0 else [f, f, n]
        while f or n:
            for source in take if f and n else [f or n]:
                if source:
                    order.append(source.pop(0))
            take = [f, n]
        orders.append(order + list(range(1, min(half, 2))) + [0])
    return orders


def exchange(packed, orders):
    owners, cores = lax.axis_size("shard"), lax.axis_size("sub")
    got = []
    for block, ks in zip(packed, zip(*orders)):
        pairs = [
            (i * cores + core, (i ^ k) * cores + core)
            for i in range(owners)
            for core, k in enumerate(ks)
        ]
        got.append(lax.ppermute(block, ("shard", "sub"), pairs) if any(ks) else block)
    return jnp.concatenate(got)


def exchange_all(packed, me):
    owners = lax.axis_size("shard")
    partner = me ^ jnp.arange(owners, dtype=jnp.int32)
    parted = packed.reshape(owners, -1, packed.shape[1])
    got = lax.all_to_all(parted[partner], "shard", 0, 0, tiled=True)
    return got[partner].reshape(packed.shape)


def local(embeddings, cluster_id, item_order, owner_map):
    owners = lax.axis_size("shard")
    local_rows, width = embeddings.shape
    rows_all = local_rows * owners * lax.axis_size("sub")
    clus_dev = owner_map.shape[0] // owners
    capacity = 2 * local_rows // owners
    slots = owners * capacity
    wide = width + LANES
    params = pltpu.CompilerParams(vmem_limit_bytes=32 << 20)
    compare_cost = pl.CostEstimate(
        flops=4 * slots * slots * width, bytes_accessed=4 * slots * wide, transcendentals=0
    )
    me = lax.axis_index(("shard", "sub")).astype(jnp.int32).reshape(1)
    ints = jnp.concatenate([owner_map, cluster_id, item_order]).reshape(1, -1)

    direct = owners <= MOST_PERMUTES
    cores = lax.axis_size("sub")
    orders = partner_orders(owners, cores) if direct else [list(range(owners))] * cores
    parts = owners if direct else 1
    slot, digit = pl.pallas_call(
        functools.partial(slot_kernel, owners, capacity, orders, local_rows),
        out_shape=[
            jax.ShapeDtypeStruct((1, local_rows), jnp.int32),
            jax.ShapeDtypeStruct((LANES, local_rows), jnp.bfloat16),
        ],
        in_specs=[SCALAR, WHOLE],
        out_specs=[WHOLE] * 2,
        compiler_params=params,
        cost_estimate=pl.CostEstimate(flops=1 << 29, bytes_accessed=1 << 16, transcendentals=0),
        name="slots",
    )(me, ints)
    packed = pl.pallas_call(
        pack_kernel,
        out_shape=[jax.ShapeDtypeStruct((slots // parts, wide), jnp.bfloat16)] * parts,
        in_specs=[WHOLE] * 3,
        out_specs=[WHOLE] * parts,
        compiler_params=params,
        name="pack",
    )(slot, digit, embeddings)
    query = exchange(packed, orders) if direct else exchange_all(packed[0], lax.axis_index("shard"))
    other = lax.ppermute(query, "sub", [(core, core ^ 1) for core in range(cores)])
    asked = slots + clus_dev
    near = pl.pallas_call(
        functools.partial(near_kernel, rows_all, owner_map.shape[0], clus_dev, cores),
        out_shape=[
            jax.ShapeDtypeStruct((asked, LANES), jnp.int32),
            jax.ShapeDtypeStruct((2, slots), jnp.int32),
            jax.ShapeDtypeStruct((1, slots), jnp.float32),
            jax.ShapeDtypeStruct((asked, wide), jnp.float32),
        ],
        in_specs=[SCALAR] + [WHOLE] * 2,
        out_specs=[WHOLE] * 4,
        compiler_params=params,
        cost_estimate=compare_cost,
        name="near",
    )(me, ints, query)
    results, norms = pl.pallas_call(
        functools.partial(far_kernel, rows_all),
        out_shape=[
            jax.ShapeDtypeStruct((owners, 2, slots), jnp.float32),
            jax.ShapeDtypeStruct((1, clus_dev), jnp.float32),
        ],
        in_specs=[WHOLE] * 6,
        out_specs=[WHOLE] * 2,
        compiler_params=params,
        cost_estimate=compare_cost,
        name="far",
    )(query, other, *near)
    results = lax.all_to_all(results, "shard", 0, 0, tiled=True)
    best, distance, cohesion = pl.pallas_call(
        functools.partial(pick_kernel, orders),
        out_shape=[jax.ShapeDtypeStruct((1, local_rows), jnp.float32)] * 2
        + [jax.ShapeDtypeStruct((1, clus_dev), jnp.float32)],
        in_specs=[SCALAR] + [WHOLE] * 3,
        out_specs=[WHOLE] * 3,
        compiler_params=params,
        name="pick",
    )(me, slot, results, norms)
    return best.reshape(local_rows), distance.reshape(local_rows), cohesion.reshape(clus_dev)


def solution(mesh):
    in_specs = (
        P(("groups", "shard", "sub"), None),
        P(("groups", "shard", "sub")),
        P(("groups", "shard", "sub")),
        P("groups"),
    )
    out_specs = (
        P(("groups", "shard", "sub")),
        P(("groups", "shard", "sub")),
        P(("groups", "shard")),
    )
    return jax.shard_map(local, mesh=mesh, in_specs=in_specs, out_specs=out_specs, check_vma=False)
```

```python
import functools

import jax
import jax.numpy as jnp
from jax import lax
from jax.experimental import pallas as pl
from jax.experimental.pallas import tpu as pltpu
from jax.sharding import PartitionSpec as P

LANES = 128
DIGITS = 3
MOST_PERMUTES = 8
WHOLE = pl.BlockSpec(memory_space=pltpu.VMEM)
SCALAR = pl.BlockSpec(memory_space=pltpu.SMEM)


def iota(shape, dim):
    return lax.broadcasted_iota(jnp.int32, shape, dim)


def matmul(a, b):
    return jnp.dot(a, b, preferred_element_type=jnp.float32)


def matmul_t(a, b, precision=None):
    return lax.dot_general(
        a, b, (((1,), (1,)), ((), ())), precision=precision, preferred_element_type=jnp.float32
    )


def bf16(x):
    return x.astype(jnp.float32).astype(jnp.bfloat16)


def ranked(hot):
    upto = (iota((LANES, LANES), 0) <= iota((LANES, LANES), 1)).astype(jnp.bfloat16)
    before, parts = jnp.zeros((1, 1), jnp.float32), []
    for start in range(0, hot.shape[1], LANES):
        piece = hot[:, start : start + LANES]
        spread = jnp.broadcast_to(piece, (16, LANES)).astype(jnp.bfloat16)
        parts.append(matmul(spread, upto)[:1] + before)
        before = before + jnp.sum(piece, axis=1, keepdims=True)
    return jnp.concatenate(parts, axis=1)


def slot_kernel(
    owners, capacity, order, parts, rows, me_ref, ints_ref, slot_ref, digit_ref
):
    clusters = ints_ref.shape[1] - 2 * rows
    cluster = ints_ref[:, clusters : clusters + rows]
    named = bf16(iota((clusters, rows), 0) == cluster)
    owner_map = bf16(jnp.broadcast_to(ints_ref[:, :clusters], (16, clusters)))
    owner = matmul(owner_map, named)[:1].astype(jnp.int32)
    hot = (iota((max(owners, 16), rows), 0) == owner).astype(jnp.float32)
    upto = bf16(iota((rows, rows), 0) <= iota((rows, rows), 1))
    rank = jnp.sum(hot * matmul(bf16(hot), upto), axis=0, keepdims=True) - 1.0
    rank = rank.astype(jnp.int32)
    partner = owner ^ me_ref[0]
    place = partner
    for index, k in enumerate(order):
        place = jnp.where(partner == k, index, place)
    if parts == 1:
        slot_ref[...] = place * capacity + rank
    else:
        half = capacity // 2
        later = (rank >= half).astype(jnp.int32)
        slot_ref[...] = place * half + rank + later * (owners * half - half)

    line = iota((8, rows), 0)
    digit = jnp.zeros((8, rows), jnp.int32)
    for first, number in ((0, cluster + 1), (DIGITS, ints_ref[:, clusters + rows :])):
        for at in range(DIGITS):
            digit = jnp.where(line == first + at, (number >> (8 * at)) & 255, digit)
    empty = jnp.zeros((LANES // 2 - 8, rows), jnp.int32)
    none = jnp.zeros((LANES // 2, rows), jnp.int32)
    early = jnp.concatenate([digit, empty, none], axis=0)
    late = jnp.concatenate([none, digit, empty], axis=0)
    digit_ref[...] = bf16(jnp.concatenate([early, late], axis=1))


def pack_kernel(slot_ref, digit_ref, embed_ref, *out_refs):
    rows, width = embed_ref.shape
    tiles, half, _ = out_refs[0].shape
    values = embed_ref[...].astype(jnp.float32)
    mean_sq = jnp.sum(values * values, axis=1, keepdims=True) * (1.0 / width)
    unit = (values * lax.rsqrt(width * (mean_sq + 1e-06))).astype(jnp.bfloat16)
    late = half * len(out_refs)
    move = bf16(iota((2 * late, rows), 0) == slot_ref[...])
    moved = matmul(move, unit).astype(jnp.bfloat16)
    both = jnp.concatenate([move[:late], move[late:]], axis=1)
    digit = matmul_t(both, digit_ref[...]).astype(jnp.bfloat16)
    each = tiles // 2
    for index, out_ref in enumerate(out_refs):
        start = index * half
        for tile in range(each):
            lanes = slice(tile * LANES, (tile + 1) * LANES)
            out_ref[tile] = moved[start : start + half, lanes]
            out_ref[each + tile] = moved[late + start : late + start + half, lanes]
        out_ref[tiles - 1] = digit[start : start + half]


def unpacked(block_ref, tiles):
    blocks = block_ref.shape[0] // tiles
    each = tiles // 2

    def column(tile):
        return jnp.concatenate([block_ref[i * tiles + tile] for i in range(blocks)], axis=0)

    halves = [
        jnp.concatenate([column(first + tile) for tile in range(each)], axis=1)
        for first in (0, each)
    ]
    return jnp.concatenate(halves, axis=0), column(tiles - 1)


def weights(number, at, half):
    value = jnp.zeros(at.shape, jnp.float32)
    for place in range(DIGITS):
        for which in (0, 1):
            lane = half * (LANES // 2) + which * DIGITS + place
            value = jnp.where((at == lane) & (number == which), 256.0**place, value)
    return value.astype(jnp.bfloat16)


def key_rows(rows_all, digit):
    at = iota((16, LANES), 0), iota((16, LANES), 1)
    numbers = [matmul_t(weights(*at, half), digit) for half in (0, 1)]
    numbers = jnp.concatenate(numbers, axis=1)
    low = (numbers[0:1].astype(jnp.int32) - 1) * rows_all
    return low, low + numbers[1:2].astype(jnp.int32)


def key_columns(rows_all, digit):
    at = iota((LANES, 2 * LANES), 1) // LANES, iota((LANES, 2 * LANES), 0)
    numbers = [matmul(digit, weights(*at, half)) for half in (0, 1)]
    numbers = jnp.concatenate(numbers, axis=0)
    low = (numbers[:, :LANES].astype(jnp.int32) - 1) * rows_all
    return low, low + numbers[:, LANES:].astype(jnp.int32)


def across(column, count):
    return jnp.concatenate([column] * (count // LANES), axis=1)


def compare(rows_all, query, query_low, query_key, lows, rows, digit):
    _, key = key_rows(rows_all, digit)
    bound = across(lows, key.shape[1])
    member = bf16((key >= bound) & (key < bound + rows_all))
    sums = matmul(member, rows)
    counts = matmul(member, jnp.ones((rows.shape[0], LANES), jnp.bfloat16))
    scores = matmul_t(rows, query)
    _, key = key_columns(rows_all, digit)
    key = across(key, query.shape[0])
    earlier = (key >= query_low) & (key < query_key)
    best = jnp.max(jnp.where(earlier, scores, -3.0), axis=0, keepdims=True)
    return best, sums, counts


def near_kernel(
    rows_all, clusters, clus_dev, tiles, me_ref, ints_ref, query_ref,
    lows_ref, key_ref, best_ref, sums_ref, counts_ref,
):
    hot = (ints_ref[:, :clusters] == me_ref[0]).astype(jnp.float32)
    rank = ranked(hot)
    shape = (clus_dev, clusters)
    kth = (rank == iota(shape, 0).astype(jnp.float32) + 1.0) & (hot > 0.0)
    own = jnp.sum(jnp.where(kth, iota(shape, 1).astype(jnp.float32), 0.0), axis=1, keepdims=True)
    own = jnp.broadcast_to(own.astype(jnp.int32) * rows_all, (clus_dev, LANES))
    query, digit = unpacked(query_ref, tiles)
    low, _ = key_columns(rows_all, digit)
    lows = jnp.concatenate([low, own], axis=0)
    query_low, query_key = key_rows(rows_all, digit)
    best, sums, counts = compare(rows_all, query, query_low, query_key, lows, query, digit)
    lows_ref[...] = lows
    key_ref[...] = jnp.concatenate([query_low, query_key], axis=0)
    best_ref[...] = best
    sums_ref[...] = sums
    counts_ref[...] = counts


def far_kernel(
    rows_all, tiles, query_ref, other_ref, lows_ref, key_ref, best_ref, sums_ref, counts_ref,
    result_ref, norm_ref,
):
    query, _ = unpacked(query_ref, tiles)
    queries, width = query.shape
    rows, digit = unpacked(other_ref, tiles)
    best, sums, counts = compare(
        rows_all, query, key_ref[0:1], key_ref[1:2], lows_ref[...], rows, digit
    )
    best = jnp.maximum(best, best_ref[...])
    best = jnp.where(best > -2.0, best, 0.0)
    share = 1.0 / jnp.maximum(counts + counts_ref[...], 1.0)
    squares = jnp.zeros(share.shape, jnp.float32)
    for start in range(0, width, LANES):
        lanes = slice(start, start + LANES)
        centroid = (sums[:, lanes] + sums_ref[:, lanes]) * share
        offset = jnp.concatenate(
            [query[:, lanes].astype(jnp.float32) - centroid[:queries], centroid[queries:]], axis=0
        )
        squares = squares + offset * offset
    ones = jnp.ones((8, LANES), jnp.float32)
    total = matmul_t(ones, squares, lax.Precision.HIGHEST)[:1]
    result = jnp.concatenate([best, total[:, :queries]], axis=0)
    for owner in range(result_ref.shape[0]):
        result_ref[owner] = result
    norm_ref[...] = total[:, queries:]


def pick_kernel(
    order, parts, me_ref, slot_ref, result_ref, norm_ref, best_ref, distance_ref, cohesion_ref
):
    cohesion_ref[...] = norm_ref[...]
    rows = slot_ref.shape[1]
    owners, lines, slots = result_ref.shape
    folds = min(parts, 2)
    place = iota((lines, slots), 1) % (slots // folds) // (slots // owners // folds)
    values = jnp.zeros((lines, slots), jnp.float32)
    for index, k in enumerate(order):
        values = jnp.where(place == index, result_ref[me_ref[0] ^ k], values)
    values = jnp.concatenate([values, jnp.zeros((8 - lines, slots), jnp.float32)], axis=0)
    at = (iota((slots, rows), 0) == slot_ref[...]).astype(jnp.float32)
    picked = jnp.dot(
        values, at, precision=lax.Precision.HIGHEST, preferred_element_type=jnp.float32
    )
    best_ref[...] = picked[0:1]
    distance_ref[...] = picked[1:2]


def from_partner(value, k, axis):
    return lax.ppermute(value, axis, [(i, i ^ k) for i in range(lax.axis_size(axis))])


def partner_order(owners):
    half = owners // 2
    far, near = list(range(half, owners)), list(range(2, half))
    return far[:1] + near + far[1:] + list(range(1, min(half, 2))) + [0]


def exchange(packed, order):
    return jnp.concatenate(
        [from_partner(block, k, "shard") if k else block for k, block in zip(order, packed)]
    )


def exchange_all(packed, me):
    owners = lax.axis_size("shard")
    tiles, half, _ = packed.shape
    each = tiles // 2
    data = packed[:-1].reshape(2, each, half, LANES).transpose(0, 2, 1, 3).reshape(2 * half, -1)
    digit = jnp.concatenate(jnp.split(packed[-1], 2, axis=1))
    parted = jnp.concatenate([data, digit], axis=1).reshape(owners, 2 * half // owners, -1)
    partner = me ^ jnp.arange(owners, dtype=jnp.int32)
    got = lax.all_to_all(parted[partner], "shard", 0, 0, tiled=True)[partner].reshape(2 * half, -1)
    data = got[:, : each * LANES].reshape(2, half, each, LANES).transpose(0, 2, 1, 3)
    digit = jnp.concatenate(jnp.split(got[:, each * LANES :], 2), axis=1)
    return jnp.concatenate([data.reshape(2 * each, half, LANES), digit[None]])


def local(embeddings, cluster_id, item_order, owner_map):
    owners = lax.axis_size("shard")
    local_rows, width = embeddings.shape
    rows_all = local_rows * owners * lax.axis_size("sub")
    clus_dev = owner_map.shape[0] // owners
    capacity = 2 * local_rows // owners
    slots = owners * capacity
    params = pltpu.CompilerParams(vmem_limit_bytes=32 << 20)
    compare_cost = pl.CostEstimate(
        flops=4 * slots * slots * width, bytes_accessed=4 * slots * width, transcendentals=0
    )
    me = lax.axis_index("shard").astype(jnp.int32).reshape(1)
    ints = jnp.concatenate([owner_map, cluster_id, item_order]).reshape(1, -1)

    direct = owners <= MOST_PERMUTES
    order = partner_order(owners) if direct else list(range(owners))
    parts = owners if direct else 1
    tiles = 2 * (width // LANES) + 1
    block = (tiles, slots // parts // 2, LANES)
    slot, digit = pl.pallas_call(
        functools.partial(slot_kernel, owners, capacity, order, parts, local_rows),
        out_shape=[
            jax.ShapeDtypeStruct((1, local_rows), jnp.int32),
            jax.ShapeDtypeStruct((LANES, 2 * local_rows), jnp.bfloat16),
        ],
        in_specs=[SCALAR, WHOLE],
        out_specs=[WHOLE] * 2,
        compiler_params=params,
        cost_estimate=pl.CostEstimate(flops=1 << 29, bytes_accessed=1 << 16, transcendentals=0),
        name="slots",
    )(me, ints)
    packed = pl.pallas_call(
        pack_kernel,
        out_shape=[jax.ShapeDtypeStruct(block, jnp.bfloat16)] * parts,
        in_specs=[WHOLE] * 3,
        out_specs=[WHOLE] * parts,
        compiler_params=params,
        name="pack",
    )(slot, digit, embeddings)
    query = exchange(packed, order) if direct else exchange_all(packed[0], me[0])
    other = from_partner(query, 1, "sub")
    asked = slots + clus_dev
    near = pl.pallas_call(
        functools.partial(near_kernel, rows_all, owner_map.shape[0], clus_dev, tiles),
        out_shape=[
            jax.ShapeDtypeStruct((asked, LANES), jnp.int32),
            jax.ShapeDtypeStruct((2, slots), jnp.int32),
            jax.ShapeDtypeStruct((1, slots), jnp.float32),
            jax.ShapeDtypeStruct((asked, width), jnp.float32),
            jax.ShapeDtypeStruct((asked, LANES), jnp.float32),
        ],
        in_specs=[SCALAR] + [WHOLE] * 2,
        out_specs=[WHOLE] * 5,
        compiler_params=params,
        cost_estimate=compare_cost,
        name="near",
    )(me, ints, query)
    results, norms = pl.pallas_call(
        functools.partial(far_kernel, rows_all, tiles),
        out_shape=[
            jax.ShapeDtypeStruct((owners, 2, slots), jnp.float32),
            jax.ShapeDtypeStruct((1, clus_dev), jnp.float32),
        ],
        in_specs=[WHOLE] * 7,
        out_specs=[WHOLE] * 2,
        compiler_params=params,
        cost_estimate=compare_cost,
        name="far",
    )(query, other, *near)
    results = lax.all_to_all(results, "shard", 0, 0, tiled=True)
    best, distance, cohesion = pl.pallas_call(
        functools.partial(pick_kernel, order, parts),
        out_shape=[jax.ShapeDtypeStruct((1, local_rows), jnp.float32)] * 2
        + [jax.ShapeDtypeStruct((1, clus_dev), jnp.float32)],
        in_specs=[SCALAR] + [WHOLE] * 3,
        out_specs=[WHOLE] * 3,
        compiler_params=params,
        name="pick",
    )(me, slot, results, norms)
    return best.reshape(local_rows), distance.reshape(local_rows), cohesion.reshape(clus_dev)


def solution(mesh):
    in_specs = (
        P(("groups", "shard", "sub"), None),
        P(("groups", "shard", "sub")),
        P(("groups", "shard", "sub")),
        P("groups"),
    )
    out_specs = (
        P(("groups", "shard", "sub")),
        P(("groups", "shard", "sub")),
        P(("groups", "shard")),
    )
    return jax.shard_map(local, mesh=mesh, in_specs=in_specs, out_specs=out_specs, check_vma=False)
```

```python
import functools

import jax
import jax.numpy as jnp
from jax import lax
from jax.experimental import pallas as pl
from jax.experimental.pallas import tpu as pltpu
from jax.sharding import PartitionSpec as P

LANES = 128
DIGITS = 3
PARTNERS = (4, 5, 1, 2, 6, 3, 7, 0)
WHOLE = pl.BlockSpec(memory_space=pltpu.VMEM)
SCALAR = pl.BlockSpec(memory_space=pltpu.SMEM)


def iota(shape, dim):
    return lax.broadcasted_iota(jnp.int32, shape, dim)


def matmul(a, b):
    return jnp.dot(a, b, preferred_element_type=jnp.float32)


def matmul_t(a, b, precision=None):
    return lax.dot_general(
        a, b, (((1,), (1,)), ((), ())), precision=precision, preferred_element_type=jnp.float32
    )


def bf16(x):
    return x.astype(jnp.float32).astype(jnp.bfloat16)


def ranked(hot):
    upto = (iota((LANES, LANES), 0) <= iota((LANES, LANES), 1)).astype(jnp.bfloat16)
    before, parts = jnp.zeros((1, 1), jnp.float32), []
    for start in range(0, hot.shape[1], LANES):
        piece = hot[:, start : start + LANES]
        spread = jnp.broadcast_to(piece, (16, LANES)).astype(jnp.bfloat16)
        parts.append(matmul(spread, upto)[:1] + before)
        before = before + jnp.sum(piece, axis=1, keepdims=True)
    return jnp.concatenate(parts, axis=1)


def slot_kernel(
    owners, capacity, order, parts, rows, me_ref, ints_ref, slot_ref, digit_ref
):
    clusters = ints_ref.shape[1] - 2 * rows
    cluster = ints_ref[:, clusters : clusters + rows]
    named = bf16(iota((clusters, rows), 0) == cluster)
    owner_map = bf16(jnp.broadcast_to(ints_ref[:, :clusters], (16, clusters)))
    owner = matmul(owner_map, named)[:1].astype(jnp.int32)
    hot = (iota((max(owners, 16), rows), 0) == owner).astype(jnp.float32)
    upto = bf16(iota((rows, rows), 0) <= iota((rows, rows), 1))
    rank = jnp.sum(hot * matmul(bf16(hot), upto), axis=0, keepdims=True) - 1.0
    rank = rank.astype(jnp.int32)
    partner = owner ^ me_ref[0]
    place = partner
    for index, k in enumerate(order):
        place = jnp.where(partner == k, index, place)
    if parts == 1:
        slot_ref[...] = place * capacity + rank
    else:
        half = capacity // 2
        later = (rank >= half).astype(jnp.int32)
        slot_ref[...] = place * half + rank + later * (owners * half - half)

    line = iota((8, rows), 0)
    digit = jnp.zeros((8, rows), jnp.int32)
    for first, number in ((0, cluster + 1), (DIGITS, ints_ref[:, clusters + rows :])):
        for at in range(DIGITS):
            digit = jnp.where(line == first + at, (number >> (8 * at)) & 255, digit)
    empty = jnp.zeros((LANES // 2 - 8, rows), jnp.int32)
    none = jnp.zeros((LANES // 2, rows), jnp.int32)
    early = jnp.concatenate([digit, empty, none], axis=0)
    late = jnp.concatenate([none, digit, empty], axis=0)
    digit_ref[...] = bf16(jnp.concatenate([early, late], axis=1))


def pack_kernel(slot_ref, digit_ref, embed_ref, *out_refs):
    rows, width = embed_ref.shape
    tiles, half, _ = out_refs[0].shape
    values = embed_ref[...].astype(jnp.float32)
    mean_sq = jnp.sum(values * values, axis=1, keepdims=True) * (1.0 / width)
    unit = (values * lax.rsqrt(width * (mean_sq + 1e-06))).astype(jnp.bfloat16)
    late = half * len(out_refs)
    move = bf16(iota((2 * late, rows), 0) == slot_ref[...])
    moved = matmul(move, unit).astype(jnp.bfloat16)
    both = jnp.concatenate([move[:late], move[late:]], axis=1)
    digit = matmul_t(both, digit_ref[...]).astype(jnp.bfloat16)
    each = tiles // 2
    for index, out_ref in enumerate(out_refs):
        start = index * half
        for tile in range(each):
            lanes = slice(tile * LANES, (tile + 1) * LANES)
            out_ref[tile] = moved[start : start + half, lanes]
            out_ref[each + tile] = moved[late + start : late + start + half, lanes]
        out_ref[tiles - 1] = digit[start : start + half]


def unpacked(block_ref, tiles):
    blocks = block_ref.shape[0] // tiles
    each = tiles // 2

    def column(tile):
        return jnp.concatenate([block_ref[i * tiles + tile] for i in range(blocks)], axis=0)

    halves = [
        jnp.concatenate([column(first + tile) for tile in range(each)], axis=1)
        for first in (0, each)
    ]
    return jnp.concatenate(halves, axis=0), column(tiles - 1)


def weights(number, at, half):
    value = jnp.zeros(at.shape, jnp.float32)
    for place in range(DIGITS):
        for which in (0, 1):
            lane = half * (LANES // 2) + which * DIGITS + place
            value = jnp.where((at == lane) & (number == which), 256.0**place, value)
    return value.astype(jnp.bfloat16)


def key_rows(rows_all, digit):
    at = iota((16, LANES), 0), iota((16, LANES), 1)
    numbers = [matmul_t(weights(*at, half), digit) for half in (0, 1)]
    numbers = jnp.concatenate(numbers, axis=1)
    low = (numbers[0:1].astype(jnp.int32) - 1) * rows_all
    return low, low + numbers[1:2].astype(jnp.int32)


def key_columns(rows_all, digit):
    at = iota((LANES, 2 * LANES), 1) // LANES, iota((LANES, 2 * LANES), 0)
    numbers = [matmul(digit, weights(*at, half)) for half in (0, 1)]
    numbers = jnp.concatenate(numbers, axis=0)
    low = (numbers[:, :LANES].astype(jnp.int32) - 1) * rows_all
    return low, low + numbers[:, LANES:].astype(jnp.int32)


def across(column, count):
    return jnp.concatenate([column] * (count // LANES), axis=1)


def compare(rows_all, query, query_low, query_key, lows, rows, digit):
    _, key = key_rows(rows_all, digit)
    bound = across(lows, key.shape[1])
    member = bf16((key >= bound) & (key < bound + rows_all))
    sums = matmul(member, rows)
    counts = matmul(member, jnp.ones((rows.shape[0], LANES), jnp.bfloat16))
    scores = matmul_t(rows, query)
    _, key = key_columns(rows_all, digit)
    key = across(key, query.shape[0])
    earlier = (key >= query_low) & (key < query_key)
    best = jnp.max(jnp.where(earlier, scores, -3.0), axis=0, keepdims=True)
    return best, sums, counts


def near_kernel(
    rows_all, clusters, clus_dev, tiles, me_ref, ints_ref, query_ref,
    lows_ref, key_ref, best_ref, sums_ref, counts_ref,
):
    hot = (ints_ref[:, :clusters] == me_ref[0]).astype(jnp.float32)
    rank = ranked(hot)
    shape = (clus_dev, clusters)
    kth = (rank == iota(shape, 0).astype(jnp.float32) + 1.0) & (hot > 0.0)
    own = jnp.sum(jnp.where(kth, iota(shape, 1).astype(jnp.float32), 0.0), axis=1, keepdims=True)
    own = jnp.broadcast_to(own.astype(jnp.int32) * rows_all, (clus_dev, LANES))
    query, digit = unpacked(query_ref, tiles)
    low, _ = key_columns(rows_all, digit)
    lows = jnp.concatenate([low, own], axis=0)
    query_low, query_key = key_rows(rows_all, digit)
    best, sums, counts = compare(rows_all, query, query_low, query_key, lows, query, digit)
    lows_ref[...] = lows
    key_ref[...] = jnp.concatenate([query_low, query_key], axis=0)
    best_ref[...] = best
    sums_ref[...] = sums
    counts_ref[...] = counts


def far_kernel(
    rows_all, tiles, query_ref, other_ref, lows_ref, key_ref, best_ref, sums_ref, counts_ref,
    result_ref, norm_ref,
):
    query, _ = unpacked(query_ref, tiles)
    queries, width = query.shape
    rows, digit = unpacked(other_ref, tiles)
    best, sums, counts = compare(
        rows_all, query, key_ref[0:1], key_ref[1:2], lows_ref[...], rows, digit
    )
    best = jnp.maximum(best, best_ref[...])
    best = jnp.where(best > -2.0, best, 0.0)
    share = 1.0 / jnp.maximum(counts + counts_ref[...], 1.0)
    squares = jnp.zeros(share.shape, jnp.float32)
    for start in range(0, width, LANES):
        lanes = slice(start, start + LANES)
        centroid = (sums[:, lanes] + sums_ref[:, lanes]) * share
        offset = jnp.concatenate(
            [query[:, lanes].astype(jnp.float32) - centroid[:queries], centroid[queries:]], axis=0
        )
        squares = squares + offset * offset
    ones = jnp.ones((8, LANES), jnp.float32)
    total = matmul_t(ones, squares, lax.Precision.HIGHEST)[:1]
    result = jnp.concatenate([best, total[:, :queries]], axis=0)
    for owner in range(result_ref.shape[0]):
        result_ref[owner] = result
    norm_ref[...] = total[:, queries:]


def pick_kernel(
    order, parts, me_ref, slot_ref, result_ref, norm_ref, best_ref, distance_ref, cohesion_ref
):
    cohesion_ref[...] = norm_ref[...]
    rows = slot_ref.shape[1]
    owners, lines, slots = result_ref.shape
    folds = min(parts, 2)
    place = iota((lines, slots), 1) % (slots // folds) // (slots // owners // folds)
    values = jnp.zeros((lines, slots), jnp.float32)
    for index, k in enumerate(order):
        values = jnp.where(place == index, result_ref[me_ref[0] ^ k], values)
    values = jnp.concatenate([values, jnp.zeros((8 - lines, slots), jnp.float32)], axis=0)
    at = (iota((slots, rows), 0) == slot_ref[...]).astype(jnp.float32)
    picked = jnp.dot(
        values, at, precision=lax.Precision.HIGHEST, preferred_element_type=jnp.float32
    )
    best_ref[...] = picked[0:1]
    distance_ref[...] = picked[1:2]


def from_partner(value, k, axis):
    return lax.ppermute(value, axis, [(i, i ^ k) for i in range(lax.axis_size(axis))])


def exchange(packed, order):
    return jnp.concatenate(
        [from_partner(block, k, "shard") if k else block for k, block in zip(order, packed)]
    )


def exchange_all(packed, me):
    owners = lax.axis_size("shard")
    tiles, half, _ = packed.shape
    each = tiles // 2
    data = packed[:-1].reshape(2, each, half, LANES).transpose(0, 2, 1, 3).reshape(2 * half, -1)
    digit = jnp.concatenate(jnp.split(packed[-1], 2, axis=1))
    parted = jnp.concatenate([data, digit], axis=1).reshape(owners, 2 * half // owners, -1)
    partner = me ^ jnp.arange(owners, dtype=jnp.int32)
    got = lax.all_to_all(parted[partner], "shard", 0, 0, tiled=True)[partner].reshape(2 * half, -1)
    data = got[:, : each * LANES].reshape(2, half, each, LANES).transpose(0, 2, 1, 3)
    digit = jnp.concatenate(jnp.split(got[:, each * LANES :], 2), axis=1)
    return jnp.concatenate([data.reshape(2 * each, half, LANES), digit[None]])


def local(embeddings, cluster_id, item_order, owner_map):
    owners = lax.axis_size("shard")
    local_rows, width = embeddings.shape
    rows_all = local_rows * owners * lax.axis_size("sub")
    clus_dev = owner_map.shape[0] // owners
    capacity = 2 * local_rows // owners
    slots = owners * capacity
    params = pltpu.CompilerParams(vmem_limit_bytes=32 << 20)
    compare_cost = pl.CostEstimate(
        flops=4 * slots * slots * width, bytes_accessed=4 * slots * width, transcendentals=0
    )
    me = lax.axis_index("shard").astype(jnp.int32).reshape(1)
    ints = jnp.concatenate([owner_map, cluster_id, item_order]).reshape(1, -1)

    direct = owners == len(PARTNERS)
    order = PARTNERS if direct else tuple(range(owners))
    parts = owners if direct else 1
    tiles = 2 * (width // LANES) + 1
    block = (tiles, slots // parts // 2, LANES)
    slot, digit = pl.pallas_call(
        functools.partial(slot_kernel, owners, capacity, order, parts, local_rows),
        out_shape=[
            jax.ShapeDtypeStruct((1, local_rows), jnp.int32),
            jax.ShapeDtypeStruct((LANES, 2 * local_rows), jnp.bfloat16),
        ],
        in_specs=[SCALAR, WHOLE],
        out_specs=[WHOLE] * 2,
        compiler_params=params,
        cost_estimate=pl.CostEstimate(flops=1 << 29, bytes_accessed=1 << 16, transcendentals=0),
        name="slots",
    )(me, ints)
    packed = pl.pallas_call(
        pack_kernel,
        out_shape=[jax.ShapeDtypeStruct(block, jnp.bfloat16)] * parts,
        in_specs=[WHOLE] * 3,
        out_specs=[WHOLE] * parts,
        compiler_params=params,
        name="pack",
    )(slot, digit, embeddings)
    query = exchange(packed, order) if direct else exchange_all(packed[0], me[0])
    other = from_partner(query, 1, "sub")
    asked = slots + clus_dev
    near = pl.pallas_call(
        functools.partial(near_kernel, rows_all, owner_map.shape[0], clus_dev, tiles),
        out_shape=[
            jax.ShapeDtypeStruct((asked, LANES), jnp.int32),
            jax.ShapeDtypeStruct((2, slots), jnp.int32),
            jax.ShapeDtypeStruct((1, slots), jnp.float32),
            jax.ShapeDtypeStruct((asked, width), jnp.float32),
            jax.ShapeDtypeStruct((asked, LANES), jnp.float32),
        ],
        in_specs=[SCALAR] + [WHOLE] * 2,
        out_specs=[WHOLE] * 5,
        compiler_params=params,
        cost_estimate=compare_cost,
        name="near",
    )(me, ints, query)
    results, norms = pl.pallas_call(
        functools.partial(far_kernel, rows_all, tiles),
        out_shape=[
            jax.ShapeDtypeStruct((owners, 2, slots), jnp.float32),
            jax.ShapeDtypeStruct((1, clus_dev), jnp.float32),
        ],
        in_specs=[WHOLE] * 7,
        out_specs=[WHOLE] * 2,
        compiler_params=params,
        cost_estimate=compare_cost,
        name="far",
    )(query, other, *near)
    results = lax.all_to_all(results, "shard", 0, 0, tiled=True)
    best, distance, cohesion = pl.pallas_call(
        functools.partial(pick_kernel, order, parts),
        out_shape=[jax.ShapeDtypeStruct((1, local_rows), jnp.float32)] * 2
        + [jax.ShapeDtypeStruct((1, clus_dev), jnp.float32)],
        in_specs=[SCALAR] + [WHOLE] * 3,
        out_specs=[WHOLE] * 3,
        compiler_params=params,
        name="pick",
    )(me, slot, results, norms)
    return best.reshape(local_rows), distance.reshape(local_rows), cohesion.reshape(clus_dev)


def solution(mesh):
    in_specs = (
        P(("groups", "shard", "sub"), None),
        P(("groups", "shard", "sub")),
        P(("groups", "shard", "sub")),
        P("groups"),
    )
    out_specs = (
        P(("groups", "shard", "sub")),
        P(("groups", "shard", "sub")),
        P(("groups", "shard")),
    )
    return jax.shard_map(local, mesh=mesh, in_specs=in_specs, out_specs=out_specs, check_vma=False)
```

```python
import functools

import jax
import jax.numpy as jnp
from jax import lax
from jax.experimental import pallas as pl
from jax.experimental.pallas import tpu as pltpu
from jax.sharding import PartitionSpec as P

LANES = 128
DIGITS = 3
PARTNERS = (4, 2, 3, 5, 6, 7, 1, 0)
WHOLE = pl.BlockSpec(memory_space=pltpu.VMEM)
SCALAR = pl.BlockSpec(memory_space=pltpu.SMEM)


def iota(shape, dim):
    return lax.broadcasted_iota(jnp.int32, shape, dim)


def matmul(a, b):
    return jnp.dot(a, b, preferred_element_type=jnp.float32)


def matmul_t(a, b, precision=None):
    return lax.dot_general(
        a, b, (((1,), (1,)), ((), ())), precision=precision, preferred_element_type=jnp.float32
    )


def bf16(x):
    return x.astype(jnp.float32).astype(jnp.bfloat16)


def ranked(hot):
    upto = (iota((LANES, LANES), 0) <= iota((LANES, LANES), 1)).astype(jnp.bfloat16)
    before, parts = jnp.zeros((1, 1), jnp.float32), []
    for start in range(0, hot.shape[1], LANES):
        piece = hot[:, start : start + LANES]
        spread = jnp.broadcast_to(piece, (16, LANES)).astype(jnp.bfloat16)
        parts.append(matmul(spread, upto)[:1] + before)
        before = before + jnp.sum(piece, axis=1, keepdims=True)
    return jnp.concatenate(parts, axis=1)


def slot_kernel(
    owners, capacity, order, parts, rows, me_ref, ints_ref, slot_ref, digit_ref
):
    clusters = ints_ref.shape[1] - 2 * rows
    cluster = ints_ref[:, clusters : clusters + rows]
    named = bf16(iota((clusters, rows), 0) == cluster)
    owner_map = bf16(jnp.broadcast_to(ints_ref[:, :clusters], (16, clusters)))
    owner = matmul(owner_map, named)[:1].astype(jnp.int32)
    hot = (iota((max(owners, 16), rows), 0) == owner).astype(jnp.float32)
    upto = bf16(iota((rows, rows), 0) <= iota((rows, rows), 1))
    rank = jnp.sum(hot * matmul(bf16(hot), upto), axis=0, keepdims=True) - 1.0
    rank = rank.astype(jnp.int32)
    partner = owner ^ me_ref[0]
    place = partner
    for index, k in enumerate(order):
        place = jnp.where(partner == k, index, place)
    if parts == 1:
        slot_ref[...] = place * capacity + rank
    else:
        half = capacity // 2
        later = (rank >= half).astype(jnp.int32)
        slot_ref[...] = place * half + rank + later * (owners * half - half)

    line = iota((8, rows), 0)
    digit = jnp.zeros((8, rows), jnp.int32)
    for first, number in ((0, cluster + 1), (DIGITS, ints_ref[:, clusters + rows :])):
        for at in range(DIGITS):
            digit = jnp.where(line == first + at, (number >> (8 * at)) & 255, digit)
    empty = jnp.zeros((LANES // 2 - 8, rows), jnp.int32)
    none = jnp.zeros((LANES // 2, rows), jnp.int32)
    early = jnp.concatenate([digit, empty, none], axis=0)
    late = jnp.concatenate([none, digit, empty], axis=0)
    digit_ref[...] = bf16(jnp.concatenate([early, late], axis=1))


def pack_kernel(slot_ref, digit_ref, embed_ref, *out_refs):
    rows, width = embed_ref.shape
    tiles, half, _ = out_refs[0].shape
    values = embed_ref[...].astype(jnp.float32)
    mean_sq = jnp.sum(values * values, axis=1, keepdims=True) * (1.0 / width)
    unit = (values * lax.rsqrt(width * (mean_sq + 1e-06))).astype(jnp.bfloat16)
    late = half * len(out_refs)
    move = bf16(iota((2 * late, rows), 0) == slot_ref[...])
    moved = matmul(move, unit).astype(jnp.bfloat16)
    both = jnp.concatenate([move[:late], move[late:]], axis=1)
    digit = matmul_t(both, digit_ref[...]).astype(jnp.bfloat16)
    each = tiles // 2
    for index, out_ref in enumerate(out_refs):
        start = index * half
        for tile in range(each):
            lanes = slice(tile * LANES, (tile + 1) * LANES)
            out_ref[tile] = moved[start : start + half, lanes]
            out_ref[each + tile] = moved[late + start : late + start + half, lanes]
        out_ref[tiles - 1] = digit[start : start + half]


def unpacked(block_ref, tiles):
    blocks = block_ref.shape[0] // tiles
    each = tiles // 2

    def column(tile):
        return jnp.concatenate([block_ref[i * tiles + tile] for i in range(blocks)], axis=0)

    halves = [
        jnp.concatenate([column(first + tile) for tile in range(each)], axis=1)
        for first in (0, each)
    ]
    return jnp.concatenate(halves, axis=0), column(tiles - 1)


def weights(number, at, half):
    value = jnp.zeros(at.shape, jnp.float32)
    for place in range(DIGITS):
        for which in (0, 1):
            lane = half * (LANES // 2) + which * DIGITS + place
            value = jnp.where((at == lane) & (number == which), 256.0**place, value)
    return value.astype(jnp.bfloat16)


def key_rows(rows_all, digit):
    at = iota((16, LANES), 0), iota((16, LANES), 1)
    numbers = [matmul_t(weights(*at, half), digit) for half in (0, 1)]
    numbers = jnp.concatenate(numbers, axis=1)
    low = (numbers[0:1].astype(jnp.int32) - 1) * rows_all
    return low, low + numbers[1:2].astype(jnp.int32)


def key_columns(rows_all, digit):
    at = iota((LANES, 2 * LANES), 1) // LANES, iota((LANES, 2 * LANES), 0)
    numbers = [matmul(digit, weights(*at, half)) for half in (0, 1)]
    numbers = jnp.concatenate(numbers, axis=0)
    low = (numbers[:, :LANES].astype(jnp.int32) - 1) * rows_all
    return low, low + numbers[:, LANES:].astype(jnp.int32)


def across(column, count):
    return jnp.concatenate([column] * (count // LANES), axis=1)


def compare(rows_all, query, query_low, query_key, lows, rows, digit):
    _, key = key_rows(rows_all, digit)
    bound = across(lows, key.shape[1])
    member = bf16((key >= bound) & (key < bound + rows_all))
    sums = matmul(member, rows)
    counts = matmul(member, jnp.ones((rows.shape[0], LANES), jnp.bfloat16))
    scores = matmul_t(rows, query)
    _, key = key_columns(rows_all, digit)
    key = across(key, query.shape[0])
    earlier = (key >= query_low) & (key < query_key)
    best = jnp.max(jnp.where(earlier, scores, -3.0), axis=0, keepdims=True)
    return best, sums, counts


def near_kernel(
    rows_all, clusters, clus_dev, tiles, me_ref, ints_ref, query_ref,
    lows_ref, key_ref, best_ref, sums_ref, counts_ref,
):
    hot = (ints_ref[:, :clusters] == me_ref[0]).astype(jnp.float32)
    rank = ranked(hot)
    shape = (clus_dev, clusters)
    kth = (rank == iota(shape, 0).astype(jnp.float32) + 1.0) & (hot > 0.0)
    own = jnp.sum(jnp.where(kth, iota(shape, 1).astype(jnp.float32), 0.0), axis=1, keepdims=True)
    own = jnp.broadcast_to(own.astype(jnp.int32) * rows_all, (clus_dev, LANES))
    query, digit = unpacked(query_ref, tiles)
    low, _ = key_columns(rows_all, digit)
    lows = jnp.concatenate([low, own], axis=0)
    query_low, query_key = key_rows(rows_all, digit)
    best, sums, counts = compare(rows_all, query, query_low, query_key, lows, query, digit)
    lows_ref[...] = lows
    key_ref[...] = jnp.concatenate([query_low, query_key], axis=0)
    best_ref[...] = best
    sums_ref[...] = sums
    counts_ref[...] = counts


def far_kernel(
    rows_all, tiles, query_ref, other_ref, lows_ref, key_ref, best_ref, sums_ref, counts_ref,
    result_ref, norm_ref,
):
    query, _ = unpacked(query_ref, tiles)
    queries, width = query.shape
    rows, digit = unpacked(other_ref, tiles)
    best, sums, counts = compare(
        rows_all, query, key_ref[0:1], key_ref[1:2], lows_ref[...], rows, digit
    )
    best = jnp.maximum(best, best_ref[...])
    best = jnp.where(best > -2.0, best, 0.0)
    share = 1.0 / jnp.maximum(counts + counts_ref[...], 1.0)
    squares = jnp.zeros(share.shape, jnp.float32)
    for start in range(0, width, LANES):
        lanes = slice(start, start + LANES)
        centroid = (sums[:, lanes] + sums_ref[:, lanes]) * share
        offset = jnp.concatenate(
            [query[:, lanes].astype(jnp.float32) - centroid[:queries], centroid[queries:]], axis=0
        )
        squares = squares + offset * offset
    ones = jnp.ones((8, LANES), jnp.float32)
    total = matmul_t(ones, squares, lax.Precision.HIGHEST)[:1]
    result = jnp.concatenate([best, total[:, :queries]], axis=0)
    for owner in range(result_ref.shape[0]):
        result_ref[owner] = result
    norm_ref[...] = total[:, queries:]


def pick_kernel(
    order, parts, me_ref, slot_ref, result_ref, norm_ref, best_ref, distance_ref, cohesion_ref
):
    cohesion_ref[...] = norm_ref[...]
    rows = slot_ref.shape[1]
    owners, lines, slots = result_ref.shape
    folds = min(parts, 2)
    place = iota((lines, slots), 1) % (slots // folds) // (slots // owners // folds)
    values = jnp.zeros((lines, slots), jnp.float32)
    for index, k in enumerate(order):
        values = jnp.where(place == index, result_ref[me_ref[0] ^ k], values)
    values = jnp.concatenate([values, jnp.zeros((8 - lines, slots), jnp.float32)], axis=0)
    at = (iota((slots, rows), 0) == slot_ref[...]).astype(jnp.float32)
    picked = jnp.dot(
        values, at, precision=lax.Precision.HIGHEST, preferred_element_type=jnp.float32
    )
    best_ref[...] = picked[0:1]
    distance_ref[...] = picked[1:2]


def from_partner(value, k, axis):
    return lax.ppermute(value, axis, [(i, i ^ k) for i in range(lax.axis_size(axis))])


def exchange(packed, order):
    return jnp.concatenate(
        [from_partner(block, k, "shard") if k else block for k, block in zip(order, packed)]
    )


def gather_pairs(value):
    owners, step = lax.axis_size("shard"), 1
    while step < owners:
        pairs = [[i, i + step] for i in range(owners) if not i & step]
        value = lax.all_gather(value, "shard", axis_index_groups=pairs, axis=0, tiled=True)
        step *= 2
    return value


def exchange_all(packed, me):
    owners = lax.axis_size("shard")
    tiles, half, _ = packed.shape
    each = tiles // 2
    data = packed[:-1].reshape(2, each, half, LANES).transpose(0, 2, 1, 3).reshape(2 * half, -1)
    digit = jnp.concatenate(jnp.split(packed[-1], 2, axis=1))
    parted = jnp.concatenate([data, digit], axis=1).reshape(owners, 2 * half // owners, -1)
    partner = me ^ jnp.arange(owners, dtype=jnp.int32)
    got = lax.all_to_all(parted[partner], "shard", 0, 0, tiled=True)[partner].reshape(2 * half, -1)
    data = got[:, : each * LANES].reshape(2, half, each, LANES).transpose(0, 2, 1, 3)
    digit = jnp.concatenate(jnp.split(got[:, each * LANES :], 2), axis=1)
    return jnp.concatenate([data.reshape(2 * each, half, LANES), digit[None]])


def local(embeddings, cluster_id, item_order, owner_map):
    owners = lax.axis_size("shard")
    local_rows, width = embeddings.shape
    rows_all = local_rows * owners * lax.axis_size("sub")
    clus_dev = owner_map.shape[0] // owners
    capacity = 2 * local_rows // owners
    slots = owners * capacity
    params = pltpu.CompilerParams(vmem_limit_bytes=32 << 20)
    compare_cost = pl.CostEstimate(
        flops=4 * slots * slots * width, bytes_accessed=4 * slots * width, transcendentals=0
    )
    me = lax.axis_index("shard").astype(jnp.int32).reshape(1)
    ints = jnp.concatenate([owner_map, cluster_id, item_order]).reshape(1, -1)

    direct = owners == len(PARTNERS)
    order = PARTNERS if direct else tuple(range(owners))
    parts = owners if direct else 1
    tiles = 2 * (width // LANES) + 1
    block = (tiles, slots // parts // 2, LANES)
    slot, digit = pl.pallas_call(
        functools.partial(slot_kernel, owners, capacity, order, parts, local_rows),
        out_shape=[
            jax.ShapeDtypeStruct((1, local_rows), jnp.int32),
            jax.ShapeDtypeStruct((LANES, 2 * local_rows), jnp.bfloat16),
        ],
        in_specs=[SCALAR, WHOLE],
        out_specs=[WHOLE] * 2,
        compiler_params=params,
        cost_estimate=pl.CostEstimate(flops=1 << 29, bytes_accessed=1 << 16, transcendentals=0),
        name="slots",
    )(me, ints)
    packed = pl.pallas_call(
        pack_kernel,
        out_shape=[jax.ShapeDtypeStruct(block, jnp.bfloat16)] * parts,
        in_specs=[WHOLE] * 3,
        out_specs=[WHOLE] * parts,
        compiler_params=params,
        name="pack",
    )(slot, digit, embeddings)
    query = exchange(packed, order) if direct else exchange_all(packed[0], me[0])
    other = from_partner(query, 1, "sub")
    asked = slots + clus_dev
    near = pl.pallas_call(
        functools.partial(near_kernel, rows_all, owner_map.shape[0], clus_dev, tiles),
        out_shape=[
            jax.ShapeDtypeStruct((asked, LANES), jnp.int32),
            jax.ShapeDtypeStruct((2, slots), jnp.int32),
            jax.ShapeDtypeStruct((1, slots), jnp.float32),
            jax.ShapeDtypeStruct((asked, width), jnp.float32),
            jax.ShapeDtypeStruct((asked, LANES), jnp.float32),
        ],
        in_specs=[SCALAR] + [WHOLE] * 2,
        out_specs=[WHOLE] * 5,
        compiler_params=params,
        cost_estimate=compare_cost,
        name="near",
    )(me, ints, query)
    results, norms = pl.pallas_call(
        functools.partial(far_kernel, rows_all, tiles),
        out_shape=[
            jax.ShapeDtypeStruct((1 if direct else owners, 2, slots), jnp.float32),
            jax.ShapeDtypeStruct((1, clus_dev), jnp.float32),
        ],
        in_specs=[WHOLE] * 7,
        out_specs=[WHOLE] * 2,
        compiler_params=params,
        cost_estimate=compare_cost,
        name="far",
    )(query, other, *near)
    if direct:
        results = gather_pairs(results)
    else:
        results = lax.all_to_all(results, "shard", 0, 0, tiled=True)
    best, distance, cohesion = pl.pallas_call(
        functools.partial(pick_kernel, order, parts),
        out_shape=[jax.ShapeDtypeStruct((1, local_rows), jnp.float32)] * 2
        + [jax.ShapeDtypeStruct((1, clus_dev), jnp.float32)],
        in_specs=[SCALAR] + [WHOLE] * 3,
        out_specs=[WHOLE] * 3,
        compiler_params=params,
        name="pick",
    )(me, slot, results, norms)
    return best.reshape(local_rows), distance.reshape(local_rows), cohesion.reshape(clus_dev)


def solution(mesh):
    in_specs = (
        P(("groups", "shard", "sub"), None),
        P(("groups", "shard", "sub")),
        P(("groups", "shard", "sub")),
        P("groups"),
    )
    out_specs = (
        P(("groups", "shard", "sub")),
        P(("groups", "shard", "sub")),
        P(("groups", "shard")),
    )
    return jax.shard_map(local, mesh=mesh, in_specs=in_specs, out_specs=out_specs, check_vma=False)
```

```python
import functools

import jax
import jax.numpy as jnp
from jax import lax
from jax.experimental import pallas as pl
from jax.experimental.pallas import tpu as pltpu
from jax.sharding import PartitionSpec as P

LANES = 128
DIGITS = 3
PARTNERS = (4, 2, 3, 7, 6, 5, 1, 0)
WHOLE = pl.BlockSpec(memory_space=pltpu.VMEM)
SCALAR = pl.BlockSpec(memory_space=pltpu.SMEM)


def iota(shape, dim):
    return lax.broadcasted_iota(jnp.int32, shape, dim)


def matmul(a, b):
    return jnp.dot(a, b, preferred_element_type=jnp.float32)


def matmul_t(a, b):
    return lax.dot_general(a, b, (((1,), (1,)), ((), ())), preferred_element_type=jnp.float32)


def bf16(x):
    return x.astype(jnp.float32).astype(jnp.bfloat16)


def ranked(hot):
    upto = (iota((LANES, LANES), 0) <= iota((LANES, LANES), 1)).astype(jnp.bfloat16)
    before, parts = jnp.zeros((1, 1), jnp.float32), []
    for start in range(0, hot.shape[1], LANES):
        piece = hot[:, start : start + LANES]
        spread = jnp.broadcast_to(piece, (16, LANES)).astype(jnp.bfloat16)
        parts.append(matmul(spread, upto)[:1] + before)
        before = before + jnp.sum(piece, axis=1, keepdims=True)
    return jnp.concatenate(parts, axis=1)


def slot_kernel(
    owners, capacity, order, parts, rows, me_ref, ints_ref, slot_ref, digit_ref
):
    clusters = ints_ref.shape[1] - 2 * rows
    cluster = ints_ref[:, clusters : clusters + rows]
    named = bf16(iota((clusters, rows), 0) == cluster)
    owner_map = bf16(jnp.broadcast_to(ints_ref[:, :clusters], (16, clusters)))
    owner = matmul(owner_map, named)[:1].astype(jnp.int32)
    hot = (iota((max(owners, 16), rows), 0) == owner).astype(jnp.float32)
    upto = bf16(iota((rows, rows), 0) <= iota((rows, rows), 1))
    rank = jnp.sum(hot * matmul(bf16(hot), upto), axis=0, keepdims=True) - 1.0
    rank = rank.astype(jnp.int32)
    partner = owner ^ me_ref[0]
    place = partner
    for index, k in enumerate(order):
        place = jnp.where(partner == k, index, place)
    if parts == 1:
        slot_ref[...] = place * capacity + rank
    else:
        half = capacity // 2
        later = (rank >= half).astype(jnp.int32)
        slot_ref[...] = place * half + rank + later * (owners * half - half)

    line = iota((8, rows), 0)
    digit = jnp.zeros((8, rows), jnp.int32)
    for first, number in ((0, cluster + 1), (DIGITS, ints_ref[:, clusters + rows :])):
        for at in range(DIGITS):
            digit = jnp.where(line == first + at, (number >> (8 * at)) & 255, digit)
    empty = jnp.zeros((LANES // 2 - 8, rows), jnp.int32)
    none = jnp.zeros((LANES // 2, rows), jnp.int32)
    early = jnp.concatenate([digit, empty, none], axis=0)
    late = jnp.concatenate([none, digit, empty], axis=0)
    digit_ref[...] = bf16(jnp.concatenate([early, late], axis=1))


def pack_kernel(slot_ref, digit_ref, embed_ref, *out_refs):
    rows, width = embed_ref.shape
    tiles, half, _ = out_refs[0].shape
    values = embed_ref[...].astype(jnp.float32)
    mean_sq = jnp.sum(values * values, axis=1, keepdims=True) * (1.0 / width)
    unit = (values * lax.rsqrt(width * (mean_sq + 1e-06))).astype(jnp.bfloat16)
    late = half * len(out_refs)
    move = bf16(iota((2 * late, rows), 0) == slot_ref[...])
    moved = matmul(move, unit).astype(jnp.bfloat16)
    both = jnp.concatenate([move[:late], move[late:]], axis=1)
    digit = matmul_t(both, digit_ref[...]).astype(jnp.bfloat16)
    each = tiles // 2
    for index, out_ref in enumerate(out_refs):
        start = index * half
        for tile in range(each):
            lanes = slice(tile * LANES, (tile + 1) * LANES)
            out_ref[tile] = moved[start : start + half, lanes]
            out_ref[each + tile] = moved[late + start : late + start + half, lanes]
        out_ref[tiles - 1] = digit[start : start + half]


def unpacked(block_ref, tiles):
    blocks = block_ref.shape[0] // tiles
    each = tiles // 2

    def column(tile):
        return jnp.concatenate([block_ref[i * tiles + tile] for i in range(blocks)], axis=0)

    halves = [
        jnp.concatenate([column(first + tile) for tile in range(each)], axis=1)
        for first in (0, each)
    ]
    return jnp.concatenate(halves, axis=0), column(tiles - 1)


def weights(number, at, half):
    value = jnp.zeros(at.shape, jnp.float32)
    for place in range(DIGITS):
        for which in (0, 1):
            lane = half * (LANES // 2) + which * DIGITS + place
            value = jnp.where((at == lane) & (number == which), 256.0**place, value)
    return value.astype(jnp.bfloat16)


def key_rows(rows_all, digit):
    at = iota((16, LANES), 0), iota((16, LANES), 1)
    numbers = [matmul_t(weights(*at, half), digit) for half in (0, 1)]
    numbers = jnp.concatenate(numbers, axis=1)
    low = (numbers[0:1].astype(jnp.int32) - 1) * rows_all
    return low, low + numbers[1:2].astype(jnp.int32)


def key_columns(rows_all, digit):
    at = iota((LANES, 2 * LANES), 1) // LANES, iota((LANES, 2 * LANES), 0)
    numbers = [matmul(digit, weights(*at, half)) for half in (0, 1)]
    numbers = jnp.concatenate(numbers, axis=0)
    low = (numbers[:, :LANES].astype(jnp.int32) - 1) * rows_all
    return low, low + numbers[:, LANES:].astype(jnp.int32)


def across(column, count):
    return jnp.concatenate([column] * (count // LANES), axis=1)


def compare(rows_all, query_t, query_low, query_key, lows, rows, digit):
    _, key = key_rows(rows_all, digit)
    bound = across(lows, key.shape[1])
    member = bf16((key >= bound) & (key < bound + rows_all))
    sums = matmul(member, rows)
    counts = matmul(member, jnp.ones((rows.shape[0], LANES), jnp.bfloat16))
    scores = matmul(rows, query_t)
    _, key = key_columns(rows_all, digit)
    key = across(key, query_t.shape[1])
    earlier = (key >= query_low) & (key < query_key)
    best = jnp.max(jnp.where(earlier, scores, -3.0), axis=0, keepdims=True)
    return best, sums, counts


def near_kernel(
    rows_all, clusters, clus_dev, tiles, me_ref, ints_ref, query_ref,
    query_t_ref, lows_ref, key_ref, best_ref, sums_ref, counts_ref,
):
    hot = (ints_ref[:, :clusters] == me_ref[0]).astype(jnp.float32)
    rank = ranked(hot)
    shape = (clus_dev, clusters)
    kth = (rank == iota(shape, 0).astype(jnp.float32) + 1.0) & (hot > 0.0)
    own = jnp.sum(jnp.where(kth, iota(shape, 1).astype(jnp.float32), 0.0), axis=1, keepdims=True)
    own = jnp.broadcast_to(own.astype(jnp.int32) * rows_all, (clus_dev, LANES))
    query, digit = unpacked(query_ref, tiles)
    low, _ = key_columns(rows_all, digit)
    lows = jnp.concatenate([low, own], axis=0)
    query_low, query_key = key_rows(rows_all, digit)
    query_t = jnp.transpose(query)
    query_t_ref[...] = query_t
    best, sums, counts = compare(rows_all, query_t, query_low, query_key, lows, query, digit)
    lows_ref[...] = lows
    key_ref[...] = jnp.concatenate([query_low, query_key], axis=0)
    best_ref[...] = best
    sums_ref[...] = sums
    counts_ref[...] = counts


def far_kernel(
    rows_all, tiles, query_ref, other_ref, query_t_ref, lows_ref, key_ref, best_ref, sums_ref, counts_ref,
    result_ref, norm_ref,
):
    query, _ = unpacked(query_ref, tiles)
    queries, width = query.shape
    rows, digit = unpacked(other_ref, tiles)
    best, sums, counts = compare(
        rows_all, query_t_ref[...], key_ref[0:1], key_ref[1:2], lows_ref[...], rows, digit
    )
    best = jnp.maximum(best, best_ref[...])
    best = jnp.where(best > -2.0, best, 0.0)
    share = 1.0 / jnp.maximum(counts + counts_ref[...], 1.0)
    squares = jnp.zeros(share.shape, jnp.float32)
    for start in range(0, width, LANES):
        lanes = slice(start, start + LANES)
        centroid = (sums[:, lanes] + sums_ref[:, lanes]) * share
        offset = jnp.concatenate(
            [query[:, lanes].astype(jnp.float32) - centroid[:queries], centroid[queries:]], axis=0
        )
        squares = squares + offset * offset
    total = jnp.sum(jnp.transpose(squares), axis=0, keepdims=True)
    result = jnp.concatenate([best, total[:, :queries]], axis=0)
    for owner in range(result_ref.shape[0]):
        result_ref[owner] = result
    norm_ref[...] = total[:, queries:]


def pick_kernel(
    order, parts, me_ref, slot_ref, result_ref, norm_ref, best_ref, distance_ref, cohesion_ref
):
    cohesion_ref[...] = norm_ref[...]
    rows = slot_ref.shape[1]
    owners, lines, slots = result_ref.shape
    folds = min(parts, 2)
    place = iota((lines, slots), 1) % (slots // folds) // (slots // owners // folds)
    values = jnp.zeros((lines, slots), jnp.float32)
    for index, k in enumerate(order):
        values = jnp.where(place == index, result_ref[me_ref[0] ^ k], values)
    values = jnp.concatenate([values, jnp.zeros((8 - lines, slots), jnp.float32)], axis=0)
    at = (iota((slots, rows), 0) == slot_ref[...]).astype(jnp.float32)
    picked = jnp.dot(
        values, at, precision=lax.Precision.HIGHEST, preferred_element_type=jnp.float32
    )
    best_ref[...] = picked[0:1]
    distance_ref[...] = picked[1:2]


def from_partner(value, k, axis):
    return lax.ppermute(value, axis, [(i, i ^ k) for i in range(lax.axis_size(axis))])


def exchange(packed, order):
    return jnp.concatenate(
        [from_partner(block, k, "shard") if k else block for k, block in zip(order, packed)]
    )


def exchange_all(packed, me):
    owners = lax.axis_size("shard")
    tiles, half, _ = packed.shape
    each = tiles // 2
    data = packed[:-1].reshape(2, each, half, LANES).transpose(0, 2, 1, 3).reshape(2 * half, -1)
    digit = jnp.concatenate(jnp.split(packed[-1], 2, axis=1))
    parted = jnp.concatenate([data, digit], axis=1).reshape(owners, 2 * half // owners, -1)
    partner = me ^ jnp.arange(owners, dtype=jnp.int32)
    got = lax.all_to_all(parted[partner], "shard", 0, 0, tiled=True)[partner].reshape(2 * half, -1)
    data = got[:, : each * LANES].reshape(2, half, each, LANES).transpose(0, 2, 1, 3)
    digit = jnp.concatenate(jnp.split(got[:, each * LANES :], 2), axis=1)
    return jnp.concatenate([data.reshape(2 * each, half, LANES), digit[None]])


def local(embeddings, cluster_id, item_order, owner_map):
    owners = lax.axis_size("shard")
    local_rows, width = embeddings.shape
    rows_all = local_rows * owners * lax.axis_size("sub")
    clus_dev = owner_map.shape[0] // owners
    capacity = 2 * local_rows // owners
    slots = owners * capacity
    params = pltpu.CompilerParams(vmem_limit_bytes=32 << 20)
    compare_cost = pl.CostEstimate(
        flops=4 * slots * slots * width, bytes_accessed=4 * slots * width, transcendentals=0
    )
    me = lax.axis_index("shard").astype(jnp.int32).reshape(1)
    ints = jnp.concatenate([owner_map, cluster_id, item_order]).reshape(1, -1)

    direct = owners == len(PARTNERS)
    order = PARTNERS if direct else tuple(range(owners))
    parts = owners if direct else 1
    tiles = 2 * (width // LANES) + 1
    block = (tiles, slots // parts // 2, LANES)
    slot, digit = pl.pallas_call(
        functools.partial(slot_kernel, owners, capacity, order, parts, local_rows),
        out_shape=[
            jax.ShapeDtypeStruct((1, local_rows), jnp.int32),
            jax.ShapeDtypeStruct((LANES, 2 * local_rows), jnp.bfloat16),
        ],
        in_specs=[SCALAR, WHOLE],
        out_specs=[WHOLE] * 2,
        compiler_params=params,
        cost_estimate=pl.CostEstimate(flops=1 << 29, bytes_accessed=1 << 16, transcendentals=0),
        name="slots",
    )(me, ints)
    packed = pl.pallas_call(
        pack_kernel,
        out_shape=[jax.ShapeDtypeStruct(block, jnp.bfloat16)] * parts,
        in_specs=[WHOLE] * 3,
        out_specs=[WHOLE] * parts,
        compiler_params=params,
        name="pack",
    )(slot, digit, embeddings)
    query = exchange(packed, order) if direct else exchange_all(packed[0], me[0])
    other = from_partner(query, 1, "sub")
    asked = slots + clus_dev
    near = pl.pallas_call(
        functools.partial(near_kernel, rows_all, owner_map.shape[0], clus_dev, tiles),
        out_shape=[
            jax.ShapeDtypeStruct((width, slots), jnp.bfloat16),
            jax.ShapeDtypeStruct((asked, LANES), jnp.int32),
            jax.ShapeDtypeStruct((2, slots), jnp.int32),
            jax.ShapeDtypeStruct((1, slots), jnp.float32),
            jax.ShapeDtypeStruct((asked, width), jnp.float32),
            jax.ShapeDtypeStruct((asked, LANES), jnp.float32),
        ],
        in_specs=[SCALAR] + [WHOLE] * 2,
        out_specs=[WHOLE] * 6,
        compiler_params=params,
        cost_estimate=compare_cost,
        name="near",
    )(me, ints, query)
    results, norms = pl.pallas_call(
        functools.partial(far_kernel, rows_all, tiles),
        out_shape=[
            jax.ShapeDtypeStruct((owners, 2, slots), jnp.float32),
            jax.ShapeDtypeStruct((1, clus_dev), jnp.float32),
        ],
        in_specs=[WHOLE] * 8,
        out_specs=[WHOLE] * 2,
        compiler_params=params,
        cost_estimate=compare_cost,
        name="far",
    )(query, other, *near)
    results = lax.all_to_all(results, "shard", 0, 0, tiled=True)
    best, distance, cohesion = pl.pallas_call(
        functools.partial(pick_kernel, order, parts),
        out_shape=[jax.ShapeDtypeStruct((1, local_rows), jnp.float32)] * 2
        + [jax.ShapeDtypeStruct((1, clus_dev), jnp.float32)],
        in_specs=[SCALAR] + [WHOLE] * 3,
        out_specs=[WHOLE] * 3,
        compiler_params=params,
        name="pick",
    )(me, slot, results, norms)
    return best.reshape(local_rows), distance.reshape(local_rows), cohesion.reshape(clus_dev)


def solution(mesh):
    in_specs = (
        P(("groups", "shard", "sub"), None),
        P(("groups", "shard", "sub")),
        P(("groups", "shard", "sub")),
        P("groups"),
    )
    out_specs = (
        P(("groups", "shard", "sub")),
        P(("groups", "shard", "sub")),
        P(("groups", "shard")),
    )
    return jax.shard_map(local, mesh=mesh, in_specs=in_specs, out_specs=out_specs, check_vma=False)
```

```python
import functools

import jax
import jax.numpy as jnp
from jax import lax
from jax.experimental import pallas as pl
from jax.experimental.pallas import tpu as pltpu
from jax.sharding import PartitionSpec as P

LANES = 128
DIGITS = 3
PARTNERS = (4, 2, 3, 5, 7, 6, 1, 0)
WHOLE = pl.BlockSpec(memory_space=pltpu.VMEM)
SCALAR = pl.BlockSpec(memory_space=pltpu.SMEM)


def iota(shape, dim):
    return lax.broadcasted_iota(jnp.int32, shape, dim)


def matmul(a, b):
    return jnp.dot(a, b, preferred_element_type=jnp.float32)


def matmul_t(a, b):
    return lax.dot_general(a, b, (((1,), (1,)), ((), ())), preferred_element_type=jnp.float32)


def bf16(x):
    return x.astype(jnp.float32).astype(jnp.bfloat16)


def ranked(hot):
    upto = (iota((LANES, LANES), 0) <= iota((LANES, LANES), 1)).astype(jnp.bfloat16)
    before, parts = jnp.zeros((1, 1), jnp.float32), []
    for start in range(0, hot.shape[1], LANES):
        piece = hot[:, start : start + LANES]
        spread = jnp.broadcast_to(piece, (16, LANES)).astype(jnp.bfloat16)
        parts.append(matmul(spread, upto)[:1] + before)
        before = before + jnp.sum(piece, axis=1, keepdims=True)
    return jnp.concatenate(parts, axis=1)


def slot_kernel(
    owners, capacity, order, parts, rows, me_ref, ints_ref, slot_ref, digit_ref
):
    clusters = ints_ref.shape[1] - 2 * rows
    cluster = ints_ref[:, clusters : clusters + rows]
    named = bf16(iota((clusters, rows), 0) == cluster)
    owner_map = bf16(jnp.broadcast_to(ints_ref[:, :clusters], (16, clusters)))
    owner = matmul(owner_map, named)[:1].astype(jnp.int32)
    hot = (iota((max(owners, 16), rows), 0) == owner).astype(jnp.float32)
    upto = bf16(iota((rows, rows), 0) <= iota((rows, rows), 1))
    rank = jnp.sum(hot * matmul(bf16(hot), upto), axis=0, keepdims=True) - 1.0
    rank = rank.astype(jnp.int32)
    partner = owner ^ me_ref[0]
    place = partner
    for index, k in enumerate(order):
        place = jnp.where(partner == k, index, place)
    if parts == 1:
        slot_ref[...] = place * capacity + rank
    else:
        half = capacity // 2
        later = (rank >= half).astype(jnp.int32)
        slot_ref[...] = place * half + rank + later * (owners * half - half)

    line = iota((8, rows), 0)
    digit = jnp.zeros((8, rows), jnp.int32)
    for first, number in ((0, cluster + 1), (DIGITS, ints_ref[:, clusters + rows :])):
        for at in range(DIGITS):
            digit = jnp.where(line == first + at, (number >> (8 * at)) & 255, digit)
    empty = jnp.zeros((LANES // 2 - 8, rows), jnp.int32)
    none = jnp.zeros((LANES // 2, rows), jnp.int32)
    early = jnp.concatenate([digit, empty, none], axis=0)
    late = jnp.concatenate([none, digit, empty], axis=0)
    digit_ref[...] = bf16(jnp.concatenate([early, late], axis=1))


def pack_kernel(slot_ref, digit_ref, embed_ref, *out_refs):
    rows, width = embed_ref.shape
    tiles, half, _ = out_refs[0].shape
    values = embed_ref[...].astype(jnp.float32)
    mean_sq = jnp.sum(values * values, axis=1, keepdims=True) * (1.0 / width)
    unit = (values * lax.rsqrt(width * (mean_sq + 1e-06))).astype(jnp.bfloat16)
    late = half * len(out_refs)
    move = bf16(iota((2 * late, rows), 0) == slot_ref[...])
    moved = matmul(move, unit).astype(jnp.bfloat16)
    both = jnp.concatenate([move[:late], move[late:]], axis=1)
    digit = matmul_t(both, digit_ref[...]).astype(jnp.bfloat16)
    each = tiles // 2
    for index, out_ref in enumerate(out_refs):
        start = index * half
        for tile in range(each):
            lanes = slice(tile * LANES, (tile + 1) * LANES)
            out_ref[tile] = moved[start : start + half, lanes]
            out_ref[each + tile] = moved[late + start : late + start + half, lanes]
        out_ref[tiles - 1] = digit[start : start + half]


def unpacked(block_ref, tiles):
    blocks = block_ref.shape[0] // tiles
    each = tiles // 2

    def column(tile):
        return jnp.concatenate([block_ref[i * tiles + tile] for i in range(blocks)], axis=0)

    halves = [
        jnp.concatenate([column(first + tile) for tile in range(each)], axis=1)
        for first in (0, each)
    ]
    return jnp.concatenate(halves, axis=0), column(tiles - 1)


def weights(number, at, half):
    value = jnp.zeros(at.shape, jnp.float32)
    for place in range(DIGITS):
        for which in (0, 1):
            lane = half * (LANES // 2) + which * DIGITS + place
            value = jnp.where((at == lane) & (number == which), 256.0**place, value)
    return value.astype(jnp.bfloat16)


def key_rows(rows_all, digit):
    at = iota((16, LANES), 0), iota((16, LANES), 1)
    numbers = [matmul_t(weights(*at, half), digit) for half in (0, 1)]
    numbers = jnp.concatenate(numbers, axis=1)
    low = (numbers[0:1].astype(jnp.int32) - 1) * rows_all
    return low, low + numbers[1:2].astype(jnp.int32)


def key_columns(rows_all, digit):
    at = iota((LANES, 2 * LANES), 1) // LANES, iota((LANES, 2 * LANES), 0)
    numbers = [matmul(digit, weights(*at, half)) for half in (0, 1)]
    numbers = jnp.concatenate(numbers, axis=0)
    low = (numbers[:, :LANES].astype(jnp.int32) - 1) * rows_all
    return low, low + numbers[:, LANES:].astype(jnp.int32)


def across(column, count):
    return jnp.concatenate([column] * (count // LANES), axis=1)


def compare(rows_all, query_t, query_low, query_key, lows, rows, digit):
    _, key = key_rows(rows_all, digit)
    bound = across(lows, key.shape[1])
    member = bf16((key >= bound) & (key < bound + rows_all))
    sums = matmul(member, rows)
    counts = matmul(member, jnp.ones((rows.shape[0], LANES), jnp.bfloat16))
    scores = matmul(rows, query_t)
    _, key = key_columns(rows_all, digit)
    key = across(key, query_t.shape[1])
    earlier = (key >= query_low) & (key < query_key)
    best = jnp.max(jnp.where(earlier, scores, -3.0), axis=0, keepdims=True)
    return best, sums, counts


def near_kernel(
    rows_all, clusters, clus_dev, tiles, me_ref, ints_ref, query_ref,
    query_t_ref, lows_ref, key_ref, best_ref, sums_ref, counts_ref,
):
    hot = (ints_ref[:, :clusters] == me_ref[0]).astype(jnp.float32)
    rank = ranked(hot)
    shape = (clus_dev, clusters)
    kth = (rank == iota(shape, 0).astype(jnp.float32) + 1.0) & (hot > 0.0)
    own = jnp.sum(jnp.where(kth, iota(shape, 1).astype(jnp.float32), 0.0), axis=1, keepdims=True)
    own = jnp.broadcast_to(own.astype(jnp.int32) * rows_all, (clus_dev, LANES))
    query, digit = unpacked(query_ref, tiles)
    low, _ = key_columns(rows_all, digit)
    lows = jnp.concatenate([low, own], axis=0)
    query_low, query_key = key_rows(rows_all, digit)
    query_t = jnp.transpose(query)
    query_t_ref[...] = query_t
    best, sums, counts = compare(rows_all, query_t, query_low, query_key, lows, query, digit)
    lows_ref[...] = lows
    key_ref[...] = jnp.concatenate([query_low, query_key], axis=0)
    best_ref[...] = best
    sums_ref[...] = sums
    counts_ref[...] = counts


def far_kernel(
    rows_all, tiles, query_ref, other_ref, query_t_ref, lows_ref, key_ref, best_ref, sums_ref, counts_ref,
    result_ref, norm_ref,
):
    query, _ = unpacked(query_ref, tiles)
    queries, width = query.shape
    rows, digit = unpacked(other_ref, tiles)
    best, sums, counts = compare(
        rows_all, query_t_ref[...], key_ref[0:1], key_ref[1:2], lows_ref[...], rows, digit
    )
    best = jnp.maximum(best, best_ref[...])
    best = jnp.where(best > -2.0, best, 0.0)
    share = 1.0 / jnp.maximum(counts + counts_ref[...], 1.0)
    squares = jnp.zeros(share.shape, jnp.float32)
    for start in range(0, width, LANES):
        lanes = slice(start, start + LANES)
        centroid = (sums[:, lanes] + sums_ref[:, lanes]) * share
        offset = jnp.concatenate(
            [query[:, lanes].astype(jnp.float32) - centroid[:queries], centroid[queries:]], axis=0
        )
        squares = squares + offset * offset
    total = jnp.sum(jnp.transpose(squares), axis=0, keepdims=True)
    result = jnp.concatenate([best, total[:, :queries]], axis=0)
    for owner in range(result_ref.shape[0]):
        result_ref[owner] = result
    norm_ref[...] = total[:, queries:]


def pick_kernel(
    order, parts, me_ref, slot_ref, result_ref, norm_ref, best_ref, distance_ref, cohesion_ref
):
    cohesion_ref[...] = norm_ref[...]
    rows = slot_ref.shape[1]
    owners, lines, slots = result_ref.shape
    folds = min(parts, 2)
    place = iota((lines, slots), 1) % (slots // folds) // (slots // owners // folds)
    values = jnp.zeros((lines, slots), jnp.float32)
    for index, k in enumerate(order):
        values = jnp.where(place == index, result_ref[me_ref[0] ^ k], values)
    values = jnp.concatenate([values, jnp.zeros((8 - lines, slots), jnp.float32)], axis=0)
    at = (iota((slots, rows), 0) == slot_ref[...]).astype(jnp.float32)
    picked = jnp.dot(
        values, at, precision=lax.Precision.HIGHEST, preferred_element_type=jnp.float32
    )
    best_ref[...] = picked[0:1]
    distance_ref[...] = picked[1:2]


def from_partner(value, k, axis):
    return lax.ppermute(value, axis, [(i, i ^ k) for i in range(lax.axis_size(axis))])


def exchange(packed, order):
    return jnp.concatenate(
        [from_partner(block, k, "shard") if k else block for k, block in zip(order, packed)]
    )


def exchange_all(packed, me):
    owners = lax.axis_size("shard")
    tiles, half, _ = packed.shape
    each = tiles // 2
    data = packed[:-1].reshape(2, each, half, LANES).transpose(0, 2, 1, 3).reshape(2 * half, -1)
    digit = jnp.concatenate(jnp.split(packed[-1], 2, axis=1))
    parted = jnp.concatenate([data, digit], axis=1).reshape(owners, 2 * half // owners, -1)
    partner = me ^ jnp.arange(owners, dtype=jnp.int32)
    got = lax.all_to_all(parted[partner], "shard", 0, 0, tiled=True)[partner].reshape(2 * half, -1)
    data = got[:, : each * LANES].reshape(2, half, each, LANES).transpose(0, 2, 1, 3)
    digit = jnp.concatenate(jnp.split(got[:, each * LANES :], 2), axis=1)
    return jnp.concatenate([data.reshape(2 * each, half, LANES), digit[None]])


def local(embeddings, cluster_id, item_order, owner_map):
    owners = lax.axis_size("shard")
    local_rows, width = embeddings.shape
    rows_all = local_rows * owners * lax.axis_size("sub")
    clus_dev = owner_map.shape[0] // owners
    capacity = 2 * local_rows // owners
    slots = owners * capacity
    params = pltpu.CompilerParams(vmem_limit_bytes=32 << 20)
    compare_cost = pl.CostEstimate(
        flops=4 * slots * slots * width, bytes_accessed=4 * slots * width, transcendentals=0
    )
    me = lax.axis_index("shard").astype(jnp.int32).reshape(1)
    ints = jnp.concatenate([owner_map, cluster_id, item_order]).reshape(1, -1)

    direct = owners == len(PARTNERS)
    order = PARTNERS if direct else tuple(range(owners))
    parts = owners if direct else 1
    tiles = 2 * (width // LANES) + 1
    block = (tiles, slots // parts // 2, LANES)
    slot, digit = pl.pallas_call(
        functools.partial(slot_kernel, owners, capacity, order, parts, local_rows),
        out_shape=[
            jax.ShapeDtypeStruct((1, local_rows), jnp.int32),
            jax.ShapeDtypeStruct((LANES, 2 * local_rows), jnp.bfloat16),
        ],
        in_specs=[SCALAR, WHOLE],
        out_specs=[WHOLE] * 2,
        compiler_params=params,
        cost_estimate=pl.CostEstimate(flops=1 << 29, bytes_accessed=1 << 16, transcendentals=0),
        name="slots",
    )(me, ints)
    packed = pl.pallas_call(
        pack_kernel,
        out_shape=[jax.ShapeDtypeStruct(block, jnp.bfloat16)] * parts,
        in_specs=[WHOLE] * 3,
        out_specs=[WHOLE] * parts,
        compiler_params=params,
        name="pack",
    )(slot, digit, embeddings)
    query = exchange(packed, order) if direct else exchange_all(packed[0], me[0])
    other = from_partner(query, 1, "sub")
    asked = slots + clus_dev
    near = pl.pallas_call(
        functools.partial(near_kernel, rows_all, owner_map.shape[0], clus_dev, tiles),
        out_shape=[
            jax.ShapeDtypeStruct((width, slots), jnp.bfloat16),
            jax.ShapeDtypeStruct((asked, LANES), jnp.int32),
            jax.ShapeDtypeStruct((2, slots), jnp.int32),
            jax.ShapeDtypeStruct((1, slots), jnp.float32),
            jax.ShapeDtypeStruct((asked, width), jnp.float32),
            jax.ShapeDtypeStruct((asked, LANES), jnp.float32),
        ],
        in_specs=[SCALAR] + [WHOLE] * 2,
        out_specs=[WHOLE] * 6,
        compiler_params=params,
        cost_estimate=compare_cost,
        name="near",
    )(me, ints, query)
    results, norms = pl.pallas_call(
        functools.partial(far_kernel, rows_all, tiles),
        out_shape=[
            jax.ShapeDtypeStruct((owners, 2, slots), jnp.float32),
            jax.ShapeDtypeStruct((1, clus_dev), jnp.float32),
        ],
        in_specs=[WHOLE] * 8,
        out_specs=[WHOLE] * 2,
        compiler_params=params,
        cost_estimate=compare_cost,
        name="far",
    )(query, other, *near)
    results = lax.all_to_all(results, "shard", 0, 0, tiled=True)
    best, distance, cohesion = pl.pallas_call(
        functools.partial(pick_kernel, order, parts),
        out_shape=[jax.ShapeDtypeStruct((1, local_rows), jnp.float32)] * 2
        + [jax.ShapeDtypeStruct((1, clus_dev), jnp.float32)],
        in_specs=[SCALAR] + [WHOLE] * 3,
        out_specs=[WHOLE] * 3,
        compiler_params=params,
        name="pick",
    )(me, slot, results, norms)
    return best.reshape(local_rows), distance.reshape(local_rows), cohesion.reshape(clus_dev)


def solution(mesh):
    in_specs = (
        P(("groups", "shard", "sub"), None),
        P(("groups", "shard", "sub")),
        P(("groups", "shard", "sub")),
        P("groups"),
    )
    out_specs = (
        P(("groups", "shard", "sub")),
        P(("groups", "shard", "sub")),
        P(("groups", "shard")),
    )
    return jax.shard_map(local, mesh=mesh, in_specs=in_specs, out_specs=out_specs, check_vma=False)
```

```python
import functools

import jax
import jax.numpy as jnp
from jax import lax
from jax.experimental import pallas as pl
from jax.experimental.pallas import tpu as pltpu
from jax.sharding import PartitionSpec as P

LANES = 128
DIGITS = 3
PARTNERS = (4, 3, 2, 5, 6, 7, 1, 0)
WHOLE = pl.BlockSpec(memory_space=pltpu.VMEM)
SCALAR = pl.BlockSpec(memory_space=pltpu.SMEM)


def iota(shape, dim):
    return lax.broadcasted_iota(jnp.int32, shape, dim)


def matmul(a, b):
    return jnp.dot(a, b, preferred_element_type=jnp.float32)


def matmul_t(a, b):
    return lax.dot_general(a, b, (((1,), (1,)), ((), ())), preferred_element_type=jnp.float32)


def bf16(x):
    return x.astype(jnp.float32).astype(jnp.bfloat16)


def ranked(hot):
    upto = (iota((LANES, LANES), 0) <= iota((LANES, LANES), 1)).astype(jnp.bfloat16)
    before, parts = jnp.zeros((1, 1), jnp.float32), []
    for start in range(0, hot.shape[1], LANES):
        piece = hot[:, start : start + LANES]
        spread = jnp.broadcast_to(piece, (16, LANES)).astype(jnp.bfloat16)
        parts.append(matmul(spread, upto)[:1] + before)
        before = before + jnp.sum(piece, axis=1, keepdims=True)
    return jnp.concatenate(parts, axis=1)


def slot_kernel(
    owners, capacity, order, parts, rows, me_ref, ints_ref, slot_ref, digit_ref
):
    clusters = ints_ref.shape[1] - 2 * rows
    cluster = ints_ref[:, clusters : clusters + rows]
    named = bf16(iota((clusters, rows), 0) == cluster)
    owner_map = bf16(jnp.broadcast_to(ints_ref[:, :clusters], (16, clusters)))
    owner = matmul(owner_map, named)[:1].astype(jnp.int32)
    hot = (iota((max(owners, 16), rows), 0) == owner).astype(jnp.float32)
    upto = bf16(iota((rows, rows), 0) <= iota((rows, rows), 1))
    rank = jnp.sum(hot * matmul(bf16(hot), upto), axis=0, keepdims=True) - 1.0
    rank = rank.astype(jnp.int32)
    partner = owner ^ me_ref[0]
    place = partner
    for index, k in enumerate(order):
        place = jnp.where(partner == k, index, place)
    if parts == 1:
        slot_ref[...] = place * capacity + rank
    else:
        half = capacity // 2
        later = (rank >= half).astype(jnp.int32)
        slot_ref[...] = place * half + rank + later * (owners * half - half)

    line = iota((8, rows), 0)
    digit = jnp.zeros((8, rows), jnp.int32)
    for first, number in ((0, cluster + 1), (DIGITS, ints_ref[:, clusters + rows :])):
        for at in range(DIGITS):
            digit = jnp.where(line == first + at, (number >> (8 * at)) & 255, digit)
    empty = jnp.zeros((LANES // 2 - 8, rows), jnp.int32)
    none = jnp.zeros((LANES // 2, rows), jnp.int32)
    early = jnp.concatenate([digit, empty, none], axis=0)
    late = jnp.concatenate([none, digit, empty], axis=0)
    digit_ref[...] = bf16(jnp.concatenate([early, late], axis=1))


def pack_kernel(slot_ref, digit_ref, embed_ref, *out_refs):
    rows, width = embed_ref.shape
    tiles, half, _ = out_refs[0].shape
    values = embed_ref[...].astype(jnp.float32)
    mean_sq = jnp.sum(values * values, axis=1, keepdims=True) * (1.0 / width)
    unit = (values * lax.rsqrt(width * (mean_sq + 1e-06))).astype(jnp.bfloat16)
    late = half * len(out_refs)
    move = bf16(iota((2 * late, rows), 0) == slot_ref[...])
    moved = matmul(move, unit).astype(jnp.bfloat16)
    both = jnp.concatenate([move[:late], move[late:]], axis=1)
    digit = matmul_t(both, digit_ref[...]).astype(jnp.bfloat16)
    each = tiles // 2
    for index, out_ref in enumerate(out_refs):
        start = index * half
        for tile in range(each):
            lanes = slice(tile * LANES, (tile + 1) * LANES)
            out_ref[tile] = moved[start : start + half, lanes]
            out_ref[each + tile] = moved[late + start : late + start + half, lanes]
        out_ref[tiles - 1] = digit[start : start + half]


def unpacked(block_ref, tiles):
    blocks = block_ref.shape[0] // tiles
    each = tiles // 2

    def column(tile):
        return jnp.concatenate([block_ref[i * tiles + tile] for i in range(blocks)], axis=0)

    halves = [
        jnp.concatenate([column(first + tile) for tile in range(each)], axis=1)
        for first in (0, each)
    ]
    return jnp.concatenate(halves, axis=0), column(tiles - 1)


def weights(number, at, half):
    value = jnp.zeros(at.shape, jnp.float32)
    for place in range(DIGITS):
        for which in (0, 1):
            lane = half * (LANES // 2) + which * DIGITS + place
            value = jnp.where((at == lane) & (number == which), 256.0**place, value)
    return value.astype(jnp.bfloat16)


def key_rows(rows_all, digit):
    at = iota((16, LANES), 0), iota((16, LANES), 1)
    numbers = [matmul_t(weights(*at, half), digit) for half in (0, 1)]
    numbers = jnp.concatenate(numbers, axis=1)
    low = (numbers[0:1].astype(jnp.int32) - 1) * rows_all
    return low, low + numbers[1:2].astype(jnp.int32)


def key_columns(rows_all, digit):
    at = iota((LANES, 2 * LANES), 1) // LANES, iota((LANES, 2 * LANES), 0)
    numbers = [matmul(digit, weights(*at, half)) for half in (0, 1)]
    numbers = jnp.concatenate(numbers, axis=0)
    low = (numbers[:, :LANES].astype(jnp.int32) - 1) * rows_all
    return low, low + numbers[:, LANES:].astype(jnp.int32)


def across(column, count):
    return jnp.concatenate([column] * (count // LANES), axis=1)


def compare(rows_all, query_t, query_low, query_key, lows, rows, digit):
    _, key = key_rows(rows_all, digit)
    bound = across(lows, key.shape[1])
    member = bf16((key >= bound) & (key < bound + rows_all))
    sums = matmul(member, rows)
    counts = matmul(member, jnp.ones((rows.shape[0], LANES), jnp.bfloat16))
    scores = matmul(rows, query_t)
    _, key = key_columns(rows_all, digit)
    key = across(key, query_t.shape[1])
    earlier = (key >= query_low) & (key < query_key)
    best = jnp.max(jnp.where(earlier, scores, -3.0), axis=0, keepdims=True)
    return best, sums, counts


def near_kernel(
    rows_all, clusters, clus_dev, tiles, me_ref, ints_ref, query_ref,
    query_t_ref, lows_ref, key_ref, best_ref, sums_ref, counts_ref,
):
    hot = (ints_ref[:, :clusters] == me_ref[0]).astype(jnp.float32)
    rank = ranked(hot)
    shape = (clus_dev, clusters)
    kth = (rank == iota(shape, 0).astype(jnp.float32) + 1.0) & (hot > 0.0)
    own = jnp.sum(jnp.where(kth, iota(shape, 1).astype(jnp.float32), 0.0), axis=1, keepdims=True)
    own = jnp.broadcast_to(own.astype(jnp.int32) * rows_all, (clus_dev, LANES))
    query, digit = unpacked(query_ref, tiles)
    low, _ = key_columns(rows_all, digit)
    lows = jnp.concatenate([low, own], axis=0)
    query_low, query_key = key_rows(rows_all, digit)
    query_t = jnp.transpose(query)
    query_t_ref[...] = query_t
    best, sums, counts = compare(rows_all, query_t, query_low, query_key, lows, query, digit)
    lows_ref[...] = lows
    key_ref[...] = jnp.concatenate([query_low, query_key], axis=0)
    best_ref[...] = best
    sums_ref[...] = sums
    counts_ref[...] = counts


def far_kernel(
    rows_all, tiles, query_ref, other_ref, query_t_ref, lows_ref, key_ref, best_ref, sums_ref, counts_ref,
    result_ref, norm_ref,
):
    query, _ = unpacked(query_ref, tiles)
    queries, width = query.shape
    rows, digit = unpacked(other_ref, tiles)
    best, sums, counts = compare(
        rows_all, query_t_ref[...], key_ref[0:1], key_ref[1:2], lows_ref[...], rows, digit
    )
    best = jnp.maximum(best, best_ref[...])
    best = jnp.where(best > -2.0, best, 0.0)
    share = 1.0 / jnp.maximum(counts + counts_ref[...], 1.0)
    squares = jnp.zeros(share.shape, jnp.float32)
    for start in range(0, width, LANES):
        lanes = slice(start, start + LANES)
        centroid = (sums[:, lanes] + sums_ref[:, lanes]) * share
        offset = jnp.concatenate(
            [query[:, lanes].astype(jnp.float32) - centroid[:queries], centroid[queries:]], axis=0
        )
        squares = squares + offset * offset
    total = jnp.sum(jnp.transpose(squares), axis=0, keepdims=True)
    result = jnp.concatenate([best, total[:, :queries]], axis=0)
    for owner in range(result_ref.shape[0]):
        result_ref[owner] = result
    norm_ref[...] = total[:, queries:]


def pick_kernel(
    order, parts, me_ref, slot_ref, result_ref, norm_ref, best_ref, distance_ref, cohesion_ref
):
    cohesion_ref[...] = norm_ref[...]
    rows = slot_ref.shape[1]
    owners, lines, slots = result_ref.shape
    folds = min(parts, 2)
    place = iota((lines, slots), 1) % (slots // folds) // (slots // owners // folds)
    values = jnp.zeros((lines, slots), jnp.float32)
    for index, k in enumerate(order):
        values = jnp.where(place == index, result_ref[me_ref[0] ^ k], values)
    values = jnp.concatenate([values, jnp.zeros((8 - lines, slots), jnp.float32)], axis=0)
    at = (iota((slots, rows), 0) == slot_ref[...]).astype(jnp.float32)
    picked = jnp.dot(
        values, at, precision=lax.Precision.HIGHEST, preferred_element_type=jnp.float32
    )
    best_ref[...] = picked[0:1]
    distance_ref[...] = picked[1:2]


def from_partner(value, k, axis):
    return lax.ppermute(value, axis, [(i, i ^ k) for i in range(lax.axis_size(axis))])


def exchange(packed, order):
    return jnp.concatenate(
        [from_partner(block, k, "shard") if k else block for k, block in zip(order, packed)]
    )


def exchange_all(packed, me):
    owners = lax.axis_size("shard")
    tiles, half, _ = packed.shape
    each = tiles // 2
    data = packed[:-1].reshape(2, each, half, LANES).transpose(0, 2, 1, 3).reshape(2 * half, -1)
    digit = jnp.concatenate(jnp.split(packed[-1], 2, axis=1))
    parted = jnp.concatenate([data, digit], axis=1).reshape(owners, 2 * half // owners, -1)
    partner = me ^ jnp.arange(owners, dtype=jnp.int32)
    got = lax.all_to_all(parted[partner], "shard", 0, 0, tiled=True)[partner].reshape(2 * half, -1)
    data = got[:, : each * LANES].reshape(2, half, each, LANES).transpose(0, 2, 1, 3)
    digit = jnp.concatenate(jnp.split(got[:, each * LANES :], 2), axis=1)
    return jnp.concatenate([data.reshape(2 * each, half, LANES), digit[None]])


def local(embeddings, cluster_id, item_order, owner_map):
    owners = lax.axis_size("shard")
    local_rows, width = embeddings.shape
    rows_all = local_rows * owners * lax.axis_size("sub")
    clus_dev = owner_map.shape[0] // owners
    capacity = 2 * local_rows // owners
    slots = owners * capacity
    params = pltpu.CompilerParams(vmem_limit_bytes=32 << 20)
    compare_cost = pl.CostEstimate(
        flops=4 * slots * slots * width, bytes_accessed=4 * slots * width, transcendentals=0
    )
    me = lax.axis_index("shard").astype(jnp.int32).reshape(1)
    ints = jnp.concatenate([owner_map, cluster_id, item_order]).reshape(1, -1)

    direct = owners == len(PARTNERS)
    order = PARTNERS if direct else tuple(range(owners))
    parts = owners if direct else 1
    tiles = 2 * (width // LANES) + 1
    block = (tiles, slots // parts // 2, LANES)
    slot, digit = pl.pallas_call(
        functools.partial(slot_kernel, owners, capacity, order, parts, local_rows),
        out_shape=[
            jax.ShapeDtypeStruct((1, local_rows), jnp.int32),
            jax.ShapeDtypeStruct((LANES, 2 * local_rows), jnp.bfloat16),
        ],
        in_specs=[SCALAR, WHOLE],
        out_specs=[WHOLE] * 2,
        compiler_params=params,
        cost_estimate=pl.CostEstimate(flops=1 << 29, bytes_accessed=1 << 16, transcendentals=0),
        name="slots",
    )(me, ints)
    packed = pl.pallas_call(
        pack_kernel,
        out_shape=[jax.ShapeDtypeStruct(block, jnp.bfloat16)] * parts,
        in_specs=[WHOLE] * 3,
        out_specs=[WHOLE] * parts,
        compiler_params=params,
        name="pack",
    )(slot, digit, embeddings)
    query = exchange(packed, order) if direct else exchange_all(packed[0], me[0])
    other = from_partner(query, 1, "sub")
    asked = slots + clus_dev
    near = pl.pallas_call(
        functools.partial(near_kernel, rows_all, owner_map.shape[0], clus_dev, tiles),
        out_shape=[
            jax.ShapeDtypeStruct((width, slots), jnp.bfloat16),
            jax.ShapeDtypeStruct((asked, LANES), jnp.int32),
            jax.ShapeDtypeStruct((2, slots), jnp.int32),
            jax.ShapeDtypeStruct((1, slots), jnp.float32),
            jax.ShapeDtypeStruct((asked, width), jnp.float32),
            jax.ShapeDtypeStruct((asked, LANES), jnp.float32),
        ],
        in_specs=[SCALAR] + [WHOLE] * 2,
        out_specs=[WHOLE] * 6,
        compiler_params=params,
        cost_estimate=compare_cost,
        name="near",
    )(me, ints, query)
    results, norms = pl.pallas_call(
        functools.partial(far_kernel, rows_all, tiles),
        out_shape=[
            jax.ShapeDtypeStruct((owners, 2, slots), jnp.float32),
            jax.ShapeDtypeStruct((1, clus_dev), jnp.float32),
        ],
        in_specs=[WHOLE] * 8,
        out_specs=[WHOLE] * 2,
        compiler_params=params,
        cost_estimate=compare_cost,
        name="far",
    )(query, other, *near)
    results = lax.all_to_all(results, "shard", 0, 0, tiled=True)
    best, distance, cohesion = pl.pallas_call(
        functools.partial(pick_kernel, order, parts),
        out_shape=[jax.ShapeDtypeStruct((1, local_rows), jnp.float32)] * 2
        + [jax.ShapeDtypeStruct((1, clus_dev), jnp.float32)],
        in_specs=[SCALAR] + [WHOLE] * 3,
        out_specs=[WHOLE] * 3,
        compiler_params=params,
        name="pick",
    )(me, slot, results, norms)
    return best.reshape(local_rows), distance.reshape(local_rows), cohesion.reshape(clus_dev)


def solution(mesh):
    in_specs = (
        P(("groups", "shard", "sub"), None),
        P(("groups", "shard", "sub")),
        P(("groups", "shard", "sub")),
        P("groups"),
    )
    out_specs = (
        P(("groups", "shard", "sub")),
        P(("groups", "shard", "sub")),
        P(("groups", "shard")),
    )
    return jax.shard_map(local, mesh=mesh, in_specs=in_specs, out_specs=out_specs, check_vma=False)
```

```python
import functools

import jax
import jax.numpy as jnp
from jax import lax
from jax.experimental import pallas as pl
from jax.experimental.pallas import tpu as pltpu
from jax.sharding import PartitionSpec as P

LANES = 128
DIGITS = 3
PARTNERS = (4, 3, 2, 0, 5, 6, 7, 1)
WHOLE = pl.BlockSpec(memory_space=pltpu.VMEM)
SCALAR = pl.BlockSpec(memory_space=pltpu.SMEM)


def iota(shape, dim):
    return lax.broadcasted_iota(jnp.int32, shape, dim)


def matmul(a, b):
    return jnp.dot(a, b, preferred_element_type=jnp.float32)


def matmul_t(a, b):
    return lax.dot_general(a, b, (((1,), (1,)), ((), ())), preferred_element_type=jnp.float32)


def bf16(x):
    return x.astype(jnp.float32).astype(jnp.bfloat16)


def ranked(hot):
    upto = (iota((LANES, LANES), 0) <= iota((LANES, LANES), 1)).astype(jnp.bfloat16)
    before, parts = jnp.zeros((1, 1), jnp.float32), []
    for start in range(0, hot.shape[1], LANES):
        piece = hot[:, start : start + LANES]
        spread = jnp.broadcast_to(piece, (16, LANES)).astype(jnp.bfloat16)
        parts.append(matmul(spread, upto)[:1] + before)
        before = before + jnp.sum(piece, axis=1, keepdims=True)
    return jnp.concatenate(parts, axis=1)


def slot_kernel(
    owners, capacity, order, parts, rows, me_ref, ints_ref, slot_ref, digit_ref
):
    clusters = ints_ref.shape[1] - 2 * rows
    cluster = ints_ref[:, clusters : clusters + rows]
    named = bf16(iota((clusters, rows), 0) == cluster)
    owner_map = bf16(jnp.broadcast_to(ints_ref[:, :clusters], (16, clusters)))
    owner = matmul(owner_map, named)[:1].astype(jnp.int32)
    hot = (iota((max(owners, 16), rows), 0) == owner).astype(jnp.float32)
    upto = bf16(iota((rows, rows), 0) <= iota((rows, rows), 1))
    rank = jnp.sum(hot * matmul(bf16(hot), upto), axis=0, keepdims=True) - 1.0
    rank = rank.astype(jnp.int32)
    partner = owner ^ me_ref[0]
    place = partner
    for index, k in enumerate(order):
        place = jnp.where(partner == k, index, place)
    if parts == 1:
        slot_ref[...] = place * capacity + rank
    else:
        half = capacity // 2
        later = (rank >= half).astype(jnp.int32)
        slot_ref[...] = place * half + rank + later * (owners * half - half)

    line = iota((8, rows), 0)
    digit = jnp.zeros((8, rows), jnp.int32)
    for first, number in ((0, cluster + 1), (DIGITS, ints_ref[:, clusters + rows :])):
        for at in range(DIGITS):
            digit = jnp.where(line == first + at, (number >> (8 * at)) & 255, digit)
    empty = jnp.zeros((LANES // 2 - 8, rows), jnp.int32)
    none = jnp.zeros((LANES // 2, rows), jnp.int32)
    early = jnp.concatenate([digit, empty, none], axis=0)
    late = jnp.concatenate([none, digit, empty], axis=0)
    digit_ref[...] = bf16(jnp.concatenate([early, late], axis=1))


def pack_kernel(slot_ref, digit_ref, embed_ref, *out_refs):
    rows, width = embed_ref.shape
    tiles, half, _ = out_refs[0].shape
    values = embed_ref[...].astype(jnp.float32)
    mean_sq = jnp.sum(values * values, axis=1, keepdims=True) * (1.0 / width)
    unit = (values * lax.rsqrt(width * (mean_sq + 1e-06))).astype(jnp.bfloat16)
    late = half * len(out_refs)
    move = bf16(iota((2 * late, rows), 0) == slot_ref[...])
    moved = matmul(move, unit).astype(jnp.bfloat16)
    both = jnp.concatenate([move[:late], move[late:]], axis=1)
    digit = matmul_t(both, digit_ref[...]).astype(jnp.bfloat16)
    each = tiles // 2
    for index, out_ref in enumerate(out_refs):
        start = index * half
        for tile in range(each):
            lanes = slice(tile * LANES, (tile + 1) * LANES)
            out_ref[tile] = moved[start : start + half, lanes]
            out_ref[each + tile] = moved[late + start : late + start + half, lanes]
        out_ref[tiles - 1] = digit[start : start + half]


def unpacked(block_ref, tiles):
    blocks = block_ref.shape[0] // tiles
    each = tiles // 2

    def column(tile):
        return jnp.concatenate([block_ref[i * tiles + tile] for i in range(blocks)], axis=0)

    halves = [
        jnp.concatenate([column(first + tile) for tile in range(each)], axis=1)
        for first in (0, each)
    ]
    return jnp.concatenate(halves, axis=0), column(tiles - 1)


def weights(number, at, half):
    value = jnp.zeros(at.shape, jnp.float32)
    for place in range(DIGITS):
        for which in (0, 1):
            lane = half * (LANES // 2) + which * DIGITS + place
            value = jnp.where((at == lane) & (number == which), 256.0**place, value)
    return value.astype(jnp.bfloat16)


def key_rows(rows_all, digit):
    at = iota((16, LANES), 0), iota((16, LANES), 1)
    numbers = [matmul_t(weights(*at, half), digit) for half in (0, 1)]
    numbers = jnp.concatenate(numbers, axis=1)
    low = (numbers[0:1].astype(jnp.int32) - 1) * rows_all
    return low, low + numbers[1:2].astype(jnp.int32)


def key_columns(rows_all, digit):
    at = iota((LANES, 2 * LANES), 1) // LANES, iota((LANES, 2 * LANES), 0)
    numbers = [matmul(digit, weights(*at, half)) for half in (0, 1)]
    numbers = jnp.concatenate(numbers, axis=0)
    low = (numbers[:, :LANES].astype(jnp.int32) - 1) * rows_all
    return low, low + numbers[:, LANES:].astype(jnp.int32)


def across(column, count):
    return jnp.concatenate([column] * (count // LANES), axis=1)


def compare(rows_all, query_t, query_low, query_key, lows, parts):
    rows = jnp.concatenate([rows for rows, _ in parts], axis=0)
    key = jnp.concatenate([key_rows(rows_all, digit)[1] for _, digit in parts], axis=1)
    bound = across(lows, key.shape[1])
    member = bf16((key >= bound) & (key < bound + rows_all))
    sums = matmul(member, rows)
    counts = matmul(member, jnp.ones((rows.shape[0], LANES), jnp.bfloat16))
    scores = matmul(rows, query_t)
    key = jnp.concatenate([key_columns(rows_all, digit)[1] for _, digit in parts], axis=0)
    key = across(key, query_t.shape[1])
    earlier = (key >= query_low) & (key < query_key)
    best = jnp.max(jnp.where(earlier, scores, -3.0), axis=0, keepdims=True)
    return best, sums, counts


def near_kernel(
    rows_all, clusters, clus_dev, tiles, me_ref, ints_ref, query_ref, other_ref,
    query_t_ref, lows_ref, key_ref, best_ref, sums_ref, counts_ref,
):
    hot = (ints_ref[:, :clusters] == me_ref[0]).astype(jnp.float32)
    rank = ranked(hot)
    shape = (clus_dev, clusters)
    kth = (rank == iota(shape, 0).astype(jnp.float32) + 1.0) & (hot > 0.0)
    own = jnp.sum(jnp.where(kth, iota(shape, 1).astype(jnp.float32), 0.0), axis=1, keepdims=True)
    own = jnp.broadcast_to(own.astype(jnp.int32) * rows_all, (clus_dev, LANES))
    query, digit = unpacked(query_ref, tiles)
    low, _ = key_columns(rows_all, digit)
    lows = jnp.concatenate([low, own], axis=0)
    query_low, query_key = key_rows(rows_all, digit)
    query_t = jnp.transpose(query)
    query_t_ref[...] = query_t
    parts = [(query, digit), unpacked(other_ref, tiles)]
    best, sums, counts = compare(rows_all, query_t, query_low, query_key, lows, parts)
    lows_ref[...] = lows
    key_ref[...] = jnp.concatenate([query_low, query_key], axis=0)
    best_ref[...] = best
    sums_ref[...] = sums
    counts_ref[...] = counts


def far_kernel(
    rows_all, tiles, query_ref, other_ref, query_t_ref, lows_ref, key_ref, best_ref, sums_ref, counts_ref,
    result_ref, norm_ref,
):
    query, _ = unpacked(query_ref, tiles)
    queries, width = query.shape
    best, sums, counts = compare(
        rows_all, query_t_ref[...], key_ref[0:1], key_ref[1:2], lows_ref[...], [unpacked(other_ref, tiles)]
    )
    best = jnp.maximum(best, best_ref[...])
    best = jnp.where(best > -2.0, best, 0.0)
    share = 1.0 / jnp.maximum(counts + counts_ref[...], 1.0)
    squares = jnp.zeros(share.shape, jnp.float32)
    for start in range(0, width, LANES):
        lanes = slice(start, start + LANES)
        centroid = (sums[:, lanes] + sums_ref[:, lanes]) * share
        offset = jnp.concatenate(
            [query[:, lanes].astype(jnp.float32) - centroid[:queries], centroid[queries:]], axis=0
        )
        squares = squares + offset * offset
    total = jnp.sum(jnp.transpose(squares), axis=0, keepdims=True)
    result = jnp.concatenate([best, total[:, :queries]], axis=0)
    for owner in range(result_ref.shape[0]):
        result_ref[owner] = result
    norm_ref[...] = total[:, queries:]


def pick_kernel(
    order, parts, me_ref, slot_ref, result_ref, norm_ref, best_ref, distance_ref, cohesion_ref
):
    cohesion_ref[...] = norm_ref[...]
    rows = slot_ref.shape[1]
    owners, lines, slots = result_ref.shape
    folds = min(parts, 2)
    place = iota((lines, slots), 1) % (slots // folds) // (slots // owners // folds)
    values = jnp.zeros((lines, slots), jnp.float32)
    for index, k in enumerate(order):
        values = jnp.where(place == index, result_ref[me_ref[0] ^ k], values)
    values = jnp.concatenate([values, jnp.zeros((8 - lines, slots), jnp.float32)], axis=0)
    at = (iota((slots, rows), 0) == slot_ref[...]).astype(jnp.float32)
    picked = jnp.dot(
        values, at, precision=lax.Precision.HIGHEST, preferred_element_type=jnp.float32
    )
    best_ref[...] = picked[0:1]
    distance_ref[...] = picked[1:2]


def from_partner(value, k, axis):
    return lax.ppermute(value, axis, [(i, i ^ k) for i in range(lax.axis_size(axis))])


def exchange(packed, order):
    got = [from_partner(block, k, "shard") if k else block for k, block in zip(order, packed)]
    half = len(got) // 2
    return jnp.concatenate(got[:half]), jnp.concatenate(got[half:])


def exchange_all(packed, me):
    owners = lax.axis_size("shard")
    tiles, half, _ = packed.shape
    each = tiles // 2
    data = packed[:-1].reshape(2, each, half, LANES).transpose(0, 2, 1, 3).reshape(2 * half, -1)
    digit = jnp.concatenate(jnp.split(packed[-1], 2, axis=1))
    parted = jnp.concatenate([data, digit], axis=1).reshape(owners, 2 * half // owners, -1)
    partner = me ^ jnp.arange(owners, dtype=jnp.int32)
    got = lax.all_to_all(parted[partner], "shard", 0, 0, tiled=True)[partner].reshape(2 * half, -1)
    data = got[:, : each * LANES].reshape(2, half, each, LANES).transpose(0, 2, 1, 3)
    digit = jnp.concatenate(jnp.split(got[:, each * LANES :], 2), axis=1)
    got = jnp.concatenate([data.reshape(2 * each, half, LANES), digit[None]])
    return jnp.split(got, 2, axis=1)


def local(embeddings, cluster_id, item_order, owner_map):
    owners = lax.axis_size("shard")
    local_rows, width = embeddings.shape
    rows_all = local_rows * owners * lax.axis_size("sub")
    clus_dev = owner_map.shape[0] // owners
    capacity = 2 * local_rows // owners
    slots = owners * capacity
    params = pltpu.CompilerParams(vmem_limit_bytes=32 << 20)
    compare_cost = pl.CostEstimate(
        flops=4 * slots * slots * width, bytes_accessed=4 * slots * width, transcendentals=0
    )
    me = lax.axis_index("shard").astype(jnp.int32).reshape(1)
    ints = jnp.concatenate([owner_map, cluster_id, item_order]).reshape(1, -1)

    direct = owners == len(PARTNERS)
    order = PARTNERS if direct else tuple(range(owners))
    parts = owners if direct else 1
    tiles = 2 * (width // LANES) + 1
    block = (tiles, slots // parts // 2, LANES)
    slot, digit = pl.pallas_call(
        functools.partial(slot_kernel, owners, capacity, order, parts, local_rows),
        out_shape=[
            jax.ShapeDtypeStruct((1, local_rows), jnp.int32),
            jax.ShapeDtypeStruct((LANES, 2 * local_rows), jnp.bfloat16),
        ],
        in_specs=[SCALAR, WHOLE],
        out_specs=[WHOLE] * 2,
        compiler_params=params,
        cost_estimate=pl.CostEstimate(flops=1 << 29, bytes_accessed=1 << 16, transcendentals=0),
        name="slots",
    )(me, ints)
    packed = pl.pallas_call(
        pack_kernel,
        out_shape=[jax.ShapeDtypeStruct(block, jnp.bfloat16)] * parts,
        in_specs=[WHOLE] * 3,
        out_specs=[WHOLE] * parts,
        compiler_params=params,
        name="pack",
    )(slot, digit, embeddings)
    first, second = exchange(packed, order) if direct else exchange_all(packed[0], me[0])
    other_first, other_second = (from_partner(rows, 1, "sub") for rows in (first, second))
    query = jnp.concatenate([first, second])
    asked = slots + clus_dev
    near = pl.pallas_call(
        functools.partial(near_kernel, rows_all, owner_map.shape[0], clus_dev, tiles),
        out_shape=[
            jax.ShapeDtypeStruct((width, slots), jnp.bfloat16),
            jax.ShapeDtypeStruct((asked, LANES), jnp.int32),
            jax.ShapeDtypeStruct((2, slots), jnp.int32),
            jax.ShapeDtypeStruct((1, slots), jnp.float32),
            jax.ShapeDtypeStruct((asked, width), jnp.float32),
            jax.ShapeDtypeStruct((asked, LANES), jnp.float32),
        ],
        in_specs=[SCALAR] + [WHOLE] * 3,
        out_specs=[WHOLE] * 6,
        compiler_params=params,
        cost_estimate=compare_cost,
        name="near",
    )(me, ints, query, other_first)
    results, norms = pl.pallas_call(
        functools.partial(far_kernel, rows_all, tiles),
        out_shape=[
            jax.ShapeDtypeStruct((owners, 2, slots), jnp.float32),
            jax.ShapeDtypeStruct((1, clus_dev), jnp.float32),
        ],
        in_specs=[WHOLE] * 8,
        out_specs=[WHOLE] * 2,
        compiler_params=params,
        cost_estimate=compare_cost,
        name="far",
    )(query, other_second, *near)
    results = lax.all_to_all(results, "shard", 0, 0, tiled=True)
    best, distance, cohesion = pl.pallas_call(
        functools.partial(pick_kernel, order, parts),
        out_shape=[jax.ShapeDtypeStruct((1, local_rows), jnp.float32)] * 2
        + [jax.ShapeDtypeStruct((1, clus_dev), jnp.float32)],
        in_specs=[SCALAR] + [WHOLE] * 3,
        out_specs=[WHOLE] * 3,
        compiler_params=params,
        name="pick",
    )(me, slot, results, norms)
    return best.reshape(local_rows), distance.reshape(local_rows), cohesion.reshape(clus_dev)


def solution(mesh):
    in_specs = (
        P(("groups", "shard", "sub"), None),
        P(("groups", "shard", "sub")),
        P(("groups", "shard", "sub")),
        P("groups"),
    )
    out_specs = (
        P(("groups", "shard", "sub")),
        P(("groups", "shard", "sub")),
        P(("groups", "shard")),
    )
    return jax.shard_map(local, mesh=mesh, in_specs=in_specs, out_specs=out_specs, check_vma=False)
```

```python
import functools

import jax
import jax.numpy as jnp
from jax import lax
from jax.experimental import pallas as pl
from jax.experimental.pallas import tpu as pltpu
from jax.sharding import PartitionSpec as P

LANES = 128
DIGITS = 3
PARTNERS = (4, 3, 5, 0, 2, 6, 7, 1)
WHOLE = pl.BlockSpec(memory_space=pltpu.VMEM)
SCALAR = pl.BlockSpec(memory_space=pltpu.SMEM)


def iota(shape, dim):
    return lax.broadcasted_iota(jnp.int32, shape, dim)


def matmul(a, b):
    return jnp.dot(a, b, preferred_element_type=jnp.float32)


def matmul_t(a, b):
    return lax.dot_general(a, b, (((1,), (1,)), ((), ())), preferred_element_type=jnp.float32)


def bf16(x):
    return x.astype(jnp.float32).astype(jnp.bfloat16)


def ranked(hot):
    upto = (iota((LANES, LANES), 0) <= iota((LANES, LANES), 1)).astype(jnp.bfloat16)
    before, parts = jnp.zeros((1, 1), jnp.float32), []
    for start in range(0, hot.shape[1], LANES):
        piece = hot[:, start : start + LANES]
        spread = jnp.broadcast_to(piece, (16, LANES)).astype(jnp.bfloat16)
        parts.append(matmul(spread, upto)[:1] + before)
        before = before + jnp.sum(piece, axis=1, keepdims=True)
    return jnp.concatenate(parts, axis=1)


def slot_kernel(
    owners, capacity, order, parts, rows, me_ref, ints_ref, slot_ref, digit_ref
):
    clusters = ints_ref.shape[1] - 2 * rows
    cluster = ints_ref[:, clusters : clusters + rows]
    named = bf16(iota((clusters, rows), 0) == cluster)
    owner_map = bf16(jnp.broadcast_to(ints_ref[:, :clusters], (16, clusters)))
    owner = matmul(owner_map, named)[:1].astype(jnp.int32)
    hot = (iota((max(owners, 16), rows), 0) == owner).astype(jnp.float32)
    upto = bf16(iota((rows, rows), 0) <= iota((rows, rows), 1))
    rank = jnp.sum(hot * matmul(bf16(hot), upto), axis=0, keepdims=True) - 1.0
    rank = rank.astype(jnp.int32)
    partner = owner ^ me_ref[0]
    place = partner
    for index, k in enumerate(order):
        place = jnp.where(partner == k, index, place)
    if parts == 1:
        slot_ref[...] = place * capacity + rank
    else:
        half = capacity // 2
        later = (rank >= half).astype(jnp.int32)
        slot_ref[...] = place * half + rank + later * (owners * half - half)

    line = iota((8, rows), 0)
    digit = jnp.zeros((8, rows), jnp.int32)
    for first, number in ((0, cluster + 1), (DIGITS, ints_ref[:, clusters + rows :])):
        for at in range(DIGITS):
            digit = jnp.where(line == first + at, (number >> (8 * at)) & 255, digit)
    empty = jnp.zeros((LANES // 2 - 8, rows), jnp.int32)
    none = jnp.zeros((LANES // 2, rows), jnp.int32)
    early = jnp.concatenate([digit, empty, none], axis=0)
    late = jnp.concatenate([none, digit, empty], axis=0)
    digit_ref[...] = bf16(jnp.concatenate([early, late], axis=1))


def pack_kernel(slot_ref, digit_ref, embed_ref, *out_refs):
    rows, width = embed_ref.shape
    tiles, half, _ = out_refs[0].shape
    values = embed_ref[...].astype(jnp.float32)
    mean_sq = jnp.sum(values * values, axis=1, keepdims=True) * (1.0 / width)
    unit = (values * lax.rsqrt(width * (mean_sq + 1e-06))).astype(jnp.bfloat16)
    late = half * len(out_refs)
    move = bf16(iota((2 * late, rows), 0) == slot_ref[...])
    moved = matmul(move, unit).astype(jnp.bfloat16)
    both = jnp.concatenate([move[:late], move[late:]], axis=1)
    digit = matmul_t(both, digit_ref[...]).astype(jnp.bfloat16)
    each = tiles // 2
    for index, out_ref in enumerate(out_refs):
        start = index * half
        for tile in range(each):
            lanes = slice(tile * LANES, (tile + 1) * LANES)
            out_ref[tile] = moved[start : start + half, lanes]
            out_ref[each + tile] = moved[late + start : late + start + half, lanes]
        out_ref[tiles - 1] = digit[start : start + half]


def unpacked(block_ref, tiles):
    blocks = block_ref.shape[0] // tiles
    each = tiles // 2

    def column(tile):
        return jnp.concatenate([block_ref[i * tiles + tile] for i in range(blocks)], axis=0)

    halves = [
        jnp.concatenate([column(first + tile) for tile in range(each)], axis=1)
        for first in (0, each)
    ]
    return jnp.concatenate(halves, axis=0), column(tiles - 1)


def weights(number, at, half):
    value = jnp.zeros(at.shape, jnp.float32)
    for place in range(DIGITS):
        for which in (0, 1):
            lane = half * (LANES // 2) + which * DIGITS + place
            value = jnp.where((at == lane) & (number == which), 256.0**place, value)
    return value.astype(jnp.bfloat16)


def key_rows(rows_all, digit):
    at = iota((16, LANES), 0), iota((16, LANES), 1)
    numbers = [matmul_t(weights(*at, half), digit) for half in (0, 1)]
    numbers = jnp.concatenate(numbers, axis=1)
    low = (numbers[0:1].astype(jnp.int32) - 1) * rows_all
    return low, low + numbers[1:2].astype(jnp.int32)


def key_columns(rows_all, digit):
    at = iota((LANES, 2 * LANES), 1) // LANES, iota((LANES, 2 * LANES), 0)
    numbers = [matmul(digit, weights(*at, half)) for half in (0, 1)]
    numbers = jnp.concatenate(numbers, axis=0)
    low = (numbers[:, :LANES].astype(jnp.int32) - 1) * rows_all
    return low, low + numbers[:, LANES:].astype(jnp.int32)


def across(column, count):
    return jnp.concatenate([column] * (count // LANES), axis=1)


def compare(rows_all, query_t, query_low, query_key, lows, parts):
    rows = jnp.concatenate([rows for rows, _ in parts], axis=0)
    key = jnp.concatenate([key_rows(rows_all, digit)[1] for _, digit in parts], axis=1)
    bound = across(lows, key.shape[1])
    member = bf16((key >= bound) & (key < bound + rows_all))
    sums = matmul(member, rows)
    counts = matmul(member, jnp.ones((rows.shape[0], LANES), jnp.bfloat16))
    scores = matmul(rows, query_t)
    key = jnp.concatenate([key_columns(rows_all, digit)[1] for _, digit in parts], axis=0)
    key = across(key, query_t.shape[1])
    earlier = (key >= query_low) & (key < query_key)
    best = jnp.max(jnp.where(earlier, scores, -3.0), axis=0, keepdims=True)
    return best, sums, counts


def near_kernel(
    rows_all, clusters, clus_dev, tiles, me_ref, ints_ref, query_ref, other_ref,
    query_t_ref, lows_ref, key_ref, best_ref, sums_ref, counts_ref,
):
    hot = (ints_ref[:, :clusters] == me_ref[0]).astype(jnp.float32)
    rank = ranked(hot)
    shape = (clus_dev, clusters)
    kth = (rank == iota(shape, 0).astype(jnp.float32) + 1.0) & (hot > 0.0)
    own = jnp.sum(jnp.where(kth, iota(shape, 1).astype(jnp.float32), 0.0), axis=1, keepdims=True)
    own = jnp.broadcast_to(own.astype(jnp.int32) * rows_all, (clus_dev, LANES))
    query, digit = unpacked(query_ref, tiles)
    low, _ = key_columns(rows_all, digit)
    lows = jnp.concatenate([low, own], axis=0)
    query_low, query_key = key_rows(rows_all, digit)
    query_t = jnp.transpose(query)
    query_t_ref[...] = query_t
    parts = [(query, digit), unpacked(other_ref, tiles)]
    best, sums, counts = compare(rows_all, query_t, query_low, query_key, lows, parts)
    lows_ref[...] = lows
    key_ref[...] = jnp.concatenate([query_low, query_key], axis=0)
    best_ref[...] = best
    sums_ref[...] = sums
    counts_ref[...] = counts


def far_kernel(
    rows_all, tiles, query_ref, other_ref, query_t_ref, lows_ref, key_ref, best_ref, sums_ref, counts_ref,
    result_ref, norm_ref,
):
    query, _ = unpacked(query_ref, tiles)
    queries, width = query.shape
    best, sums, counts = compare(
        rows_all, query_t_ref[...], key_ref[0:1], key_ref[1:2], lows_ref[...], [unpacked(other_ref, tiles)]
    )
    best = jnp.maximum(best, best_ref[...])
    best = jnp.where(best > -2.0, best, 0.0)
    share = 1.0 / jnp.maximum(counts + counts_ref[...], 1.0)
    squares = jnp.zeros(share.shape, jnp.float32)
    for start in range(0, width, LANES):
        lanes = slice(start, start + LANES)
        centroid = (sums[:, lanes] + sums_ref[:, lanes]) * share
        offset = jnp.concatenate(
            [query[:, lanes].astype(jnp.float32) - centroid[:queries], centroid[queries:]], axis=0
        )
        squares = squares + offset * offset
    total = jnp.sum(jnp.transpose(squares), axis=0, keepdims=True)
    result = jnp.concatenate([best, total[:, :queries]], axis=0)
    for owner in range(result_ref.shape[0]):
        result_ref[owner] = result
    norm_ref[...] = total[:, queries:]


def pick_kernel(
    order, parts, me_ref, slot_ref, result_ref, norm_ref, best_ref, distance_ref, cohesion_ref
):
    cohesion_ref[...] = norm_ref[...]
    rows = slot_ref.shape[1]
    owners, lines, slots = result_ref.shape
    folds = min(parts, 2)
    place = iota((lines, slots), 1) % (slots // folds) // (slots // owners // folds)
    values = jnp.zeros((lines, slots), jnp.float32)
    for index, k in enumerate(order):
        values = jnp.where(place == index, result_ref[me_ref[0] ^ k], values)
    values = jnp.concatenate([values, jnp.zeros((8 - lines, slots), jnp.float32)], axis=0)
    at = (iota((slots, rows), 0) == slot_ref[...]).astype(jnp.float32)
    picked = jnp.dot(
        values, at, precision=lax.Precision.HIGHEST, preferred_element_type=jnp.float32
    )
    best_ref[...] = picked[0:1]
    distance_ref[...] = picked[1:2]


def from_partner(value, k, axis):
    return lax.ppermute(value, axis, [(i, i ^ k) for i in range(lax.axis_size(axis))])


def exchange(packed, order):
    got = [from_partner(block, k, "shard") if k else block for k, block in zip(order, packed)]
    half = len(got) // 2
    return jnp.concatenate(got[:half]), jnp.concatenate(got[half:])


def exchange_all(packed, me):
    owners = lax.axis_size("shard")
    tiles, half, _ = packed.shape
    each = tiles // 2
    data = packed[:-1].reshape(2, each, half, LANES).transpose(0, 2, 1, 3).reshape(2 * half, -1)
    digit = jnp.concatenate(jnp.split(packed[-1], 2, axis=1))
    parted = jnp.concatenate([data, digit], axis=1).reshape(owners, 2 * half // owners, -1)
    partner = me ^ jnp.arange(owners, dtype=jnp.int32)
    got = lax.all_to_all(parted[partner], "shard", 0, 0, tiled=True)[partner].reshape(2 * half, -1)
    data = got[:, : each * LANES].reshape(2, half, each, LANES).transpose(0, 2, 1, 3)
    digit = jnp.concatenate(jnp.split(got[:, each * LANES :], 2), axis=1)
    got = jnp.concatenate([data.reshape(2 * each, half, LANES), digit[None]])
    return jnp.split(got, 2, axis=1)


def local(embeddings, cluster_id, item_order, owner_map):
    owners = lax.axis_size("shard")
    local_rows, width = embeddings.shape
    rows_all = local_rows * owners * lax.axis_size("sub")
    clus_dev = owner_map.shape[0] // owners
    capacity = 2 * local_rows // owners
    slots = owners * capacity
    params = pltpu.CompilerParams(vmem_limit_bytes=32 << 20)
    compare_cost = pl.CostEstimate(
        flops=4 * slots * slots * width, bytes_accessed=4 * slots * width, transcendentals=0
    )
    me = lax.axis_index("shard").astype(jnp.int32).reshape(1)
    ints = jnp.concatenate([owner_map, cluster_id, item_order]).reshape(1, -1)

    direct = owners == len(PARTNERS)
    order = PARTNERS if direct else tuple(range(owners))
    parts = owners if direct else 1
    tiles = 2 * (width // LANES) + 1
    block = (tiles, slots // parts // 2, LANES)
    slot, digit = pl.pallas_call(
        functools.partial(slot_kernel, owners, capacity, order, parts, local_rows),
        out_shape=[
            jax.ShapeDtypeStruct((1, local_rows), jnp.int32),
            jax.ShapeDtypeStruct((LANES, 2 * local_rows), jnp.bfloat16),
        ],
        in_specs=[SCALAR, WHOLE],
        out_specs=[WHOLE] * 2,
        compiler_params=params,
        cost_estimate=pl.CostEstimate(flops=1 << 29, bytes_accessed=1 << 16, transcendentals=0),
        name="slots",
    )(me, ints)
    packed = pl.pallas_call(
        pack_kernel,
        out_shape=[jax.ShapeDtypeStruct(block, jnp.bfloat16)] * parts,
        in_specs=[WHOLE] * 3,
        out_specs=[WHOLE] * parts,
        compiler_params=params,
        name="pack",
    )(slot, digit, embeddings)
    first, second = exchange(packed, order) if direct else exchange_all(packed[0], me[0])
    other_first, other_second = (from_partner(rows, 1, "sub") for rows in (first, second))
    query = jnp.concatenate([first, second])
    asked = slots + clus_dev
    near = pl.pallas_call(
        functools.partial(near_kernel, rows_all, owner_map.shape[0], clus_dev, tiles),
        out_shape=[
            jax.ShapeDtypeStruct((width, slots), jnp.bfloat16),
            jax.ShapeDtypeStruct((asked, LANES), jnp.int32),
            jax.ShapeDtypeStruct((2, slots), jnp.int32),
            jax.ShapeDtypeStruct((1, slots), jnp.float32),
            jax.ShapeDtypeStruct((asked, width), jnp.float32),
            jax.ShapeDtypeStruct((asked, LANES), jnp.float32),
        ],
        in_specs=[SCALAR] + [WHOLE] * 3,
        out_specs=[WHOLE] * 6,
        compiler_params=params,
        cost_estimate=compare_cost,
        name="near",
    )(me, ints, query, other_first)
    results, norms = pl.pallas_call(
        functools.partial(far_kernel, rows_all, tiles),
        out_shape=[
            jax.ShapeDtypeStruct((owners, 2, slots), jnp.float32),
            jax.ShapeDtypeStruct((1, clus_dev), jnp.float32),
        ],
        in_specs=[WHOLE] * 8,
        out_specs=[WHOLE] * 2,
        compiler_params=params,
        cost_estimate=compare_cost,
        name="far",
    )(query, other_second, *near)
    results = lax.all_to_all(results, "shard", 0, 0, tiled=True)
    best, distance, cohesion = pl.pallas_call(
        functools.partial(pick_kernel, order, parts),
        out_shape=[jax.ShapeDtypeStruct((1, local_rows), jnp.float32)] * 2
        + [jax.ShapeDtypeStruct((1, clus_dev), jnp.float32)],
        in_specs=[SCALAR] + [WHOLE] * 3,
        out_specs=[WHOLE] * 3,
        compiler_params=params,
        name="pick",
    )(me, slot, results, norms)
    return best.reshape(local_rows), distance.reshape(local_rows), cohesion.reshape(clus_dev)


def solution(mesh):
    in_specs = (
        P(("groups", "shard", "sub"), None),
        P(("groups", "shard", "sub")),
        P(("groups", "shard", "sub")),
        P("groups"),
    )
    out_specs = (
        P(("groups", "shard", "sub")),
        P(("groups", "shard", "sub")),
        P(("groups", "shard")),
    )
    return jax.shard_map(local, mesh=mesh, in_specs=in_specs, out_specs=out_specs, check_vma=False)
```

```python
import functools

import jax
import jax.numpy as jnp
from jax import lax
from jax.experimental import pallas as pl
from jax.experimental.pallas import tpu as pltpu
from jax.sharding import PartitionSpec as P

LANES = 128
DIGITS = 3
PARTNERS = (3, 4, 2, 0, 5, 6, 7, 1)
WHOLE = pl.BlockSpec(memory_space=pltpu.VMEM)
SCALAR = pl.BlockSpec(memory_space=pltpu.SMEM)


def iota(shape, dim):
    return lax.broadcasted_iota(jnp.int32, shape, dim)


def matmul(a, b):
    return jnp.dot(a, b, preferred_element_type=jnp.float32)


def matmul_t(a, b):
    return lax.dot_general(a, b, (((1,), (1,)), ((), ())), preferred_element_type=jnp.float32)


def bf16(x):
    return x.astype(jnp.float32).astype(jnp.bfloat16)


def ranked(hot):
    upto = (iota((LANES, LANES), 0) <= iota((LANES, LANES), 1)).astype(jnp.bfloat16)
    before, parts = jnp.zeros((1, 1), jnp.float32), []
    for start in range(0, hot.shape[1], LANES):
        piece = hot[:, start : start + LANES]
        spread = jnp.broadcast_to(piece, (16, LANES)).astype(jnp.bfloat16)
        parts.append(matmul(spread, upto)[:1] + before)
        before = before + jnp.sum(piece, axis=1, keepdims=True)
    return jnp.concatenate(parts, axis=1)


def slot_kernel(
    owners, capacity, order, parts, rows, me_ref, ints_ref, slot_ref, digit_ref
):
    clusters = ints_ref.shape[1] - 2 * rows
    cluster = ints_ref[:, clusters : clusters + rows]
    named = bf16(iota((clusters, rows), 0) == cluster)
    owner_map = bf16(jnp.broadcast_to(ints_ref[:, :clusters], (16, clusters)))
    owner = matmul(owner_map, named)[:1].astype(jnp.int32)
    hot = (iota((max(owners, 16), rows), 0) == owner).astype(jnp.float32)
    upto = bf16(iota((rows, rows), 0) <= iota((rows, rows), 1))
    rank = jnp.sum(hot * matmul(bf16(hot), upto), axis=0, keepdims=True) - 1.0
    rank = rank.astype(jnp.int32)
    partner = owner ^ me_ref[0]
    place = partner
    for index, k in enumerate(order):
        place = jnp.where(partner == k, index, place)
    if parts == 1:
        slot_ref[...] = place * capacity + rank
    else:
        half = capacity // 2
        later = (rank >= half).astype(jnp.int32)
        slot_ref[...] = place * half + rank + later * (owners * half - half)

    line = iota((8, rows), 0)
    digit = jnp.zeros((8, rows), jnp.int32)
    for first, number in ((0, cluster + 1), (DIGITS, ints_ref[:, clusters + rows :])):
        for at in range(DIGITS):
            digit = jnp.where(line == first + at, (number >> (8 * at)) & 255, digit)
    empty = jnp.zeros((LANES // 2 - 8, rows), jnp.int32)
    none = jnp.zeros((LANES // 2, rows), jnp.int32)
    early = jnp.concatenate([digit, empty, none], axis=0)
    late = jnp.concatenate([none, digit, empty], axis=0)
    digit_ref[...] = bf16(jnp.concatenate([early, late], axis=1))


def pack_kernel(slot_ref, digit_ref, embed_ref, *out_refs):
    rows, width = embed_ref.shape
    tiles, half, _ = out_refs[0].shape
    values = embed_ref[...].astype(jnp.float32)
    mean_sq = jnp.sum(values * values, axis=1, keepdims=True) * (1.0 / width)
    unit = (values * lax.rsqrt(width * (mean_sq + 1e-06))).astype(jnp.bfloat16)
    late = half * len(out_refs)
    move = bf16(iota((2 * late, rows), 0) == slot_ref[...])
    moved = matmul(move, unit).astype(jnp.bfloat16)
    both = jnp.concatenate([move[:late], move[late:]], axis=1)
    digit = matmul_t(both, digit_ref[...]).astype(jnp.bfloat16)
    each = tiles // 2
    for index, out_ref in enumerate(out_refs):
        start = index * half
        for tile in range(each):
            lanes = slice(tile * LANES, (tile + 1) * LANES)
            out_ref[tile] = moved[start : start + half, lanes]
            out_ref[each + tile] = moved[late + start : late + start + half, lanes]
        out_ref[tiles - 1] = digit[start : start + half]


def unpacked(block_ref, tiles):
    blocks = block_ref.shape[0] // tiles
    each = tiles // 2

    def column(tile):
        return jnp.concatenate([block_ref[i * tiles + tile] for i in range(blocks)], axis=0)

    halves = [
        jnp.concatenate([column(first + tile) for tile in range(each)], axis=1)
        for first in (0, each)
    ]
    return jnp.concatenate(halves, axis=0), column(tiles - 1)


def weights(number, at, half):
    value = jnp.zeros(at.shape, jnp.float32)
    for place in range(DIGITS):
        for which in (0, 1):
            lane = half * (LANES // 2) + which * DIGITS + place
            value = jnp.where((at == lane) & (number == which), 256.0**place, value)
    return value.astype(jnp.bfloat16)


def key_rows(rows_all, digit):
    at = iota((16, LANES), 0), iota((16, LANES), 1)
    numbers = [matmul_t(weights(*at, half), digit) for half in (0, 1)]
    numbers = jnp.concatenate(numbers, axis=1)
    low = (numbers[0:1].astype(jnp.int32) - 1) * rows_all
    return low, low + numbers[1:2].astype(jnp.int32)


def key_columns(rows_all, digit):
    at = iota((LANES, 2 * LANES), 1) // LANES, iota((LANES, 2 * LANES), 0)
    numbers = [matmul(digit, weights(*at, half)) for half in (0, 1)]
    numbers = jnp.concatenate(numbers, axis=0)
    low = (numbers[:, :LANES].astype(jnp.int32) - 1) * rows_all
    return low, low + numbers[:, LANES:].astype(jnp.int32)


def across(column, count):
    return jnp.concatenate([column] * (count // LANES), axis=1)


def compare(rows_all, query_t, query_low, query_key, lows, parts):
    rows = jnp.concatenate([rows for rows, _ in parts], axis=0)
    key = jnp.concatenate([key_rows(rows_all, digit)[1] for _, digit in parts], axis=1)
    bound = across(lows, key.shape[1])
    member = bf16((key >= bound) & (key < bound + rows_all))
    sums = matmul(member, rows)
    counts = matmul(member, jnp.ones((rows.shape[0], LANES), jnp.bfloat16))
    scores = matmul(rows, query_t)
    key = jnp.concatenate([key_columns(rows_all, digit)[1] for _, digit in parts], axis=0)
    key = across(key, query_t.shape[1])
    earlier = (key >= query_low) & (key < query_key)
    best = jnp.max(jnp.where(earlier, scores, -3.0), axis=0, keepdims=True)
    return best, sums, counts


def near_kernel(
    rows_all, clusters, clus_dev, tiles, me_ref, ints_ref, query_ref, other_ref,
    query_t_ref, lows_ref, key_ref, best_ref, sums_ref, counts_ref,
):
    hot = (ints_ref[:, :clusters] == me_ref[0]).astype(jnp.float32)
    rank = ranked(hot)
    shape = (clus_dev, clusters)
    kth = (rank == iota(shape, 0).astype(jnp.float32) + 1.0) & (hot > 0.0)
    own = jnp.sum(jnp.where(kth, iota(shape, 1).astype(jnp.float32), 0.0), axis=1, keepdims=True)
    own = jnp.broadcast_to(own.astype(jnp.int32) * rows_all, (clus_dev, LANES))
    query, digit = unpacked(query_ref, tiles)
    low, _ = key_columns(rows_all, digit)
    lows = jnp.concatenate([low, own], axis=0)
    query_low, query_key = key_rows(rows_all, digit)
    query_t = jnp.transpose(query)
    query_t_ref[...] = query_t
    parts = [(query, digit), unpacked(other_ref, tiles)]
    best, sums, counts = compare(rows_all, query_t, query_low, query_key, lows, parts)
    lows_ref[...] = lows
    key_ref[...] = jnp.concatenate([query_low, query_key], axis=0)
    best_ref[...] = best
    sums_ref[...] = sums
    counts_ref[...] = counts


def far_kernel(
    rows_all, tiles, query_ref, other_ref, query_t_ref, lows_ref, key_ref, best_ref, sums_ref, counts_ref,
    result_ref, norm_ref,
):
    query, _ = unpacked(query_ref, tiles)
    queries, width = query.shape
    best, sums, counts = compare(
        rows_all, query_t_ref[...], key_ref[0:1], key_ref[1:2], lows_ref[...], [unpacked(other_ref, tiles)]
    )
    best = jnp.maximum(best, best_ref[...])
    best = jnp.where(best > -2.0, best, 0.0)
    share = 1.0 / jnp.maximum(counts + counts_ref[...], 1.0)
    squares = jnp.zeros(share.shape, jnp.float32)
    for start in range(0, width, LANES):
        lanes = slice(start, start + LANES)
        centroid = (sums[:, lanes] + sums_ref[:, lanes]) * share
        offset = jnp.concatenate(
            [query[:, lanes].astype(jnp.float32) - centroid[:queries], centroid[queries:]], axis=0
        )
        squares = squares + offset * offset
    total = jnp.sum(jnp.transpose(squares), axis=0, keepdims=True)
    result = jnp.concatenate([best, total[:, :queries]], axis=0)
    for owner in range(result_ref.shape[0]):
        result_ref[owner] = result
    norm_ref[...] = total[:, queries:]


def pick_kernel(
    order, parts, me_ref, slot_ref, result_ref, norm_ref, best_ref, distance_ref, cohesion_ref
):
    cohesion_ref[...] = norm_ref[...]
    rows = slot_ref.shape[1]
    owners, lines, slots = result_ref.shape
    folds = min(parts, 2)
    place = iota((lines, slots), 1) % (slots // folds) // (slots // owners // folds)
    values = jnp.zeros((lines, slots), jnp.float32)
    for index, k in enumerate(order):
        values = jnp.where(place == index, result_ref[me_ref[0] ^ k], values)
    values = jnp.concatenate([values, jnp.zeros((8 - lines, slots), jnp.float32)], axis=0)
    at = (iota((slots, rows), 0) == slot_ref[...]).astype(jnp.float32)
    picked = jnp.dot(
        values, at, precision=lax.Precision.HIGHEST, preferred_element_type=jnp.float32
    )
    best_ref[...] = picked[0:1]
    distance_ref[...] = picked[1:2]


def from_partner(value, k, axis):
    return lax.ppermute(value, axis, [(i, i ^ k) for i in range(lax.axis_size(axis))])


def exchange(packed, order):
    got = [from_partner(block, k, "shard") if k else block for k, block in zip(order, packed)]
    half = len(got) // 2
    return jnp.concatenate(got[:half]), jnp.concatenate(got[half:])


def exchange_all(packed, me):
    owners = lax.axis_size("shard")
    tiles, half, _ = packed.shape
    each = tiles // 2
    data = packed[:-1].reshape(2, each, half, LANES).transpose(0, 2, 1, 3).reshape(2 * half, -1)
    digit = jnp.concatenate(jnp.split(packed[-1], 2, axis=1))
    parted = jnp.concatenate([data, digit], axis=1).reshape(owners, 2 * half // owners, -1)
    partner = me ^ jnp.arange(owners, dtype=jnp.int32)
    got = lax.all_to_all(parted[partner], "shard", 0, 0, tiled=True)[partner].reshape(2 * half, -1)
    data = got[:, : each * LANES].reshape(2, half, each, LANES).transpose(0, 2, 1, 3)
    digit = jnp.concatenate(jnp.split(got[:, each * LANES :], 2), axis=1)
    got = jnp.concatenate([data.reshape(2 * each, half, LANES), digit[None]])
    return jnp.split(got, 2, axis=1)


def local(embeddings, cluster_id, item_order, owner_map):
    owners = lax.axis_size("shard")
    local_rows, width = embeddings.shape
    rows_all = local_rows * owners * lax.axis_size("sub")
    clus_dev = owner_map.shape[0] // owners
    capacity = 2 * local_rows // owners
    slots = owners * capacity
    params = pltpu.CompilerParams(vmem_limit_bytes=32 << 20)
    compare_cost = pl.CostEstimate(
        flops=4 * slots * slots * width, bytes_accessed=4 * slots * width, transcendentals=0
    )
    me = lax.axis_index("shard").astype(jnp.int32).reshape(1)
    ints = jnp.concatenate([owner_map, cluster_id, item_order]).reshape(1, -1)

    direct = owners == len(PARTNERS)
    order = PARTNERS if direct else tuple(range(owners))
    parts = owners if direct else 1
    tiles = 2 * (width // LANES) + 1
    block = (tiles, slots // parts // 2, LANES)
    slot, digit = pl.pallas_call(
        functools.partial(slot_kernel, owners, capacity, order, parts, local_rows),
        out_shape=[
            jax.ShapeDtypeStruct((1, local_rows), jnp.int32),
            jax.ShapeDtypeStruct((LANES, 2 * local_rows), jnp.bfloat16),
        ],
        in_specs=[SCALAR, WHOLE],
        out_specs=[WHOLE] * 2,
        compiler_params=params,
        cost_estimate=pl.CostEstimate(flops=1 << 29, bytes_accessed=1 << 16, transcendentals=0),
        name="slots",
    )(me, ints)
    packed = pl.pallas_call(
        pack_kernel,
        out_shape=[jax.ShapeDtypeStruct(block, jnp.bfloat16)] * parts,
        in_specs=[WHOLE] * 3,
        out_specs=[WHOLE] * parts,
        compiler_params=params,
        name="pack",
    )(slot, digit, embeddings)
    first, second = exchange(packed, order) if direct else exchange_all(packed[0], me[0])
    other_first, other_second = (from_partner(rows, 1, "sub") for rows in (first, second))
    query = jnp.concatenate([first, second])
    asked = slots + clus_dev
    near = pl.pallas_call(
        functools.partial(near_kernel, rows_all, owner_map.shape[0], clus_dev, tiles),
        out_shape=[
            jax.ShapeDtypeStruct((width, slots), jnp.bfloat16),
            jax.ShapeDtypeStruct((asked, LANES), jnp.int32),
            jax.ShapeDtypeStruct((2, slots), jnp.int32),
            jax.ShapeDtypeStruct((1, slots), jnp.float32),
            jax.ShapeDtypeStruct((asked, width), jnp.float32),
            jax.ShapeDtypeStruct((asked, LANES), jnp.float32),
        ],
        in_specs=[SCALAR] + [WHOLE] * 3,
        out_specs=[WHOLE] * 6,
        compiler_params=params,
        cost_estimate=compare_cost,
        name="near",
    )(me, ints, query, other_first)
    results, norms = pl.pallas_call(
        functools.partial(far_kernel, rows_all, tiles),
        out_shape=[
            jax.ShapeDtypeStruct((owners, 2, slots), jnp.float32),
            jax.ShapeDtypeStruct((1, clus_dev), jnp.float32),
        ],
        in_specs=[WHOLE] * 8,
        out_specs=[WHOLE] * 2,
        compiler_params=params,
        cost_estimate=compare_cost,
        name="far",
    )(query, other_second, *near)
    results = lax.all_to_all(results, "shard", 0, 0, tiled=True)
    best, distance, cohesion = pl.pallas_call(
        functools.partial(pick_kernel, order, parts),
        out_shape=[jax.ShapeDtypeStruct((1, local_rows), jnp.float32)] * 2
        + [jax.ShapeDtypeStruct((1, clus_dev), jnp.float32)],
        in_specs=[SCALAR] + [WHOLE] * 3,
        out_specs=[WHOLE] * 3,
        compiler_params=params,
        name="pick",
    )(me, slot, results, norms)
    return best.reshape(local_rows), distance.reshape(local_rows), cohesion.reshape(clus_dev)


def solution(mesh):
    in_specs = (
        P(("groups", "shard", "sub"), None),
        P(("groups", "shard", "sub")),
        P(("groups", "shard", "sub")),
        P("groups"),
    )
    out_specs = (
        P(("groups", "shard", "sub")),
        P(("groups", "shard", "sub")),
        P(("groups", "shard")),
    )
    return jax.shard_map(local, mesh=mesh, in_specs=in_specs, out_specs=out_specs, check_vma=False)
```

```python
import functools

import jax
import jax.numpy as jnp
from jax import lax
from jax.experimental import pallas as pl
from jax.experimental.pallas import tpu as pltpu
from jax.sharding import PartitionSpec as P

LANES = 128
DIGITS = 3
PARTNERS = (4, 3, 2, 0, 5, 7, 6, 1)
WHOLE = pl.BlockSpec(memory_space=pltpu.VMEM)
SCALAR = pl.BlockSpec(memory_space=pltpu.SMEM)


def iota(shape, dim):
    return lax.broadcasted_iota(jnp.int32, shape, dim)


def matmul(a, b):
    return jnp.dot(a, b, preferred_element_type=jnp.float32)


def matmul_t(a, b):
    return lax.dot_general(a, b, (((1,), (1,)), ((), ())), preferred_element_type=jnp.float32)


def bf16(x):
    return x.astype(jnp.float32).astype(jnp.bfloat16)


def ranked(hot):
    upto = (iota((LANES, LANES), 0) <= iota((LANES, LANES), 1)).astype(jnp.bfloat16)
    before, parts = jnp.zeros((1, 1), jnp.float32), []
    for start in range(0, hot.shape[1], LANES):
        piece = hot[:, start : start + LANES]
        spread = jnp.broadcast_to(piece, (16, LANES)).astype(jnp.bfloat16)
        parts.append(matmul(spread, upto)[:1] + before)
        before = before + jnp.sum(piece, axis=1, keepdims=True)
    return jnp.concatenate(parts, axis=1)


def slot_kernel(
    owners, capacity, order, parts, rows, me_ref, ints_ref, slot_ref, digit_ref
):
    clusters = ints_ref.shape[1] - 2 * rows
    cluster = ints_ref[:, clusters : clusters + rows]
    named = bf16(iota((clusters, rows), 0) == cluster)
    owner_map = bf16(jnp.broadcast_to(ints_ref[:, :clusters], (16, clusters)))
    owner = matmul(owner_map, named)[:1].astype(jnp.int32)
    hot = (iota((max(owners, 16), rows), 0) == owner).astype(jnp.float32)
    upto = bf16(iota((rows, rows), 0) <= iota((rows, rows), 1))
    rank = jnp.sum(hot * matmul(bf16(hot), upto), axis=0, keepdims=True) - 1.0
    rank = rank.astype(jnp.int32)
    partner = owner ^ me_ref[0]
    place = partner
    for index, k in enumerate(order):
        place = jnp.where(partner == k, index, place)
    if parts == 1:
        slot_ref[...] = place * capacity + rank
    else:
        half = capacity // 2
        later = (rank >= half).astype(jnp.int32)
        slot_ref[...] = place * half + rank + later * (owners * half - half)

    line = iota((8, rows), 0)
    digit = jnp.zeros((8, rows), jnp.int32)
    for first, number in ((0, cluster + 1), (DIGITS, ints_ref[:, clusters + rows :])):
        for at in range(DIGITS):
            digit = jnp.where(line == first + at, (number >> (8 * at)) & 255, digit)
    empty = jnp.zeros((LANES // 2 - 8, rows), jnp.int32)
    none = jnp.zeros((LANES // 2, rows), jnp.int32)
    early = jnp.concatenate([digit, empty, none], axis=0)
    late = jnp.concatenate([none, digit, empty], axis=0)
    digit_ref[...] = bf16(jnp.concatenate([early, late], axis=1))


def pack_kernel(slot_ref, digit_ref, embed_ref, *out_refs):
    rows, width = embed_ref.shape
    tiles, half, _ = out_refs[0].shape
    values = embed_ref[...].astype(jnp.float32)
    mean_sq = jnp.sum(values * values, axis=1, keepdims=True) * (1.0 / width)
    unit = (values * lax.rsqrt(width * (mean_sq + 1e-06))).astype(jnp.bfloat16)
    late = half * len(out_refs)
    move = bf16(iota((2 * late, rows), 0) == slot_ref[...])
    moved = matmul(move, unit).astype(jnp.bfloat16)
    both = jnp.concatenate([move[:late], move[late:]], axis=1)
    digit = matmul_t(both, digit_ref[...]).astype(jnp.bfloat16)
    each = tiles // 2
    for index, out_ref in enumerate(out_refs):
        start = index * half
        for tile in range(each):
            lanes = slice(tile * LANES, (tile + 1) * LANES)
            out_ref[tile] = moved[start : start + half, lanes]
            out_ref[each + tile] = moved[late + start : late + start + half, lanes]
        out_ref[tiles - 1] = digit[start : start + half]


def unpacked(block_ref, tiles):
    blocks = block_ref.shape[0] // tiles
    each = tiles // 2

    def column(tile):
        return jnp.concatenate([block_ref[i * tiles + tile] for i in range(blocks)], axis=0)

    halves = [
        jnp.concatenate([column(first + tile) for tile in range(each)], axis=1)
        for first in (0, each)
    ]
    return jnp.concatenate(halves, axis=0), column(tiles - 1)


def weights(number, at, half):
    value = jnp.zeros(at.shape, jnp.float32)
    for place in range(DIGITS):
        for which in (0, 1):
            lane = half * (LANES // 2) + which * DIGITS + place
            value = jnp.where((at == lane) & (number == which), 256.0**place, value)
    return value.astype(jnp.bfloat16)


def key_rows(rows_all, digit):
    at = iota((16, LANES), 0), iota((16, LANES), 1)
    numbers = [matmul_t(weights(*at, half), digit) for half in (0, 1)]
    numbers = jnp.concatenate(numbers, axis=1)
    low = (numbers[0:1].astype(jnp.int32) - 1) * rows_all
    return low, low + numbers[1:2].astype(jnp.int32)


def key_columns(rows_all, digit):
    at = iota((LANES, 2 * LANES), 1) // LANES, iota((LANES, 2 * LANES), 0)
    numbers = [matmul(digit, weights(*at, half)) for half in (0, 1)]
    numbers = jnp.concatenate(numbers, axis=0)
    low = (numbers[:, :LANES].astype(jnp.int32) - 1) * rows_all
    return low, low + numbers[:, LANES:].astype(jnp.int32)


def across(column, count):
    return jnp.concatenate([column] * (count // LANES), axis=1)


def compare(rows_all, query_t, query_low, query_key, lows, parts):
    rows = jnp.concatenate([rows for rows, _ in parts], axis=0)
    key = jnp.concatenate([key_rows(rows_all, digit)[1] for _, digit in parts], axis=1)
    bound = across(lows, key.shape[1])
    member = bf16((key >= bound) & (key < bound + rows_all))
    sums = matmul(member, rows)
    counts = matmul(member, jnp.ones((rows.shape[0], LANES), jnp.bfloat16))
    scores = matmul(rows, query_t)
    key = jnp.concatenate([key_columns(rows_all, digit)[1] for _, digit in parts], axis=0)
    key = across(key, query_t.shape[1])
    earlier = (key >= query_low) & (key < query_key)
    best = jnp.max(jnp.where(earlier, scores, -3.0), axis=0, keepdims=True)
    return best, sums, counts


def near_kernel(
    rows_all, clusters, clus_dev, tiles, me_ref, ints_ref, query_ref, other_ref,
    query_t_ref, lows_ref, key_ref, best_ref, sums_ref, counts_ref,
):
    hot = (ints_ref[:, :clusters] == me_ref[0]).astype(jnp.float32)
    rank = ranked(hot)
    shape = (clus_dev, clusters)
    kth = (rank == iota(shape, 0).astype(jnp.float32) + 1.0) & (hot > 0.0)
    own = jnp.sum(jnp.where(kth, iota(shape, 1).astype(jnp.float32), 0.0), axis=1, keepdims=True)
    own = jnp.broadcast_to(own.astype(jnp.int32) * rows_all, (clus_dev, LANES))
    query, digit = unpacked(query_ref, tiles)
    low, _ = key_columns(rows_all, digit)
    lows = jnp.concatenate([low, own], axis=0)
    query_low, query_key = key_rows(rows_all, digit)
    query_t = jnp.transpose(query)
    query_t_ref[...] = query_t
    parts = [(query, digit), unpacked(other_ref, tiles)]
    best, sums, counts = compare(rows_all, query_t, query_low, query_key, lows, parts)
    lows_ref[...] = lows
    key_ref[...] = jnp.concatenate([query_low, query_key], axis=0)
    best_ref[...] = best
    sums_ref[...] = sums
    counts_ref[...] = counts


def far_kernel(
    rows_all, tiles, query_ref, other_ref, query_t_ref, lows_ref, key_ref, best_ref, sums_ref, counts_ref,
    result_ref, norm_ref,
):
    query, _ = unpacked(query_ref, tiles)
    queries, width = query.shape
    best, sums, counts = compare(
        rows_all, query_t_ref[...], key_ref[0:1], key_ref[1:2], lows_ref[...], [unpacked(other_ref, tiles)]
    )
    best = jnp.maximum(best, best_ref[...])
    best = jnp.where(best > -2.0, best, 0.0)
    share = 1.0 / jnp.maximum(counts + counts_ref[...], 1.0)
    squares = jnp.zeros((queries, LANES), jnp.float32)
    norms = jnp.zeros((share.shape[0] - queries, LANES), jnp.float32)
    for start in range(0, width, LANES):
        lanes = slice(start, start + LANES)
        centroid = (sums[:, lanes] + sums_ref[:, lanes]) * share
        offset = query[:, lanes].astype(jnp.float32) - centroid[:queries]
        squares = squares + offset * offset
        norms = norms + centroid[queries:] * centroid[queries:]
    distance = jnp.sum(jnp.transpose(squares), axis=0, keepdims=True)
    result = jnp.concatenate([best, distance], axis=0)
    for owner in range(result_ref.shape[0]):
        result_ref[owner] = result
    norms = jnp.concatenate([norms] * (LANES // norms.shape[0]), axis=0)
    norm_ref[...] = jnp.sum(jnp.transpose(norms), axis=0, keepdims=True)[:, : norm_ref.shape[1]]


def pick_kernel(
    order, parts, me_ref, slot_ref, result_ref, norm_ref, best_ref, distance_ref, cohesion_ref
):
    cohesion_ref[...] = norm_ref[...]
    rows = slot_ref.shape[1]
    owners, lines, slots = result_ref.shape
    folds = min(parts, 2)
    place = iota((lines, slots), 1) % (slots // folds) // (slots // owners // folds)
    values = jnp.zeros((lines, slots), jnp.float32)
    for index, k in enumerate(order):
        values = jnp.where(place == index, result_ref[me_ref[0] ^ k], values)
    values = jnp.concatenate([values, jnp.zeros((8 - lines, slots), jnp.float32)], axis=0)
    at = (iota((slots, rows), 0) == slot_ref[...]).astype(jnp.float32)
    picked = jnp.dot(
        values, at, precision=lax.Precision.HIGHEST, preferred_element_type=jnp.float32
    )
    best_ref[...] = picked[0:1]
    distance_ref[...] = picked[1:2]


def from_partner(value, k, axis):
    return lax.ppermute(value, axis, [(i, i ^ k) for i in range(lax.axis_size(axis))])


def exchange(packed, order):
    got = [from_partner(block, k, "shard") if k else block for k, block in zip(order, packed)]
    half = len(got) // 2
    return jnp.concatenate(got[:half]), jnp.concatenate(got[half:])


def exchange_all(packed, me):
    owners = lax.axis_size("shard")
    tiles, half, _ = packed.shape
    each = tiles // 2
    data = packed[:-1].reshape(2, each, half, LANES).transpose(0, 2, 1, 3).reshape(2 * half, -1)
    digit = jnp.concatenate(jnp.split(packed[-1], 2, axis=1))
    parted = jnp.concatenate([data, digit], axis=1).reshape(owners, 2 * half // owners, -1)
    partner = me ^ jnp.arange(owners, dtype=jnp.int32)
    got = lax.all_to_all(parted[partner], "shard", 0, 0, tiled=True)[partner].reshape(2 * half, -1)
    data = got[:, : each * LANES].reshape(2, half, each, LANES).transpose(0, 2, 1, 3)
    digit = jnp.concatenate(jnp.split(got[:, each * LANES :], 2), axis=1)
    got = jnp.concatenate([data.reshape(2 * each, half, LANES), digit[None]])
    return jnp.split(got, 2, axis=1)


def local(embeddings, cluster_id, item_order, owner_map):
    owners = lax.axis_size("shard")
    local_rows, width = embeddings.shape
    rows_all = local_rows * owners * lax.axis_size("sub")
    clus_dev = owner_map.shape[0] // owners
    capacity = 2 * local_rows // owners
    slots = owners * capacity
    params = pltpu.CompilerParams(vmem_limit_bytes=32 << 20)
    compare_cost = pl.CostEstimate(
        flops=4 * slots * slots * width, bytes_accessed=4 * slots * width, transcendentals=0
    )
    me = lax.axis_index("shard").astype(jnp.int32).reshape(1)
    ints = jnp.concatenate([owner_map, cluster_id, item_order]).reshape(1, -1)

    direct = owners == len(PARTNERS)
    order = PARTNERS if direct else tuple(range(owners))
    parts = owners if direct else 1
    tiles = 2 * (width // LANES) + 1
    block = (tiles, slots // parts // 2, LANES)
    slot, digit = pl.pallas_call(
        functools.partial(slot_kernel, owners, capacity, order, parts, local_rows),
        out_shape=[
            jax.ShapeDtypeStruct((1, local_rows), jnp.int32),
            jax.ShapeDtypeStruct((LANES, 2 * local_rows), jnp.bfloat16),
        ],
        in_specs=[SCALAR, WHOLE],
        out_specs=[WHOLE] * 2,
        compiler_params=params,
        cost_estimate=pl.CostEstimate(flops=1 << 29, bytes_accessed=1 << 16, transcendentals=0),
        name="slots",
    )(me, ints)
    packed = pl.pallas_call(
        pack_kernel,
        out_shape=[jax.ShapeDtypeStruct(block, jnp.bfloat16)] * parts,
        in_specs=[WHOLE] * 3,
        out_specs=[WHOLE] * parts,
        compiler_params=params,
        name="pack",
    )(slot, digit, embeddings)
    first, second = exchange(packed, order) if direct else exchange_all(packed[0], me[0])
    other_first, other_second = (from_partner(rows, 1, "sub") for rows in (first, second))
    query = jnp.concatenate([first, second])
    asked = slots + clus_dev
    near = pl.pallas_call(
        functools.partial(near_kernel, rows_all, owner_map.shape[0], clus_dev, tiles),
        out_shape=[
            jax.ShapeDtypeStruct((width, slots), jnp.bfloat16),
            jax.ShapeDtypeStruct((asked, LANES), jnp.int32),
            jax.ShapeDtypeStruct((2, slots), jnp.int32),
            jax.ShapeDtypeStruct((1, slots), jnp.float32),
            jax.ShapeDtypeStruct((asked, width), jnp.float32),
            jax.ShapeDtypeStruct((asked, LANES), jnp.float32),
        ],
        in_specs=[SCALAR] + [WHOLE] * 3,
        out_specs=[WHOLE] * 6,
        compiler_params=params,
        cost_estimate=compare_cost,
        name="near",
    )(me, ints, query, other_first)
    results, norms = pl.pallas_call(
        functools.partial(far_kernel, rows_all, tiles),
        out_shape=[
            jax.ShapeDtypeStruct((owners, 2, slots), jnp.float32),
            jax.ShapeDtypeStruct((1, clus_dev), jnp.float32),
        ],
        in_specs=[WHOLE] * 8,
        out_specs=[WHOLE] * 2,
        compiler_params=params,
        cost_estimate=compare_cost,
        name="far",
    )(query, other_second, *near)
    results = lax.all_to_all(results, "shard", 0, 0, tiled=True)
    best, distance, cohesion = pl.pallas_call(
        functools.partial(pick_kernel, order, parts),
        out_shape=[jax.ShapeDtypeStruct((1, local_rows), jnp.float32)] * 2
        + [jax.ShapeDtypeStruct((1, clus_dev), jnp.float32)],
        in_specs=[SCALAR] + [WHOLE] * 3,
        out_specs=[WHOLE] * 3,
        compiler_params=params,
        name="pick",
    )(me, slot, results, norms)
    return best.reshape(local_rows), distance.reshape(local_rows), cohesion.reshape(clus_dev)


def solution(mesh):
    in_specs = (
        P(("groups", "shard", "sub"), None),
        P(("groups", "shard", "sub")),
        P(("groups", "shard", "sub")),
        P("groups"),
    )
    out_specs = (
        P(("groups", "shard", "sub")),
        P(("groups", "shard", "sub")),
        P(("groups", "shard")),
    )
    return jax.shard_map(local, mesh=mesh, in_specs=in_specs, out_specs=out_specs, check_vma=False)
```

```python
import functools

import jax
import jax.numpy as jnp
from jax import lax
from jax.experimental import pallas as pl
from jax.experimental.pallas import tpu as pltpu
from jax.sharding import PartitionSpec as P

LANES = 128
DIGITS = 3
SENDS = ((4,), (2, 3), (5,), (7,), (6,), (1,), (0,))
PARTNERS = (4, 2, 0, 5, 7, 6, 1, 3)
WHOLE = pl.BlockSpec(memory_space=pltpu.VMEM)
SCALAR = pl.BlockSpec(memory_space=pltpu.SMEM)


def iota(shape, dim):
    return lax.broadcasted_iota(jnp.int32, shape, dim)


def matmul(a, b):
    return jnp.dot(a, b, preferred_element_type=jnp.float32)


def matmul_t(a, b):
    return lax.dot_general(a, b, (((1,), (1,)), ((), ())), preferred_element_type=jnp.float32)


def bf16(x):
    return x.astype(jnp.float32).astype(jnp.bfloat16)


def ranked(hot):
    upto = (iota((LANES, LANES), 0) <= iota((LANES, LANES), 1)).astype(jnp.bfloat16)
    before, parts = jnp.zeros((1, 1), jnp.float32), []
    for start in range(0, hot.shape[1], LANES):
        piece = hot[:, start : start + LANES]
        spread = jnp.broadcast_to(piece, (16, LANES)).astype(jnp.bfloat16)
        parts.append(matmul(spread, upto)[:1] + before)
        before = before + jnp.sum(piece, axis=1, keepdims=True)
    return jnp.concatenate(parts, axis=1)


def slot_kernel(
    owners, capacity, order, parts, rows, me_ref, ints_ref, slot_ref, digit_ref
):
    clusters = ints_ref.shape[1] - 2 * rows
    cluster = ints_ref[:, clusters : clusters + rows]
    named = bf16(iota((clusters, rows), 0) == cluster)
    owner_map = bf16(jnp.broadcast_to(ints_ref[:, :clusters], (16, clusters)))
    owner = matmul(owner_map, named)[:1].astype(jnp.int32)
    hot = (iota((max(owners, 16), rows), 0) == owner).astype(jnp.float32)
    upto = bf16(iota((rows, rows), 0) <= iota((rows, rows), 1))
    rank = jnp.sum(hot * matmul(bf16(hot), upto), axis=0, keepdims=True) - 1.0
    rank = rank.astype(jnp.int32)
    partner = owner ^ me_ref[0]
    place = partner
    for index, k in enumerate(order):
        place = jnp.where(partner == k, index, place)
    if parts == 1:
        slot_ref[...] = place * capacity + rank
    else:
        half = capacity // 2
        later = (rank >= half).astype(jnp.int32)
        slot_ref[...] = place * half + rank + later * (owners * half - half)

    line = iota((8, rows), 0)
    digit = jnp.zeros((8, rows), jnp.int32)
    for first, number in ((0, cluster + 1), (DIGITS, ints_ref[:, clusters + rows :])):
        for at in range(DIGITS):
            digit = jnp.where(line == first + at, (number >> (8 * at)) & 255, digit)
    empty = jnp.zeros((LANES // 2 - 8, rows), jnp.int32)
    none = jnp.zeros((LANES // 2, rows), jnp.int32)
    early = jnp.concatenate([digit, empty, none], axis=0)
    late = jnp.concatenate([none, digit, empty], axis=0)
    digit_ref[...] = bf16(jnp.concatenate([early, late], axis=1))


def pack_kernel(sends, slot_ref, digit_ref, embed_ref, *out_refs):
    rows, width = embed_ref.shape
    half = out_refs[0].shape[1]
    tiles = 2 * (width // LANES) + 1
    values = embed_ref[...].astype(jnp.float32)
    mean_sq = jnp.sum(values * values, axis=1, keepdims=True) * (1.0 / width)
    unit = (values * lax.rsqrt(width * (mean_sq + 1e-06))).astype(jnp.bfloat16)
    late = half * sum(len(places) for places in sends)
    move = bf16(iota((2 * late, rows), 0) == slot_ref[...])
    moved = matmul(move, unit).astype(jnp.bfloat16)
    both = jnp.concatenate([move[:late], move[late:]], axis=1)
    digit = matmul_t(both, digit_ref[...]).astype(jnp.bfloat16)
    each = tiles // 2
    for places, out_ref in zip(sends, out_refs):
        for index, place in enumerate(places):
            base, start = index * tiles, place * half
            for tile in range(each):
                lanes = slice(tile * LANES, (tile + 1) * LANES)
                out_ref[base + tile] = moved[start : start + half, lanes]
                out_ref[base + each + tile] = moved[late + start : late + start + half, lanes]
            out_ref[base + tiles - 1] = digit[start : start + half]


def unpacked(block_ref, tiles):
    blocks = block_ref.shape[0] // tiles
    each = tiles // 2

    def column(tile):
        return jnp.concatenate([block_ref[i * tiles + tile] for i in range(blocks)], axis=0)

    halves = [
        jnp.concatenate([column(first + tile) for tile in range(each)], axis=1)
        for first in (0, each)
    ]
    return jnp.concatenate(halves, axis=0), column(tiles - 1)


def weights(number, at, half):
    value = jnp.zeros(at.shape, jnp.float32)
    for place in range(DIGITS):
        for which in (0, 1):
            lane = half * (LANES // 2) + which * DIGITS + place
            value = jnp.where((at == lane) & (number == which), 256.0**place, value)
    return value.astype(jnp.bfloat16)


def key_rows(rows_all, digit):
    at = iota((16, LANES), 0), iota((16, LANES), 1)
    numbers = [matmul_t(weights(*at, half), digit) for half in (0, 1)]
    numbers = jnp.concatenate(numbers, axis=1)
    low = (numbers[0:1].astype(jnp.int32) - 1) * rows_all
    return low, low + numbers[1:2].astype(jnp.int32)


def key_columns(rows_all, digit):
    at = iota((LANES, 2 * LANES), 1) // LANES, iota((LANES, 2 * LANES), 0)
    numbers = [matmul(digit, weights(*at, half)) for half in (0, 1)]
    numbers = jnp.concatenate(numbers, axis=0)
    low = (numbers[:, :LANES].astype(jnp.int32) - 1) * rows_all
    return low, low + numbers[:, LANES:].astype(jnp.int32)


def across(column, count):
    return jnp.concatenate([column] * (count // LANES), axis=1)


def compare(rows_all, query_t, query_low, query_key, lows, parts):
    rows = jnp.concatenate([rows for rows, _ in parts], axis=0)
    key = jnp.concatenate([key_rows(rows_all, digit)[1] for _, digit in parts], axis=1)
    bound = across(lows, key.shape[1])
    member = bf16((key >= bound) & (key < bound + rows_all))
    sums = matmul(member, rows)
    counts = matmul(member, jnp.ones((rows.shape[0], LANES), jnp.bfloat16))
    scores = matmul(rows, query_t)
    key = jnp.concatenate([key_columns(rows_all, digit)[1] for _, digit in parts], axis=0)
    key = across(key, query_t.shape[1])
    earlier = (key >= query_low) & (key < query_key)
    best = jnp.max(jnp.where(earlier, scores, -3.0), axis=0, keepdims=True)
    return best, sums, counts


def near_kernel(
    rows_all, clusters, clus_dev, tiles, me_ref, ints_ref, query_ref, other_ref,
    query_t_ref, lows_ref, key_ref, best_ref, sums_ref, counts_ref,
):
    hot = (ints_ref[:, :clusters] == me_ref[0]).astype(jnp.float32)
    rank = ranked(hot)
    shape = (clus_dev, clusters)
    kth = (rank == iota(shape, 0).astype(jnp.float32) + 1.0) & (hot > 0.0)
    own = jnp.sum(jnp.where(kth, iota(shape, 1).astype(jnp.float32), 0.0), axis=1, keepdims=True)
    own = jnp.broadcast_to(own.astype(jnp.int32) * rows_all, (clus_dev, LANES))
    query, digit = unpacked(query_ref, tiles)
    low, _ = key_columns(rows_all, digit)
    lows = jnp.concatenate([low, own], axis=0)
    query_low, query_key = key_rows(rows_all, digit)
    query_t = jnp.transpose(query)
    query_t_ref[...] = query_t
    parts = [(query, digit), unpacked(other_ref, tiles)]
    best, sums, counts = compare(rows_all, query_t, query_low, query_key, lows, parts)
    lows_ref[...] = lows
    key_ref[...] = jnp.concatenate([query_low, query_key], axis=0)
    best_ref[...] = best
    sums_ref[...] = sums
    counts_ref[...] = counts


def far_kernel(
    rows_all, tiles, query_ref, other_ref, query_t_ref, lows_ref, key_ref, best_ref, sums_ref, counts_ref,
    result_ref, norm_ref,
):
    query, _ = unpacked(query_ref, tiles)
    queries, width = query.shape
    best, sums, counts = compare(
        rows_all, query_t_ref[...], key_ref[0:1], key_ref[1:2], lows_ref[...], [unpacked(other_ref, tiles)]
    )
    best = jnp.maximum(best, best_ref[...])
    best = jnp.where(best > -2.0, best, 0.0)
    share = 1.0 / jnp.maximum(counts + counts_ref[...], 1.0)
    squares = jnp.zeros((queries, LANES), jnp.float32)
    norms = jnp.zeros((share.shape[0] - queries, LANES), jnp.float32)
    for start in range(0, width, LANES):
        lanes = slice(start, start + LANES)
        centroid = (sums[:, lanes] + sums_ref[:, lanes]) * share
        offset = query[:, lanes].astype(jnp.float32) - centroid[:queries]
        squares = squares + offset * offset
        norms = norms + centroid[queries:] * centroid[queries:]
    distance = jnp.sum(jnp.transpose(squares), axis=0, keepdims=True)
    result = jnp.concatenate([best, distance], axis=0)
    for owner in range(result_ref.shape[0]):
        result_ref[owner] = result
    norms = jnp.concatenate([norms] * (LANES // norms.shape[0]), axis=0)
    norm_ref[...] = jnp.sum(jnp.transpose(norms), axis=0, keepdims=True)[:, : norm_ref.shape[1]]


def pick_kernel(
    order, parts, me_ref, slot_ref, result_ref, norm_ref, best_ref, distance_ref, cohesion_ref
):
    cohesion_ref[...] = norm_ref[...]
    rows = slot_ref.shape[1]
    owners, lines, slots = result_ref.shape
    folds = min(parts, 2)
    place = iota((lines, slots), 1) % (slots // folds) // (slots // owners // folds)
    values = jnp.zeros((lines, slots), jnp.float32)
    for index, k in enumerate(order):
        values = jnp.where(place == index, result_ref[me_ref[0] ^ k], values)
    values = jnp.concatenate([values, jnp.zeros((8 - lines, slots), jnp.float32)], axis=0)
    at = (iota((slots, rows), 0) == slot_ref[...]).astype(jnp.float32)
    picked = jnp.dot(
        values, at, precision=lax.Precision.HIGHEST, preferred_element_type=jnp.float32
    )
    best_ref[...] = picked[0:1]
    distance_ref[...] = picked[1:2]


def from_partner(value, k, axis):
    return lax.ppermute(value, axis, [(i, i ^ k) for i in range(lax.axis_size(axis))])


def exchange(packed, tiles):
    sent = dict(zip(SENDS, packed))
    got = {0: sent[0,]}
    for k in (4, 5, 7, 6):
        got[k] = from_partner(sent[k,], k, "shard")
    pair = from_partner(sent[2, 3], 2, "shard")
    got[2] = pair[:tiles]
    pair = from_partner(jnp.concatenate([sent[1,], pair[tiles:]]), 1, "shard")
    got[1], got[3] = pair[:tiles], pair[tiles:]
    got = [got[k] for k in PARTNERS]
    half = len(got) // 2
    return jnp.concatenate(got[:half]), jnp.concatenate(got[half:])


def exchange_all(packed, me):
    owners = lax.axis_size("shard")
    tiles, half, _ = packed.shape
    each = tiles // 2
    data = packed[:-1].reshape(2, each, half, LANES).transpose(0, 2, 1, 3).reshape(2 * half, -1)
    digit = jnp.concatenate(jnp.split(packed[-1], 2, axis=1))
    parted = jnp.concatenate([data, digit], axis=1).reshape(owners, 2 * half // owners, -1)
    partner = me ^ jnp.arange(owners, dtype=jnp.int32)
    got = lax.all_to_all(parted[partner], "shard", 0, 0, tiled=True)[partner].reshape(2 * half, -1)
    data = got[:, : each * LANES].reshape(2, half, each, LANES).transpose(0, 2, 1, 3)
    digit = jnp.concatenate(jnp.split(got[:, each * LANES :], 2), axis=1)
    got = jnp.concatenate([data.reshape(2 * each, half, LANES), digit[None]])
    return jnp.split(got, 2, axis=1)


def local(embeddings, cluster_id, item_order, owner_map):
    owners = lax.axis_size("shard")
    local_rows, width = embeddings.shape
    rows_all = local_rows * owners * lax.axis_size("sub")
    clus_dev = owner_map.shape[0] // owners
    capacity = 2 * local_rows // owners
    slots = owners * capacity
    params = pltpu.CompilerParams(vmem_limit_bytes=32 << 20)
    compare_cost = pl.CostEstimate(
        flops=4 * slots * slots * width, bytes_accessed=4 * slots * width, transcendentals=0
    )
    me = lax.axis_index("shard").astype(jnp.int32).reshape(1)
    ints = jnp.concatenate([owner_map, cluster_id, item_order]).reshape(1, -1)

    direct = owners == len(PARTNERS)
    order = PARTNERS if direct else tuple(range(owners))
    parts = owners if direct else 1
    tiles = 2 * (width // LANES) + 1
    sends = [[PARTNERS.index(k) for k in ks] for ks in SENDS] if direct else [[0]]
    half = slots // parts // 2
    slot, digit = pl.pallas_call(
        functools.partial(slot_kernel, owners, capacity, order, parts, local_rows),
        out_shape=[
            jax.ShapeDtypeStruct((1, local_rows), jnp.int32),
            jax.ShapeDtypeStruct((LANES, 2 * local_rows), jnp.bfloat16),
        ],
        in_specs=[SCALAR, WHOLE],
        out_specs=[WHOLE] * 2,
        compiler_params=params,
        cost_estimate=pl.CostEstimate(flops=1 << 29, bytes_accessed=1 << 16, transcendentals=0),
        name="slots",
    )(me, ints)
    packed = pl.pallas_call(
        functools.partial(pack_kernel, sends),
        out_shape=[
            jax.ShapeDtypeStruct((len(places) * tiles, half, LANES), jnp.bfloat16) for places in sends
        ],
        in_specs=[WHOLE] * 3,
        out_specs=[WHOLE] * len(sends),
        compiler_params=params,
        name="pack",
    )(slot, digit, embeddings)
    first, second = exchange(packed, tiles) if direct else exchange_all(packed[0], me[0])
    other_first, other_second = (from_partner(rows, 1, "sub") for rows in (first, second))
    query = jnp.concatenate([first, second])
    asked = slots + clus_dev
    near = pl.pallas_call(
        functools.partial(near_kernel, rows_all, owner_map.shape[0], clus_dev, tiles),
        out_shape=[
            jax.ShapeDtypeStruct((width, slots), jnp.bfloat16),
            jax.ShapeDtypeStruct((asked, LANES), jnp.int32),
            jax.ShapeDtypeStruct((2, slots), jnp.int32),
            jax.ShapeDtypeStruct((1, slots), jnp.float32),
            jax.ShapeDtypeStruct((asked, width), jnp.float32),
            jax.ShapeDtypeStruct((asked, LANES), jnp.float32),
        ],
        in_specs=[SCALAR] + [WHOLE] * 3,
        out_specs=[WHOLE] * 6,
        compiler_params=params,
        cost_estimate=compare_cost,
        name="near",
    )(me, ints, query, other_first)
    results, norms = pl.pallas_call(
        functools.partial(far_kernel, rows_all, tiles),
        out_shape=[
            jax.ShapeDtypeStruct((owners, 2, slots), jnp.float32),
            jax.ShapeDtypeStruct((1, clus_dev), jnp.float32),
        ],
        in_specs=[WHOLE] * 8,
        out_specs=[WHOLE] * 2,
        compiler_params=params,
        cost_estimate=compare_cost,
        name="far",
    )(query, other_second, *near)
    results = lax.all_to_all(results, "shard", 0, 0, tiled=True)
    best, distance, cohesion = pl.pallas_call(
        functools.partial(pick_kernel, order, parts),
        out_shape=[jax.ShapeDtypeStruct((1, local_rows), jnp.float32)] * 2
        + [jax.ShapeDtypeStruct((1, clus_dev), jnp.float32)],
        in_specs=[SCALAR] + [WHOLE] * 3,
        out_specs=[WHOLE] * 3,
        compiler_params=params,
        name="pick",
    )(me, slot, results, norms)
    return best.reshape(local_rows), distance.reshape(local_rows), cohesion.reshape(clus_dev)


def solution(mesh):
    in_specs = (
        P(("groups", "shard", "sub"), None),
        P(("groups", "shard", "sub")),
        P(("groups", "shard", "sub")),
        P("groups"),
    )
    out_specs = (
        P(("groups", "shard", "sub")),
        P(("groups", "shard", "sub")),
        P(("groups", "shard")),
    )
    return jax.shard_map(local, mesh=mesh, in_specs=in_specs, out_specs=out_specs, check_vma=False)
```

```python
import functools

import jax
import jax.numpy as jnp
from jax import lax
from jax.experimental import pallas as pl
from jax.experimental.pallas import tpu as pltpu
from jax.sharding import PartitionSpec as P

LANES = 128
DIGITS = 3
SENDS = ((4,), (2, 3), (5,), (7,), (6,), (1,), (0,))
PARTNERS = (4, 2, 0, 6, 5, 7, 1, 3)
WHOLE = pl.BlockSpec(memory_space=pltpu.VMEM)
SCALAR = pl.BlockSpec(memory_space=pltpu.SMEM)


def iota(shape, dim):
    return lax.broadcasted_iota(jnp.int32, shape, dim)


def matmul(a, b):
    return jnp.dot(a, b, preferred_element_type=jnp.float32)


def matmul_t(a, b):
    return lax.dot_general(a, b, (((1,), (1,)), ((), ())), preferred_element_type=jnp.float32)


def bf16(x):
    return x.astype(jnp.float32).astype(jnp.bfloat16)


def ranked(hot):
    upto = (iota((LANES, LANES), 0) <= iota((LANES, LANES), 1)).astype(jnp.bfloat16)
    before, parts = jnp.zeros((1, 1), jnp.float32), []
    for start in range(0, hot.shape[1], LANES):
        piece = hot[:, start : start + LANES]
        spread = jnp.broadcast_to(piece, (16, LANES)).astype(jnp.bfloat16)
        parts.append(matmul(spread, upto)[:1] + before)
        before = before + jnp.sum(piece, axis=1, keepdims=True)
    return jnp.concatenate(parts, axis=1)


def slot_kernel(
    owners, capacity, order, parts, rows, me_ref, ints_ref, slot_ref, digit_ref
):
    clusters = ints_ref.shape[1] - 2 * rows
    cluster = ints_ref[:, clusters : clusters + rows]
    named = bf16(iota((clusters, rows), 0) == cluster)
    owner_map = bf16(jnp.broadcast_to(ints_ref[:, :clusters], (16, clusters)))
    owner = matmul(owner_map, named)[:1].astype(jnp.int32)
    hot = (iota((max(owners, 16), rows), 0) == owner).astype(jnp.float32)
    upto = bf16(iota((rows, rows), 0) <= iota((rows, rows), 1))
    rank = jnp.sum(hot * matmul(bf16(hot), upto), axis=0, keepdims=True) - 1.0
    rank = rank.astype(jnp.int32)
    partner = owner ^ me_ref[0]
    place = partner
    for index, k in enumerate(order):
        place = jnp.where(partner == k, index, place)
    if parts == 1:
        slot_ref[...] = place * capacity + rank
    else:
        half = capacity // 2
        later = (rank >= half).astype(jnp.int32)
        slot_ref[...] = place * half + rank + later * (owners * half - half)

    line = iota((8, rows), 0)
    digit = jnp.zeros((8, rows), jnp.int32)
    for first, number in ((0, cluster + 1), (DIGITS, ints_ref[:, clusters + rows :])):
        for at in range(DIGITS):
            digit = jnp.where(line == first + at, (number >> (8 * at)) & 255, digit)
    empty = jnp.zeros((LANES // 2 - 8, rows), jnp.int32)
    none = jnp.zeros((LANES // 2, rows), jnp.int32)
    early = jnp.concatenate([digit, empty, none], axis=0)
    late = jnp.concatenate([none, digit, empty], axis=0)
    digit_ref[...] = bf16(jnp.concatenate([early, late], axis=1))


def pack_kernel(sends, slot_ref, digit_ref, embed_ref, *out_refs):
    rows, width = embed_ref.shape
    half = out_refs[0].shape[1]
    tiles = 2 * (width // LANES) + 1
    values = embed_ref[...].astype(jnp.float32)
    mean_sq = jnp.sum(values * values, axis=1, keepdims=True) * (1.0 / width)
    unit = (values * lax.rsqrt(width * (mean_sq + 1e-06))).astype(jnp.bfloat16)
    late = half * sum(len(places) for places in sends)
    move = bf16(iota((2 * late, rows), 0) == slot_ref[...])
    moved = matmul(move, unit).astype(jnp.bfloat16)
    both = jnp.concatenate([move[:late], move[late:]], axis=1)
    digit = matmul_t(both, digit_ref[...]).astype(jnp.bfloat16)
    each = tiles // 2
    for places, out_ref in zip(sends, out_refs):
        for index, place in enumerate(places):
            base, start = index * tiles, place * half
            for tile in range(each):
                lanes = slice(tile * LANES, (tile + 1) * LANES)
                out_ref[base + tile] = moved[start : start + half, lanes]
                out_ref[base + each + tile] = moved[late + start : late + start + half, lanes]
            out_ref[base + tiles - 1] = digit[start : start + half]


def unpacked(block_ref, tiles):
    blocks = block_ref.shape[0] // tiles
    each = tiles // 2

    def column(tile):
        return jnp.concatenate([block_ref[i * tiles + tile] for i in range(blocks)], axis=0)

    halves = [
        jnp.concatenate([column(first + tile) for tile in range(each)], axis=1)
        for first in (0, each)
    ]
    return jnp.concatenate(halves, axis=0), column(tiles - 1)


def weights(number, at, half):
    value = jnp.zeros(at.shape, jnp.float32)
    for place in range(DIGITS):
        for which in (0, 1):
            lane = half * (LANES // 2) + which * DIGITS + place
            value = jnp.where((at == lane) & (number == which), 256.0**place, value)
    return value.astype(jnp.bfloat16)


def key_rows(rows_all, digit):
    at = iota((16, LANES), 0), iota((16, LANES), 1)
    numbers = [matmul_t(weights(*at, half), digit) for half in (0, 1)]
    numbers = jnp.concatenate(numbers, axis=1)
    low = (numbers[0:1].astype(jnp.int32) - 1) * rows_all
    return low, low + numbers[1:2].astype(jnp.int32)


def key_columns(rows_all, digit):
    at = iota((LANES, 2 * LANES), 1) // LANES, iota((LANES, 2 * LANES), 0)
    numbers = [matmul(digit, weights(*at, half)) for half in (0, 1)]
    numbers = jnp.concatenate(numbers, axis=0)
    low = (numbers[:, :LANES].astype(jnp.int32) - 1) * rows_all
    return low, low + numbers[:, LANES:].astype(jnp.int32)


def across(column, count):
    return jnp.concatenate([column] * (count // LANES), axis=1)


def compare(rows_all, query_t, query_low, query_key, lows, parts):
    rows = jnp.concatenate([rows for rows, _ in parts], axis=0)
    key = jnp.concatenate([key_rows(rows_all, digit)[1] for _, digit in parts], axis=1)
    bound = across(lows, key.shape[1])
    member = bf16((key >= bound) & (key < bound + rows_all))
    sums = matmul(member, rows)
    counts = matmul(member, jnp.ones((rows.shape[0], LANES), jnp.bfloat16))
    scores = matmul(rows, query_t)
    key = jnp.concatenate([key_columns(rows_all, digit)[1] for _, digit in parts], axis=0)
    key = across(key, query_t.shape[1])
    earlier = (key >= query_low) & (key < query_key)
    best = jnp.max(jnp.where(earlier, scores, -3.0), axis=0, keepdims=True)
    return best, sums, counts


def near_kernel(
    rows_all, clusters, clus_dev, tiles, me_ref, ints_ref, query_ref, other_ref,
    query_t_ref, lows_ref, key_ref, best_ref, sums_ref, counts_ref,
):
    hot = (ints_ref[:, :clusters] == me_ref[0]).astype(jnp.float32)
    rank = ranked(hot)
    shape = (clus_dev, clusters)
    kth = (rank == iota(shape, 0).astype(jnp.float32) + 1.0) & (hot > 0.0)
    own = jnp.sum(jnp.where(kth, iota(shape, 1).astype(jnp.float32), 0.0), axis=1, keepdims=True)
    own = jnp.broadcast_to(own.astype(jnp.int32) * rows_all, (clus_dev, LANES))
    query, digit = unpacked(query_ref, tiles)
    low, _ = key_columns(rows_all, digit)
    lows = jnp.concatenate([low, own], axis=0)
    query_low, query_key = key_rows(rows_all, digit)
    query_t = jnp.transpose(query)
    query_t_ref[...] = query_t
    parts = [(query, digit), unpacked(other_ref, tiles)]
    best, sums, counts = compare(rows_all, query_t, query_low, query_key, lows, parts)
    lows_ref[...] = lows
    key_ref[...] = jnp.concatenate([query_low, query_key], axis=0)
    best_ref[...] = best
    sums_ref[...] = sums
    counts_ref[...] = counts


def far_kernel(
    rows_all, tiles, query_ref, other_ref, query_t_ref, lows_ref, key_ref, best_ref, sums_ref, counts_ref,
    result_ref, norm_ref,
):
    query, _ = unpacked(query_ref, tiles)
    queries, width = query.shape
    best, sums, counts = compare(
        rows_all, query_t_ref[...], key_ref[0:1], key_ref[1:2], lows_ref[...], [unpacked(other_ref, tiles)]
    )
    best = jnp.maximum(best, best_ref[...])
    best = jnp.where(best > -2.0, best, 0.0)
    share = 1.0 / jnp.maximum(counts + counts_ref[...], 1.0)
    squares = jnp.zeros((queries, LANES), jnp.float32)
    norms = jnp.zeros((share.shape[0] - queries, LANES), jnp.float32)
    for start in range(0, width, LANES):
        lanes = slice(start, start + LANES)
        centroid = (sums[:, lanes] + sums_ref[:, lanes]) * share
        offset = query[:, lanes].astype(jnp.float32) - centroid[:queries]
        squares = squares + offset * offset
        norms = norms + centroid[queries:] * centroid[queries:]
    distance = jnp.sum(jnp.transpose(squares), axis=0, keepdims=True)
    result = jnp.concatenate([best, distance], axis=0)
    for owner in range(result_ref.shape[0]):
        result_ref[owner] = result
    norms = jnp.concatenate([norms] * (LANES // norms.shape[0]), axis=0)
    norm_ref[...] = jnp.sum(jnp.transpose(norms), axis=0, keepdims=True)[:, : norm_ref.shape[1]]


def pick_kernel(
    order, parts, me_ref, slot_ref, result_ref, norm_ref, best_ref, distance_ref, cohesion_ref
):
    cohesion_ref[...] = norm_ref[...]
    rows = slot_ref.shape[1]
    owners, lines, slots = result_ref.shape
    folds = min(parts, 2)
    place = iota((lines, slots), 1) % (slots // folds) // (slots // owners // folds)
    values = jnp.zeros((lines, slots), jnp.float32)
    for index, k in enumerate(order):
        values = jnp.where(place == index, result_ref[me_ref[0] ^ k], values)
    values = jnp.concatenate([values, jnp.zeros((8 - lines, slots), jnp.float32)], axis=0)
    at = (iota((slots, rows), 0) == slot_ref[...]).astype(jnp.float32)
    picked = jnp.dot(
        values, at, precision=lax.Precision.HIGHEST, preferred_element_type=jnp.float32
    )
    best_ref[...] = picked[0:1]
    distance_ref[...] = picked[1:2]


def from_partner(value, k, axis):
    return lax.ppermute(value, axis, [(i, i ^ k) for i in range(lax.axis_size(axis))])


def exchange(packed, tiles):
    sent = dict(zip(SENDS, packed))
    got = {0: sent[0,]}
    for k in (4, 5, 7, 6):
        got[k] = from_partner(sent[k,], k, "shard")
    pair = from_partner(sent[2, 3], 2, "shard")
    got[2] = pair[:tiles]
    pair = from_partner(jnp.concatenate([sent[1,], pair[tiles:]]), 1, "shard")
    got[1], got[3] = pair[:tiles], pair[tiles:]
    got = [got[k] for k in PARTNERS]
    half = len(got) // 2
    return jnp.concatenate(got[:half]), jnp.concatenate(got[half:])


def exchange_all(packed, me):
    owners = lax.axis_size("shard")
    tiles, half, _ = packed.shape
    each = tiles // 2
    data = packed[:-1].reshape(2, each, half, LANES).transpose(0, 2, 1, 3).reshape(2 * half, -1)
    digit = jnp.concatenate(jnp.split(packed[-1], 2, axis=1))
    parted = jnp.concatenate([data, digit], axis=1).reshape(owners, 2 * half // owners, -1)
    partner = me ^ jnp.arange(owners, dtype=jnp.int32)
    got = lax.all_to_all(parted[partner], "shard", 0, 0, tiled=True)[partner].reshape(2 * half, -1)
    data = got[:, : each * LANES].reshape(2, half, each, LANES).transpose(0, 2, 1, 3)
    digit = jnp.concatenate(jnp.split(got[:, each * LANES :], 2), axis=1)
    got = jnp.concatenate([data.reshape(2 * each, half, LANES), digit[None]])
    return jnp.split(got, 2, axis=1)


def local(embeddings, cluster_id, item_order, owner_map):
    owners = lax.axis_size("shard")
    local_rows, width = embeddings.shape
    rows_all = local_rows * owners * lax.axis_size("sub")
    clus_dev = owner_map.shape[0] // owners
    capacity = 2 * local_rows // owners
    slots = owners * capacity
    params = pltpu.CompilerParams(vmem_limit_bytes=32 << 20)
    compare_cost = pl.CostEstimate(
        flops=4 * slots * slots * width, bytes_accessed=4 * slots * width, transcendentals=0
    )
    me = lax.axis_index("shard").astype(jnp.int32).reshape(1)
    ints = jnp.concatenate([owner_map, cluster_id, item_order]).reshape(1, -1)

    direct = owners == len(PARTNERS)
    order = PARTNERS if direct else tuple(range(owners))
    parts = owners if direct else 1
    tiles = 2 * (width // LANES) + 1
    sends = [[PARTNERS.index(k) for k in ks] for ks in SENDS] if direct else [[0]]
    half = slots // parts // 2
    slot, digit = pl.pallas_call(
        functools.partial(slot_kernel, owners, capacity, order, parts, local_rows),
        out_shape=[
            jax.ShapeDtypeStruct((1, local_rows), jnp.int32),
            jax.ShapeDtypeStruct((LANES, 2 * local_rows), jnp.bfloat16),
        ],
        in_specs=[SCALAR, WHOLE],
        out_specs=[WHOLE] * 2,
        compiler_params=params,
        cost_estimate=pl.CostEstimate(flops=1 << 29, bytes_accessed=1 << 16, transcendentals=0),
        name="slots",
    )(me, ints)
    packed = pl.pallas_call(
        functools.partial(pack_kernel, sends),
        out_shape=[
            jax.ShapeDtypeStruct((len(places) * tiles, half, LANES), jnp.bfloat16) for places in sends
        ],
        in_specs=[WHOLE] * 3,
        out_specs=[WHOLE] * len(sends),
        compiler_params=params,
        name="pack",
    )(slot, digit, embeddings)
    first, second = exchange(packed, tiles) if direct else exchange_all(packed[0], me[0])
    other_first, other_second = (from_partner(rows, 1, "sub") for rows in (first, second))
    query = jnp.concatenate([first, second])
    asked = slots + clus_dev
    near = pl.pallas_call(
        functools.partial(near_kernel, rows_all, owner_map.shape[0], clus_dev, tiles),
        out_shape=[
            jax.ShapeDtypeStruct((width, slots), jnp.bfloat16),
            jax.ShapeDtypeStruct((asked, LANES), jnp.int32),
            jax.ShapeDtypeStruct((2, slots), jnp.int32),
            jax.ShapeDtypeStruct((1, slots), jnp.float32),
            jax.ShapeDtypeStruct((asked, width), jnp.float32),
            jax.ShapeDtypeStruct((asked, LANES), jnp.float32),
        ],
        in_specs=[SCALAR] + [WHOLE] * 3,
        out_specs=[WHOLE] * 6,
        compiler_params=params,
        cost_estimate=compare_cost,
        name="near",
    )(me, ints, query, other_first)
    results, norms = pl.pallas_call(
        functools.partial(far_kernel, rows_all, tiles),
        out_shape=[
            jax.ShapeDtypeStruct((owners, 2, slots), jnp.float32),
            jax.ShapeDtypeStruct((1, clus_dev), jnp.float32),
        ],
        in_specs=[WHOLE] * 8,
        out_specs=[WHOLE] * 2,
        compiler_params=params,
        cost_estimate=compare_cost,
        name="far",
    )(query, other_second, *near)
    results = lax.all_to_all(results, "shard", 0, 0, tiled=True)
    best, distance, cohesion = pl.pallas_call(
        functools.partial(pick_kernel, order, parts),
        out_shape=[jax.ShapeDtypeStruct((1, local_rows), jnp.float32)] * 2
        + [jax.ShapeDtypeStruct((1, clus_dev), jnp.float32)],
        in_specs=[SCALAR] + [WHOLE] * 3,
        out_specs=[WHOLE] * 3,
        compiler_params=params,
        name="pick",
    )(me, slot, results, norms)
    return best.reshape(local_rows), distance.reshape(local_rows), cohesion.reshape(clus_dev)


def solution(mesh):
    in_specs = (
        P(("groups", "shard", "sub"), None),
        P(("groups", "shard", "sub")),
        P(("groups", "shard", "sub")),
        P("groups"),
    )
    out_specs = (
        P(("groups", "shard", "sub")),
        P(("groups", "shard", "sub")),
        P(("groups", "shard")),
    )
    return jax.shard_map(local, mesh=mesh, in_specs=in_specs, out_specs=out_specs, check_vma=False)
```

```python
import functools

import jax
import jax.numpy as jnp
from jax import lax
from jax.experimental import pallas as pl
from jax.experimental.pallas import tpu as pltpu
from jax.sharding import PartitionSpec as P

LANES = 128
DIGITS = 3
SENDS = ((4,), (2, 3), (5,), (7,), (6,), (1,), (0,))
PARTNERS = (2, 4, 5, 0, 7, 6, 1, 3)
WHOLE = pl.BlockSpec(memory_space=pltpu.VMEM)
SCALAR = pl.BlockSpec(memory_space=pltpu.SMEM)


def iota(shape, dim):
    return lax.broadcasted_iota(jnp.int32, shape, dim)


def matmul(a, b):
    return jnp.dot(a, b, preferred_element_type=jnp.float32)


def matmul_t(a, b):
    return lax.dot_general(a, b, (((1,), (1,)), ((), ())), preferred_element_type=jnp.float32)


def bf16(x):
    return x.astype(jnp.float32).astype(jnp.bfloat16)


def ranked(hot):
    upto = (iota((LANES, LANES), 0) <= iota((LANES, LANES), 1)).astype(jnp.bfloat16)
    before, parts = jnp.zeros((1, 1), jnp.float32), []
    for start in range(0, hot.shape[1], LANES):
        piece = hot[:, start : start + LANES]
        spread = jnp.broadcast_to(piece, (16, LANES)).astype(jnp.bfloat16)
        parts.append(matmul(spread, upto)[:1] + before)
        before = before + jnp.sum(piece, axis=1, keepdims=True)
    return jnp.concatenate(parts, axis=1)


def slot_kernel(
    owners, capacity, order, parts, rows, me_ref, ints_ref, slot_ref, digit_ref
):
    clusters = ints_ref.shape[1] - 2 * rows
    cluster = ints_ref[:, clusters : clusters + rows]
    named = bf16(iota((clusters, rows), 0) == cluster)
    owner_map = bf16(jnp.broadcast_to(ints_ref[:, :clusters], (16, clusters)))
    owner = matmul(owner_map, named)[:1].astype(jnp.int32)
    hot = (iota((max(owners, 16), rows), 0) == owner).astype(jnp.float32)
    upto = bf16(iota((rows, rows), 0) <= iota((rows, rows), 1))
    rank = jnp.sum(hot * matmul(bf16(hot), upto), axis=0, keepdims=True) - 1.0
    rank = rank.astype(jnp.int32)
    partner = owner ^ me_ref[0]
    place = partner
    for index, k in enumerate(order):
        place = jnp.where(partner == k, index, place)
    if parts == 1:
        slot_ref[...] = place * capacity + rank
    else:
        half = capacity // 2
        later = (rank >= half).astype(jnp.int32)
        slot_ref[...] = place * half + rank + later * (owners * half - half)

    line = iota((8, rows), 0)
    digit = jnp.zeros((8, rows), jnp.int32)
    for first, number in ((0, cluster + 1), (DIGITS, ints_ref[:, clusters + rows :])):
        for at in range(DIGITS):
            digit = jnp.where(line == first + at, (number >> (8 * at)) & 255, digit)
    empty = jnp.zeros((LANES // 2 - 8, rows), jnp.int32)
    none = jnp.zeros((LANES // 2, rows), jnp.int32)
    early = jnp.concatenate([digit, empty, none], axis=0)
    late = jnp.concatenate([none, digit, empty], axis=0)
    digit_ref[...] = bf16(jnp.concatenate([early, late], axis=1))


def pack_kernel(sends, slot_ref, digit_ref, embed_ref, *out_refs):
    rows, width = embed_ref.shape
    half = out_refs[0].shape[1]
    tiles = 2 * (width // LANES) + 1
    values = embed_ref[...].astype(jnp.float32)
    mean_sq = jnp.sum(values * values, axis=1, keepdims=True) * (1.0 / width)
    unit = (values * lax.rsqrt(width * (mean_sq + 1e-06))).astype(jnp.bfloat16)
    late = half * sum(len(places) for places in sends)
    move = bf16(iota((2 * late, rows), 0) == slot_ref[...])
    moved = matmul(move, unit).astype(jnp.bfloat16)
    both = jnp.concatenate([move[:late], move[late:]], axis=1)
    digit = matmul_t(both, digit_ref[...]).astype(jnp.bfloat16)
    each = tiles // 2
    for places, out_ref in zip(sends, out_refs):
        for index, place in enumerate(places):
            base, start = index * tiles, place * half
            for tile in range(each):
                lanes = slice(tile * LANES, (tile + 1) * LANES)
                out_ref[base + tile] = moved[start : start + half, lanes]
                out_ref[base + each + tile] = moved[late + start : late + start + half, lanes]
            out_ref[base + tiles - 1] = digit[start : start + half]


def unpacked(block_ref, tiles):
    blocks = block_ref.shape[0] // tiles
    each = tiles // 2

    def column(tile):
        return jnp.concatenate([block_ref[i * tiles + tile] for i in range(blocks)], axis=0)

    halves = [
        jnp.concatenate([column(first + tile) for tile in range(each)], axis=1)
        for first in (0, each)
    ]
    return jnp.concatenate(halves, axis=0), column(tiles - 1)


def weights(number, at, half):
    value = jnp.zeros(at.shape, jnp.float32)
    for place in range(DIGITS):
        for which in (0, 1):
            lane = half * (LANES // 2) + which * DIGITS + place
            value = jnp.where((at == lane) & (number == which), 256.0**place, value)
    return value.astype(jnp.bfloat16)


def key_rows(rows_all, digit):
    at = iota((16, LANES), 0), iota((16, LANES), 1)
    numbers = [matmul_t(weights(*at, half), digit) for half in (0, 1)]
    numbers = jnp.concatenate(numbers, axis=1)
    low = (numbers[0:1].astype(jnp.int32) - 1) * rows_all
    return low, low + numbers[1:2].astype(jnp.int32)


def key_columns(rows_all, digit):
    at = iota((LANES, 2 * LANES), 1) // LANES, iota((LANES, 2 * LANES), 0)
    numbers = [matmul(digit, weights(*at, half)) for half in (0, 1)]
    numbers = jnp.concatenate(numbers, axis=0)
    low = (numbers[:, :LANES].astype(jnp.int32) - 1) * rows_all
    return low, low + numbers[:, LANES:].astype(jnp.int32)


def across(column, count):
    return jnp.concatenate([column] * (count // LANES), axis=1)


def compare(rows_all, query_t, query_low, query_key, lows, parts):
    rows = jnp.concatenate([rows for rows, _ in parts], axis=0)
    key = jnp.concatenate([key_rows(rows_all, digit)[1] for _, digit in parts], axis=1)
    bound = across(lows, key.shape[1])
    member = bf16((key >= bound) & (key < bound + rows_all))
    sums = matmul(member, rows)
    counts = matmul(member, jnp.ones((rows.shape[0], LANES), jnp.bfloat16))
    scores = matmul(rows, query_t)
    key = jnp.concatenate([key_columns(rows_all, digit)[1] for _, digit in parts], axis=0)
    key = across(key, query_t.shape[1])
    earlier = (key >= query_low) & (key < query_key)
    best = jnp.max(jnp.where(earlier, scores, -3.0), axis=0, keepdims=True)
    return best, sums, counts


def near_kernel(
    rows_all, clusters, clus_dev, tiles, me_ref, ints_ref, query_ref, other_ref,
    query_t_ref, lows_ref, key_ref, best_ref, sums_ref, counts_ref,
):
    hot = (ints_ref[:, :clusters] == me_ref[0]).astype(jnp.float32)
    rank = ranked(hot)
    shape = (clus_dev, clusters)
    kth = (rank == iota(shape, 0).astype(jnp.float32) + 1.0) & (hot > 0.0)
    own = jnp.sum(jnp.where(kth, iota(shape, 1).astype(jnp.float32), 0.0), axis=1, keepdims=True)
    own = jnp.broadcast_to(own.astype(jnp.int32) * rows_all, (clus_dev, LANES))
    query, digit = unpacked(query_ref, tiles)
    low, _ = key_columns(rows_all, digit)
    lows = jnp.concatenate([low, own], axis=0)
    query_low, query_key = key_rows(rows_all, digit)
    query_t = jnp.transpose(query)
    query_t_ref[...] = query_t
    parts = [(query, digit), unpacked(other_ref, tiles)]
    best, sums, counts = compare(rows_all, query_t, query_low, query_key, lows, parts)
    lows_ref[...] = lows
    key_ref[...] = jnp.concatenate([query_low, query_key], axis=0)
    best_ref[...] = best
    sums_ref[...] = sums
    counts_ref[...] = counts


def far_kernel(
    rows_all, tiles, query_ref, other_ref, query_t_ref, lows_ref, key_ref, best_ref, sums_ref, counts_ref,
    result_ref, norm_ref,
):
    query, _ = unpacked(query_ref, tiles)
    queries, width = query.shape
    best, sums, counts = compare(
        rows_all, query_t_ref[...], key_ref[0:1], key_ref[1:2], lows_ref[...], [unpacked(other_ref, tiles)]
    )
    best = jnp.maximum(best, best_ref[...])
    best = jnp.where(best > -2.0, best, 0.0)
    share = 1.0 / jnp.maximum(counts + counts_ref[...], 1.0)
    squares = jnp.zeros((queries, LANES), jnp.float32)
    norms = jnp.zeros((share.shape[0] - queries, LANES), jnp.float32)
    for start in range(0, width, LANES):
        lanes = slice(start, start + LANES)
        centroid = (sums[:, lanes] + sums_ref[:, lanes]) * share
        offset = query[:, lanes].astype(jnp.float32) - centroid[:queries]
        squares = squares + offset * offset
        norms = norms + centroid[queries:] * centroid[queries:]
    distance = jnp.sum(jnp.transpose(squares), axis=0, keepdims=True)
    result = jnp.concatenate([best, distance], axis=0)
    for owner in range(result_ref.shape[0]):
        result_ref[owner] = result
    norms = jnp.concatenate([norms] * (LANES // norms.shape[0]), axis=0)
    norm_ref[...] = jnp.sum(jnp.transpose(norms), axis=0, keepdims=True)[:, : norm_ref.shape[1]]


def pick_kernel(
    order, parts, me_ref, slot_ref, result_ref, norm_ref, best_ref, distance_ref, cohesion_ref
):
    cohesion_ref[...] = norm_ref[...]
    rows = slot_ref.shape[1]
    owners, lines, slots = result_ref.shape
    folds = min(parts, 2)
    place = iota((lines, slots), 1) % (slots // folds) // (slots // owners // folds)
    values = jnp.zeros((lines, slots), jnp.float32)
    for index, k in enumerate(order):
        values = jnp.where(place == index, result_ref[me_ref[0] ^ k], values)
    values = jnp.concatenate([values, jnp.zeros((8 - lines, slots), jnp.float32)], axis=0)
    at = (iota((slots, rows), 0) == slot_ref[...]).astype(jnp.float32)
    picked = jnp.dot(
        values, at, precision=lax.Precision.HIGHEST, preferred_element_type=jnp.float32
    )
    best_ref[...] = picked[0:1]
    distance_ref[...] = picked[1:2]


def from_partner(value, k, axis):
    return lax.ppermute(value, axis, [(i, i ^ k) for i in range(lax.axis_size(axis))])


def exchange(packed, tiles):
    sent = dict(zip(SENDS, packed))
    got = {0: sent[0,]}
    for k in (4, 5, 7, 6):
        got[k] = from_partner(sent[k,], k, "shard")
    pair = from_partner(sent[2, 3], 2, "shard")
    got[2] = pair[:tiles]
    pair = from_partner(jnp.concatenate([sent[1,], pair[tiles:]]), 1, "shard")
    got[1], got[3] = pair[:tiles], pair[tiles:]
    got = [got[k] for k in PARTNERS]
    half = len(got) // 2
    return jnp.concatenate(got[:half]), jnp.concatenate(got[half:])


def exchange_all(packed, me):
    owners = lax.axis_size("shard")
    tiles, half, _ = packed.shape
    each = tiles // 2
    data = packed[:-1].reshape(2, each, half, LANES).transpose(0, 2, 1, 3).reshape(2 * half, -1)
    digit = jnp.concatenate(jnp.split(packed[-1], 2, axis=1))
    parted = jnp.concatenate([data, digit], axis=1).reshape(owners, 2 * half // owners, -1)
    partner = me ^ jnp.arange(owners, dtype=jnp.int32)
    got = lax.all_to_all(parted[partner], "shard", 0, 0, tiled=True)[partner].reshape(2 * half, -1)
    data = got[:, : each * LANES].reshape(2, half, each, LANES).transpose(0, 2, 1, 3)
    digit = jnp.concatenate(jnp.split(got[:, each * LANES :], 2), axis=1)
    got = jnp.concatenate([data.reshape(2 * each, half, LANES), digit[None]])
    return jnp.split(got, 2, axis=1)


def local(embeddings, cluster_id, item_order, owner_map):
    owners = lax.axis_size("shard")
    local_rows, width = embeddings.shape
    rows_all = local_rows * owners * lax.axis_size("sub")
    clus_dev = owner_map.shape[0] // owners
    capacity = 2 * local_rows // owners
    slots = owners * capacity
    params = pltpu.CompilerParams(vmem_limit_bytes=32 << 20)
    compare_cost = pl.CostEstimate(
        flops=4 * slots * slots * width, bytes_accessed=4 * slots * width, transcendentals=0
    )
    me = lax.axis_index("shard").astype(jnp.int32).reshape(1)
    ints = jnp.concatenate([owner_map, cluster_id, item_order]).reshape(1, -1)

    direct = owners == len(PARTNERS)
    order = PARTNERS if direct else tuple(range(owners))
    parts = owners if direct else 1
    tiles = 2 * (width // LANES) + 1
    sends = [[PARTNERS.index(k) for k in ks] for ks in SENDS] if direct else [[0]]
    half = slots // parts // 2
    slot, digit = pl.pallas_call(
        functools.partial(slot_kernel, owners, capacity, order, parts, local_rows),
        out_shape=[
            jax.ShapeDtypeStruct((1, local_rows), jnp.int32),
            jax.ShapeDtypeStruct((LANES, 2 * local_rows), jnp.bfloat16),
        ],
        in_specs=[SCALAR, WHOLE],
        out_specs=[WHOLE] * 2,
        compiler_params=params,
        cost_estimate=pl.CostEstimate(flops=1 << 29, bytes_accessed=1 << 16, transcendentals=0),
        name="slots",
    )(me, ints)
    packed = pl.pallas_call(
        functools.partial(pack_kernel, sends),
        out_shape=[
            jax.ShapeDtypeStruct((len(places) * tiles, half, LANES), jnp.bfloat16) for places in sends
        ],
        in_specs=[WHOLE] * 3,
        out_specs=[WHOLE] * len(sends),
        compiler_params=params,
        name="pack",
    )(slot, digit, embeddings)
    first, second = exchange(packed, tiles) if direct else exchange_all(packed[0], me[0])
    other_first, other_second = (from_partner(rows, 1, "sub") for rows in (first, second))
    query = jnp.concatenate([first, second])
    asked = slots + clus_dev
    near = pl.pallas_call(
        functools.partial(near_kernel, rows_all, owner_map.shape[0], clus_dev, tiles),
        out_shape=[
            jax.ShapeDtypeStruct((width, slots), jnp.bfloat16),
            jax.ShapeDtypeStruct((asked, LANES), jnp.int32),
            jax.ShapeDtypeStruct((2, slots), jnp.int32),
            jax.ShapeDtypeStruct((1, slots), jnp.float32),
            jax.ShapeDtypeStruct((asked, width), jnp.float32),
            jax.ShapeDtypeStruct((asked, LANES), jnp.float32),
        ],
        in_specs=[SCALAR] + [WHOLE] * 3,
        out_specs=[WHOLE] * 6,
        compiler_params=params,
        cost_estimate=compare_cost,
        name="near",
    )(me, ints, query, other_first)
    results, norms = pl.pallas_call(
        functools.partial(far_kernel, rows_all, tiles),
        out_shape=[
            jax.ShapeDtypeStruct((owners, 2, slots), jnp.float32),
            jax.ShapeDtypeStruct((1, clus_dev), jnp.float32),
        ],
        in_specs=[WHOLE] * 8,
        out_specs=[WHOLE] * 2,
        compiler_params=params,
        cost_estimate=compare_cost,
        name="far",
    )(query, other_second, *near)
    results = lax.all_to_all(results, "shard", 0, 0, tiled=True)
    best, distance, cohesion = pl.pallas_call(
        functools.partial(pick_kernel, order, parts),
        out_shape=[jax.ShapeDtypeStruct((1, local_rows), jnp.float32)] * 2
        + [jax.ShapeDtypeStruct((1, clus_dev), jnp.float32)],
        in_specs=[SCALAR] + [WHOLE] * 3,
        out_specs=[WHOLE] * 3,
        compiler_params=params,
        name="pick",
    )(me, slot, results, norms)
    return best.reshape(local_rows), distance.reshape(local_rows), cohesion.reshape(clus_dev)


def solution(mesh):
    in_specs = (
        P(("groups", "shard", "sub"), None),
        P(("groups", "shard", "sub")),
        P(("groups", "shard", "sub")),
        P("groups"),
    )
    out_specs = (
        P(("groups", "shard", "sub")),
        P(("groups", "shard", "sub")),
        P(("groups", "shard")),
    )
    return jax.shard_map(local, mesh=mesh, in_specs=in_specs, out_specs=out_specs, check_vma=False)
```

```python
import functools

import jax
import jax.numpy as jnp
from jax import lax
from jax.experimental import pallas as pl
from jax.experimental.pallas import tpu as pltpu
from jax.sharding import PartitionSpec as P

LANES = 128
DIGITS = 3
SENDS = ((4,), (2, 3), (5,), (7,), (6,), (1,), (0,))
PARTNERS = (4, 2, 0, 5, 7, 6, 1, 3)
WHOLE = pl.BlockSpec(memory_space=pltpu.VMEM)
SCALAR = pl.BlockSpec(memory_space=pltpu.SMEM)


def iota(shape, dim):
    return lax.broadcasted_iota(jnp.int32, shape, dim)


def matmul(a, b):
    return jnp.dot(a, b, preferred_element_type=jnp.float32)


def matmul_t(a, b):
    return lax.dot_general(a, b, (((1,), (1,)), ((), ())), preferred_element_type=jnp.float32)


def bf16(x):
    return x.astype(jnp.float32).astype(jnp.bfloat16)


def ranked(hot):
    upto = (iota((LANES, LANES), 0) <= iota((LANES, LANES), 1)).astype(jnp.bfloat16)
    before, parts = jnp.zeros((1, 1), jnp.float32), []
    for start in range(0, hot.shape[1], LANES):
        piece = hot[:, start : start + LANES]
        spread = jnp.broadcast_to(piece, (16, LANES)).astype(jnp.bfloat16)
        parts.append(matmul(spread, upto)[:1] + before)
        before = before + jnp.sum(piece, axis=1, keepdims=True)
    return jnp.concatenate(parts, axis=1)


def slot_kernel(
    owners, capacity, order, parts, rows, me_ref, ints_ref, slot_ref, digit_ref
):
    clusters = ints_ref.shape[1] - 2 * rows
    cluster = ints_ref[:, clusters : clusters + rows]
    named = bf16(iota((clusters, rows), 0) == cluster)
    owner_map = bf16(jnp.broadcast_to(ints_ref[:, :clusters], (16, clusters)))
    owner = matmul(owner_map, named)[:1].astype(jnp.int32)
    hot = (iota((max(owners, 16), rows), 0) == owner).astype(jnp.float32)
    upto = bf16(iota((rows, rows), 0) <= iota((rows, rows), 1))
    rank = jnp.sum(hot * matmul(bf16(hot), upto), axis=0, keepdims=True) - 1.0
    rank = rank.astype(jnp.int32)
    partner = owner ^ me_ref[0]
    place = partner
    for index, k in enumerate(order):
        place = jnp.where(partner == k, index, place)
    if parts == 1:
        slot_ref[...] = place * capacity + rank
    else:
        half = capacity // 2
        later = (rank >= half).astype(jnp.int32)
        slot_ref[...] = place * half + rank + later * (owners * half - half)

    line = iota((8, rows), 0)
    digit = jnp.zeros((8, rows), jnp.int32)
    for first, number in ((0, cluster + 1), (DIGITS, ints_ref[:, clusters + rows :])):
        for at in range(DIGITS):
            digit = jnp.where(line == first + at, (number >> (8 * at)) & 255, digit)
    empty = jnp.zeros((LANES // 2 - 8, rows), jnp.int32)
    none = jnp.zeros((LANES // 2, rows), jnp.int32)
    early = jnp.concatenate([digit, empty, none], axis=0)
    late = jnp.concatenate([none, digit, empty], axis=0)
    digit_ref[...] = bf16(jnp.concatenate([early, late], axis=1))


def pack_kernel(sends, slot_ref, digit_ref, embed_ref, *out_refs):
    rows, width = embed_ref.shape
    half = out_refs[0].shape[1]
    tiles = 2 * (width // LANES) + 1
    values = embed_ref[...].astype(jnp.float32)
    mean_sq = jnp.sum(values * values, axis=1, keepdims=True) * (1.0 / width)
    unit = (values * lax.rsqrt(width * (mean_sq + 1e-06))).astype(jnp.bfloat16)
    late = half * sum(len(places) for places in sends)
    move = bf16(iota((2 * late, rows), 0) == slot_ref[...])
    moved = matmul(move, unit).astype(jnp.bfloat16)
    both = jnp.concatenate([move[:late], move[late:]], axis=1)
    digit = matmul_t(both, digit_ref[...]).astype(jnp.bfloat16)
    each = tiles // 2
    for places, out_ref in zip(sends, out_refs):
        for index, place in enumerate(places):
            base, start = index * tiles, place * half
            for tile in range(each):
                lanes = slice(tile * LANES, (tile + 1) * LANES)
                out_ref[base + tile] = moved[start : start + half, lanes]
                out_ref[base + each + tile] = moved[late + start : late + start + half, lanes]
            out_ref[base + tiles - 1] = digit[start : start + half]


def unpacked(block_ref, tiles):
    blocks = block_ref.shape[0] // tiles
    each = tiles // 2

    def column(tile):
        return jnp.concatenate([block_ref[i * tiles + tile] for i in range(blocks)], axis=0)

    halves = [
        jnp.concatenate([column(first + tile) for tile in range(each)], axis=1)
        for first in (0, each)
    ]
    return jnp.concatenate(halves, axis=0), column(tiles - 1)


def weights(number, at, half):
    value = jnp.zeros(at.shape, jnp.float32)
    for place in range(DIGITS):
        for which in (0, 1):
            lane = half * (LANES // 2) + which * DIGITS + place
            value = jnp.where((at == lane) & (number == which), 256.0**place, value)
    return value.astype(jnp.bfloat16)


def key_rows(rows_all, digit):
    at = iota((16, LANES), 0), iota((16, LANES), 1)
    numbers = [matmul_t(weights(*at, half), digit) for half in (0, 1)]
    numbers = jnp.concatenate(numbers, axis=1)
    low = (numbers[0:1].astype(jnp.int32) - 1) * rows_all
    return low, low + numbers[1:2].astype(jnp.int32)


def key_columns(rows_all, digit):
    at = iota((LANES, 2 * LANES), 1) // LANES, iota((LANES, 2 * LANES), 0)
    numbers = [matmul(digit, weights(*at, half)) for half in (0, 1)]
    numbers = jnp.concatenate(numbers, axis=0)
    low = (numbers[:, :LANES].astype(jnp.int32) - 1) * rows_all
    return low, low + numbers[:, LANES:].astype(jnp.int32)


def across(column, count):
    return jnp.concatenate([column] * (count // LANES), axis=1)


def compare(rows_all, query_t, query_low, query_key, lows, parts):
    rows = jnp.concatenate([rows for rows, _ in parts], axis=0)
    key = jnp.concatenate([key_rows(rows_all, digit)[1] for _, digit in parts], axis=1)
    bound = across(lows, key.shape[1])
    member = bf16((key >= bound) & (key < bound + rows_all))
    sums = matmul(member, rows)
    counts = matmul(member, jnp.ones((rows.shape[0], LANES), jnp.bfloat16))
    scores = matmul(rows, query_t)
    key = jnp.concatenate([key_columns(rows_all, digit)[1] for _, digit in parts], axis=0)
    key = across(key, query_t.shape[1])
    earlier = (key >= query_low) & (key < query_key)
    best = jnp.max(jnp.where(earlier, scores, -3.0), axis=0, keepdims=True)
    return best, sums, counts


def near_kernel(
    rows_all, clusters, clus_dev, tiles, me_ref, ints_ref, query_ref, other_ref,
    query_t_ref, lows_ref, key_ref, best_ref, sums_ref, counts_ref,
):
    hot = (ints_ref[:, :clusters] == me_ref[0]).astype(jnp.float32)
    rank = ranked(hot)
    shape = (clus_dev, clusters)
    kth = (rank == iota(shape, 0).astype(jnp.float32) + 1.0) & (hot > 0.0)
    own = jnp.sum(jnp.where(kth, iota(shape, 1).astype(jnp.float32), 0.0), axis=1, keepdims=True)
    own = jnp.broadcast_to(own.astype(jnp.int32) * rows_all, (clus_dev, LANES))
    query, digit = unpacked(query_ref, tiles)
    low, _ = key_columns(rows_all, digit)
    lows = jnp.concatenate([low, own], axis=0)
    query_low, query_key = key_rows(rows_all, digit)
    query_t = jnp.transpose(query)
    query_t_ref[...] = query_t
    parts = [(query, digit), unpacked(other_ref, tiles)]
    best, sums, counts = compare(rows_all, query_t, query_low, query_key, lows, parts)
    lows_ref[...] = lows
    key_ref[...] = jnp.concatenate([query_low, query_key], axis=0)
    best_ref[...] = best
    sums_ref[...] = sums
    counts_ref[...] = counts


def far_kernel(
    rows_all, tiles, summed, me_ref, query_ref, other_ref, query_t_ref, lows_ref, key_ref, best_ref, sums_ref, counts_ref,
    result_ref, norm_ref,
):
    query, _ = unpacked(query_ref, tiles)
    queries, width = query.shape
    best, sums, counts = compare(
        rows_all, query_t_ref[...], key_ref[0:1], key_ref[1:2], lows_ref[...], [unpacked(other_ref, tiles)]
    )
    best = jnp.maximum(best, best_ref[...])
    best = jnp.where(best > -2.0, best, 0.0)
    share = 1.0 / jnp.maximum(counts + counts_ref[...], 1.0)
    squares = jnp.zeros((queries, LANES), jnp.float32)
    norms = jnp.zeros((share.shape[0] - queries, LANES), jnp.float32)
    for start in range(0, width, LANES):
        lanes = slice(start, start + LANES)
        centroid = (sums[:, lanes] + sums_ref[:, lanes]) * share
        offset = query[:, lanes].astype(jnp.float32) - centroid[:queries]
        squares = squares + offset * offset
        norms = norms + centroid[queries:] * centroid[queries:]
    distance = jnp.sum(jnp.transpose(squares), axis=0, keepdims=True)
    result = jnp.concatenate([best, distance], axis=0)
    for owner in range(result_ref.shape[0]):
        mine = jnp.where(owner == me_ref[0], 1.0, 0.0) if summed else 1.0
        result_ref[owner] = result * mine
    norms = jnp.concatenate([norms] * (LANES // norms.shape[0]), axis=0)
    norm_ref[...] = jnp.sum(jnp.transpose(norms), axis=0, keepdims=True)[:, : norm_ref.shape[1]]


def pick_kernel(
    order, parts, me_ref, slot_ref, result_ref, norm_ref, best_ref, distance_ref, cohesion_ref
):
    cohesion_ref[...] = norm_ref[...]
    rows = slot_ref.shape[1]
    owners, lines, slots = result_ref.shape
    folds = min(parts, 2)
    place = iota((lines, slots), 1) % (slots // folds) // (slots // owners // folds)
    values = jnp.zeros((lines, slots), jnp.float32)
    for index, k in enumerate(order):
        values = jnp.where(place == index, result_ref[me_ref[0] ^ k], values)
    values = jnp.concatenate([values, jnp.zeros((8 - lines, slots), jnp.float32)], axis=0)
    at = (iota((slots, rows), 0) == slot_ref[...]).astype(jnp.float32)
    picked = jnp.dot(
        values, at, precision=lax.Precision.HIGHEST, preferred_element_type=jnp.float32
    )
    best_ref[...] = picked[0:1]
    distance_ref[...] = picked[1:2]


def from_partner(value, k, axis):
    return lax.ppermute(value, axis, [(i, i ^ k) for i in range(lax.axis_size(axis))])


def exchange(packed, tiles):
    sent = dict(zip(SENDS, packed))
    got = {0: sent[0,]}
    for k in (4, 5, 7, 6):
        got[k] = from_partner(sent[k,], k, "shard")
    pair = from_partner(sent[2, 3], 2, "shard")
    got[2] = pair[:tiles]
    pair = from_partner(jnp.concatenate([sent[1,], pair[tiles:]]), 1, "shard")
    got[1], got[3] = pair[:tiles], pair[tiles:]
    got = [got[k] for k in PARTNERS]
    half = len(got) // 2
    return jnp.concatenate(got[:half]), jnp.concatenate(got[half:])


def exchange_all(packed, me):
    owners = lax.axis_size("shard")
    tiles, half, _ = packed.shape
    each = tiles // 2
    data = packed[:-1].reshape(2, each, half, LANES).transpose(0, 2, 1, 3).reshape(2 * half, -1)
    digit = jnp.concatenate(jnp.split(packed[-1], 2, axis=1))
    parted = jnp.concatenate([data, digit], axis=1).reshape(owners, 2 * half // owners, -1)
    partner = me ^ jnp.arange(owners, dtype=jnp.int32)
    got = lax.all_to_all(parted[partner], "shard", 0, 0, tiled=True)[partner].reshape(2 * half, -1)
    data = got[:, : each * LANES].reshape(2, half, each, LANES).transpose(0, 2, 1, 3)
    digit = jnp.concatenate(jnp.split(got[:, each * LANES :], 2), axis=1)
    got = jnp.concatenate([data.reshape(2 * each, half, LANES), digit[None]])
    return jnp.split(got, 2, axis=1)


def local(embeddings, cluster_id, item_order, owner_map):
    owners = lax.axis_size("shard")
    local_rows, width = embeddings.shape
    rows_all = local_rows * owners * lax.axis_size("sub")
    clus_dev = owner_map.shape[0] // owners
    capacity = 2 * local_rows // owners
    slots = owners * capacity
    params = pltpu.CompilerParams(vmem_limit_bytes=32 << 20)
    compare_cost = pl.CostEstimate(
        flops=4 * slots * slots * width, bytes_accessed=4 * slots * width, transcendentals=0
    )
    me = lax.axis_index("shard").astype(jnp.int32).reshape(1)
    ints = jnp.concatenate([owner_map, cluster_id, item_order]).reshape(1, -1)

    direct = owners == len(PARTNERS)
    order = PARTNERS if direct else tuple(range(owners))
    parts = owners if direct else 1
    tiles = 2 * (width // LANES) + 1
    sends = [[PARTNERS.index(k) for k in ks] for ks in SENDS] if direct else [[0]]
    half = slots // parts // 2
    slot, digit = pl.pallas_call(
        functools.partial(slot_kernel, owners, capacity, order, parts, local_rows),
        out_shape=[
            jax.ShapeDtypeStruct((1, local_rows), jnp.int32),
            jax.ShapeDtypeStruct((LANES, 2 * local_rows), jnp.bfloat16),
        ],
        in_specs=[SCALAR, WHOLE],
        out_specs=[WHOLE] * 2,
        compiler_params=params,
        cost_estimate=pl.CostEstimate(flops=1 << 29, bytes_accessed=1 << 16, transcendentals=0),
        name="slots",
    )(me, ints)
    packed = pl.pallas_call(
        functools.partial(pack_kernel, sends),
        out_shape=[
            jax.ShapeDtypeStruct((len(places) * tiles, half, LANES), jnp.bfloat16) for places in sends
        ],
        in_specs=[WHOLE] * 3,
        out_specs=[WHOLE] * len(sends),
        compiler_params=params,
        name="pack",
    )(slot, digit, embeddings)
    first, second = exchange(packed, tiles) if direct else exchange_all(packed[0], me[0])
    other_first, other_second = (from_partner(rows, 1, "sub") for rows in (first, second))
    query = jnp.concatenate([first, second])
    asked = slots + clus_dev
    near = pl.pallas_call(
        functools.partial(near_kernel, rows_all, owner_map.shape[0], clus_dev, tiles),
        out_shape=[
            jax.ShapeDtypeStruct((width, slots), jnp.bfloat16),
            jax.ShapeDtypeStruct((asked, LANES), jnp.int32),
            jax.ShapeDtypeStruct((2, slots), jnp.int32),
            jax.ShapeDtypeStruct((1, slots), jnp.float32),
            jax.ShapeDtypeStruct((asked, width), jnp.float32),
            jax.ShapeDtypeStruct((asked, LANES), jnp.float32),
        ],
        in_specs=[SCALAR] + [WHOLE] * 3,
        out_specs=[WHOLE] * 6,
        compiler_params=params,
        cost_estimate=compare_cost,
        name="near",
    )(me, ints, query, other_first)
    results, norms = pl.pallas_call(
        functools.partial(far_kernel, rows_all, tiles, direct),
        out_shape=[
            jax.ShapeDtypeStruct((owners, 2, slots), jnp.float32),
            jax.ShapeDtypeStruct((1, clus_dev), jnp.float32),
        ],
        in_specs=[SCALAR] + [WHOLE] * 8,
        out_specs=[WHOLE] * 2,
        compiler_params=params,
        cost_estimate=compare_cost,
        name="far",
    )(me, query, other_second, *near)
    if direct:
        results = lax.psum(results, "shard")
    else:
        results = lax.all_to_all(results, "shard", 0, 0, tiled=True)
    best, distance, cohesion = pl.pallas_call(
        functools.partial(pick_kernel, order, parts),
        out_shape=[jax.ShapeDtypeStruct((1, local_rows), jnp.float32)] * 2
        + [jax.ShapeDtypeStruct((1, clus_dev), jnp.float32)],
        in_specs=[SCALAR] + [WHOLE] * 3,
        out_specs=[WHOLE] * 3,
        compiler_params=params,
        name="pick",
    )(me, slot, results, norms)
    return best.reshape(local_rows), distance.reshape(local_rows), cohesion.reshape(clus_dev)


def solution(mesh):
    in_specs = (
        P(("groups", "shard", "sub"), None),
        P(("groups", "shard", "sub")),
        P(("groups", "shard", "sub")),
        P("groups"),
    )
    out_specs = (
        P(("groups", "shard", "sub")),
        P(("groups", "shard", "sub")),
        P(("groups", "shard")),
    )
    return jax.shard_map(local, mesh=mesh, in_specs=in_specs, out_specs=out_specs, check_vma=False)
```

```python
import functools

import jax
import jax.numpy as jnp
from jax import lax
from jax.experimental import pallas as pl
from jax.experimental.pallas import tpu as pltpu
from jax.sharding import PartitionSpec as P

LANES = 128
DIGITS = 3
SENDS = ((4,), (2, 3), (5,), (7,), (6,), (1,), (0,))
PARTNERS = (4, 2, 0, 5, 7, 6, 1, 3)
WHOLE = pl.BlockSpec(memory_space=pltpu.VMEM)
SCALAR = pl.BlockSpec(memory_space=pltpu.SMEM)


def iota(shape, dim):
    return lax.broadcasted_iota(jnp.int32, shape, dim)


def matmul(a, b):
    return jnp.dot(a, b, preferred_element_type=jnp.float32)


def matmul_t(a, b):
    return lax.dot_general(a, b, (((1,), (1,)), ((), ())), preferred_element_type=jnp.float32)


def bf16(x):
    return x.astype(jnp.float32).astype(jnp.bfloat16)


def ranked(hot):
    upto = (iota((LANES, LANES), 0) <= iota((LANES, LANES), 1)).astype(jnp.bfloat16)
    before, parts = jnp.zeros((1, 1), jnp.float32), []
    for start in range(0, hot.shape[1], LANES):
        piece = hot[:, start : start + LANES]
        spread = jnp.broadcast_to(piece, (16, LANES)).astype(jnp.bfloat16)
        parts.append(matmul(spread, upto)[:1] + before)
        before = before + jnp.sum(piece, axis=1, keepdims=True)
    return jnp.concatenate(parts, axis=1)


def slot_kernel(
    owners, capacity, order, parts, rows, me_ref, ints_ref, slot_ref, digit_ref
):
    clusters = ints_ref.shape[1] - 2 * rows
    cluster = ints_ref[:, clusters : clusters + rows]
    named = bf16(iota((clusters, rows), 0) == cluster)
    owner_map = bf16(jnp.broadcast_to(ints_ref[:, :clusters], (16, clusters)))
    owner = matmul(owner_map, named)[:1].astype(jnp.int32)
    hot = (iota((max(owners, 16), rows), 0) == owner).astype(jnp.float32)
    upto = bf16(iota((rows, rows), 0) <= iota((rows, rows), 1))
    rank = jnp.sum(hot * matmul(bf16(hot), upto), axis=0, keepdims=True) - 1.0
    rank = rank.astype(jnp.int32)
    partner = owner ^ me_ref[0]
    place = partner
    for index, k in enumerate(order):
        place = jnp.where(partner == k, index, place)
    if parts == 1:
        slot_ref[...] = place * capacity + rank
    else:
        half = capacity // 2
        later = (rank >= half).astype(jnp.int32)
        slot_ref[...] = place * half + rank + later * (owners * half - half)

    line = iota((8, rows), 0)
    digit = jnp.zeros((8, rows), jnp.int32)
    for first, number in ((0, cluster + 1), (DIGITS, ints_ref[:, clusters + rows :])):
        for at in range(DIGITS):
            digit = jnp.where(line == first + at, (number >> (8 * at)) & 255, digit)
    empty = jnp.zeros((LANES // 2 - 8, rows), jnp.int32)
    none = jnp.zeros((LANES // 2, rows), jnp.int32)
    early = jnp.concatenate([digit, empty, none], axis=0)
    late = jnp.concatenate([none, digit, empty], axis=0)
    digit_ref[...] = bf16(jnp.concatenate([early, late], axis=1))


def pack_kernel(sends, slot_ref, digit_ref, embed_ref, *out_refs):
    rows, width = embed_ref.shape
    half = out_refs[0].shape[1]
    tiles = 2 * (width // LANES) + 1
    values = embed_ref[...].astype(jnp.float32)
    mean_sq = jnp.sum(values * values, axis=1, keepdims=True) * (1.0 / width)
    unit = (values * lax.rsqrt(width * (mean_sq + 1e-06))).astype(jnp.bfloat16)
    late = half * sum(len(places) for places in sends)
    move = bf16(iota((2 * late, rows), 0) == slot_ref[...])
    moved = matmul(move, unit).astype(jnp.bfloat16)
    both = jnp.concatenate([move[:late], move[late:]], axis=1)
    digit = matmul_t(both, digit_ref[...]).astype(jnp.bfloat16)
    each = tiles // 2
    for places, out_ref in zip(sends, out_refs):
        for index, place in enumerate(places):
            base, start = index * tiles, place * half
            for tile in range(each):
                lanes = slice(tile * LANES, (tile + 1) * LANES)
                out_ref[base + tile] = moved[start : start + half, lanes]
                out_ref[base + each + tile] = moved[late + start : late + start + half, lanes]
            out_ref[base + tiles - 1] = digit[start : start + half]


def unpacked(block_ref, tiles):
    blocks = block_ref.shape[0] // tiles
    each = tiles // 2

    def column(tile):
        return jnp.concatenate([block_ref[i * tiles + tile] for i in range(blocks)], axis=0)

    halves = [
        jnp.concatenate([column(first + tile) for tile in range(each)], axis=1)
        for first in (0, each)
    ]
    return jnp.concatenate(halves, axis=0), column(tiles - 1)


def weights(number, at, half):
    value = jnp.zeros(at.shape, jnp.float32)
    for place in range(DIGITS):
        for which in (0, 1):
            lane = half * (LANES // 2) + which * DIGITS + place
            value = jnp.where((at == lane) & (number == which), 256.0**place, value)
    return value.astype(jnp.bfloat16)


def key_rows(rows_all, digit):
    at = iota((16, LANES), 0), iota((16, LANES), 1)
    numbers = [matmul_t(weights(*at, half), digit) for half in (0, 1)]
    numbers = jnp.concatenate(numbers, axis=1)
    low = (numbers[0:1].astype(jnp.int32) - 1) * rows_all
    return low, low + numbers[1:2].astype(jnp.int32)


def key_columns(rows_all, digit):
    at = iota((LANES, 2 * LANES), 1) // LANES, iota((LANES, 2 * LANES), 0)
    numbers = [matmul(digit, weights(*at, half)) for half in (0, 1)]
    numbers = jnp.concatenate(numbers, axis=0)
    low = (numbers[:, :LANES].astype(jnp.int32) - 1) * rows_all
    return low, low + numbers[:, LANES:].astype(jnp.int32)


def across(column, count):
    return jnp.concatenate([column] * (count // LANES), axis=1)


def compare(rows_all, query_t, query_low, query_key, lows, parts):
    rows = jnp.concatenate([rows for rows, _ in parts], axis=0)
    key = jnp.concatenate([key_rows(rows_all, digit)[1] for _, digit in parts], axis=1)
    bound = across(lows, key.shape[1])
    member = bf16((key >= bound) & (key < bound + rows_all))
    sums = matmul(member, rows)
    counts = matmul(member, jnp.ones((rows.shape[0], LANES), jnp.bfloat16))
    scores = matmul(rows, query_t)
    key = jnp.concatenate([key_columns(rows_all, digit)[1] for _, digit in parts], axis=0)
    key = across(key, query_t.shape[1])
    earlier = (key >= query_low) & (key < query_key)
    best = jnp.max(jnp.where(earlier, scores, -3.0), axis=0, keepdims=True)
    return best, sums, counts


def near_kernel(
    rows_all, clusters, clus_dev, tiles, me_ref, ints_ref, query_ref, other_ref,
    query_t_ref, lows_ref, key_ref, best_ref, sums_ref, counts_ref,
):
    hot = (ints_ref[:, :clusters] == me_ref[0]).astype(jnp.float32)
    rank = ranked(hot)
    shape = (clus_dev, clusters)
    kth = (rank == iota(shape, 0).astype(jnp.float32) + 1.0) & (hot > 0.0)
    own = jnp.sum(jnp.where(kth, iota(shape, 1).astype(jnp.float32), 0.0), axis=1, keepdims=True)
    own = jnp.broadcast_to(own.astype(jnp.int32) * rows_all, (clus_dev, LANES))
    query, digit = unpacked(query_ref, tiles)
    low, _ = key_columns(rows_all, digit)
    lows = jnp.concatenate([low, own], axis=0)
    query_low, query_key = key_rows(rows_all, digit)
    query_t = jnp.transpose(query)
    query_t_ref[...] = query_t
    parts = [(query, digit), unpacked(other_ref, tiles)]
    best, sums, counts = compare(rows_all, query_t, query_low, query_key, lows, parts)
    lows_ref[...] = lows
    key_ref[...] = jnp.concatenate([query_low, query_key], axis=0)
    best_ref[...] = best
    sums_ref[...] = sums
    counts_ref[...] = counts


def far_kernel(
    rows_all, tiles, query_ref, other_ref, query_t_ref, lows_ref, key_ref, best_ref, sums_ref, counts_ref,
    result_ref, norm_ref,
):
    query, _ = unpacked(query_ref, tiles)
    queries, width = query.shape
    best, sums, counts = compare(
        rows_all, query_t_ref[...], key_ref[0:1], key_ref[1:2], lows_ref[...], [unpacked(other_ref, tiles)]
    )
    best = jnp.maximum(best, best_ref[...])
    best = jnp.where(best > -2.0, best, 0.0)
    share = 1.0 / jnp.maximum(counts + counts_ref[...], 1.0)
    squares = jnp.zeros((queries, LANES), jnp.float32)
    norms = jnp.zeros((share.shape[0] - queries, LANES), jnp.float32)
    for start in range(0, width, LANES):
        lanes = slice(start, start + LANES)
        centroid = (sums[:, lanes] + sums_ref[:, lanes]) * share
        offset = query[:, lanes].astype(jnp.float32) - centroid[:queries]
        squares = squares + offset * offset
        norms = norms + centroid[queries:] * centroid[queries:]
    distance = jnp.sum(jnp.transpose(squares), axis=0, keepdims=True)
    result = jnp.concatenate([best, distance], axis=0)
    for owner in range(result_ref.shape[0]):
        result_ref[owner] = result
    norms = jnp.concatenate([norms] * (LANES // norms.shape[0]), axis=0)
    norm_ref[...] = jnp.sum(jnp.transpose(norms), axis=0, keepdims=True)[:, : norm_ref.shape[1]]


def pick_kernel(
    order, parts, me_ref, slot_ref, norm_ref, *refs
):
    *result_refs, best_ref, distance_ref, cohesion_ref = refs
    cohesion_ref[...] = norm_ref[...]
    rows = slot_ref.shape[1]
    _, lines, slots = result_refs[0].shape
    owners, sides = len(order), len(result_refs)
    folds = min(parts, 2)
    place = iota((lines, slots), 1) % (slots // folds) // (slots // owners // folds)
    values = jnp.zeros((lines, slots), jnp.float32)
    for index, k in enumerate(order):
        values = jnp.where(place == index, result_refs[k % sides][(me_ref[0] ^ k) // sides], values)
    values = jnp.concatenate([values, jnp.zeros((8 - lines, slots), jnp.float32)], axis=0)
    at = (iota((slots, rows), 0) == slot_ref[...]).astype(jnp.float32)
    picked = jnp.dot(
        values, at, precision=lax.Precision.HIGHEST, preferred_element_type=jnp.float32
    )
    best_ref[...] = picked[0:1]
    distance_ref[...] = picked[1:2]


def from_partner(value, k, axis):
    return lax.ppermute(value, axis, [(i, i ^ k) for i in range(lax.axis_size(axis))])


def exchange(packed, tiles):
    sent = dict(zip(SENDS, packed))
    got = {0: sent[0,]}
    for k in (4, 5, 7, 6):
        got[k] = from_partner(sent[k,], k, "shard")
    pair = from_partner(sent[2, 3], 2, "shard")
    got[2] = pair[:tiles]
    pair = from_partner(jnp.concatenate([sent[1,], pair[tiles:]]), 1, "shard")
    got[1], got[3] = pair[:tiles], pair[tiles:]
    got = [got[k] for k in PARTNERS]
    half = len(got) // 2
    return jnp.concatenate(got[:half]), jnp.concatenate(got[half:])


def exchange_all(packed, me):
    owners = lax.axis_size("shard")
    tiles, half, _ = packed.shape
    each = tiles // 2
    data = packed[:-1].reshape(2, each, half, LANES).transpose(0, 2, 1, 3).reshape(2 * half, -1)
    digit = jnp.concatenate(jnp.split(packed[-1], 2, axis=1))
    parted = jnp.concatenate([data, digit], axis=1).reshape(owners, 2 * half // owners, -1)
    partner = me ^ jnp.arange(owners, dtype=jnp.int32)
    got = lax.all_to_all(parted[partner], "shard", 0, 0, tiled=True)[partner].reshape(2 * half, -1)
    data = got[:, : each * LANES].reshape(2, half, each, LANES).transpose(0, 2, 1, 3)
    digit = jnp.concatenate(jnp.split(got[:, each * LANES :], 2), axis=1)
    got = jnp.concatenate([data.reshape(2 * each, half, LANES), digit[None]])
    return jnp.split(got, 2, axis=1)


def local(embeddings, cluster_id, item_order, owner_map):
    owners = lax.axis_size("shard")
    local_rows, width = embeddings.shape
    rows_all = local_rows * owners * lax.axis_size("sub")
    clus_dev = owner_map.shape[0] // owners
    capacity = 2 * local_rows // owners
    slots = owners * capacity
    params = pltpu.CompilerParams(vmem_limit_bytes=32 << 20)
    compare_cost = pl.CostEstimate(
        flops=4 * slots * slots * width, bytes_accessed=4 * slots * width, transcendentals=0
    )
    me = lax.axis_index("shard").astype(jnp.int32).reshape(1)
    ints = jnp.concatenate([owner_map, cluster_id, item_order]).reshape(1, -1)

    direct = owners == len(PARTNERS)
    order = PARTNERS if direct else tuple(range(owners))
    parts = owners if direct else 1
    tiles = 2 * (width // LANES) + 1
    sends = [[PARTNERS.index(k) for k in ks] for ks in SENDS] if direct else [[0]]
    half = slots // parts // 2
    slot, digit = pl.pallas_call(
        functools.partial(slot_kernel, owners, capacity, order, parts, local_rows),
        out_shape=[
            jax.ShapeDtypeStruct((1, local_rows), jnp.int32),
            jax.ShapeDtypeStruct((LANES, 2 * local_rows), jnp.bfloat16),
        ],
        in_specs=[SCALAR, WHOLE],
        out_specs=[WHOLE] * 2,
        compiler_params=params,
        cost_estimate=pl.CostEstimate(flops=1 << 29, bytes_accessed=1 << 16, transcendentals=0),
        name="slots",
    )(me, ints)
    packed = pl.pallas_call(
        functools.partial(pack_kernel, sends),
        out_shape=[
            jax.ShapeDtypeStruct((len(places) * tiles, half, LANES), jnp.bfloat16) for places in sends
        ],
        in_specs=[WHOLE] * 3,
        out_specs=[WHOLE] * len(sends),
        compiler_params=params,
        name="pack",
    )(slot, digit, embeddings)
    first, second = exchange(packed, tiles) if direct else exchange_all(packed[0], me[0])
    other_first, other_second = (from_partner(rows, 1, "sub") for rows in (first, second))
    query = jnp.concatenate([first, second])
    asked = slots + clus_dev
    near = pl.pallas_call(
        functools.partial(near_kernel, rows_all, owner_map.shape[0], clus_dev, tiles),
        out_shape=[
            jax.ShapeDtypeStruct((width, slots), jnp.bfloat16),
            jax.ShapeDtypeStruct((asked, LANES), jnp.int32),
            jax.ShapeDtypeStruct((2, slots), jnp.int32),
            jax.ShapeDtypeStruct((1, slots), jnp.float32),
            jax.ShapeDtypeStruct((asked, width), jnp.float32),
            jax.ShapeDtypeStruct((asked, LANES), jnp.float32),
        ],
        in_specs=[SCALAR] + [WHOLE] * 3,
        out_specs=[WHOLE] * 6,
        compiler_params=params,
        cost_estimate=compare_cost,
        name="near",
    )(me, ints, query, other_first)
    results, norms = pl.pallas_call(
        functools.partial(far_kernel, rows_all, tiles),
        out_shape=[
            jax.ShapeDtypeStruct((owners // 2 if direct else owners, 2, slots), jnp.float32),
            jax.ShapeDtypeStruct((1, clus_dev), jnp.float32),
        ],
        in_specs=[WHOLE] * 8,
        out_specs=[WHOLE] * 2,
        compiler_params=params,
        cost_estimate=compare_cost,
        name="far",
    )(query, other_second, *near)
    if direct:
        lines = [list(range(side, owners, 2)) for side in (0, 1)]
        results = lax.all_to_all(results, "shard", 0, 0, axis_index_groups=lines, tiled=True)
        results = [results, from_partner(results, 1, "shard")]
    else:
        results = [lax.all_to_all(results, "shard", 0, 0, tiled=True)]
    best, distance, cohesion = pl.pallas_call(
        functools.partial(pick_kernel, order, parts),
        out_shape=[jax.ShapeDtypeStruct((1, local_rows), jnp.float32)] * 2
        + [jax.ShapeDtypeStruct((1, clus_dev), jnp.float32)],
        in_specs=[SCALAR] + [WHOLE] * (2 + len(results)),
        out_specs=[WHOLE] * 3,
        compiler_params=params,
        name="pick",
    )(me, slot, norms, *results)
    return best.reshape(local_rows), distance.reshape(local_rows), cohesion.reshape(clus_dev)


def solution(mesh):
    in_specs = (
        P(("groups", "shard", "sub"), None),
        P(("groups", "shard", "sub")),
        P(("groups", "shard", "sub")),
        P("groups"),
    )
    out_specs = (
        P(("groups", "shard", "sub")),
        P(("groups", "shard", "sub")),
        P(("groups", "shard")),
    )
    return jax.shard_map(local, mesh=mesh, in_specs=in_specs, out_specs=out_specs, check_vma=False)
```

```python
import functools

import jax
import jax.numpy as jnp
from jax import lax
from jax.experimental import pallas as pl
from jax.experimental.pallas import tpu as pltpu
from jax.sharding import PartitionSpec as P

LANES = 128
DIGITS = 3
SENDS = ((4,), (2, 3), (5,), (7,), (6,), (1,), (0,))
PARTNERS = (4, 2, 0, 5, 7, 6, 1, 3)
EARLY = 3
WHOLE = pl.BlockSpec(memory_space=pltpu.VMEM)
SCALAR = pl.BlockSpec(memory_space=pltpu.SMEM)


def iota(shape, dim):
    return lax.broadcasted_iota(jnp.int32, shape, dim)


def matmul(a, b):
    return jnp.dot(a, b, preferred_element_type=jnp.float32)


def matmul_t(a, b):
    return lax.dot_general(a, b, (((1,), (1,)), ((), ())), preferred_element_type=jnp.float32)


def bf16(x):
    return x.astype(jnp.float32).astype(jnp.bfloat16)


def ranked(hot):
    upto = (iota((LANES, LANES), 0) <= iota((LANES, LANES), 1)).astype(jnp.bfloat16)
    before, parts = jnp.zeros((1, 1), jnp.float32), []
    for start in range(0, hot.shape[1], LANES):
        piece = hot[:, start : start + LANES]
        spread = jnp.broadcast_to(piece, (16, LANES)).astype(jnp.bfloat16)
        parts.append(matmul(spread, upto)[:1] + before)
        before = before + jnp.sum(piece, axis=1, keepdims=True)
    return jnp.concatenate(parts, axis=1)


def slot_kernel(
    owners, capacity, order, parts, rows, me_ref, ints_ref, slot_ref, digit_ref
):
    clusters = ints_ref.shape[1] - 2 * rows
    cluster = ints_ref[:, clusters : clusters + rows]
    named = bf16(iota((clusters, rows), 0) == cluster)
    owner_map = bf16(jnp.broadcast_to(ints_ref[:, :clusters], (16, clusters)))
    owner = matmul(owner_map, named)[:1].astype(jnp.int32)
    hot = (iota((max(owners, 16), rows), 0) == owner).astype(jnp.float32)
    upto = bf16(iota((rows, rows), 0) <= iota((rows, rows), 1))
    rank = jnp.sum(hot * matmul(bf16(hot), upto), axis=0, keepdims=True) - 1.0
    rank = rank.astype(jnp.int32)
    partner = owner ^ me_ref[0]
    place = partner
    for index, k in enumerate(order):
        place = jnp.where(partner == k, index, place)
    if parts == 1:
        slot_ref[...] = place * capacity + rank
    else:
        half = capacity // 2
        later = (rank >= half).astype(jnp.int32)
        slot_ref[...] = place * half + rank + later * (owners * half - half)

    line = iota((8, rows), 0)
    digit = jnp.zeros((8, rows), jnp.int32)
    for first, number in ((0, cluster + 1), (DIGITS, ints_ref[:, clusters + rows :])):
        for at in range(DIGITS):
            digit = jnp.where(line == first + at, (number >> (8 * at)) & 255, digit)
    empty = jnp.zeros((LANES // 2 - 8, rows), jnp.int32)
    none = jnp.zeros((LANES // 2, rows), jnp.int32)
    early = jnp.concatenate([digit, empty, none], axis=0)
    late = jnp.concatenate([none, digit, empty], axis=0)
    digit_ref[...] = bf16(jnp.concatenate([early, late], axis=1))


def pack_kernel(sends, slot_ref, digit_ref, embed_ref, *out_refs):
    rows, width = embed_ref.shape
    half = out_refs[0].shape[1]
    tiles = 2 * (width // LANES) + 1
    values = embed_ref[...].astype(jnp.float32)
    mean_sq = jnp.sum(values * values, axis=1, keepdims=True) * (1.0 / width)
    unit = (values * lax.rsqrt(width * (mean_sq + 1e-06))).astype(jnp.bfloat16)
    late = half * sum(len(places) for places in sends)
    move = bf16(iota((2 * late, rows), 0) == slot_ref[...])
    moved = matmul(move, unit).astype(jnp.bfloat16)
    both = jnp.concatenate([move[:late], move[late:]], axis=1)
    digit = matmul_t(both, digit_ref[...]).astype(jnp.bfloat16)
    each = tiles // 2
    for places, out_ref in zip(sends, out_refs):
        for index, place in enumerate(places):
            base, start = index * tiles, place * half
            for tile in range(each):
                lanes = slice(tile * LANES, (tile + 1) * LANES)
                out_ref[base + tile] = moved[start : start + half, lanes]
                out_ref[base + each + tile] = moved[late + start : late + start + half, lanes]
            out_ref[base + tiles - 1] = digit[start : start + half]


def unpacked(block_ref, tiles):
    blocks, half = block_ref.shape[0] // tiles, block_ref.shape[1]
    each = tiles // 2
    empty = [jnp.zeros((half, LANES), block_ref.dtype)] * (-blocks % max(LANES // (2 * half), 1))

    def column(tile):
        return jnp.concatenate([block_ref[i * tiles + tile] for i in range(blocks)] + empty, axis=0)

    halves = [
        jnp.concatenate([column(first + tile) for tile in range(each)], axis=1)
        for first in (0, each)
    ]
    return jnp.concatenate(halves, axis=0), column(tiles - 1)


def weights(number, at, half):
    value = jnp.zeros(at.shape, jnp.float32)
    for place in range(DIGITS):
        for which in (0, 1):
            lane = half * (LANES // 2) + which * DIGITS + place
            value = jnp.where((at == lane) & (number == which), 256.0**place, value)
    return value.astype(jnp.bfloat16)


def key_rows(rows_all, digit):
    at = iota((16, LANES), 0), iota((16, LANES), 1)
    numbers = [matmul_t(weights(*at, half), digit) for half in (0, 1)]
    numbers = jnp.concatenate(numbers, axis=1)
    low = (numbers[0:1].astype(jnp.int32) - 1) * rows_all
    return low, low + numbers[1:2].astype(jnp.int32)


def key_columns(rows_all, digit):
    at = iota((LANES, 2 * LANES), 1) // LANES, iota((LANES, 2 * LANES), 0)
    numbers = [matmul(digit, weights(*at, half)) for half in (0, 1)]
    numbers = jnp.concatenate(numbers, axis=0)
    low = (numbers[:, :LANES].astype(jnp.int32) - 1) * rows_all
    return low, low + numbers[:, LANES:].astype(jnp.int32)


def across(column, count):
    return jnp.concatenate([column] * (count // LANES), axis=1)


def compare(rows_all, query_t, query_low, query_key, lows, parts):
    rows = jnp.concatenate([rows for rows, _ in parts], axis=0)
    key = jnp.concatenate([key_rows(rows_all, digit)[1] for _, digit in parts], axis=1)
    bound = across(lows, key.shape[1])
    member = bf16((key >= bound) & (key < bound + rows_all))
    sums = matmul(member, rows)
    counts = matmul(member, jnp.ones((rows.shape[0], LANES), jnp.bfloat16))
    scores = matmul(rows, query_t)
    key = jnp.concatenate([key_columns(rows_all, digit)[1] for _, digit in parts], axis=0)
    key = across(key, query_t.shape[1])
    earlier = (key >= query_low) & (key < query_key)
    best = jnp.max(jnp.where(earlier, scores, -3.0), axis=0, keepdims=True)
    return best, sums, counts


def near_kernel(
    rows_all, clusters, clus_dev, tiles, me_ref, ints_ref, query_ref, other_ref,
    query_t_ref, lows_ref, key_ref, best_ref, sums_ref, counts_ref,
):
    hot = (ints_ref[:, :clusters] == me_ref[0]).astype(jnp.float32)
    rank = ranked(hot)
    shape = (clus_dev, clusters)
    kth = (rank == iota(shape, 0).astype(jnp.float32) + 1.0) & (hot > 0.0)
    own = jnp.sum(jnp.where(kth, iota(shape, 1).astype(jnp.float32), 0.0), axis=1, keepdims=True)
    own = jnp.broadcast_to(own.astype(jnp.int32) * rows_all, (clus_dev, LANES))
    query, digit = unpacked(query_ref, tiles)
    low, _ = key_columns(rows_all, digit)
    lows = jnp.concatenate([low, own], axis=0)
    query_low, query_key = key_rows(rows_all, digit)
    query_t = jnp.transpose(query)
    query_t_ref[...] = query_t
    parts = [(query, digit), unpacked(other_ref, tiles)]
    best, sums, counts = compare(rows_all, query_t, query_low, query_key, lows, parts)
    lows_ref[...] = lows
    key_ref[...] = jnp.concatenate([query_low, query_key], axis=0)
    best_ref[...] = best
    sums_ref[...] = sums
    counts_ref[...] = counts


def far_kernel(
    rows_all, tiles, query_ref, other_ref, query_t_ref, lows_ref, key_ref, best_ref, sums_ref, counts_ref,
    result_ref, norm_ref,
):
    query, _ = unpacked(query_ref, tiles)
    queries, width = query.shape
    best, sums, counts = compare(
        rows_all, query_t_ref[...], key_ref[0:1], key_ref[1:2], lows_ref[...], [unpacked(other_ref, tiles)]
    )
    best = jnp.maximum(best, best_ref[...])
    best = jnp.where(best > -2.0, best, 0.0)
    share = 1.0 / jnp.maximum(counts + counts_ref[...], 1.0)
    squares = jnp.zeros((queries, LANES), jnp.float32)
    norms = jnp.zeros((share.shape[0] - queries, LANES), jnp.float32)
    for start in range(0, width, LANES):
        lanes = slice(start, start + LANES)
        centroid = (sums[:, lanes] + sums_ref[:, lanes]) * share
        offset = query[:, lanes].astype(jnp.float32) - centroid[:queries]
        squares = squares + offset * offset
        norms = norms + centroid[queries:] * centroid[queries:]
    distance = jnp.sum(jnp.transpose(squares), axis=0, keepdims=True)
    result = jnp.concatenate([best, distance], axis=0)
    for owner in range(result_ref.shape[0]):
        result_ref[owner] = result
    norms = jnp.concatenate([norms] * (LANES // norms.shape[0]), axis=0)
    norm_ref[...] = jnp.sum(jnp.transpose(norms), axis=0, keepdims=True)[:, : norm_ref.shape[1]]


def pick_kernel(
    order, parts, me_ref, slot_ref, result_ref, norm_ref, best_ref, distance_ref, cohesion_ref
):
    cohesion_ref[...] = norm_ref[...]
    rows = slot_ref.shape[1]
    owners, lines, slots = result_ref.shape
    folds = min(parts, 2)
    place = iota((lines, slots), 1) % (slots // folds) // (slots // owners // folds)
    values = jnp.zeros((lines, slots), jnp.float32)
    for index, k in enumerate(order):
        values = jnp.where(place == index, result_ref[me_ref[0] ^ k], values)
    values = jnp.concatenate([values, jnp.zeros((8 - lines, slots), jnp.float32)], axis=0)
    at = (iota((slots, rows), 0) == slot_ref[...]).astype(jnp.float32)
    picked = jnp.dot(
        values, at, precision=lax.Precision.HIGHEST, preferred_element_type=jnp.float32
    )
    best_ref[...] = picked[0:1]
    distance_ref[...] = picked[1:2]


def from_partner(value, k, axis):
    return lax.ppermute(value, axis, [(i, i ^ k) for i in range(lax.axis_size(axis))])


def exchange(packed, tiles):
    sent = dict(zip(SENDS, packed))
    got = {0: sent[0,]}
    for k in (4, 5, 7, 6):
        got[k] = from_partner(sent[k,], k, "shard")
    pair = from_partner(sent[2, 3], 2, "shard")
    got[2] = pair[:tiles]
    pair = from_partner(jnp.concatenate([sent[1,], pair[tiles:]]), 1, "shard")
    got[1], got[3] = pair[:tiles], pair[tiles:]
    got = [got[k] for k in PARTNERS]
    return jnp.concatenate(got[:EARLY]), jnp.concatenate(got[EARLY:])


def exchange_all(packed, me):
    owners = lax.axis_size("shard")
    tiles, half, _ = packed.shape
    each = tiles // 2
    data = packed[:-1].reshape(2, each, half, LANES).transpose(0, 2, 1, 3).reshape(2 * half, -1)
    digit = jnp.concatenate(jnp.split(packed[-1], 2, axis=1))
    parted = jnp.concatenate([data, digit], axis=1).reshape(owners, 2 * half // owners, -1)
    partner = me ^ jnp.arange(owners, dtype=jnp.int32)
    got = lax.all_to_all(parted[partner], "shard", 0, 0, tiled=True)[partner].reshape(2 * half, -1)
    data = got[:, : each * LANES].reshape(2, half, each, LANES).transpose(0, 2, 1, 3)
    digit = jnp.concatenate(jnp.split(got[:, each * LANES :], 2), axis=1)
    got = jnp.concatenate([data.reshape(2 * each, half, LANES), digit[None]])
    return jnp.split(got, 2, axis=1)


def local(embeddings, cluster_id, item_order, owner_map):
    owners = lax.axis_size("shard")
    local_rows, width = embeddings.shape
    rows_all = local_rows * owners * lax.axis_size("sub")
    clus_dev = owner_map.shape[0] // owners
    capacity = 2 * local_rows // owners
    slots = owners * capacity
    params = pltpu.CompilerParams(vmem_limit_bytes=32 << 20)
    compare_cost = pl.CostEstimate(
        flops=4 * slots * slots * width, bytes_accessed=4 * slots * width, transcendentals=0
    )
    me = lax.axis_index("shard").astype(jnp.int32).reshape(1)
    ints = jnp.concatenate([owner_map, cluster_id, item_order]).reshape(1, -1)

    direct = owners == len(PARTNERS)
    order = PARTNERS if direct else tuple(range(owners))
    parts = owners if direct else 1
    tiles = 2 * (width // LANES) + 1
    sends = [[PARTNERS.index(k) for k in ks] for ks in SENDS] if direct else [[0]]
    half = slots // parts // 2
    slot, digit = pl.pallas_call(
        functools.partial(slot_kernel, owners, capacity, order, parts, local_rows),
        out_shape=[
            jax.ShapeDtypeStruct((1, local_rows), jnp.int32),
            jax.ShapeDtypeStruct((LANES, 2 * local_rows), jnp.bfloat16),
        ],
        in_specs=[SCALAR, WHOLE],
        out_specs=[WHOLE] * 2,
        compiler_params=params,
        cost_estimate=pl.CostEstimate(flops=1 << 29, bytes_accessed=1 << 16, transcendentals=0),
        name="slots",
    )(me, ints)
    packed = pl.pallas_call(
        functools.partial(pack_kernel, sends),
        out_shape=[
            jax.ShapeDtypeStruct((len(places) * tiles, half, LANES), jnp.bfloat16) for places in sends
        ],
        in_specs=[WHOLE] * 3,
        out_specs=[WHOLE] * len(sends),
        compiler_params=params,
        name="pack",
    )(slot, digit, embeddings)
    first, second = exchange(packed, tiles) if direct else exchange_all(packed[0], me[0])
    other_first, other_second = (from_partner(rows, 1, "sub") for rows in (first, second))
    query = jnp.concatenate([first, second])
    asked = slots + clus_dev
    near = pl.pallas_call(
        functools.partial(near_kernel, rows_all, owner_map.shape[0], clus_dev, tiles),
        out_shape=[
            jax.ShapeDtypeStruct((width, slots), jnp.bfloat16),
            jax.ShapeDtypeStruct((asked, LANES), jnp.int32),
            jax.ShapeDtypeStruct((2, slots), jnp.int32),
            jax.ShapeDtypeStruct((1, slots), jnp.float32),
            jax.ShapeDtypeStruct((asked, width), jnp.float32),
            jax.ShapeDtypeStruct((asked, LANES), jnp.float32),
        ],
        in_specs=[SCALAR] + [WHOLE] * 3,
        out_specs=[WHOLE] * 6,
        compiler_params=params,
        cost_estimate=compare_cost,
        name="near",
    )(me, ints, query, other_first)
    results, norms = pl.pallas_call(
        functools.partial(far_kernel, rows_all, tiles),
        out_shape=[
            jax.ShapeDtypeStruct((owners, 2, slots), jnp.float32),
            jax.ShapeDtypeStruct((1, clus_dev), jnp.float32),
        ],
        in_specs=[WHOLE] * 8,
        out_specs=[WHOLE] * 2,
        compiler_params=params,
        cost_estimate=compare_cost,
        name="far",
    )(query, other_second, *near)
    results = lax.all_to_all(results, "shard", 0, 0, tiled=True)
    best, distance, cohesion = pl.pallas_call(
        functools.partial(pick_kernel, order, parts),
        out_shape=[jax.ShapeDtypeStruct((1, local_rows), jnp.float32)] * 2
        + [jax.ShapeDtypeStruct((1, clus_dev), jnp.float32)],
        in_specs=[SCALAR] + [WHOLE] * 3,
        out_specs=[WHOLE] * 3,
        compiler_params=params,
        name="pick",
    )(me, slot, results, norms)
    return best.reshape(local_rows), distance.reshape(local_rows), cohesion.reshape(clus_dev)


def solution(mesh):
    in_specs = (
        P(("groups", "shard", "sub"), None),
        P(("groups", "shard", "sub")),
        P(("groups", "shard", "sub")),
        P("groups"),
    )
    out_specs = (
        P(("groups", "shard", "sub")),
        P(("groups", "shard", "sub")),
        P(("groups", "shard")),
    )
    return jax.shard_map(local, mesh=mesh, in_specs=in_specs, out_specs=out_specs, check_vma=False)
```

```python
import functools

import jax
import jax.numpy as jnp
from jax import lax
from jax.experimental import pallas as pl
from jax.experimental.pallas import tpu as pltpu
from jax.sharding import PartitionSpec as P

LANES = 128
DIGITS = 3
SENDS = ((4,), (2, 3), (5,), (7,), (6,), (1,), (0,))
PARTNERS = (4, 2, 0, 5, 7, 6, 1, 3)
WHOLE = pl.BlockSpec(memory_space=pltpu.VMEM)
SCALAR = pl.BlockSpec(memory_space=pltpu.SMEM)


def iota(shape, dim):
    return lax.broadcasted_iota(jnp.int32, shape, dim)


def matmul(a, b):
    return jnp.dot(a, b, preferred_element_type=jnp.float32)


def matmul_t(a, b):
    return lax.dot_general(a, b, (((1,), (1,)), ((), ())), preferred_element_type=jnp.float32)


def bf16(x):
    return x.astype(jnp.float32).astype(jnp.bfloat16)


def ranked(hot):
    upto = (iota((LANES, LANES), 0) <= iota((LANES, LANES), 1)).astype(jnp.bfloat16)
    before, parts = jnp.zeros((1, 1), jnp.float32), []
    for start in range(0, hot.shape[1], LANES):
        piece = hot[:, start : start + LANES]
        spread = jnp.broadcast_to(piece, (16, LANES)).astype(jnp.bfloat16)
        parts.append(matmul(spread, upto)[:1] + before)
        before = before + jnp.sum(piece, axis=1, keepdims=True)
    return jnp.concatenate(parts, axis=1)


def slot_kernel(
    owners, capacity, order, parts, rows, me_ref, ints_ref, slot_ref, digit_ref
):
    clusters = ints_ref.shape[1] - 2 * rows
    cluster = ints_ref[:, clusters : clusters + rows]
    named = bf16(iota((clusters, rows), 0) == cluster)
    owner_map = bf16(jnp.broadcast_to(ints_ref[:, :clusters], (16, clusters)))
    owner = matmul(owner_map, named)[:1].astype(jnp.int32)
    hot = (iota((max(owners, 16), rows), 0) == owner).astype(jnp.float32)
    upto = bf16(iota((rows, rows), 0) <= iota((rows, rows), 1))
    rank = jnp.sum(hot * matmul(bf16(hot), upto), axis=0, keepdims=True) - 1.0
    rank = rank.astype(jnp.int32)
    partner = owner ^ me_ref[0]
    place = partner
    for index, k in enumerate(order):
        place = jnp.where(partner == k, index, place)
    if parts == 1:
        slot_ref[...] = place * capacity + rank
    else:
        half = capacity // 2
        later = (rank >= half).astype(jnp.int32)
        slot_ref[...] = place * half + rank + later * (owners * half - half)

    line = iota((8, rows), 0)
    digit = jnp.zeros((8, rows), jnp.int32)
    for first, number in ((0, cluster + 1), (DIGITS, ints_ref[:, clusters + rows :])):
        for at in range(DIGITS):
            digit = jnp.where(line == first + at, (number >> (8 * at)) & 255, digit)
    empty = jnp.zeros((LANES // 2 - 8, rows), jnp.int32)
    none = jnp.zeros((LANES // 2, rows), jnp.int32)
    early = jnp.concatenate([digit, empty, none], axis=0)
    late = jnp.concatenate([none, digit, empty], axis=0)
    digit_ref[...] = bf16(jnp.concatenate([early, late], axis=1))


def pack_kernel(sends, slot_ref, digit_ref, embed_ref, *out_refs):
    rows, width = embed_ref.shape
    half = out_refs[0].shape[1]
    tiles = 2 * (width // LANES) + 1
    values = embed_ref[...].astype(jnp.float32)
    mean_sq = jnp.sum(values * values, axis=1, keepdims=True) * (1.0 / width)
    unit = (values * lax.rsqrt(width * (mean_sq + 1e-06))).astype(jnp.bfloat16)
    late = half * sum(len(places) for places in sends)
    move = bf16(iota((2 * late, rows), 0) == slot_ref[...])
    moved = matmul(move, unit).astype(jnp.bfloat16)
    both = jnp.concatenate([move[:late], move[late:]], axis=1)
    digit = matmul_t(both, digit_ref[...]).astype(jnp.bfloat16)
    each = tiles // 2
    for places, out_ref in zip(sends, out_refs):
        for index, place in enumerate(places):
            base, start = index * tiles, place * half
            for tile in range(each):
                lanes = slice(tile * LANES, (tile + 1) * LANES)
                out_ref[base + tile] = moved[start : start + half, lanes]
                out_ref[base + each + tile] = moved[late + start : late + start + half, lanes]
            out_ref[base + tiles - 1] = digit[start : start + half]


def unpacked(block_ref, tiles):
    blocks = block_ref.shape[0] // tiles
    each = tiles // 2

    def column(tile):
        return jnp.concatenate([block_ref[i * tiles + tile] for i in range(blocks)], axis=0)

    halves = [
        jnp.concatenate([column(first + tile) for tile in range(each)], axis=1)
        for first in (0, each)
    ]
    return jnp.concatenate(halves, axis=0), column(tiles - 1)


def weights(number, at, half):
    value = jnp.zeros(at.shape, jnp.float32)
    for place in range(DIGITS):
        for which in (0, 1):
            lane = half * (LANES // 2) + which * DIGITS + place
            value = jnp.where((at == lane) & (number == which), 256.0**place, value)
    return value.astype(jnp.bfloat16)


def key_rows(rows_all, digit):
    at = iota((16, LANES), 0), iota((16, LANES), 1)
    numbers = [matmul_t(weights(*at, half), digit) for half in (0, 1)]
    numbers = jnp.concatenate(numbers, axis=1)
    low = (numbers[0:1].astype(jnp.int32) - 1) * rows_all
    return low, low + numbers[1:2].astype(jnp.int32)


def key_columns(rows_all, digit):
    at = iota((LANES, 2 * LANES), 1) // LANES, iota((LANES, 2 * LANES), 0)
    numbers = [matmul(digit, weights(*at, half)) for half in (0, 1)]
    numbers = jnp.concatenate(numbers, axis=0)
    low = (numbers[:, :LANES].astype(jnp.int32) - 1) * rows_all
    return low, low + numbers[:, LANES:].astype(jnp.int32)


def across(column, count):
    return jnp.concatenate([column] * (count // LANES), axis=1)


def compare(rows_all, query_t, query_low, query_key, lows, parts):
    rows = jnp.concatenate([rows for rows, _ in parts], axis=0)
    key = jnp.concatenate([key_rows(rows_all, digit)[1] for _, digit in parts], axis=1)
    bound = across(lows, key.shape[1])
    member = bf16((key >= bound) & (key < bound + rows_all))
    sums = matmul(member, rows)
    counts = matmul(member, jnp.ones((rows.shape[0], LANES), jnp.bfloat16))
    scores = matmul(rows, query_t)
    key = jnp.concatenate([key_columns(rows_all, digit)[1] for _, digit in parts], axis=0)
    key = across(key, query_t.shape[1])
    earlier = (key >= query_low) & (key < query_key)
    best = jnp.max(jnp.where(earlier, scores, -3.0), axis=0, keepdims=True)
    return best, sums, counts


def near_kernel(
    rows_all, clusters, clus_dev, tiles, me_ref, ints_ref, query_ref, other_ref,
    query_t_ref, lows_ref, key_ref, best_ref, sums_ref, counts_ref,
):
    hot = (ints_ref[:, :clusters] == me_ref[0]).astype(jnp.float32)
    rank = ranked(hot)
    shape = (clus_dev, clusters)
    kth = (rank == iota(shape, 0).astype(jnp.float32) + 1.0) & (hot > 0.0)
    own = jnp.sum(jnp.where(kth, iota(shape, 1).astype(jnp.float32), 0.0), axis=1, keepdims=True)
    own = jnp.broadcast_to(own.astype(jnp.int32) * rows_all, (clus_dev, LANES))
    query, digit = unpacked(query_ref, tiles)
    low, _ = key_columns(rows_all, digit)
    lows = jnp.concatenate([low, own], axis=0)
    query_low, query_key = key_rows(rows_all, digit)
    query_t = jnp.transpose(query)
    query_t_ref[...] = query_t
    parts = [(query, digit), unpacked(other_ref, tiles)]
    best, sums, counts = compare(rows_all, query_t, query_low, query_key, lows, parts)
    lows_ref[...] = lows
    key_ref[...] = jnp.concatenate([query_low, query_key], axis=0)
    best_ref[...] = best
    sums_ref[...] = sums
    counts_ref[...] = counts


def far_kernel(
    rows_all, tiles, query_ref, other_ref, query_t_ref, lows_ref, key_ref, best_ref, sums_ref, counts_ref,
    result_ref, norm_ref,
):
    query, _ = unpacked(query_ref, tiles)
    queries, width = query.shape
    best, sums, counts = compare(
        rows_all, query_t_ref[...], key_ref[0:1], key_ref[1:2], lows_ref[...], [unpacked(other_ref, tiles)]
    )
    best = jnp.maximum(best, best_ref[...])
    best = jnp.where(best > -2.0, best, 0.0)
    share = 1.0 / jnp.maximum(counts + counts_ref[...], 1.0)
    squares = jnp.zeros((queries, LANES), jnp.float32)
    norms = jnp.zeros((share.shape[0] - queries, LANES), jnp.float32)
    for start in range(0, width, LANES):
        lanes = slice(start, start + LANES)
        centroid = (sums[:, lanes] + sums_ref[:, lanes]) * share
        offset = query[:, lanes].astype(jnp.float32) - centroid[:queries]
        squares = squares + offset * offset
        norms = norms + centroid[queries:] * centroid[queries:]
    distance = jnp.sum(jnp.transpose(squares), axis=0, keepdims=True)
    result = jnp.concatenate([best, distance], axis=0)
    for owner in range(result_ref.shape[0]):
        result_ref[owner] = result
    norms = jnp.concatenate([norms] * (LANES // norms.shape[0]), axis=0)
    norm_ref[...] = jnp.sum(jnp.transpose(norms), axis=0, keepdims=True)[:, : norm_ref.shape[1]]


def pick_kernel(
    order, parts, me_ref, slot_ref, result_ref, norm_ref, best_ref, distance_ref, cohesion_ref
):
    cohesion_ref[...] = norm_ref[...]
    rows = slot_ref.shape[1]
    owners, lines, slots = result_ref.shape
    folds = min(parts, 2)
    place = iota((lines, slots), 1) % (slots // folds) // (slots // owners // folds)
    values = jnp.zeros((lines, slots), jnp.float32)
    for index, k in enumerate(order):
        values = jnp.where(place == index, result_ref[owners - 1 - (me_ref[0] ^ k)], values)
    values = jnp.concatenate([values, jnp.zeros((8 - lines, slots), jnp.float32)], axis=0)
    at = (iota((slots, rows), 0) == slot_ref[...]).astype(jnp.float32)
    picked = jnp.dot(
        values, at, precision=lax.Precision.HIGHEST, preferred_element_type=jnp.float32
    )
    best_ref[...] = picked[0:1]
    distance_ref[...] = picked[1:2]


def from_partner(value, k, axis):
    return lax.ppermute(value, axis, [(i, i ^ k) for i in range(lax.axis_size(axis))])


def exchange(packed, tiles):
    sent = dict(zip(SENDS, packed))
    got = {0: sent[0,]}
    for k in (4, 5, 7, 6):
        got[k] = from_partner(sent[k,], k, "shard")
    pair = from_partner(sent[2, 3], 2, "shard")
    got[2] = pair[:tiles]
    pair = from_partner(jnp.concatenate([sent[1,], pair[tiles:]]), 1, "shard")
    got[1], got[3] = pair[:tiles], pair[tiles:]
    got = [got[k] for k in PARTNERS]
    half = len(got) // 2
    return jnp.concatenate(got[:half]), jnp.concatenate(got[half:])


def exchange_all(packed, me):
    owners = lax.axis_size("shard")
    tiles, half, _ = packed.shape
    each = tiles // 2
    data = packed[:-1].reshape(2, each, half, LANES).transpose(0, 2, 1, 3).reshape(2 * half, -1)
    digit = jnp.concatenate(jnp.split(packed[-1], 2, axis=1))
    parted = jnp.concatenate([data, digit], axis=1).reshape(owners, 2 * half // owners, -1)
    partner = me ^ jnp.arange(owners, dtype=jnp.int32)
    got = lax.all_to_all(parted[partner], "shard", 0, 0, tiled=True)[partner].reshape(2 * half, -1)
    data = got[:, : each * LANES].reshape(2, half, each, LANES).transpose(0, 2, 1, 3)
    digit = jnp.concatenate(jnp.split(got[:, each * LANES :], 2), axis=1)
    got = jnp.concatenate([data.reshape(2 * each, half, LANES), digit[None]])
    return jnp.split(got, 2, axis=1)


def local(embeddings, cluster_id, item_order, owner_map):
    owners = lax.axis_size("shard")
    local_rows, width = embeddings.shape
    rows_all = local_rows * owners * lax.axis_size("sub")
    clus_dev = owner_map.shape[0] // owners
    capacity = 2 * local_rows // owners
    slots = owners * capacity
    params = pltpu.CompilerParams(vmem_limit_bytes=32 << 20)
    compare_cost = pl.CostEstimate(
        flops=4 * slots * slots * width, bytes_accessed=4 * slots * width, transcendentals=0
    )
    me = lax.axis_index("shard").astype(jnp.int32).reshape(1)
    ints = jnp.concatenate([owner_map, cluster_id, item_order]).reshape(1, -1)

    direct = owners == len(PARTNERS)
    order = PARTNERS if direct else tuple(range(owners))
    parts = owners if direct else 1
    tiles = 2 * (width // LANES) + 1
    sends = [[PARTNERS.index(k) for k in ks] for ks in SENDS] if direct else [[0]]
    half = slots // parts // 2
    slot, digit = pl.pallas_call(
        functools.partial(slot_kernel, owners, capacity, order, parts, local_rows),
        out_shape=[
            jax.ShapeDtypeStruct((1, local_rows), jnp.int32),
            jax.ShapeDtypeStruct((LANES, 2 * local_rows), jnp.bfloat16),
        ],
        in_specs=[SCALAR, WHOLE],
        out_specs=[WHOLE] * 2,
        compiler_params=params,
        cost_estimate=pl.CostEstimate(flops=1 << 29, bytes_accessed=1 << 16, transcendentals=0),
        name="slots",
    )(me, ints)
    packed = pl.pallas_call(
        functools.partial(pack_kernel, sends),
        out_shape=[
            jax.ShapeDtypeStruct((len(places) * tiles, half, LANES), jnp.bfloat16) for places in sends
        ],
        in_specs=[WHOLE] * 3,
        out_specs=[WHOLE] * len(sends),
        compiler_params=params,
        name="pack",
    )(slot, digit, embeddings)
    first, second = exchange(packed, tiles) if direct else exchange_all(packed[0], me[0])
    other_first, other_second = (from_partner(rows, 1, "sub") for rows in (first, second))
    query = jnp.concatenate([first, second])
    asked = slots + clus_dev
    near = pl.pallas_call(
        functools.partial(near_kernel, rows_all, owner_map.shape[0], clus_dev, tiles),
        out_shape=[
            jax.ShapeDtypeStruct((width, slots), jnp.bfloat16),
            jax.ShapeDtypeStruct((asked, LANES), jnp.int32),
            jax.ShapeDtypeStruct((2, slots), jnp.int32),
            jax.ShapeDtypeStruct((1, slots), jnp.float32),
            jax.ShapeDtypeStruct((asked, width), jnp.float32),
            jax.ShapeDtypeStruct((asked, LANES), jnp.float32),
        ],
        in_specs=[SCALAR] + [WHOLE] * 3,
        out_specs=[WHOLE] * 6,
        compiler_params=params,
        cost_estimate=compare_cost,
        name="near",
    )(me, ints, query, other_first)
    results, norms = pl.pallas_call(
        functools.partial(far_kernel, rows_all, tiles),
        out_shape=[
            jax.ShapeDtypeStruct((owners, 2, slots), jnp.float32),
            jax.ShapeDtypeStruct((1, clus_dev), jnp.float32),
        ],
        in_specs=[WHOLE] * 8,
        out_specs=[WHOLE] * 2,
        compiler_params=params,
        cost_estimate=compare_cost,
        name="far",
    )(query, other_second, *near)
    members = [list(range(owners - 1, -1, -1))]
    results = lax.all_to_all(results, "shard", 0, 0, axis_index_groups=members, tiled=True)
    best, distance, cohesion = pl.pallas_call(
        functools.partial(pick_kernel, order, parts),
        out_shape=[jax.ShapeDtypeStruct((1, local_rows), jnp.float32)] * 2
        + [jax.ShapeDtypeStruct((1, clus_dev), jnp.float32)],
        in_specs=[SCALAR] + [WHOLE] * 3,
        out_specs=[WHOLE] * 3,
        compiler_params=params,
        name="pick",
    )(me, slot, results, norms)
    return best.reshape(local_rows), distance.reshape(local_rows), cohesion.reshape(clus_dev)


def solution(mesh):
    in_specs = (
        P(("groups", "shard", "sub"), None),
        P(("groups", "shard", "sub")),
        P(("groups", "shard", "sub")),
        P("groups"),
    )
    out_specs = (
        P(("groups", "shard", "sub")),
        P(("groups", "shard", "sub")),
        P(("groups", "shard")),
    )
    return jax.shard_map(local, mesh=mesh, in_specs=in_specs, out_specs=out_specs, check_vma=False)
```

```python
import functools

import jax
import jax.numpy as jnp
from jax import lax
from jax.experimental import pallas as pl
from jax.experimental.pallas import tpu as pltpu
from jax.sharding import PartitionSpec as P

LANES = 128
DIGITS = 3
SENDS = ((4,), (2, 3), (5,), (7,), (6,), (1,), (0,))
PARTNERS = (4, 2, 0, 5, 7, 6, 1, 3)
WHOLE = pl.BlockSpec(memory_space=pltpu.VMEM)
SCALAR = pl.BlockSpec(memory_space=pltpu.SMEM)


def iota(shape, dim):
    return lax.broadcasted_iota(jnp.int32, shape, dim)


def matmul(a, b):
    return jnp.dot(a, b, preferred_element_type=jnp.float32)


def matmul_t(a, b):
    return lax.dot_general(a, b, (((1,), (1,)), ((), ())), preferred_element_type=jnp.float32)


def bf16(x):
    return x.astype(jnp.float32).astype(jnp.bfloat16)


def ranked(hot):
    upto = (iota((LANES, LANES), 0) <= iota((LANES, LANES), 1)).astype(jnp.bfloat16)
    before, parts = jnp.zeros((1, 1), jnp.float32), []
    for start in range(0, hot.shape[1], LANES):
        piece = hot[:, start : start + LANES]
        spread = jnp.broadcast_to(piece, (16, LANES)).astype(jnp.bfloat16)
        parts.append(matmul(spread, upto)[:1] + before)
        before = before + jnp.sum(piece, axis=1, keepdims=True)
    return jnp.concatenate(parts, axis=1)


def slot_kernel(
    owners, capacity, order, parts, rows, me_ref, ints_ref, slot_ref, digit_ref
):
    clusters = ints_ref.shape[1] - 2 * rows
    cluster = ints_ref[:, clusters : clusters + rows]
    named = bf16(iota((clusters, rows), 0) == cluster)
    owner_map = bf16(jnp.broadcast_to(ints_ref[:, :clusters], (16, clusters)))
    owner = matmul(owner_map, named)[:1].astype(jnp.int32)
    hot = (iota((max(owners, 16), rows), 0) == owner).astype(jnp.float32)
    upto = bf16(iota((rows, rows), 0) <= iota((rows, rows), 1))
    rank = jnp.sum(hot * matmul(bf16(hot), upto), axis=0, keepdims=True) - 1.0
    rank = rank.astype(jnp.int32)
    partner = owner ^ me_ref[0]
    place = partner
    for index, k in enumerate(order):
        place = jnp.where(partner == k, index, place)
    if parts == 1:
        slot_ref[...] = place * capacity + rank
    else:
        half = capacity // 2
        later = (rank >= half).astype(jnp.int32)
        slot_ref[...] = place * half + rank + later * (owners * half - half)

    line = iota((8, rows), 0)
    digit = jnp.zeros((8, rows), jnp.int32)
    for first, number in ((0, cluster + 1), (DIGITS, ints_ref[:, clusters + rows :])):
        for at in range(DIGITS):
            digit = jnp.where(line == first + at, (number >> (8 * at)) & 255, digit)
    empty = jnp.zeros((LANES // 2 - 8, rows), jnp.int32)
    none = jnp.zeros((LANES // 2, rows), jnp.int32)
    early = jnp.concatenate([digit, empty, none], axis=0)
    late = jnp.concatenate([none, digit, empty], axis=0)
    digit_ref[...] = bf16(jnp.concatenate([early, late], axis=1))


def pack_kernel(sends, slot_ref, digit_ref, embed_ref, *out_refs):
    rows, width = embed_ref.shape
    half = out_refs[0].shape[1]
    tiles = 2 * (width // LANES) + 1
    values = embed_ref[...].astype(jnp.float32)
    mean_sq = jnp.sum(values * values, axis=1, keepdims=True) * (1.0 / width)
    unit = (values * lax.rsqrt(width * (mean_sq + 1e-06))).astype(jnp.bfloat16)
    late = half * sum(len(places) for places in sends)
    move = bf16(iota((2 * late, rows), 0) == slot_ref[...])
    moved = matmul(move, unit).astype(jnp.bfloat16)
    both = jnp.concatenate([move[:late], move[late:]], axis=1)
    digit = matmul_t(both, digit_ref[...]).astype(jnp.bfloat16)
    each = tiles // 2
    for places, out_ref in zip(sends, out_refs):
        for index, place in enumerate(places):
            base, start = index * tiles, place * half
            for tile in range(each):
                lanes = slice(tile * LANES, (tile + 1) * LANES)
                out_ref[base + tile] = moved[start : start + half, lanes]
                out_ref[base + each + tile] = moved[late + start : late + start + half, lanes]
            out_ref[base + tiles - 1] = digit[start : start + half]


def unpacked(block_ref, tiles):
    blocks = block_ref.shape[0] // tiles
    each = tiles // 2

    def column(tile):
        return jnp.concatenate([block_ref[i * tiles + tile] for i in range(blocks)], axis=0)

    halves = [
        jnp.concatenate([column(first + tile) for tile in range(each)], axis=1)
        for first in (0, each)
    ]
    return jnp.concatenate(halves, axis=0), column(tiles - 1)


def weights(number, at, half):
    value = jnp.zeros(at.shape, jnp.float32)
    for place in range(DIGITS):
        for which in (0, 1):
            lane = half * (LANES // 2) + which * DIGITS + place
            value = jnp.where((at == lane) & (number == which), 256.0**place, value)
    return value.astype(jnp.bfloat16)


def key_rows(rows_all, digit):
    at = iota((16, LANES), 0), iota((16, LANES), 1)
    numbers = [matmul_t(weights(*at, half), digit) for half in (0, 1)]
    numbers = jnp.concatenate(numbers, axis=1)
    low = (numbers[0:1].astype(jnp.int32) - 1) * rows_all
    return low, low + numbers[1:2].astype(jnp.int32)


def key_columns(rows_all, digit):
    at = iota((LANES, 2 * LANES), 1) // LANES, iota((LANES, 2 * LANES), 0)
    numbers = [matmul(digit, weights(*at, half)) for half in (0, 1)]
    numbers = jnp.concatenate(numbers, axis=0)
    low = (numbers[:, :LANES].astype(jnp.int32) - 1) * rows_all
    return low, low + numbers[:, LANES:].astype(jnp.int32)


def across(column, count):
    return jnp.concatenate([column] * (count // LANES), axis=1)


def compare(rows_all, query_t, query_low, query_key, lows, parts):
    rows = jnp.concatenate([rows for rows, _ in parts], axis=0)
    key = jnp.concatenate([key_rows(rows_all, digit)[1] for _, digit in parts], axis=1)
    bound = across(lows, key.shape[1])
    member = bf16((key >= bound) & (key < bound + rows_all))
    sums = matmul(member, rows)
    counts = matmul(member, jnp.ones((rows.shape[0], LANES), jnp.bfloat16))
    scores = matmul(rows, query_t)
    key = jnp.concatenate([key_columns(rows_all, digit)[1] for _, digit in parts], axis=0)
    key = across(key, query_t.shape[1])
    earlier = (key >= query_low) & (key < query_key)
    best = jnp.max(jnp.where(earlier, scores, -3.0), axis=0, keepdims=True)
    return best, sums, counts


def near_kernel(
    rows_all, clusters, clus_dev, tiles, me_ref, ints_ref, query_ref, other_ref,
    query_t_ref, lows_ref, key_ref, best_ref, sums_ref, counts_ref,
):
    hot = (ints_ref[:, :clusters] == me_ref[0]).astype(jnp.float32)
    rank = ranked(hot)
    shape = (clus_dev, clusters)
    kth = (rank == iota(shape, 0).astype(jnp.float32) + 1.0) & (hot > 0.0)
    own = jnp.sum(jnp.where(kth, iota(shape, 1).astype(jnp.float32), 0.0), axis=1, keepdims=True)
    own = jnp.broadcast_to(own.astype(jnp.int32) * rows_all, (clus_dev, LANES))
    query, digit = unpacked(query_ref, tiles)
    low, _ = key_columns(rows_all, digit)
    lows = jnp.concatenate([low, own], axis=0)
    query_low, query_key = key_rows(rows_all, digit)
    query_t = jnp.transpose(query)
    query_t_ref[...] = query_t
    parts = [(query, digit), unpacked(other_ref, tiles)]
    best, sums, counts = compare(rows_all, query_t, query_low, query_key, lows, parts)
    lows_ref[...] = lows
    key_ref[...] = jnp.concatenate([query_low, query_key], axis=0)
    best_ref[...] = best
    sums_ref[...] = sums
    counts_ref[...] = counts


def far_kernel(
    rows_all, tiles, query_ref, other_ref, query_t_ref, lows_ref, key_ref, best_ref, sums_ref, counts_ref,
    result_ref, norm_ref,
):
    query, _ = unpacked(query_ref, tiles)
    queries, width = query.shape
    best, sums, counts = compare(
        rows_all, query_t_ref[...], key_ref[0:1], key_ref[1:2], lows_ref[...], [unpacked(other_ref, tiles)]
    )
    best = jnp.maximum(best, best_ref[...])
    best = jnp.where(best > -2.0, best, 0.0)
    share = 1.0 / jnp.maximum(counts + counts_ref[...], 1.0)
    squares = jnp.zeros((queries, LANES), jnp.float32)
    norms = jnp.zeros((share.shape[0] - queries, LANES), jnp.float32)
    for start in range(0, width, LANES):
        lanes = slice(start, start + LANES)
        centroid = (sums[:, lanes] + sums_ref[:, lanes]) * share
        offset = query[:, lanes].astype(jnp.float32) - centroid[:queries]
        squares = squares + offset * offset
        norms = norms + centroid[queries:] * centroid[queries:]
    distance = jnp.sum(jnp.transpose(squares), axis=0, keepdims=True)
    result = jnp.concatenate([best, distance], axis=0)
    for owner in range(result_ref.shape[0]):
        result_ref[owner] = result
    norms = jnp.concatenate([norms] * (LANES // norms.shape[0]), axis=0)
    norm_ref[...] = jnp.sum(jnp.transpose(norms), axis=0, keepdims=True)[:, : norm_ref.shape[1]]


def pick_kernel(
    order, parts, me_ref, slot_ref, result_ref, norm_ref, best_ref, distance_ref, cohesion_ref
):
    cohesion_ref[...] = norm_ref[...]
    rows = slot_ref.shape[1]
    owners, lines, slots = result_ref.shape
    folds = min(parts, 2)
    place = iota((lines, slots), 1) % (slots // folds) // (slots // owners // folds)
    values = jnp.zeros((lines, slots), jnp.float32)
    for index, k in enumerate(order):
        values = jnp.where(place == index, result_ref[((me_ref[0] ^ k) + owners - 1) % owners], values)
    values = jnp.concatenate([values, jnp.zeros((8 - lines, slots), jnp.float32)], axis=0)
    at = (iota((slots, rows), 0) == slot_ref[...]).astype(jnp.float32)
    picked = jnp.dot(
        values, at, precision=lax.Precision.HIGHEST, preferred_element_type=jnp.float32
    )
    best_ref[...] = picked[0:1]
    distance_ref[...] = picked[1:2]


def from_partner(value, k, axis):
    return lax.ppermute(value, axis, [(i, i ^ k) for i in range(lax.axis_size(axis))])


def exchange(packed, tiles):
    sent = dict(zip(SENDS, packed))
    got = {0: sent[0,]}
    for k in (4, 5, 7, 6):
        got[k] = from_partner(sent[k,], k, "shard")
    pair = from_partner(sent[2, 3], 2, "shard")
    got[2] = pair[:tiles]
    pair = from_partner(jnp.concatenate([sent[1,], pair[tiles:]]), 1, "shard")
    got[1], got[3] = pair[:tiles], pair[tiles:]
    got = [got[k] for k in PARTNERS]
    half = len(got) // 2
    return jnp.concatenate(got[:half]), jnp.concatenate(got[half:])


def exchange_all(packed, me):
    owners = lax.axis_size("shard")
    tiles, half, _ = packed.shape
    each = tiles // 2
    data = packed[:-1].reshape(2, each, half, LANES).transpose(0, 2, 1, 3).reshape(2 * half, -1)
    digit = jnp.concatenate(jnp.split(packed[-1], 2, axis=1))
    parted = jnp.concatenate([data, digit], axis=1).reshape(owners, 2 * half // owners, -1)
    partner = me ^ jnp.arange(owners, dtype=jnp.int32)
    got = lax.all_to_all(parted[partner], "shard", 0, 0, tiled=True)[partner].reshape(2 * half, -1)
    data = got[:, : each * LANES].reshape(2, half, each, LANES).transpose(0, 2, 1, 3)
    digit = jnp.concatenate(jnp.split(got[:, each * LANES :], 2), axis=1)
    got = jnp.concatenate([data.reshape(2 * each, half, LANES), digit[None]])
    return jnp.split(got, 2, axis=1)


def local(embeddings, cluster_id, item_order, owner_map):
    owners = lax.axis_size("shard")
    local_rows, width = embeddings.shape
    rows_all = local_rows * owners * lax.axis_size("sub")
    clus_dev = owner_map.shape[0] // owners
    capacity = 2 * local_rows // owners
    slots = owners * capacity
    params = pltpu.CompilerParams(vmem_limit_bytes=32 << 20)
    compare_cost = pl.CostEstimate(
        flops=4 * slots * slots * width, bytes_accessed=4 * slots * width, transcendentals=0
    )
    me = lax.axis_index("shard").astype(jnp.int32).reshape(1)
    ints = jnp.concatenate([owner_map, cluster_id, item_order]).reshape(1, -1)

    direct = owners == len(PARTNERS)
    order = PARTNERS if direct else tuple(range(owners))
    parts = owners if direct else 1
    tiles = 2 * (width // LANES) + 1
    sends = [[PARTNERS.index(k) for k in ks] for ks in SENDS] if direct else [[0]]
    half = slots // parts // 2
    slot, digit = pl.pallas_call(
        functools.partial(slot_kernel, owners, capacity, order, parts, local_rows),
        out_shape=[
            jax.ShapeDtypeStruct((1, local_rows), jnp.int32),
            jax.ShapeDtypeStruct((LANES, 2 * local_rows), jnp.bfloat16),
        ],
        in_specs=[SCALAR, WHOLE],
        out_specs=[WHOLE] * 2,
        compiler_params=params,
        cost_estimate=pl.CostEstimate(flops=1 << 29, bytes_accessed=1 << 16, transcendentals=0),
        name="slots",
    )(me, ints)
    packed = pl.pallas_call(
        functools.partial(pack_kernel, sends),
        out_shape=[
            jax.ShapeDtypeStruct((len(places) * tiles, half, LANES), jnp.bfloat16) for places in sends
        ],
        in_specs=[WHOLE] * 3,
        out_specs=[WHOLE] * len(sends),
        compiler_params=params,
        name="pack",
    )(slot, digit, embeddings)
    first, second = exchange(packed, tiles) if direct else exchange_all(packed[0], me[0])
    other_first, other_second = (from_partner(rows, 1, "sub") for rows in (first, second))
    query = jnp.concatenate([first, second])
    asked = slots + clus_dev
    near = pl.pallas_call(
        functools.partial(near_kernel, rows_all, owner_map.shape[0], clus_dev, tiles),
        out_shape=[
            jax.ShapeDtypeStruct((width, slots), jnp.bfloat16),
            jax.ShapeDtypeStruct((asked, LANES), jnp.int32),
            jax.ShapeDtypeStruct((2, slots), jnp.int32),
            jax.ShapeDtypeStruct((1, slots), jnp.float32),
            jax.ShapeDtypeStruct((asked, width), jnp.float32),
            jax.ShapeDtypeStruct((asked, LANES), jnp.float32),
        ],
        in_specs=[SCALAR] + [WHOLE] * 3,
        out_specs=[WHOLE] * 6,
        compiler_params=params,
        cost_estimate=compare_cost,
        name="near",
    )(me, ints, query, other_first)
    results, norms = pl.pallas_call(
        functools.partial(far_kernel, rows_all, tiles),
        out_shape=[
            jax.ShapeDtypeStruct((owners, 2, slots), jnp.float32),
            jax.ShapeDtypeStruct((1, clus_dev), jnp.float32),
        ],
        in_specs=[WHOLE] * 8,
        out_specs=[WHOLE] * 2,
        compiler_params=params,
        cost_estimate=compare_cost,
        name="far",
    )(query, other_second, *near)
    members = [list(range(1, owners)) + [0]]
    results = lax.all_to_all(results, "shard", 0, 0, axis_index_groups=members, tiled=True)
    best, distance, cohesion = pl.pallas_call(
        functools.partial(pick_kernel, order, parts),
        out_shape=[jax.ShapeDtypeStruct((1, local_rows), jnp.float32)] * 2
        + [jax.ShapeDtypeStruct((1, clus_dev), jnp.float32)],
        in_specs=[SCALAR] + [WHOLE] * 3,
        out_specs=[WHOLE] * 3,
        compiler_params=params,
        name="pick",
    )(me, slot, results, norms)
    return best.reshape(local_rows), distance.reshape(local_rows), cohesion.reshape(clus_dev)


def solution(mesh):
    in_specs = (
        P(("groups", "shard", "sub"), None),
        P(("groups", "shard", "sub")),
        P(("groups", "shard", "sub")),
        P("groups"),
    )
    out_specs = (
        P(("groups", "shard", "sub")),
        P(("groups", "shard", "sub")),
        P(("groups", "shard")),
    )
    return jax.shard_map(local, mesh=mesh, in_specs=in_specs, out_specs=out_specs, check_vma=False)
```

```python
import functools

import jax
import jax.numpy as jnp
from jax import lax
from jax.experimental import pallas as pl
from jax.experimental.pallas import tpu as pltpu
from jax.sharding import PartitionSpec as P

LANES = 128
DIGITS = 3
SENDS = ((4,), (2, 3), (5,), (7,), (6,), (1,), (0,))
PARTNERS = (4, 2, 0, 5, 7, 6, 1, 3)
WHOLE = pl.BlockSpec(memory_space=pltpu.VMEM)
SCALAR = pl.BlockSpec(memory_space=pltpu.SMEM)


def iota(shape, dim):
    return lax.broadcasted_iota(jnp.int32, shape, dim)


def matmul(a, b):
    return jnp.dot(a, b, preferred_element_type=jnp.float32)


def matmul_t(a, b):
    return lax.dot_general(a, b, (((1,), (1,)), ((), ())), preferred_element_type=jnp.float32)


def bf16(x):
    return x.astype(jnp.float32).astype(jnp.bfloat16)


def ranked(hot):
    upto = (iota((LANES, LANES), 0) <= iota((LANES, LANES), 1)).astype(jnp.bfloat16)
    before, parts = jnp.zeros((1, 1), jnp.float32), []
    for start in range(0, hot.shape[1], LANES):
        piece = hot[:, start : start + LANES]
        spread = jnp.broadcast_to(piece, (16, LANES)).astype(jnp.bfloat16)
        parts.append(matmul(spread, upto)[:1] + before)
        before = before + jnp.sum(piece, axis=1, keepdims=True)
    return jnp.concatenate(parts, axis=1)


def slot_kernel(
    owners, capacity, order, parts, rows, me_ref, ints_ref, slot_ref, digit_ref
):
    clusters = ints_ref.shape[1] - 2 * rows
    cluster = ints_ref[:, clusters : clusters + rows]
    named = bf16(iota((clusters, rows), 0) == cluster)
    owner_map = bf16(jnp.broadcast_to(ints_ref[:, :clusters], (16, clusters)))
    owner = matmul(owner_map, named)[:1].astype(jnp.int32)
    hot = (iota((max(owners, 16), rows), 0) == owner).astype(jnp.float32)
    upto = bf16(iota((rows, rows), 0) <= iota((rows, rows), 1))
    rank = jnp.sum(hot * matmul(bf16(hot), upto), axis=0, keepdims=True) - 1.0
    rank = rank.astype(jnp.int32)
    partner = owner ^ me_ref[0]
    place = partner
    for index, k in enumerate(order):
        place = jnp.where(partner == k, index, place)
    if parts == 1:
        slot_ref[...] = place * capacity + rank
    else:
        half = capacity // 2
        later = (rank >= half).astype(jnp.int32)
        slot_ref[...] = place * half + rank + later * (owners * half - half)

    line = iota((8, rows), 0)
    digit = jnp.zeros((8, rows), jnp.int32)
    for first, number in ((0, cluster + 1), (DIGITS, ints_ref[:, clusters + rows :])):
        for at in range(DIGITS):
            digit = jnp.where(line == first + at, (number >> (8 * at)) & 255, digit)
    empty = jnp.zeros((LANES // 2 - 8, rows), jnp.int32)
    none = jnp.zeros((LANES // 2, rows), jnp.int32)
    early = jnp.concatenate([digit, empty, none], axis=0)
    late = jnp.concatenate([none, digit, empty], axis=0)
    digit_ref[...] = bf16(jnp.concatenate([early, late], axis=1))


def pack_kernel(sends, slot_ref, digit_ref, embed_ref, *out_refs):
    rows, width = embed_ref.shape
    half = out_refs[0].shape[1]
    tiles = 2 * (width // LANES) + 1
    values = embed_ref[...].astype(jnp.float32)
    mean_sq = jnp.sum(values * values, axis=1, keepdims=True) * (1.0 / width)
    unit = (values * lax.rsqrt(width * (mean_sq + 1e-06))).astype(jnp.bfloat16)
    late = half * sum(len(places) for places in sends)
    move = bf16(iota((2 * late, rows), 0) == slot_ref[...])
    moved = matmul(move, unit).astype(jnp.bfloat16)
    both = jnp.concatenate([move[:late], move[late:]], axis=1)
    digit = matmul_t(both, digit_ref[...]).astype(jnp.bfloat16)
    each = tiles // 2
    for places, out_ref in zip(sends, out_refs):
        for index, place in enumerate(places):
            base, start = index * tiles, place * half
            for tile in range(each):
                lanes = slice(tile * LANES, (tile + 1) * LANES)
                out_ref[base + tile] = moved[start : start + half, lanes]
                out_ref[base + each + tile] = moved[late + start : late + start + half, lanes]
            out_ref[base + tiles - 1] = digit[start : start + half]


def unpacked(block_ref, tiles):
    blocks = block_ref.shape[0] // tiles
    each = tiles // 2

    def column(tile):
        return jnp.concatenate([block_ref[i * tiles + tile] for i in range(blocks)], axis=0)

    halves = [
        jnp.concatenate([column(first + tile) for tile in range(each)], axis=1)
        for first in (0, each)
    ]
    return jnp.concatenate(halves, axis=0), column(tiles - 1)


def weights(number, at, half):
    value = jnp.zeros(at.shape, jnp.float32)
    for place in range(DIGITS):
        for which in (0, 1):
            lane = half * (LANES // 2) + which * DIGITS + place
            value = jnp.where((at == lane) & (number == which), 256.0**place, value)
    return value.astype(jnp.bfloat16)


def key_rows(rows_all, digit):
    at = iota((16, LANES), 0), iota((16, LANES), 1)
    numbers = [matmul_t(weights(*at, half), digit) for half in (0, 1)]
    numbers = jnp.concatenate(numbers, axis=1)
    low = (numbers[0:1].astype(jnp.int32) - 1) * rows_all
    return low, low + numbers[1:2].astype(jnp.int32)


def key_columns(rows_all, digit):
    at = iota((LANES, 2 * LANES), 1) // LANES, iota((LANES, 2 * LANES), 0)
    numbers = [matmul(digit, weights(*at, half)) for half in (0, 1)]
    numbers = jnp.concatenate(numbers, axis=0)
    low = (numbers[:, :LANES].astype(jnp.int32) - 1) * rows_all
    return low, low + numbers[:, LANES:].astype(jnp.int32)


def across(column, count):
    return jnp.concatenate([column] * (count // LANES), axis=1)


def compare(rows_all, query_t, query_low, query_key, lows, parts):
    rows = jnp.concatenate([rows for rows, _ in parts], axis=0)
    key = jnp.concatenate([key_rows(rows_all, digit)[1] for _, digit in parts], axis=1)
    bound = across(lows, key.shape[1])
    member = bf16((key >= bound) & (key < bound + rows_all))
    sums = matmul(member, rows)
    counts = matmul(member, jnp.ones((rows.shape[0], LANES), jnp.bfloat16))
    scores = matmul(rows, query_t)
    key = jnp.concatenate([key_columns(rows_all, digit)[1] for _, digit in parts], axis=0)
    key = across(key, query_t.shape[1])
    earlier = (key >= query_low) & (key < query_key)
    best = jnp.max(jnp.where(earlier, scores, -3.0), axis=0, keepdims=True)
    return best, sums, counts


def near_kernel(
    rows_all, clusters, clus_dev, tiles, me_ref, ints_ref, query_ref, other_ref,
    query_t_ref, lows_ref, key_ref, best_ref, sums_ref, counts_ref,
):
    hot = (ints_ref[:, :clusters] == me_ref[0]).astype(jnp.float32)
    rank = ranked(hot)
    shape = (clus_dev, clusters)
    kth = (rank == iota(shape, 0).astype(jnp.float32) + 1.0) & (hot > 0.0)
    own = jnp.sum(jnp.where(kth, iota(shape, 1).astype(jnp.float32), 0.0), axis=1, keepdims=True)
    own = jnp.broadcast_to(own.astype(jnp.int32) * rows_all, (clus_dev, LANES))
    query, digit = unpacked(query_ref, tiles)
    low, _ = key_columns(rows_all, digit)
    lows = jnp.concatenate([low, own], axis=0)
    query_low, query_key = key_rows(rows_all, digit)
    query_t = jnp.transpose(query)
    query_t_ref[...] = query_t
    parts = [(query, digit), unpacked(other_ref, tiles)]
    best, sums, counts = compare(rows_all, query_t, query_low, query_key, lows, parts)
    lows_ref[...] = lows
    key_ref[...] = jnp.concatenate([query_low, query_key], axis=0)
    best_ref[...] = best
    sums_ref[...] = sums
    counts_ref[...] = counts


def far_kernel(
    rows_all, tiles, query_ref, other_ref, query_t_ref, lows_ref, key_ref, best_ref, sums_ref, counts_ref,
    result_ref, norm_ref,
):
    query, _ = unpacked(query_ref, tiles)
    queries, width = query.shape
    best, sums, counts = compare(
        rows_all, query_t_ref[...], key_ref[0:1], key_ref[1:2], lows_ref[...], [unpacked(other_ref, tiles)]
    )
    best = jnp.maximum(best, best_ref[...])
    best = jnp.where(best > -2.0, best, 0.0)
    share = 1.0 / jnp.maximum(counts + counts_ref[...], 1.0)
    squares = jnp.zeros((queries, LANES), jnp.float32)
    norms = jnp.zeros((share.shape[0] - queries, LANES), jnp.float32)
    for start in range(0, width, LANES):
        lanes = slice(start, start + LANES)
        centroid = (sums[:, lanes] + sums_ref[:, lanes]) * share
        offset = query[:, lanes].astype(jnp.float32) - centroid[:queries]
        squares = squares + offset * offset
        norms = norms + centroid[queries:] * centroid[queries:]
    distance = jnp.sum(jnp.transpose(squares), axis=0, keepdims=True)
    result = jnp.concatenate([best, distance], axis=0)
    for owner in range(result_ref.shape[0]):
        result_ref[owner] = result
    norms = jnp.concatenate([norms] * (LANES // norms.shape[0]), axis=0)
    norm_ref[...] = jnp.sum(jnp.transpose(norms), axis=0, keepdims=True)[:, : norm_ref.shape[1]]


def pick_kernel(
    order, parts, me_ref, slot_ref, result_ref, norm_ref, best_ref, distance_ref, cohesion_ref
):
    cohesion_ref[...] = norm_ref[...]
    rows = slot_ref.shape[1]
    owners, lines, slots = result_ref.shape
    folds = min(parts, 2)
    place = iota((lines, slots), 1) % (slots // folds) // (slots // owners // folds)
    values = jnp.zeros((lines, slots), jnp.float32)
    for index, k in enumerate(order):
        owner = me_ref[0] ^ k
        member = jnp.where(owner % 2 == 1, owner // 2, owners - 1 - owner // 2)
        values = jnp.where(place == index, result_ref[member], values)
    values = jnp.concatenate([values, jnp.zeros((8 - lines, slots), jnp.float32)], axis=0)
    at = (iota((slots, rows), 0) == slot_ref[...]).astype(jnp.float32)
    picked = jnp.dot(
        values, at, precision=lax.Precision.HIGHEST, preferred_element_type=jnp.float32
    )
    best_ref[...] = picked[0:1]
    distance_ref[...] = picked[1:2]


def from_partner(value, k, axis):
    return lax.ppermute(value, axis, [(i, i ^ k) for i in range(lax.axis_size(axis))])


def exchange(packed, tiles):
    sent = dict(zip(SENDS, packed))
    got = {0: sent[0,]}
    for k in (4, 5, 7, 6):
        got[k] = from_partner(sent[k,], k, "shard")
    pair = from_partner(sent[2, 3], 2, "shard")
    got[2] = pair[:tiles]
    pair = from_partner(jnp.concatenate([sent[1,], pair[tiles:]]), 1, "shard")
    got[1], got[3] = pair[:tiles], pair[tiles:]
    got = [got[k] for k in PARTNERS]
    half = len(got) // 2
    return jnp.concatenate(got[:half]), jnp.concatenate(got[half:])


def exchange_all(packed, me):
    owners = lax.axis_size("shard")
    tiles, half, _ = packed.shape
    each = tiles // 2
    data = packed[:-1].reshape(2, each, half, LANES).transpose(0, 2, 1, 3).reshape(2 * half, -1)
    digit = jnp.concatenate(jnp.split(packed[-1], 2, axis=1))
    parted = jnp.concatenate([data, digit], axis=1).reshape(owners, 2 * half // owners, -1)
    partner = me ^ jnp.arange(owners, dtype=jnp.int32)
    got = lax.all_to_all(parted[partner], "shard", 0, 0, tiled=True)[partner].reshape(2 * half, -1)
    data = got[:, : each * LANES].reshape(2, half, each, LANES).transpose(0, 2, 1, 3)
    digit = jnp.concatenate(jnp.split(got[:, each * LANES :], 2), axis=1)
    got = jnp.concatenate([data.reshape(2 * each, half, LANES), digit[None]])
    return jnp.split(got, 2, axis=1)


def local(embeddings, cluster_id, item_order, owner_map):
    owners = lax.axis_size("shard")
    local_rows, width = embeddings.shape
    rows_all = local_rows * owners * lax.axis_size("sub")
    clus_dev = owner_map.shape[0] // owners
    capacity = 2 * local_rows // owners
    slots = owners * capacity
    params = pltpu.CompilerParams(vmem_limit_bytes=32 << 20)
    compare_cost = pl.CostEstimate(
        flops=4 * slots * slots * width, bytes_accessed=4 * slots * width, transcendentals=0
    )
    me = lax.axis_index("shard").astype(jnp.int32).reshape(1)
    ints = jnp.concatenate([owner_map, cluster_id, item_order]).reshape(1, -1)

    direct = owners == len(PARTNERS)
    order = PARTNERS if direct else tuple(range(owners))
    parts = owners if direct else 1
    tiles = 2 * (width // LANES) + 1
    sends = [[PARTNERS.index(k) for k in ks] for ks in SENDS] if direct else [[0]]
    half = slots // parts // 2
    slot, digit = pl.pallas_call(
        functools.partial(slot_kernel, owners, capacity, order, parts, local_rows),
        out_shape=[
            jax.ShapeDtypeStruct((1, local_rows), jnp.int32),
            jax.ShapeDtypeStruct((LANES, 2 * local_rows), jnp.bfloat16),
        ],
        in_specs=[SCALAR, WHOLE],
        out_specs=[WHOLE] * 2,
        compiler_params=params,
        cost_estimate=pl.CostEstimate(flops=1 << 29, bytes_accessed=1 << 16, transcendentals=0),
        name="slots",
    )(me, ints)
    packed = pl.pallas_call(
        functools.partial(pack_kernel, sends),
        out_shape=[
            jax.ShapeDtypeStruct((len(places) * tiles, half, LANES), jnp.bfloat16) for places in sends
        ],
        in_specs=[WHOLE] * 3,
        out_specs=[WHOLE] * len(sends),
        compiler_params=params,
        name="pack",
    )(slot, digit, embeddings)
    first, second = exchange(packed, tiles) if direct else exchange_all(packed[0], me[0])
    other_first, other_second = (from_partner(rows, 1, "sub") for rows in (first, second))
    query = jnp.concatenate([first, second])
    asked = slots + clus_dev
    near = pl.pallas_call(
        functools.partial(near_kernel, rows_all, owner_map.shape[0], clus_dev, tiles),
        out_shape=[
            jax.ShapeDtypeStruct((width, slots), jnp.bfloat16),
            jax.ShapeDtypeStruct((asked, LANES), jnp.int32),
            jax.ShapeDtypeStruct((2, slots), jnp.int32),
            jax.ShapeDtypeStruct((1, slots), jnp.float32),
            jax.ShapeDtypeStruct((asked, width), jnp.float32),
            jax.ShapeDtypeStruct((asked, LANES), jnp.float32),
        ],
        in_specs=[SCALAR] + [WHOLE] * 3,
        out_specs=[WHOLE] * 6,
        compiler_params=params,
        cost_estimate=compare_cost,
        name="near",
    )(me, ints, query, other_first)
    results, norms = pl.pallas_call(
        functools.partial(far_kernel, rows_all, tiles),
        out_shape=[
            jax.ShapeDtypeStruct((owners, 2, slots), jnp.float32),
            jax.ShapeDtypeStruct((1, clus_dev), jnp.float32),
        ],
        in_specs=[WHOLE] * 8,
        out_specs=[WHOLE] * 2,
        compiler_params=params,
        cost_estimate=compare_cost,
        name="far",
    )(query, other_second, *near)
    members = [list(range(1, owners, 2)) + list(range(owners - 2, -1, -2))]
    results = lax.all_to_all(results, "shard", 0, 0, axis_index_groups=members, tiled=True)
    best, distance, cohesion = pl.pallas_call(
        functools.partial(pick_kernel, order, parts),
        out_shape=[jax.ShapeDtypeStruct((1, local_rows), jnp.float32)] * 2
        + [jax.ShapeDtypeStruct((1, clus_dev), jnp.float32)],
        in_specs=[SCALAR] + [WHOLE] * 3,
        out_specs=[WHOLE] * 3,
        compiler_params=params,
        name="pick",
    )(me, slot, results, norms)
    return best.reshape(local_rows), distance.reshape(local_rows), cohesion.reshape(clus_dev)


def solution(mesh):
    in_specs = (
        P(("groups", "shard", "sub"), None),
        P(("groups", "shard", "sub")),
        P(("groups", "shard", "sub")),
        P("groups"),
    )
    out_specs = (
        P(("groups", "shard", "sub")),
        P(("groups", "shard", "sub")),
        P(("groups", "shard")),
    )
    return jax.shard_map(local, mesh=mesh, in_specs=in_specs, out_specs=out_specs, check_vma=False)
```

```python
import functools

import jax
import jax.numpy as jnp
from jax import lax
from jax.experimental import pallas as pl
from jax.experimental.pallas import tpu as pltpu
from jax.sharding import PartitionSpec as P

LANES = 128
DIGITS = 3
SENDS = ((4,), (2, 3), (5,), (7,), (6,), (1,), (0,))
PARTNERS = (4, 2, 0, 5, 7, 6, 1, 3)
MEMBERS = (5, 7, 6, 4, 3, 2, 1, 0)
WHOLE = pl.BlockSpec(memory_space=pltpu.VMEM)
SCALAR = pl.BlockSpec(memory_space=pltpu.SMEM)


def iota(shape, dim):
    return lax.broadcasted_iota(jnp.int32, shape, dim)


def matmul(a, b):
    return jnp.dot(a, b, preferred_element_type=jnp.float32)


def matmul_t(a, b):
    return lax.dot_general(a, b, (((1,), (1,)), ((), ())), preferred_element_type=jnp.float32)


def bf16(x):
    return x.astype(jnp.float32).astype(jnp.bfloat16)


def ranked(hot):
    upto = (iota((LANES, LANES), 0) <= iota((LANES, LANES), 1)).astype(jnp.bfloat16)
    before, parts = jnp.zeros((1, 1), jnp.float32), []
    for start in range(0, hot.shape[1], LANES):
        piece = hot[:, start : start + LANES]
        spread = jnp.broadcast_to(piece, (16, LANES)).astype(jnp.bfloat16)
        parts.append(matmul(spread, upto)[:1] + before)
        before = before + jnp.sum(piece, axis=1, keepdims=True)
    return jnp.concatenate(parts, axis=1)


def slot_kernel(
    owners, capacity, order, parts, rows, me_ref, ints_ref, slot_ref, digit_ref
):
    clusters = ints_ref.shape[1] - 2 * rows
    cluster = ints_ref[:, clusters : clusters + rows]
    named = bf16(iota((clusters, rows), 0) == cluster)
    owner_map = bf16(jnp.broadcast_to(ints_ref[:, :clusters], (16, clusters)))
    owner = matmul(owner_map, named)[:1].astype(jnp.int32)
    hot = (iota((max(owners, 16), rows), 0) == owner).astype(jnp.float32)
    upto = bf16(iota((rows, rows), 0) <= iota((rows, rows), 1))
    rank = jnp.sum(hot * matmul(bf16(hot), upto), axis=0, keepdims=True) - 1.0
    rank = rank.astype(jnp.int32)
    partner = owner ^ me_ref[0]
    place = partner
    for index, k in enumerate(order):
        place = jnp.where(partner == k, index, place)
    if parts == 1:
        slot_ref[...] = place * capacity + rank
    else:
        half = capacity // 2
        later = (rank >= half).astype(jnp.int32)
        slot_ref[...] = place * half + rank + later * (owners * half - half)

    line = iota((8, rows), 0)
    digit = jnp.zeros((8, rows), jnp.int32)
    for first, number in ((0, cluster + 1), (DIGITS, ints_ref[:, clusters + rows :])):
        for at in range(DIGITS):
            digit = jnp.where(line == first + at, (number >> (8 * at)) & 255, digit)
    empty = jnp.zeros((LANES // 2 - 8, rows), jnp.int32)
    none = jnp.zeros((LANES // 2, rows), jnp.int32)
    early = jnp.concatenate([digit, empty, none], axis=0)
    late = jnp.concatenate([none, digit, empty], axis=0)
    digit_ref[...] = bf16(jnp.concatenate([early, late], axis=1))


def pack_kernel(sends, slot_ref, digit_ref, embed_ref, *out_refs):
    rows, width = embed_ref.shape
    half = out_refs[0].shape[1]
    tiles = 2 * (width // LANES) + 1
    values = embed_ref[...].astype(jnp.float32)
    mean_sq = jnp.sum(values * values, axis=1, keepdims=True) * (1.0 / width)
    unit = (values * lax.rsqrt(width * (mean_sq + 1e-06))).astype(jnp.bfloat16)
    late = half * sum(len(places) for places in sends)
    move = bf16(iota((2 * late, rows), 0) == slot_ref[...])
    moved = matmul(move, unit).astype(jnp.bfloat16)
    both = jnp.concatenate([move[:late], move[late:]], axis=1)
    digit = matmul_t(both, digit_ref[...]).astype(jnp.bfloat16)
    each = tiles // 2
    for places, out_ref in zip(sends, out_refs):
        for index, place in enumerate(places):
            base, start = index * tiles, place * half
            for tile in range(each):
                lanes = slice(tile * LANES, (tile + 1) * LANES)
                out_ref[base + tile] = moved[start : start + half, lanes]
                out_ref[base + each + tile] = moved[late + start : late + start + half, lanes]
            out_ref[base + tiles - 1] = digit[start : start + half]


def unpacked(block_ref, tiles):
    blocks = block_ref.shape[0] // tiles
    each = tiles // 2

    def column(tile):
        return jnp.concatenate([block_ref[i * tiles + tile] for i in range(blocks)], axis=0)

    halves = [
        jnp.concatenate([column(first + tile) for tile in range(each)], axis=1)
        for first in (0, each)
    ]
    return jnp.concatenate(halves, axis=0), column(tiles - 1)


def weights(number, at, half):
    value = jnp.zeros(at.shape, jnp.float32)
    for place in range(DIGITS):
        for which in (0, 1):
            lane = half * (LANES // 2) + which * DIGITS + place
            value = jnp.where((at == lane) & (number == which), 256.0**place, value)
    return value.astype(jnp.bfloat16)


def key_rows(rows_all, digit):
    at = iota((16, LANES), 0), iota((16, LANES), 1)
    numbers = [matmul_t(weights(*at, half), digit) for half in (0, 1)]
    numbers = jnp.concatenate(numbers, axis=1)
    low = (numbers[0:1].astype(jnp.int32) - 1) * rows_all
    return low, low + numbers[1:2].astype(jnp.int32)


def key_columns(rows_all, digit):
    at = iota((LANES, 2 * LANES), 1) // LANES, iota((LANES, 2 * LANES), 0)
    numbers = [matmul(digit, weights(*at, half)) for half in (0, 1)]
    numbers = jnp.concatenate(numbers, axis=0)
    low = (numbers[:, :LANES].astype(jnp.int32) - 1) * rows_all
    return low, low + numbers[:, LANES:].astype(jnp.int32)


def across(column, count):
    return jnp.concatenate([column] * (count // LANES), axis=1)


def compare(rows_all, query_t, query_low, query_key, lows, parts):
    rows = jnp.concatenate([rows for rows, _ in parts], axis=0)
    key = jnp.concatenate([key_rows(rows_all, digit)[1] for _, digit in parts], axis=1)
    bound = across(lows, key.shape[1])
    member = bf16((key >= bound) & (key < bound + rows_all))
    sums = matmul(member, rows)
    counts = matmul(member, jnp.ones((rows.shape[0], LANES), jnp.bfloat16))
    scores = matmul(rows, query_t)
    key = jnp.concatenate([key_columns(rows_all, digit)[1] for _, digit in parts], axis=0)
    key = across(key, query_t.shape[1])
    earlier = (key >= query_low) & (key < query_key)
    best = jnp.max(jnp.where(earlier, scores, -3.0), axis=0, keepdims=True)
    return best, sums, counts


def near_kernel(
    rows_all, clusters, clus_dev, tiles, me_ref, ints_ref, query_ref, other_ref,
    query_t_ref, lows_ref, key_ref, best_ref, sums_ref, counts_ref,
):
    hot = (ints_ref[:, :clusters] == me_ref[0]).astype(jnp.float32)
    rank = ranked(hot)
    shape = (clus_dev, clusters)
    kth = (rank == iota(shape, 0).astype(jnp.float32) + 1.0) & (hot > 0.0)
    own = jnp.sum(jnp.where(kth, iota(shape, 1).astype(jnp.float32), 0.0), axis=1, keepdims=True)
    own = jnp.broadcast_to(own.astype(jnp.int32) * rows_all, (clus_dev, LANES))
    query, digit = unpacked(query_ref, tiles)
    low, _ = key_columns(rows_all, digit)
    lows = jnp.concatenate([low, own], axis=0)
    query_low, query_key = key_rows(rows_all, digit)
    query_t = jnp.transpose(query)
    query_t_ref[...] = query_t
    parts = [(query, digit), unpacked(other_ref, tiles)]
    best, sums, counts = compare(rows_all, query_t, query_low, query_key, lows, parts)
    lows_ref[...] = lows
    key_ref[...] = jnp.concatenate([query_low, query_key], axis=0)
    best_ref[...] = best
    sums_ref[...] = sums
    counts_ref[...] = counts


def far_kernel(
    rows_all, tiles, query_ref, other_ref, query_t_ref, lows_ref, key_ref, best_ref, sums_ref, counts_ref,
    result_ref, norm_ref,
):
    query, _ = unpacked(query_ref, tiles)
    queries, width = query.shape
    best, sums, counts = compare(
        rows_all, query_t_ref[...], key_ref[0:1], key_ref[1:2], lows_ref[...], [unpacked(other_ref, tiles)]
    )
    best = jnp.maximum(best, best_ref[...])
    best = jnp.where(best > -2.0, best, 0.0)
    share = 1.0 / jnp.maximum(counts + counts_ref[...], 1.0)
    squares = jnp.zeros((queries, LANES), jnp.float32)
    norms = jnp.zeros((share.shape[0] - queries, LANES), jnp.float32)
    for start in range(0, width, LANES):
        lanes = slice(start, start + LANES)
        centroid = (sums[:, lanes] + sums_ref[:, lanes]) * share
        offset = query[:, lanes].astype(jnp.float32) - centroid[:queries]
        squares = squares + offset * offset
        norms = norms + centroid[queries:] * centroid[queries:]
    distance = jnp.sum(jnp.transpose(squares), axis=0, keepdims=True)
    result = jnp.concatenate([best, distance], axis=0)
    for owner in range(result_ref.shape[0]):
        result_ref[owner] = result
    norms = jnp.concatenate([norms] * (LANES // norms.shape[0]), axis=0)
    norm_ref[...] = jnp.sum(jnp.transpose(norms), axis=0, keepdims=True)[:, : norm_ref.shape[1]]


def pick_kernel(
    order, parts, me_ref, slot_ref, result_ref, norm_ref, best_ref, distance_ref, cohesion_ref
):
    cohesion_ref[...] = norm_ref[...]
    rows = slot_ref.shape[1]
    owners, lines, slots = result_ref.shape
    folds = min(parts, 2)
    place = iota((lines, slots), 1) % (slots // folds) // (slots // owners // folds)
    values = jnp.zeros((lines, slots), jnp.float32)
    for index, k in enumerate(order):
        owner = me_ref[0] ^ k
        member = owner
        if owners == len(MEMBERS):
            member = sum(jnp.where(owner == name, at, 0) for at, name in enumerate(MEMBERS))
        values = jnp.where(place == index, result_ref[member], values)
    values = jnp.concatenate([values, jnp.zeros((8 - lines, slots), jnp.float32)], axis=0)
    at = (iota((slots, rows), 0) == slot_ref[...]).astype(jnp.float32)
    picked = jnp.dot(
        values, at, precision=lax.Precision.HIGHEST, preferred_element_type=jnp.float32
    )
    best_ref[...] = picked[0:1]
    distance_ref[...] = picked[1:2]


def from_partner(value, k, axis):
    return lax.ppermute(value, axis, [(i, i ^ k) for i in range(lax.axis_size(axis))])


def exchange(packed, tiles):
    sent = dict(zip(SENDS, packed))
    got = {0: sent[0,]}
    for k in (4, 5, 7, 6):
        got[k] = from_partner(sent[k,], k, "shard")
    pair = from_partner(sent[2, 3], 2, "shard")
    got[2] = pair[:tiles]
    pair = from_partner(jnp.concatenate([sent[1,], pair[tiles:]]), 1, "shard")
    got[1], got[3] = pair[:tiles], pair[tiles:]
    got = [got[k] for k in PARTNERS]
    half = len(got) // 2
    return jnp.concatenate(got[:half]), jnp.concatenate(got[half:])


def exchange_all(packed, me):
    owners = lax.axis_size("shard")
    tiles, half, _ = packed.shape
    each = tiles // 2
    data = packed[:-1].reshape(2, each, half, LANES).transpose(0, 2, 1, 3).reshape(2 * half, -1)
    digit = jnp.concatenate(jnp.split(packed[-1], 2, axis=1))
    parted = jnp.concatenate([data, digit], axis=1).reshape(owners, 2 * half // owners, -1)
    partner = me ^ jnp.arange(owners, dtype=jnp.int32)
    got = lax.all_to_all(parted[partner], "shard", 0, 0, tiled=True)[partner].reshape(2 * half, -1)
    data = got[:, : each * LANES].reshape(2, half, each, LANES).transpose(0, 2, 1, 3)
    digit = jnp.concatenate(jnp.split(got[:, each * LANES :], 2), axis=1)
    got = jnp.concatenate([data.reshape(2 * each, half, LANES), digit[None]])
    return jnp.split(got, 2, axis=1)


def local(embeddings, cluster_id, item_order, owner_map):
    owners = lax.axis_size("shard")
    local_rows, width = embeddings.shape
    rows_all = local_rows * owners * lax.axis_size("sub")
    clus_dev = owner_map.shape[0] // owners
    capacity = 2 * local_rows // owners
    slots = owners * capacity
    params = pltpu.CompilerParams(vmem_limit_bytes=32 << 20)
    compare_cost = pl.CostEstimate(
        flops=4 * slots * slots * width, bytes_accessed=4 * slots * width, transcendentals=0
    )
    me = lax.axis_index("shard").astype(jnp.int32).reshape(1)
    ints = jnp.concatenate([owner_map, cluster_id, item_order]).reshape(1, -1)

    direct = owners == len(PARTNERS)
    order = PARTNERS if direct else tuple(range(owners))
    parts = owners if direct else 1
    tiles = 2 * (width // LANES) + 1
    members = MEMBERS if direct else tuple(range(owners))
    sends = [[PARTNERS.index(k) for k in ks] for ks in SENDS] if direct else [[0]]
    half = slots // parts // 2
    slot, digit = pl.pallas_call(
        functools.partial(slot_kernel, owners, capacity, order, parts, local_rows),
        out_shape=[
            jax.ShapeDtypeStruct((1, local_rows), jnp.int32),
            jax.ShapeDtypeStruct((LANES, 2 * local_rows), jnp.bfloat16),
        ],
        in_specs=[SCALAR, WHOLE],
        out_specs=[WHOLE] * 2,
        compiler_params=params,
        cost_estimate=pl.CostEstimate(flops=1 << 29, bytes_accessed=1 << 16, transcendentals=0),
        name="slots",
    )(me, ints)
    packed = pl.pallas_call(
        functools.partial(pack_kernel, sends),
        out_shape=[
            jax.ShapeDtypeStruct((len(places) * tiles, half, LANES), jnp.bfloat16) for places in sends
        ],
        in_specs=[WHOLE] * 3,
        out_specs=[WHOLE] * len(sends),
        compiler_params=params,
        name="pack",
    )(slot, digit, embeddings)
    first, second = exchange(packed, tiles) if direct else exchange_all(packed[0], me[0])
    other_first, other_second = (from_partner(rows, 1, "sub") for rows in (first, second))
    query = jnp.concatenate([first, second])
    asked = slots + clus_dev
    near = pl.pallas_call(
        functools.partial(near_kernel, rows_all, owner_map.shape[0], clus_dev, tiles),
        out_shape=[
            jax.ShapeDtypeStruct((width, slots), jnp.bfloat16),
            jax.ShapeDtypeStruct((asked, LANES), jnp.int32),
            jax.ShapeDtypeStruct((2, slots), jnp.int32),
            jax.ShapeDtypeStruct((1, slots), jnp.float32),
            jax.ShapeDtypeStruct((asked, width), jnp.float32),
            jax.ShapeDtypeStruct((asked, LANES), jnp.float32),
        ],
        in_specs=[SCALAR] + [WHOLE] * 3,
        out_specs=[WHOLE] * 6,
        compiler_params=params,
        cost_estimate=compare_cost,
        name="near",
    )(me, ints, query, other_first)
    results, norms = pl.pallas_call(
        functools.partial(far_kernel, rows_all, tiles),
        out_shape=[
            jax.ShapeDtypeStruct((owners, 2, slots), jnp.float32),
            jax.ShapeDtypeStruct((1, clus_dev), jnp.float32),
        ],
        in_specs=[WHOLE] * 8,
        out_specs=[WHOLE] * 2,
        compiler_params=params,
        cost_estimate=compare_cost,
        name="far",
    )(query, other_second, *near)
    groups = [list(members)]
    results = lax.all_to_all(results, "shard", 0, 0, axis_index_groups=groups, tiled=True)
    best, distance, cohesion = pl.pallas_call(
        functools.partial(pick_kernel, order, parts),
        out_shape=[jax.ShapeDtypeStruct((1, local_rows), jnp.float32)] * 2
        + [jax.ShapeDtypeStruct((1, clus_dev), jnp.float32)],
        in_specs=[SCALAR] + [WHOLE] * 3,
        out_specs=[WHOLE] * 3,
        compiler_params=params,
        name="pick",
    )(me, slot, results, norms)
    return best.reshape(local_rows), distance.reshape(local_rows), cohesion.reshape(clus_dev)


def solution(mesh):
    in_specs = (
        P(("groups", "shard", "sub"), None),
        P(("groups", "shard", "sub")),
        P(("groups", "shard", "sub")),
        P("groups"),
    )
    out_specs = (
        P(("groups", "shard", "sub")),
        P(("groups", "shard", "sub")),
        P(("groups", "shard")),
    )
    return jax.shard_map(local, mesh=mesh, in_specs=in_specs, out_specs=out_specs, check_vma=False)
```

```python
import functools

import jax
import jax.numpy as jnp
from jax import lax
from jax.experimental import pallas as pl
from jax.experimental.pallas import tpu as pltpu
from jax.sharding import PartitionSpec as P

LANES = 128
DIGITS = 3
SENDS = ((4,), (2, 3), (5,), (7,), (6,), (1,), (0,))
PARTNERS = (4, 2, 0, 5, 7, 6, 1, 3)
EARLY = 3
MEMBERS = (5, 7, 6, 4, 3, 2, 1, 0)
WHOLE = pl.BlockSpec(memory_space=pltpu.VMEM)
SCALAR = pl.BlockSpec(memory_space=pltpu.SMEM)


def iota(shape, dim):
    return lax.broadcasted_iota(jnp.int32, shape, dim)


def matmul(a, b):
    return jnp.dot(a, b, preferred_element_type=jnp.float32)


def matmul_t(a, b):
    return lax.dot_general(a, b, (((1,), (1,)), ((), ())), preferred_element_type=jnp.float32)


def bf16(x):
    return x.astype(jnp.float32).astype(jnp.bfloat16)


def ranked(hot):
    upto = (iota((LANES, LANES), 0) <= iota((LANES, LANES), 1)).astype(jnp.bfloat16)
    before, parts = jnp.zeros((1, 1), jnp.float32), []
    for start in range(0, hot.shape[1], LANES):
        piece = hot[:, start : start + LANES]
        spread = jnp.broadcast_to(piece, (16, LANES)).astype(jnp.bfloat16)
        parts.append(matmul(spread, upto)[:1] + before)
        before = before + jnp.sum(piece, axis=1, keepdims=True)
    return jnp.concatenate(parts, axis=1)


def slot_kernel(
    owners, capacity, order, parts, rows, me_ref, ints_ref, slot_ref, digit_ref
):
    clusters = ints_ref.shape[1] - 2 * rows
    cluster = ints_ref[:, clusters : clusters + rows]
    named = bf16(iota((clusters, rows), 0) == cluster)
    owner_map = bf16(jnp.broadcast_to(ints_ref[:, :clusters], (16, clusters)))
    owner = matmul(owner_map, named)[:1].astype(jnp.int32)
    hot = (iota((max(owners, 16), rows), 0) == owner).astype(jnp.float32)
    upto = bf16(iota((rows, rows), 0) <= iota((rows, rows), 1))
    rank = jnp.sum(hot * matmul(bf16(hot), upto), axis=0, keepdims=True) - 1.0
    rank = rank.astype(jnp.int32)
    partner = owner ^ me_ref[0]
    place = partner
    for index, k in enumerate(order):
        place = jnp.where(partner == k, index, place)
    if parts == 1:
        slot_ref[...] = place * capacity + rank
    else:
        half = capacity // 2
        later = (rank >= half).astype(jnp.int32)
        slot_ref[...] = place * half + rank + later * (owners * half - half)

    line = iota((8, rows), 0)
    digit = jnp.zeros((8, rows), jnp.int32)
    for first, number in ((0, cluster + 1), (DIGITS, ints_ref[:, clusters + rows :])):
        for at in range(DIGITS):
            digit = jnp.where(line == first + at, (number >> (8 * at)) & 255, digit)
    empty = jnp.zeros((LANES // 2 - 8, rows), jnp.int32)
    none = jnp.zeros((LANES // 2, rows), jnp.int32)
    early = jnp.concatenate([digit, empty, none], axis=0)
    late = jnp.concatenate([none, digit, empty], axis=0)
    digit_ref[...] = bf16(jnp.concatenate([early, late], axis=1))


def pack_kernel(sends, slot_ref, digit_ref, embed_ref, *out_refs):
    rows, width = embed_ref.shape
    half = out_refs[0].shape[1]
    tiles = 2 * (width // LANES) + 1
    values = embed_ref[...].astype(jnp.float32)
    mean_sq = jnp.sum(values * values, axis=1, keepdims=True) * (1.0 / width)
    unit = (values * lax.rsqrt(width * (mean_sq + 1e-06))).astype(jnp.bfloat16)
    late = half * sum(len(places) for places in sends)
    move = bf16(iota((2 * late, rows), 0) == slot_ref[...])
    moved = matmul(move, unit).astype(jnp.bfloat16)
    both = jnp.concatenate([move[:late], move[late:]], axis=1)
    digit = matmul_t(both, digit_ref[...]).astype(jnp.bfloat16)
    each = tiles // 2
    for places, out_ref in zip(sends, out_refs):
        for index, place in enumerate(places):
            base, start = index * tiles, place * half
            for tile in range(each):
                lanes = slice(tile * LANES, (tile + 1) * LANES)
                out_ref[base + tile] = moved[start : start + half, lanes]
                out_ref[base + each + tile] = moved[late + start : late + start + half, lanes]
            out_ref[base + tiles - 1] = digit[start : start + half]


def unpacked(block_ref, tiles):
    blocks, half = block_ref.shape[0] // tiles, block_ref.shape[1]
    each = tiles // 2
    empty = [jnp.zeros((half, LANES), block_ref.dtype)] * (-blocks % max(LANES // (2 * half), 1))

    def column(tile):
        return jnp.concatenate([block_ref[i * tiles + tile] for i in range(blocks)] + empty, axis=0)

    halves = [
        jnp.concatenate([column(first + tile) for tile in range(each)], axis=1)
        for first in (0, each)
    ]
    return jnp.concatenate(halves, axis=0), column(tiles - 1)


def weights(number, at, half):
    value = jnp.zeros(at.shape, jnp.float32)
    for place in range(DIGITS):
        for which in (0, 1):
            lane = half * (LANES // 2) + which * DIGITS + place
            value = jnp.where((at == lane) & (number == which), 256.0**place, value)
    return value.astype(jnp.bfloat16)


def key_rows(rows_all, digit):
    at = iota((16, LANES), 0), iota((16, LANES), 1)
    numbers = [matmul_t(weights(*at, half), digit) for half in (0, 1)]
    numbers = jnp.concatenate(numbers, axis=1)
    low = (numbers[0:1].astype(jnp.int32) - 1) * rows_all
    return low, low + numbers[1:2].astype(jnp.int32)


def key_columns(rows_all, digit):
    at = iota((LANES, 2 * LANES), 1) // LANES, iota((LANES, 2 * LANES), 0)
    numbers = [matmul(digit, weights(*at, half)) for half in (0, 1)]
    numbers = jnp.concatenate(numbers, axis=0)
    low = (numbers[:, :LANES].astype(jnp.int32) - 1) * rows_all
    return low, low + numbers[:, LANES:].astype(jnp.int32)


def across(column, count):
    return jnp.concatenate([column] * (count // LANES), axis=1)


def compare(rows_all, query_t, query_low, query_key, lows, parts):
    rows = jnp.concatenate([rows for rows, _ in parts], axis=0)
    key = jnp.concatenate([key_rows(rows_all, digit)[1] for _, digit in parts], axis=1)
    bound = across(lows, key.shape[1])
    member = bf16((key >= bound) & (key < bound + rows_all))
    sums = matmul(member, rows)
    counts = matmul(member, jnp.ones((rows.shape[0], LANES), jnp.bfloat16))
    scores = matmul(rows, query_t)
    key = jnp.concatenate([key_columns(rows_all, digit)[1] for _, digit in parts], axis=0)
    key = across(key, query_t.shape[1])
    earlier = (key >= query_low) & (key < query_key)
    best = jnp.max(jnp.where(earlier, scores, -3.0), axis=0, keepdims=True)
    return best, sums, counts


def near_kernel(
    rows_all, clusters, clus_dev, tiles, me_ref, ints_ref, query_ref, other_ref,
    query_t_ref, lows_ref, key_ref, best_ref, sums_ref, counts_ref,
):
    hot = (ints_ref[:, :clusters] == me_ref[0]).astype(jnp.float32)
    rank = ranked(hot)
    shape = (clus_dev, clusters)
    kth = (rank == iota(shape, 0).astype(jnp.float32) + 1.0) & (hot > 0.0)
    own = jnp.sum(jnp.where(kth, iota(shape, 1).astype(jnp.float32), 0.0), axis=1, keepdims=True)
    own = jnp.broadcast_to(own.astype(jnp.int32) * rows_all, (clus_dev, LANES))
    query, digit = unpacked(query_ref, tiles)
    low, _ = key_columns(rows_all, digit)
    lows = jnp.concatenate([low, own], axis=0)
    query_low, query_key = key_rows(rows_all, digit)
    query_t = jnp.transpose(query)
    query_t_ref[...] = query_t
    parts = [(query, digit), unpacked(other_ref, tiles)]
    best, sums, counts = compare(rows_all, query_t, query_low, query_key, lows, parts)
    lows_ref[...] = lows
    key_ref[...] = jnp.concatenate([query_low, query_key], axis=0)
    best_ref[...] = best
    sums_ref[...] = sums
    counts_ref[...] = counts


def far_kernel(
    rows_all, tiles, query_ref, other_ref, query_t_ref, lows_ref, key_ref, best_ref, sums_ref, counts_ref,
    result_ref, norm_ref,
):
    query, _ = unpacked(query_ref, tiles)
    queries, width = query.shape
    best, sums, counts = compare(
        rows_all, query_t_ref[...], key_ref[0:1], key_ref[1:2], lows_ref[...], [unpacked(other_ref, tiles)]
    )
    best = jnp.maximum(best, best_ref[...])
    best = jnp.where(best > -2.0, best, 0.0)
    share = 1.0 / jnp.maximum(counts + counts_ref[...], 1.0)
    squares = jnp.zeros((queries, LANES), jnp.float32)
    norms = jnp.zeros((share.shape[0] - queries, LANES), jnp.float32)
    for start in range(0, width, LANES):
        lanes = slice(start, start + LANES)
        centroid = (sums[:, lanes] + sums_ref[:, lanes]) * share
        offset = query[:, lanes].astype(jnp.float32) - centroid[:queries]
        squares = squares + offset * offset
        norms = norms + centroid[queries:] * centroid[queries:]
    distance = jnp.sum(jnp.transpose(squares), axis=0, keepdims=True)
    result = jnp.concatenate([best, distance], axis=0)
    for owner in range(result_ref.shape[0]):
        result_ref[owner] = result
    norms = jnp.concatenate([norms] * (LANES // norms.shape[0]), axis=0)
    norm_ref[...] = jnp.sum(jnp.transpose(norms), axis=0, keepdims=True)[:, : norm_ref.shape[1]]


def pick_kernel(
    order, parts, me_ref, slot_ref, result_ref, norm_ref, best_ref, distance_ref, cohesion_ref
):
    cohesion_ref[...] = norm_ref[...]
    rows = slot_ref.shape[1]
    owners, lines, slots = result_ref.shape
    folds = min(parts, 2)
    place = iota((lines, slots), 1) % (slots // folds) // (slots // owners // folds)
    values = jnp.zeros((lines, slots), jnp.float32)
    for index, k in enumerate(order):
        owner = me_ref[0] ^ k
        member = owner
        if owners == len(MEMBERS):
            member = sum(jnp.where(owner == name, at, 0) for at, name in enumerate(MEMBERS))
        values = jnp.where(place == index, result_ref[member], values)
    values = jnp.concatenate([values, jnp.zeros((8 - lines, slots), jnp.float32)], axis=0)
    at = (iota((slots, rows), 0) == slot_ref[...]).astype(jnp.float32)
    picked = jnp.dot(
        values, at, precision=lax.Precision.HIGHEST, preferred_element_type=jnp.float32
    )
    best_ref[...] = picked[0:1]
    distance_ref[...] = picked[1:2]


def from_partner(value, k, axis):
    return lax.ppermute(value, axis, [(i, i ^ k) for i in range(lax.axis_size(axis))])


def exchange(packed, tiles):
    sent = dict(zip(SENDS, packed))
    got = {0: sent[0,]}
    for k in (4, 5, 7, 6):
        got[k] = from_partner(sent[k,], k, "shard")
    pair = from_partner(sent[2, 3], 2, "shard")
    got[2] = pair[:tiles]
    pair = from_partner(jnp.concatenate([sent[1,], pair[tiles:]]), 1, "shard")
    got[1], got[3] = pair[:tiles], pair[tiles:]
    got = [got[k] for k in PARTNERS]
    return jnp.concatenate(got[:EARLY]), jnp.concatenate(got[EARLY:])


def exchange_all(packed, me):
    owners = lax.axis_size("shard")
    tiles, half, _ = packed.shape
    each = tiles // 2
    data = packed[:-1].reshape(2, each, half, LANES).transpose(0, 2, 1, 3).reshape(2 * half, -1)
    digit = jnp.concatenate(jnp.split(packed[-1], 2, axis=1))
    parted = jnp.concatenate([data, digit], axis=1).reshape(owners, 2 * half // owners, -1)
    partner = me ^ jnp.arange(owners, dtype=jnp.int32)
    got = lax.all_to_all(parted[partner], "shard", 0, 0, tiled=True)[partner].reshape(2 * half, -1)
    data = got[:, : each * LANES].reshape(2, half, each, LANES).transpose(0, 2, 1, 3)
    digit = jnp.concatenate(jnp.split(got[:, each * LANES :], 2), axis=1)
    got = jnp.concatenate([data.reshape(2 * each, half, LANES), digit[None]])
    return jnp.split(got, 2, axis=1)


def local(embeddings, cluster_id, item_order, owner_map):
    owners = lax.axis_size("shard")
    local_rows, width = embeddings.shape
    rows_all = local_rows * owners * lax.axis_size("sub")
    clus_dev = owner_map.shape[0] // owners
    capacity = 2 * local_rows // owners
    slots = owners * capacity
    params = pltpu.CompilerParams(vmem_limit_bytes=32 << 20)
    compare_cost = pl.CostEstimate(
        flops=4 * slots * slots * width, bytes_accessed=4 * slots * width, transcendentals=0
    )
    me = lax.axis_index("shard").astype(jnp.int32).reshape(1)
    ints = jnp.concatenate([owner_map, cluster_id, item_order]).reshape(1, -1)

    direct = owners == len(PARTNERS)
    order = PARTNERS if direct else tuple(range(owners))
    parts = owners if direct else 1
    tiles = 2 * (width // LANES) + 1
    members = MEMBERS if direct else tuple(range(owners))
    sends = [[PARTNERS.index(k) for k in ks] for ks in SENDS] if direct else [[0]]
    half = slots // parts // 2
    slot, digit = pl.pallas_call(
        functools.partial(slot_kernel, owners, capacity, order, parts, local_rows),
        out_shape=[
            jax.ShapeDtypeStruct((1, local_rows), jnp.int32),
            jax.ShapeDtypeStruct((LANES, 2 * local_rows), jnp.bfloat16),
        ],
        in_specs=[SCALAR, WHOLE],
        out_specs=[WHOLE] * 2,
        compiler_params=params,
        cost_estimate=pl.CostEstimate(flops=1 << 29, bytes_accessed=1 << 16, transcendentals=0),
        name="slots",
    )(me, ints)
    packed = pl.pallas_call(
        functools.partial(pack_kernel, sends),
        out_shape=[
            jax.ShapeDtypeStruct((len(places) * tiles, half, LANES), jnp.bfloat16) for places in sends
        ],
        in_specs=[WHOLE] * 3,
        out_specs=[WHOLE] * len(sends),
        compiler_params=params,
        name="pack",
    )(slot, digit, embeddings)
    first, second = exchange(packed, tiles) if direct else exchange_all(packed[0], me[0])
    other_first, other_second = (from_partner(rows, 1, "sub") for rows in (first, second))
    query = jnp.concatenate([first, second])
    asked = slots + clus_dev
    near = pl.pallas_call(
        functools.partial(near_kernel, rows_all, owner_map.shape[0], clus_dev, tiles),
        out_shape=[
            jax.ShapeDtypeStruct((width, slots), jnp.bfloat16),
            jax.ShapeDtypeStruct((asked, LANES), jnp.int32),
            jax.ShapeDtypeStruct((2, slots), jnp.int32),
            jax.ShapeDtypeStruct((1, slots), jnp.float32),
            jax.ShapeDtypeStruct((asked, width), jnp.float32),
            jax.ShapeDtypeStruct((asked, LANES), jnp.float32),
        ],
        in_specs=[SCALAR] + [WHOLE] * 3,
        out_specs=[WHOLE] * 6,
        compiler_params=params,
        cost_estimate=compare_cost,
        name="near",
    )(me, ints, query, other_first)
    results, norms = pl.pallas_call(
        functools.partial(far_kernel, rows_all, tiles),
        out_shape=[
            jax.ShapeDtypeStruct((owners, 2, slots), jnp.float32),
            jax.ShapeDtypeStruct((1, clus_dev), jnp.float32),
        ],
        in_specs=[WHOLE] * 8,
        out_specs=[WHOLE] * 2,
        compiler_params=params,
        cost_estimate=compare_cost,
        name="far",
    )(query, other_second, *near)
    groups = [list(members)]
    results = lax.all_to_all(results, "shard", 0, 0, axis_index_groups=groups, tiled=True)
    best, distance, cohesion = pl.pallas_call(
        functools.partial(pick_kernel, order, parts),
        out_shape=[jax.ShapeDtypeStruct((1, local_rows), jnp.float32)] * 2
        + [jax.ShapeDtypeStruct((1, clus_dev), jnp.float32)],
        in_specs=[SCALAR] + [WHOLE] * 3,
        out_specs=[WHOLE] * 3,
        compiler_params=params,
        name="pick",
    )(me, slot, results, norms)
    return best.reshape(local_rows), distance.reshape(local_rows), cohesion.reshape(clus_dev)


def solution(mesh):
    in_specs = (
        P(("groups", "shard", "sub"), None),
        P(("groups", "shard", "sub")),
        P(("groups", "shard", "sub")),
        P("groups"),
    )
    out_specs = (
        P(("groups", "shard", "sub")),
        P(("groups", "shard", "sub")),
        P(("groups", "shard")),
    )
    return jax.shard_map(local, mesh=mesh, in_specs=in_specs, out_specs=out_specs, check_vma=False)
```

```python
import functools

import jax
import jax.numpy as jnp
from jax import lax
from jax.experimental import pallas as pl
from jax.experimental.pallas import tpu as pltpu
from jax.sharding import PartitionSpec as P

LANES = 128
DIGITS = 3
SENDS = ((4,), (2, 3), (5,), (7,), (6,), (1,), (0,))
PARTNERS = (4, 2, 0, 5, 7, 6, 1, 3)
MEMBERS = (7, 5, 6, 4, 3, 2, 1, 0)
WHOLE = pl.BlockSpec(memory_space=pltpu.VMEM)
SCALAR = pl.BlockSpec(memory_space=pltpu.SMEM)


def iota(shape, dim):
    return lax.broadcasted_iota(jnp.int32, shape, dim)


def matmul(a, b):
    return jnp.dot(a, b, preferred_element_type=jnp.float32)


def matmul_t(a, b):
    return lax.dot_general(a, b, (((1,), (1,)), ((), ())), preferred_element_type=jnp.float32)


def bf16(x):
    return x.astype(jnp.float32).astype(jnp.bfloat16)


def ranked(hot):
    upto = (iota((LANES, LANES), 0) <= iota((LANES, LANES), 1)).astype(jnp.bfloat16)
    before, parts = jnp.zeros((1, 1), jnp.float32), []
    for start in range(0, hot.shape[1], LANES):
        piece = hot[:, start : start + LANES]
        spread = jnp.broadcast_to(piece, (16, LANES)).astype(jnp.bfloat16)
        parts.append(matmul(spread, upto)[:1] + before)
        before = before + jnp.sum(piece, axis=1, keepdims=True)
    return jnp.concatenate(parts, axis=1)


def slot_kernel(
    owners, capacity, order, parts, rows, me_ref, ints_ref, slot_ref, digit_ref
):
    clusters = ints_ref.shape[1] - 2 * rows
    cluster = ints_ref[:, clusters : clusters + rows]
    named = bf16(iota((clusters, rows), 0) == cluster)
    owner_map = bf16(jnp.broadcast_to(ints_ref[:, :clusters], (16, clusters)))
    owner = matmul(owner_map, named)[:1].astype(jnp.int32)
    hot = (iota((max(owners, 16), rows), 0) == owner).astype(jnp.float32)
    upto = bf16(iota((rows, rows), 0) <= iota((rows, rows), 1))
    rank = jnp.sum(hot * matmul(bf16(hot), upto), axis=0, keepdims=True) - 1.0
    rank = rank.astype(jnp.int32)
    partner = owner ^ me_ref[0]
    place = partner
    for index, k in enumerate(order):
        place = jnp.where(partner == k, index, place)
    if parts == 1:
        slot_ref[...] = place * capacity + rank
    else:
        half = capacity // 2
        later = (rank >= half).astype(jnp.int32)
        slot_ref[...] = place * half + rank + later * (owners * half - half)

    line = iota((8, rows), 0)
    digit = jnp.zeros((8, rows), jnp.int32)
    for first, number in ((0, cluster + 1), (DIGITS, ints_ref[:, clusters + rows :])):
        for at in range(DIGITS):
            digit = jnp.where(line == first + at, (number >> (8 * at)) & 255, digit)
    empty = jnp.zeros((LANES // 2 - 8, rows), jnp.int32)
    none = jnp.zeros((LANES // 2, rows), jnp.int32)
    early = jnp.concatenate([digit, empty, none], axis=0)
    late = jnp.concatenate([none, digit, empty], axis=0)
    digit_ref[...] = bf16(jnp.concatenate([early, late], axis=1))


def pack_kernel(sends, slot_ref, digit_ref, embed_ref, *out_refs):
    rows, width = embed_ref.shape
    half = out_refs[0].shape[1]
    tiles = 2 * (width // LANES) + 1
    values = embed_ref[...].astype(jnp.float32)
    mean_sq = jnp.sum(values * values, axis=1, keepdims=True) * (1.0 / width)
    unit = (values * lax.rsqrt(width * (mean_sq + 1e-06))).astype(jnp.bfloat16)
    late = half * sum(len(places) for places in sends)
    move = bf16(iota((2 * late, rows), 0) == slot_ref[...])
    moved = matmul(move, unit).astype(jnp.bfloat16)
    both = jnp.concatenate([move[:late], move[late:]], axis=1)
    digit = matmul_t(both, digit_ref[...]).astype(jnp.bfloat16)
    each = tiles // 2
    for places, out_ref in zip(sends, out_refs):
        for index, place in enumerate(places):
            base, start = index * tiles, place * half
            for tile in range(each):
                lanes = slice(tile * LANES, (tile + 1) * LANES)
                out_ref[base + tile] = moved[start : start + half, lanes]
                out_ref[base + each + tile] = moved[late + start : late + start + half, lanes]
            out_ref[base + tiles - 1] = digit[start : start + half]


def unpacked(block_ref, tiles):
    blocks = block_ref.shape[0] // tiles
    each = tiles // 2

    def column(tile):
        return jnp.concatenate([block_ref[i * tiles + tile] for i in range(blocks)], axis=0)

    halves = [
        jnp.concatenate([column(first + tile) for tile in range(each)], axis=1)
        for first in (0, each)
    ]
    return jnp.concatenate(halves, axis=0), column(tiles - 1)


def weights(number, at, half):
    value = jnp.zeros(at.shape, jnp.float32)
    for place in range(DIGITS):
        for which in (0, 1):
            lane = half * (LANES // 2) + which * DIGITS + place
            value = jnp.where((at == lane) & (number == which), 256.0**place, value)
    return value.astype(jnp.bfloat16)


def key_rows(rows_all, digit):
    at = iota((16, LANES), 0), iota((16, LANES), 1)
    numbers = [matmul_t(weights(*at, half), digit) for half in (0, 1)]
    numbers = jnp.concatenate(numbers, axis=1)
    low = (numbers[0:1].astype(jnp.int32) - 1) * rows_all
    return low, low + numbers[1:2].astype(jnp.int32)


def key_columns(rows_all, digit):
    at = iota((LANES, 2 * LANES), 1) // LANES, iota((LANES, 2 * LANES), 0)
    numbers = [matmul(digit, weights(*at, half)) for half in (0, 1)]
    numbers = jnp.concatenate(numbers, axis=0)
    low = (numbers[:, :LANES].astype(jnp.int32) - 1) * rows_all
    return low, low + numbers[:, LANES:].astype(jnp.int32)


def across(column, count):
    return jnp.concatenate([column] * (count // LANES), axis=1)


def compare(rows_all, query_t, query_low, query_key, lows, parts):
    rows = jnp.concatenate([rows for rows, _ in parts], axis=0)
    key = jnp.concatenate([key_rows(rows_all, digit)[1] for _, digit in parts], axis=1)
    bound = across(lows, key.shape[1])
    member = bf16((key >= bound) & (key < bound + rows_all))
    sums = matmul(member, rows)
    counts = matmul(member, jnp.ones((rows.shape[0], LANES), jnp.bfloat16))
    scores = matmul(rows, query_t)
    key = jnp.concatenate([key_columns(rows_all, digit)[1] for _, digit in parts], axis=0)
    key = across(key, query_t.shape[1])
    earlier = (key >= query_low) & (key < query_key)
    best = jnp.max(jnp.where(earlier, scores, -3.0), axis=0, keepdims=True)
    return best, sums, counts


def near_kernel(
    rows_all, clusters, clus_dev, tiles, me_ref, ints_ref, query_ref, other_ref,
    query_t_ref, lows_ref, key_ref, best_ref, sums_ref, counts_ref,
):
    hot = (ints_ref[:, :clusters] == me_ref[0]).astype(jnp.float32)
    rank = ranked(hot)
    shape = (clus_dev, clusters)
    kth = (rank == iota(shape, 0).astype(jnp.float32) + 1.0) & (hot > 0.0)
    own = jnp.sum(jnp.where(kth, iota(shape, 1).astype(jnp.float32), 0.0), axis=1, keepdims=True)
    own = jnp.broadcast_to(own.astype(jnp.int32) * rows_all, (clus_dev, LANES))
    query, digit = unpacked(query_ref, tiles)
    low, _ = key_columns(rows_all, digit)
    lows = jnp.concatenate([low, own], axis=0)
    query_low, query_key = key_rows(rows_all, digit)
    query_t = jnp.transpose(query)
    query_t_ref[...] = query_t
    parts = [(query, digit), unpacked(other_ref, tiles)]
    best, sums, counts = compare(rows_all, query_t, query_low, query_key, lows, parts)
    lows_ref[...] = lows
    key_ref[...] = jnp.concatenate([query_low, query_key], axis=0)
    best_ref[...] = best
    sums_ref[...] = sums
    counts_ref[...] = counts


def far_kernel(
    rows_all, tiles, query_ref, other_ref, query_t_ref, lows_ref, key_ref, best_ref, sums_ref, counts_ref,
    result_ref, norm_ref,
):
    query, _ = unpacked(query_ref, tiles)
    queries, width = query.shape
    best, sums, counts = compare(
        rows_all, query_t_ref[...], key_ref[0:1], key_ref[1:2], lows_ref[...], [unpacked(other_ref, tiles)]
    )
    best = jnp.maximum(best, best_ref[...])
    best = jnp.where(best > -2.0, best, 0.0)
    share = 1.0 / jnp.maximum(counts + counts_ref[...], 1.0)
    squares = jnp.zeros((queries, LANES), jnp.float32)
    norms = jnp.zeros((share.shape[0] - queries, LANES), jnp.float32)
    for start in range(0, width, LANES):
        lanes = slice(start, start + LANES)
        centroid = (sums[:, lanes] + sums_ref[:, lanes]) * share
        offset = query[:, lanes].astype(jnp.float32) - centroid[:queries]
        squares = squares + offset * offset
        norms = norms + centroid[queries:] * centroid[queries:]
    distance = jnp.sum(jnp.transpose(squares), axis=0, keepdims=True)
    result = jnp.concatenate([best, distance], axis=0)
    for owner in range(result_ref.shape[0]):
        result_ref[owner] = result
    norms = jnp.concatenate([norms] * (LANES // norms.shape[0]), axis=0)
    norm_ref[...] = jnp.sum(jnp.transpose(norms), axis=0, keepdims=True)[:, : norm_ref.shape[1]]


def pick_kernel(
    order, parts, me_ref, slot_ref, result_ref, norm_ref, best_ref, distance_ref, cohesion_ref
):
    cohesion_ref[...] = norm_ref[...]
    rows = slot_ref.shape[1]
    owners, lines, slots = result_ref.shape
    folds = min(parts, 2)
    place = iota((lines, slots), 1) % (slots // folds) // (slots // owners // folds)
    values = jnp.zeros((lines, slots), jnp.float32)
    for index, k in enumerate(order):
        owner = me_ref[0] ^ k
        member = owner
        if owners == len(MEMBERS):
            member = sum(jnp.where(owner == name, at, 0) for at, name in enumerate(MEMBERS))
        values = jnp.where(place == index, result_ref[member], values)
    values = jnp.concatenate([values, jnp.zeros((8 - lines, slots), jnp.float32)], axis=0)
    at = (iota((slots, rows), 0) == slot_ref[...]).astype(jnp.float32)
    picked = jnp.dot(
        values, at, precision=lax.Precision.HIGHEST, preferred_element_type=jnp.float32
    )
    best_ref[...] = picked[0:1]
    distance_ref[...] = picked[1:2]


def from_partner(value, k, axis):
    return lax.ppermute(value, axis, [(i, i ^ k) for i in range(lax.axis_size(axis))])


def exchange(packed, tiles):
    sent = dict(zip(SENDS, packed))
    got = {0: sent[0,]}
    for k in (4, 5, 7, 6):
        got[k] = from_partner(sent[k,], k, "shard")
    pair = from_partner(sent[2, 3], 2, "shard")
    got[2] = pair[:tiles]
    pair = from_partner(jnp.concatenate([sent[1,], pair[tiles:]]), 1, "shard")
    got[1], got[3] = pair[:tiles], pair[tiles:]
    got = [got[k] for k in PARTNERS]
    half = len(got) // 2
    return jnp.concatenate(got[:half]), jnp.concatenate(got[half:])


def exchange_all(packed, me):
    owners = lax.axis_size("shard")
    tiles, half, _ = packed.shape
    each = tiles // 2
    data = packed[:-1].reshape(2, each, half, LANES).transpose(0, 2, 1, 3).reshape(2 * half, -1)
    digit = jnp.concatenate(jnp.split(packed[-1], 2, axis=1))
    parted = jnp.concatenate([data, digit], axis=1).reshape(owners, 2 * half // owners, -1)
    partner = me ^ jnp.arange(owners, dtype=jnp.int32)
    got = lax.all_to_all(parted[partner], "shard", 0, 0, tiled=True)[partner].reshape(2 * half, -1)
    data = got[:, : each * LANES].reshape(2, half, each, LANES).transpose(0, 2, 1, 3)
    digit = jnp.concatenate(jnp.split(got[:, each * LANES :], 2), axis=1)
    got = jnp.concatenate([data.reshape(2 * each, half, LANES), digit[None]])
    return jnp.split(got, 2, axis=1)


def local(embeddings, cluster_id, item_order, owner_map):
    owners = lax.axis_size("shard")
    local_rows, width = embeddings.shape
    rows_all = local_rows * owners * lax.axis_size("sub")
    clus_dev = owner_map.shape[0] // owners
    capacity = 2 * local_rows // owners
    slots = owners * capacity
    params = pltpu.CompilerParams(vmem_limit_bytes=32 << 20)
    compare_cost = pl.CostEstimate(
        flops=4 * slots * slots * width, bytes_accessed=4 * slots * width, transcendentals=0
    )
    me = lax.axis_index("shard").astype(jnp.int32).reshape(1)
    ints = jnp.concatenate([owner_map, cluster_id, item_order]).reshape(1, -1)

    direct = owners == len(PARTNERS)
    order = PARTNERS if direct else tuple(range(owners))
    parts = owners if direct else 1
    tiles = 2 * (width // LANES) + 1
    members = MEMBERS if direct else tuple(range(owners))
    sends = [[PARTNERS.index(k) for k in ks] for ks in SENDS] if direct else [[0]]
    half = slots // parts // 2
    slot, digit = pl.pallas_call(
        functools.partial(slot_kernel, owners, capacity, order, parts, local_rows),
        out_shape=[
            jax.ShapeDtypeStruct((1, local_rows), jnp.int32),
            jax.ShapeDtypeStruct((LANES, 2 * local_rows), jnp.bfloat16),
        ],
        in_specs=[SCALAR, WHOLE],
        out_specs=[WHOLE] * 2,
        compiler_params=params,
        cost_estimate=pl.CostEstimate(flops=1 << 29, bytes_accessed=1 << 16, transcendentals=0),
        name="slots",
    )(me, ints)
    packed = pl.pallas_call(
        functools.partial(pack_kernel, sends),
        out_shape=[
            jax.ShapeDtypeStruct((len(places) * tiles, half, LANES), jnp.bfloat16) for places in sends
        ],
        in_specs=[WHOLE] * 3,
        out_specs=[WHOLE] * len(sends),
        compiler_params=params,
        name="pack",
    )(slot, digit, embeddings)
    first, second = exchange(packed, tiles) if direct else exchange_all(packed[0], me[0])
    other_first, other_second = (from_partner(rows, 1, "sub") for rows in (first, second))
    query = jnp.concatenate([first, second])
    asked = slots + clus_dev
    near = pl.pallas_call(
        functools.partial(near_kernel, rows_all, owner_map.shape[0], clus_dev, tiles),
        out_shape=[
            jax.ShapeDtypeStruct((width, slots), jnp.bfloat16),
            jax.ShapeDtypeStruct((asked, LANES), jnp.int32),
            jax.ShapeDtypeStruct((2, slots), jnp.int32),
            jax.ShapeDtypeStruct((1, slots), jnp.float32),
            jax.ShapeDtypeStruct((asked, width), jnp.float32),
            jax.ShapeDtypeStruct((asked, LANES), jnp.float32),
        ],
        in_specs=[SCALAR] + [WHOLE] * 3,
        out_specs=[WHOLE] * 6,
        compiler_params=params,
        cost_estimate=compare_cost,
        name="near",
    )(me, ints, query, other_first)
    results, norms = pl.pallas_call(
        functools.partial(far_kernel, rows_all, tiles),
        out_shape=[
            jax.ShapeDtypeStruct((owners, 2, slots), jnp.float32),
            jax.ShapeDtypeStruct((1, clus_dev), jnp.float32),
        ],
        in_specs=[WHOLE] * 8,
        out_specs=[WHOLE] * 2,
        compiler_params=params,
        cost_estimate=compare_cost,
        name="far",
    )(query, other_second, *near)
    groups = [list(members)]
    results = lax.all_to_all(results, "shard", 0, 0, axis_index_groups=groups, tiled=True)
    best, distance, cohesion = pl.pallas_call(
        functools.partial(pick_kernel, order, parts),
        out_shape=[jax.ShapeDtypeStruct((1, local_rows), jnp.float32)] * 2
        + [jax.ShapeDtypeStruct((1, clus_dev), jnp.float32)],
        in_specs=[SCALAR] + [WHOLE] * 3,
        out_specs=[WHOLE] * 3,
        compiler_params=params,
        name="pick",
    )(me, slot, results, norms)
    return best.reshape(local_rows), distance.reshape(local_rows), cohesion.reshape(clus_dev)


def solution(mesh):
    in_specs = (
        P(("groups", "shard", "sub"), None),
        P(("groups", "shard", "sub")),
        P(("groups", "shard", "sub")),
        P("groups"),
    )
    out_specs = (
        P(("groups", "shard", "sub")),
        P(("groups", "shard", "sub")),
        P(("groups", "shard")),
    )
    return jax.shard_map(local, mesh=mesh, in_specs=in_specs, out_specs=out_specs, check_vma=False)
```
